32 devices in a mesh: groups: 2 (over y), row: 16 (over z, x, core).
Axes of the slice: x: 2, y: 2, z: 4, core: 2. Of those that a mesh axis runs over, the one named last changes fastest.
Arguments:
- pair_rep: bfloat16 [96, 48, 128], P(('groups', 'row')), parts along dimension 0, may hold values from -6 to 6
- residue_valid: int32 [96], P('groups'), parts along dimension 0, may hold values from 0 to 1
- tri_norm_gain: float32 [128], replicated, may hold values from 0.5 to 1.5
- tri_norm_bias: float32 [128], replicated, may hold values from -3 to 3
- w_edges: bfloat16 [128, 512], replicated, may hold values from -0.5 to 0.5
- w_tri_gate: bfloat16 [128, 128], replicated, may hold values from -0.5 to 0.5
- out_norm_gain: float32 [128], replicated, may hold values from 0.5 to 1.5
- out_norm_bias: float32 [128], replicated, may hold values from -3 to 3
- w_tri_out: bfloat16 [128, 128], replicated, may hold values from -0.5 to 0.5
- att_norm_gain: float32 [128], replicated, may hold values from 0.5 to 1.5
- att_norm_bias: float32 [128], replicated, may hold values from -3 to 3
- w_query: bfloat16 [128, 128], replicated, may hold values from -2.4748737 to 2.4748737
- w_key: bfloat16 [128, 128], replicated, may hold values from -2.4748737 to 2.4748737
- w_value: bfloat16 [128, 128], replicated, may hold values from -0.5 to 0.5
- w_att_gate: bfloat16 [128, 128], replicated, may hold values from -0.5 to 0.5
- w_pair_bias: bfloat16 [128, 4], replicated, may hold values from -1.0546875 to 1.0546875
- w_att_out: bfloat16 [128, 128], replicated, may hold values from -0.5 to 0.5
Outputs:
- updated_pair: bfloat16 [96, 48, 128], P(('groups', 'row')), parts along dimension 0
The draws below stay inside these ranges and needn't reach their ends.
There are 2 independent parts, one for each index of `groups`. The reference program is written for one: setup_inputs(seed, part) draws one part's arguments, and reference() takes and returns one part's arrays. A program takes and returns all parts, laid end to end along the dimension named above; an argument that names none is the same for every part. Nothing has to cross between parts.
All inputs are finite; a program needn't handle non-finite values.
Results may differ from the reference program's by a relative error of at most 0.0097.
Values may be sent and summed in bfloat16 or wider, within the bound.
No kernel may reach another device: no remote copies, remote signals or barrier semaphores. Data moves between devices by JAX's collectives and lax.ppermute only.
A program may use at most 64 MiB of HBM per device.

```python
import math
import jax
import jax.numpy as jnp
from jax import lax

C = 128
HEADS = 4
HEAD_DIM = 32
N_RES = 48


def draw_residue_valid(key, part):
    flags = (jax.random.randint(key, (N_RES,), 0, 8) > 0).astype(jnp.int32)
    return flags.at[0].set(1)


def draw_w_query(key, part):
    result = jnp.clip(jax.random.normal(jax.random.fold_in(key, 11), (C, HEADS * HEAD_DIM), jnp.float32), -4.0, 4.0) / C ** 0.5
    return jnp.clip(result, -28.0 / C ** 0.5, 28.0 / C ** 0.5).astype(jnp.bfloat16)


def draw_w_key(key, part):
    result = jnp.clip(jax.random.normal(jax.random.fold_in(key, 13), (C, HEADS * HEAD_DIM), jnp.float32), -4.0, 4.0) / C ** 0.5
    return jnp.clip(result, -28.0 / C ** 0.5, 28.0 / C ** 0.5).astype(jnp.bfloat16)


def level_of(key, shape, shards, low, largest):
    def one(position, shards_of):
        steps = jax.random.uniform(jax.random.fold_in(jax.random.fold_in(key, 6), position), (shards_of,), jnp.float32, low / len(shards), largest / len(shards))
        return jnp.repeat(jnp.exp(steps), shape[position] // shards_of).reshape((-1,) + (1,) * (len(shape) - position - 1))

    gain = one(*shards[0])
    for cut in shards[1:]:
        gain = gain * one(*cut)
    return gain


def normal_values(rng, extent, scale, limit, shards=(), held_as=jnp.bfloat16):
    gain = level_of(rng, extent, shards, -0.22, 0.18) if shards else 1.0
    drawn = jax.random.normal(rng, extent, jnp.float32) * scale * gain
    return jnp.minimum(jnp.maximum(drawn, -limit), limit).astype(held_as)


def setup_inputs(seed: int = 0, part: int = 0) -> dict:
    key_of = jax.random.split(jax.random.key(seed), 18)
    part_keys = jax.random.split(jax.random.fold_in(key_of[17], part), 18)
    pair_rep = normal_values(part_keys[0], (N_RES, N_RES, C), 1.0, 6.0, ((0, 16),))
    residue_valid = draw_residue_valid(jax.random.fold_in(jax.random.fold_in(key_of[17], part), 71), part)
    tri_norm_gain = jnp.clip(1.0 + 0.1 * jax.random.normal(key_of[2], (C,), jnp.float32), 0.5, 1.5)
    tri_norm_bias = normal_values(key_of[3], (C,), 0.5, 3.0, (), jnp.float32)
    w_edges = normal_values(key_of[4], (C, 4 * C), C ** -0.5, 0.5)
    w_tri_gate = normal_values(key_of[5], (C, C), C ** -0.5, 0.5)
    out_norm_gain = jnp.clip(1.0 + 0.1 * jax.random.normal(key_of[6], (C,), jnp.float32), 0.5, 1.5)
    out_norm_bias = normal_values(key_of[7], (C,), 0.5, 3.0, (), jnp.float32)
    w_tri_out = normal_values(key_of[8], (C, C), C ** -0.5, 0.5)
    att_norm_gain = jnp.clip(1.0 + 0.1 * jax.random.normal(key_of[9], (C,), jnp.float32), 0.5, 1.5)
    att_norm_bias = normal_values(key_of[10], (C,), 0.5, 3.0, (), jnp.float32)
    w_query = draw_w_query(jax.random.fold_in(key_of[17], 71), part)
    w_key = draw_w_key(jax.random.fold_in(key_of[17], 71), part)
    w_value = normal_values(key_of[13], (C, HEADS * HEAD_DIM), C ** -0.5, 0.5)
    w_att_gate = normal_values(key_of[14], (C, HEADS * HEAD_DIM), C ** -0.5, 0.5)
    w_pair_bias = normal_values(key_of[15], (C, HEADS), (1.5 / C ** 0.5), 1.0546875)
    w_att_out = normal_values(key_of[16], (HEADS * HEAD_DIM, C), (HEADS * HEAD_DIM) ** -0.5, 0.5)
    return {"pair_rep": pair_rep, "residue_valid": residue_valid, "tri_norm_gain": tri_norm_gain, "tri_norm_bias": tri_norm_bias, "w_edges": w_edges, "w_tri_gate": w_tri_gate, "out_norm_gain": out_norm_gain, "out_norm_bias": out_norm_bias, "w_tri_out": w_tri_out, "att_norm_gain": att_norm_gain, "att_norm_bias": att_norm_bias, "w_query": w_query, "w_key": w_key, "w_value": w_value, "w_att_gate": w_att_gate, "w_pair_bias": w_pair_bias, "w_att_out": w_att_out}


def layer_norm(values, norm_gain, norm_bias):
    centre = values - lax.optimization_barrier(jnp.mean(values, axis=-1, keepdims=True))
    spread = lax.optimization_barrier(jnp.mean(centre * centre, axis=-1, keepdims=True))
    return centre * lax.rsqrt(spread + 1e-05) * norm_gain + norm_bias

def reference(pair_rep, residue_valid, tri_norm_gain, tri_norm_bias, w_edges, w_tri_gate, out_norm_gain, out_norm_bias, w_tri_out, att_norm_gain, att_norm_bias, w_query, w_key, w_value, w_att_gate, w_pair_bias, w_att_out):
    res_count = pair_rep.shape[0]
    hidden_width = HEADS * HEAD_DIM
    valid_flags = residue_valid.astype(jnp.float32)
    normed = layer_norm(pair_rep.astype(jnp.float32), tri_norm_gain, tri_norm_bias).astype(jnp.bfloat16)
    flat_normed = normed.reshape(-1, C)
    projected = jnp.dot(flat_normed, w_edges, preferred_element_type=jnp.float32).reshape(res_count, res_count, 4, C)
    pair_mask = (valid_flags[:, None] * valid_flags[None, :])[:, :, None]
    left_edges = (jax.nn.sigmoid(projected[:, :, 1]) * projected[:, :, 0] * pair_mask).astype(jnp.bfloat16)
    right_edges = (jax.nn.sigmoid(projected[:, :, 3]) * projected[:, :, 2] * pair_mask).astype(jnp.bfloat16)
    triangle = jnp.einsum('ikc,jkc->ijc', left_edges.astype(jnp.float32), right_edges.astype(jnp.float32), precision=lax.Precision.HIGHEST).astype(jnp.bfloat16)
    tri_normed = layer_norm(triangle.astype(jnp.float32), out_norm_gain, out_norm_bias).astype(jnp.bfloat16)
    tri_gate = jax.nn.sigmoid(jnp.dot(flat_normed, w_tri_gate, preferred_element_type=jnp.float32))
    tri_update = jnp.dot(tri_normed.reshape(-1, C), w_tri_out, preferred_element_type=jnp.float32)
    after_tri = pair_rep.astype(jnp.float32) + (tri_gate * tri_update).reshape(res_count, res_count, C)
    att_in = layer_norm(after_tri, att_norm_gain, att_norm_bias).astype(jnp.bfloat16)
    flat_in = att_in.reshape(-1, C)
    query_all = jnp.dot(flat_in, w_query, preferred_element_type=jnp.float32).astype(jnp.bfloat16).reshape(res_count, res_count, HEADS, HEAD_DIM)
    key_all = jnp.dot(flat_in, w_key, preferred_element_type=jnp.float32).astype(jnp.bfloat16).reshape(res_count, res_count, HEADS, HEAD_DIM)
    value_all = jnp.dot(flat_in, w_value, preferred_element_type=jnp.float32).astype(jnp.bfloat16).reshape(res_count, res_count, HEADS, HEAD_DIM)
    att_gate = jax.nn.sigmoid(jnp.dot(flat_in, w_att_gate, preferred_element_type=jnp.float32)).reshape(res_count, res_count, hidden_width)
    pair_bias = jnp.dot(flat_in, w_pair_bias, preferred_element_type=jnp.float32).astype(jnp.bfloat16).reshape(res_count, res_count, HEADS)
    bias_hki = jnp.transpose(pair_bias, (2, 0, 1)).astype(jnp.float32)
    key_mask = 1000000000.0 * (valid_flags - 1.0)
    factor = 1.0 / math.sqrt(HEAD_DIM)

    def one_column(column_data):
        query_col, key_col, value_col = column_data
        scores = jnp.einsum('khd,ihd->hki', key_col.astype(jnp.float32), query_col.astype(jnp.float32)) * factor
        scores = scores + bias_hki + key_mask[None, :, None]
        scores = scores - lax.optimization_barrier(jnp.max(scores, axis=1, keepdims=True))
        exponent = jnp.exp(scores)
        weights = (exponent / lax.optimization_barrier(jnp.sum(exponent, axis=1, keepdims=True))).astype(jnp.bfloat16)
        return jnp.einsum('hki,khd->ihd', weights.astype(jnp.float32), value_col.astype(jnp.float32))
    attended = lax.map(one_column, (jnp.swapaxes(query_all, 0, 1), jnp.swapaxes(key_all, 0, 1), jnp.swapaxes(value_all, 0, 1)))
    attended = jnp.swapaxes(attended, 0, 1).reshape(res_count, res_count, hidden_width)
    gated = (attended * att_gate).astype(jnp.bfloat16)
    final = after_tri + jnp.dot(gated.reshape(-1, hidden_width), w_att_out, preferred_element_type=jnp.float32).reshape(res_count, res_count, C)
    return final.astype(jnp.bfloat16)
```

```python
import functools
import math

import jax
import jax.numpy as jnp
from jax import lax
from jax.experimental import pallas as pl
from jax.experimental.pallas import tpu as pltpu
from jax.sharding import PartitionSpec as P

HEADS = 4
HEAD_DIM = 32


def layer_norm(values, norm_gain, norm_bias, along_axis):
    centre = values - jnp.mean(values, axis=along_axis, keepdims=True)
    spread = jnp.mean(centre * centre, axis=along_axis, keepdims=True)
    return centre * lax.rsqrt(spread + 1e-05) * norm_gain + norm_bias


def attend(query_cols, key_cols, value_cols, whole_bias, key_mask):
    factor = 1.0 / math.sqrt(HEAD_DIM)
    scores = (
        jnp.einsum("kjhd,ijhd->jhki", key_cols, query_cols, preferred_element_type=jnp.float32)
        * factor
    )
    scores = scores + whole_bias.astype(jnp.float32)[None] + key_mask[None, None, :, None]
    scores = scores - jnp.max(scores, axis=2, keepdims=True)
    exponent = jnp.exp(scores)
    weights = (exponent / jnp.sum(exponent, axis=2, keepdims=True)).astype(jnp.bfloat16)
    return jnp.einsum("jhki,kjhd->ijhd", weights, value_cols, preferred_element_type=jnp.float32)


def split_over_devices(
    pair_rep,
    residue_valid,
    tri_norm_gain,
    tri_norm_bias,
    w_edges,
    w_tri_gate,
    out_norm_gain,
    out_norm_bias,
    w_tri_out,
    att_norm_gain,
    att_norm_bias,
    w_query,
    w_key,
    w_value,
    w_att_gate,
    w_pair_bias,
    w_att_out,
):
    row_count = pair_rep.shape[0]
    res_count = pair_rep.shape[1]
    channels = pair_rep.shape[2]
    hidden_width = HEADS * HEAD_DIM
    row_start = lax.axis_index("row") * row_count
    valid_flags = residue_valid.astype(jnp.float32)
    own_valid = lax.dynamic_slice_in_dim(valid_flags, row_start, row_count)
    normed = layer_norm(pair_rep.astype(jnp.float32), tri_norm_gain, tri_norm_bias, 2).astype(
        jnp.bfloat16
    )
    projected = jnp.einsum("ikd,de->eik", normed, w_edges, preferred_element_type=jnp.float32)
    projected = projected.reshape(4, channels, row_count, res_count)
    pair_mask = (own_valid[:, None] * valid_flags[None, :])[None, :, :]
    left_edges = (jax.nn.sigmoid(projected[1]) * projected[0] * pair_mask).astype(jnp.bfloat16)
    right_edges = (jax.nn.sigmoid(projected[3]) * projected[2] * pair_mask).astype(jnp.bfloat16)
    left_cols, right_cols = (
        lax.all_to_all(left_edges, "row", split_axis=0, concat_axis=1, tiled=True),
        lax.all_to_all(right_edges, "row", split_axis=0, concat_axis=1, tiled=True),
    )
    block_product = jnp.einsum(
        "cik,cjk->cij", left_cols, right_cols, preferred_element_type=jnp.float32
    ).astype(jnp.bfloat16)
    triangle = lax.all_to_all(block_product, "row", split_axis=1, concat_axis=0, tiled=True)
    tri_normed = layer_norm(
        triangle.astype(jnp.float32), out_norm_gain[:, None, None], out_norm_bias[:, None, None], 0
    ).astype(jnp.bfloat16)
    tri_gate = jax.nn.sigmoid(
        jnp.einsum("ijc,ce->ije", normed, w_tri_gate, preferred_element_type=jnp.float32)
    )
    tri_update = jnp.einsum(
        "cij,ce->ije", tri_normed, w_tri_out, preferred_element_type=jnp.float32
    )
    after_tri = pair_rep.astype(jnp.float32) + tri_gate * tri_update
    att_in = layer_norm(after_tri, att_norm_gain, att_norm_bias, 2).astype(jnp.bfloat16)
    pair_bias = jnp.einsum(
        "kic,ch->hki", att_in, w_pair_bias, preferred_element_type=jnp.float32
    ).astype(jnp.bfloat16)
    whole_bias = lax.all_gather(pair_bias, "row", axis=1, tiled=True)
    key_mask = 1000000000.0 * (valid_flags - 1.0)
    columns = lax.all_to_all(att_in, "row", split_axis=1, concat_axis=0, tiled=True)
    all_weights = jnp.concatenate([w_query, w_key, w_value, w_att_gate], axis=1)
    joined = jnp.dot(columns.reshape(-1, channels), all_weights, preferred_element_type=jnp.float32)
    query_cols = (
        joined[:, :hidden_width].astype(jnp.bfloat16).reshape(res_count, row_count, HEADS, HEAD_DIM)
    )
    key_cols = (
        joined[:, hidden_width : 2 * hidden_width]
        .astype(jnp.bfloat16)
        .reshape(res_count, row_count, HEADS, HEAD_DIM)
    )
    value_cols = (
        joined[:, 2 * hidden_width : 3 * hidden_width]
        .astype(jnp.bfloat16)
        .reshape(res_count, row_count, HEADS, HEAD_DIM)
    )
    gate_cols = jax.nn.sigmoid(joined[:, 3 * hidden_width :]).reshape(
        res_count, row_count, hidden_width
    )
    attended = attend(query_cols, key_cols, value_cols, whole_bias, key_mask)
    gated = (attended.reshape(res_count, row_count, hidden_width) * gate_cols).astype(jnp.bfloat16)
    gated_rows = lax.all_to_all(gated, "row", split_axis=0, concat_axis=1, tiled=True)
    final = after_tri + jnp.einsum(
        "ije,ec->ijc", gated_rows, w_att_out, preferred_element_type=jnp.float32
    )
    return final.astype(jnp.bfloat16)


def sigmoid(values):
    return 0.5 * jnp.tanh(0.5 * values) + 0.5


def dot(left, right):
    return jnp.dot(left, right, preferred_element_type=jnp.float32)


def whole_complex_kernel(
    row_count,
    pair_ref,
    valid_scalars,
    valid_ref,
    tri_norm_gain,
    tri_norm_bias,
    w_edges,
    w_tri_gate,
    out_norm_gain,
    out_norm_bias,
    w_tri_out,
    att_norm_gain,
    att_norm_bias,
    w_query,
    w_key,
    w_value,
    w_att_gate,
    w_pair_bias,
    w_att_out,
    out_ref,
    normed_ref,
    left_ref,
    right_ref,
    after_ref,
    att_ref,
    key_ref,
    value_ref,
    score_ref,
    bias_ref,
):
    f32, bf16 = jnp.float32, jnp.bfloat16
    res = pair_ref.shape[0]
    channels = pair_ref.shape[2]
    chunk = 4
    height = chunk * res
    own = lax.axis_index("row") * row_count

    diagonal = lax.broadcasted_iota(jnp.int32, (res, res), 0) == lax.broadcasted_iota(
        jnp.int32, (res, res), 1
    )
    spread_valid = jnp.where(diagonal, valid_ref[...].astype(f32), 0.0)
    valid_column = jnp.broadcast_to(
        jnp.sum(spread_valid, axis=1, keepdims=True), (res, channels)
    )

    def edges_of(step, carry):
        first = step * chunk
        start = pl.multiple_of(first * res, height)
        pairs = pair_ref[pl.ds(first, chunk)].astype(f32).reshape(height, channels)
        normed = layer_norm(pairs, tri_norm_gain[...], tri_norm_bias[...], 1).astype(bf16)
        normed_ref[pl.ds(start, height), :] = normed
        projected = dot(normed, w_edges[...])
        pa, ga, pb, gb = (projected[:, e * channels : (e + 1) * channels] for e in range(4))
        left = sigmoid(ga) * pa
        right = sigmoid(gb) * pb
        for r in range(chunk):
            rows = slice(r * res, (r + 1) * res)
            mask = valid_column * valid_scalars[first + r].astype(f32)
            left_ref[pl.ds(start + r * res, res), :] = (left[rows] * mask).astype(bf16).astype(f32)
            right_ref[pl.ds(first + r, res, stride=res), :] = (
                (right[rows] * mask).astype(bf16).astype(f32)
            )
        return carry

    lax.fori_loop(0, res // chunk, edges_of, 0)

    key_value = jnp.concatenate([w_key[...], w_value[...]], axis=1)

    def triangle_of(step, carry):
        first = step * chunk
        start = pl.multiple_of(first * res, height)
        totals = [jnp.zeros((res, channels), f32) for _ in range(chunk)]
        for k in range(res):
            right = right_ref[pl.ds(k * res, res), :]
            for r in range(chunk):
                totals[r] = totals[r] + left_ref[pl.ds(start + r * res + k, 1), :] * right
        triangle = jnp.concatenate(totals, axis=0).astype(bf16).astype(f32)
        tri_normed = layer_norm(triangle, out_norm_gain[...], out_norm_bias[...], 1).astype(bf16)
        gate = sigmoid(dot(normed_ref[pl.ds(start, height), :], w_tri_gate[...]))
        pairs = pair_ref[pl.ds(first, chunk)].astype(f32).reshape(height, channels)
        after_tri = pairs + gate * dot(tri_normed, w_tri_out[...])
        after_ref[pl.ds(start, height), :] = after_tri
        att_in = layer_norm(after_tri, att_norm_gain[...], att_norm_bias[...], 1).astype(bf16)
        att_ref[pl.ds(start, height), :] = att_in.astype(f32)
        joined = dot(att_in, key_value)
        key_ref[pl.ds(start, height), :] = joined[:, :channels].astype(bf16).astype(f32)
        value_ref[pl.ds(start, height), :] = joined[:, channels:].astype(bf16).astype(f32)
        return carry

    lax.fori_loop(0, res // chunk, triangle_of, 0)

    factor = 1.0 / math.sqrt(HEAD_DIM)
    head_of_row = lax.broadcasted_iota(jnp.int32, (2 * channels, channels), 0) % channels // HEAD_DIM
    head_of_column = lax.broadcasted_iota(jnp.int32, (2 * channels, channels), 1) // HEAD_DIM
    same_head = jnp.where(head_of_row == head_of_column, 1.0, 0.0).astype(bf16)
    to_head = lax.broadcasted_iota(jnp.int32, (HEADS, channels), 0)
    to_column = lax.broadcasted_iota(jnp.int32, (HEADS, channels), 1) // HEAD_DIM
    repeat_head = jnp.where(to_head == to_column, 1.0, 0.0).astype(bf16)
    wide_bias = dot(w_pair_bias[...], repeat_head).astype(bf16)

    own_start = pl.multiple_of(own * res, res)
    own_in = att_ref[pl.ds(own_start, row_count * res), :].astype(bf16)
    query = dot(own_in, w_query[...]).astype(bf16).astype(f32)
    att_gate = sigmoid(dot(own_in, w_att_gate[...]))
    for r in range(row_count):
        column = att_ref[pl.ds(own + r, res, stride=res), :].astype(bf16)
        bias_ref[r * res : (r + 1) * res, :] = dot(column, wide_bias).astype(bf16).astype(f32)

    def scores_of(step, maxima):
        maxima = list(maxima)
        for offset in range(chunk):
            k = step * chunk + offset
            key_mask = 1000000000.0 * (valid_scalars[k].astype(f32) - 1.0)
            keys = key_ref[pl.ds(k * res, res), :]
            for r in range(row_count):
                product = query[r * res : (r + 1) * res] * keys
                high = product.astype(bf16)
                low = (product - high.astype(f32)).astype(bf16)
                scores = dot(jnp.concatenate([high, low], axis=1), same_head) * factor
                scores = scores + bias_ref[pl.ds(r * res + k, 1), :] + key_mask
                score_ref[pl.ds((r * res + k) * res, res), :] = scores
                maxima[r] = jnp.maximum(maxima[r], scores)
        return tuple(maxima)

    lowest = jnp.full((res, channels), -jnp.inf, f32)
    maxima = lax.fori_loop(0, res // chunk, scores_of, (lowest,) * row_count)

    zeros = jnp.zeros((res, channels), f32)
    attended = []
    for r in range(row_count):

        def weigh(step, totals, r=r):
            total, mixed = totals
            for offset in range(chunk):
                k = step * chunk + offset
                weight = jnp.exp(score_ref[pl.ds((r * res + k) * res, res), :] - maxima[r])
                total = total + weight
                mixed = mixed + weight * value_ref[pl.ds(k * res, res), :]
            return total, mixed

        total, mixed = lax.fori_loop(0, res // chunk, weigh, (zeros, zeros))
        attended.append(mixed / total)
    gated = (jnp.concatenate(attended, axis=0) * att_gate).astype(bf16)
    after_own = after_ref[pl.ds(own_start, row_count * res), :]
    final = after_own + dot(gated, w_att_out[...])
    out_ref[...] = final.astype(bf16).reshape(row_count, res, channels)


def on_whole_complex(pair_rep, residue_valid, *parameters):
    row_count, res, channels = pair_rep.shape
    whole = lax.all_gather(pair_rep, "row", axis=0, tiled=True)
    parameters = [p[None, :] if p.ndim == 1 else p for p in parameters]
    in_vmem = pl.BlockSpec(memory_space=pltpu.VMEM)
    in_smem = pl.BlockSpec(memory_space=pltpu.SMEM)
    pairs = res * res
    return pl.pallas_call(
        functools.partial(whole_complex_kernel, row_count),
        out_shape=jax.ShapeDtypeStruct((row_count, res, channels), jnp.bfloat16),
        in_specs=[in_vmem, in_smem, in_vmem] + [in_vmem] * len(parameters),
        out_specs=in_vmem,
        scratch_shapes=[
            pltpu.VMEM((pairs, channels), jnp.bfloat16),
            pltpu.VMEM((pairs, channels), jnp.float32),
            pltpu.VMEM((pairs, channels), jnp.float32),
            pltpu.VMEM((pairs, channels), jnp.float32),
            pltpu.VMEM((pairs, channels), jnp.float32),
            pltpu.VMEM((pairs, channels), jnp.float32),
            pltpu.VMEM((pairs, channels), jnp.float32),
            pltpu.VMEM((row_count * pairs, channels), jnp.float32),
            pltpu.VMEM((row_count * res, channels), jnp.float32),
        ],
        compiler_params=pltpu.CompilerParams(vmem_limit_bytes=40 * 1024 * 1024),
    )(whole, residue_valid, residue_valid[None, :], *parameters)


def per_device(pair_rep, residue_valid, *parameters):
    row_count, res, channels = pair_rep.shape
    if res % 16 == 0 and 40 * res * res * channels <= 32 * 1024 * 1024:
        return on_whole_complex(pair_rep, residue_valid, *parameters)
    return split_over_devices(pair_rep, residue_valid, *parameters)


def solution(mesh):
    return jax.shard_map(
        per_device,
        mesh=mesh,
        in_specs=(
            P(("groups", "row"), None, None),
            P("groups"),
            P(),
            P(),
            P(),
            P(),
            P(),
            P(),
            P(),
            P(),
            P(),
            P(),
            P(),
            P(),
            P(),
            P(),
            P(),
        ),
        out_specs=P(("groups", "row"), None, None),
        check_vma=False,
    )
```

```python
import functools
import math

import jax
import jax.numpy as jnp
from jax import lax
from jax.experimental import pallas as pl
from jax.experimental.pallas import tpu as pltpu
from jax.sharding import PartitionSpec as P

HEADS = 4
HEAD_DIM = 32


def layer_norm(values, norm_gain, norm_bias, along_axis):
    centre = values - jnp.mean(values, axis=along_axis, keepdims=True)
    spread = jnp.mean(centre * centre, axis=along_axis, keepdims=True)
    return centre * lax.rsqrt(spread + 1e-05) * norm_gain + norm_bias


def attend(query_cols, key_cols, value_cols, whole_bias, key_mask):
    factor = 1.0 / math.sqrt(HEAD_DIM)
    scores = (
        jnp.einsum("kjhd,ijhd->jhki", key_cols, query_cols, preferred_element_type=jnp.float32)
        * factor
    )
    scores = scores + whole_bias.astype(jnp.float32)[None] + key_mask[None, None, :, None]
    scores = scores - jnp.max(scores, axis=2, keepdims=True)
    exponent = jnp.exp(scores)
    weights = (exponent / jnp.sum(exponent, axis=2, keepdims=True)).astype(jnp.bfloat16)
    return jnp.einsum("jhki,kjhd->ijhd", weights, value_cols, preferred_element_type=jnp.float32)


def split_over_devices(
    pair_rep,
    residue_valid,
    tri_norm_gain,
    tri_norm_bias,
    w_edges,
    w_tri_gate,
    out_norm_gain,
    out_norm_bias,
    w_tri_out,
    att_norm_gain,
    att_norm_bias,
    w_query,
    w_key,
    w_value,
    w_att_gate,
    w_pair_bias,
    w_att_out,
):
    row_count = pair_rep.shape[0]
    res_count = pair_rep.shape[1]
    channels = pair_rep.shape[2]
    hidden_width = HEADS * HEAD_DIM
    row_start = lax.axis_index("row") * row_count
    valid_flags = residue_valid.astype(jnp.float32)
    own_valid = lax.dynamic_slice_in_dim(valid_flags, row_start, row_count)
    normed = layer_norm(pair_rep.astype(jnp.float32), tri_norm_gain, tri_norm_bias, 2).astype(
        jnp.bfloat16
    )
    projected = jnp.einsum("ikd,de->eik", normed, w_edges, preferred_element_type=jnp.float32)
    projected = projected.reshape(4, channels, row_count, res_count)
    pair_mask = (own_valid[:, None] * valid_flags[None, :])[None, :, :]
    left_edges = (jax.nn.sigmoid(projected[1]) * projected[0] * pair_mask).astype(jnp.bfloat16)
    right_edges = (jax.nn.sigmoid(projected[3]) * projected[2] * pair_mask).astype(jnp.bfloat16)
    left_cols, right_cols = (
        lax.all_to_all(left_edges, "row", split_axis=0, concat_axis=1, tiled=True),
        lax.all_to_all(right_edges, "row", split_axis=0, concat_axis=1, tiled=True),
    )
    block_product = jnp.einsum(
        "cik,cjk->cij", left_cols, right_cols, preferred_element_type=jnp.float32
    ).astype(jnp.bfloat16)
    triangle = lax.all_to_all(block_product, "row", split_axis=1, concat_axis=0, tiled=True)
    tri_normed = layer_norm(
        triangle.astype(jnp.float32), out_norm_gain[:, None, None], out_norm_bias[:, None, None], 0
    ).astype(jnp.bfloat16)
    tri_gate = jax.nn.sigmoid(
        jnp.einsum("ijc,ce->ije", normed, w_tri_gate, preferred_element_type=jnp.float32)
    )
    tri_update = jnp.einsum(
        "cij,ce->ije", tri_normed, w_tri_out, preferred_element_type=jnp.float32
    )
    after_tri = pair_rep.astype(jnp.float32) + tri_gate * tri_update
    att_in = layer_norm(after_tri, att_norm_gain, att_norm_bias, 2).astype(jnp.bfloat16)
    pair_bias = jnp.einsum(
        "kic,ch->hki", att_in, w_pair_bias, preferred_element_type=jnp.float32
    ).astype(jnp.bfloat16)
    whole_bias = lax.all_gather(pair_bias, "row", axis=1, tiled=True)
    key_mask = 1000000000.0 * (valid_flags - 1.0)
    columns = lax.all_to_all(att_in, "row", split_axis=1, concat_axis=0, tiled=True)
    all_weights = jnp.concatenate([w_query, w_key, w_value, w_att_gate], axis=1)
    joined = jnp.dot(columns.reshape(-1, channels), all_weights, preferred_element_type=jnp.float32)
    query_cols = (
        joined[:, :hidden_width].astype(jnp.bfloat16).reshape(res_count, row_count, HEADS, HEAD_DIM)
    )
    key_cols = (
        joined[:, hidden_width : 2 * hidden_width]
        .astype(jnp.bfloat16)
        .reshape(res_count, row_count, HEADS, HEAD_DIM)
    )
    value_cols = (
        joined[:, 2 * hidden_width : 3 * hidden_width]
        .astype(jnp.bfloat16)
        .reshape(res_count, row_count, HEADS, HEAD_DIM)
    )
    gate_cols = jax.nn.sigmoid(joined[:, 3 * hidden_width :]).reshape(
        res_count, row_count, hidden_width
    )
    attended = attend(query_cols, key_cols, value_cols, whole_bias, key_mask)
    gated = (attended.reshape(res_count, row_count, hidden_width) * gate_cols).astype(jnp.bfloat16)
    gated_rows = lax.all_to_all(gated, "row", split_axis=0, concat_axis=1, tiled=True)
    final = after_tri + jnp.einsum(
        "ije,ec->ijc", gated_rows, w_att_out, preferred_element_type=jnp.float32
    )
    return final.astype(jnp.bfloat16)


def sigmoid(values):
    return 0.5 * jnp.tanh(0.5 * values) + 0.5


def dot(left, right):
    return jnp.dot(left, right, preferred_element_type=jnp.float32)


def rounded(values):
    return values.astype(jnp.bfloat16).astype(jnp.float32)


def whole_complex_kernel(
    row_count,
    exchange_bits,
    near_ref,
    far_ref,
    valid_scalars,
    valid_ref,
    tri_norm_gain,
    tri_norm_bias,
    w_edges,
    w_tri_gate,
    out_norm_gain,
    out_norm_bias,
    w_tri_out,
    att_norm_gain,
    att_norm_bias,
    w_query,
    w_key,
    w_value,
    w_att_gate,
    w_pair_bias,
    w_att_out,
    out_ref,
    normed_ref,
    left_ref,
    right_ref,
    gate_ref,
    triangle_ref,
    after_ref,
    att_ref,
    key_ref,
    value_ref,
    score_ref,
    bias_ref,
):
    f32, bf16 = jnp.float32, jnp.bfloat16
    res = near_ref.shape[1]
    channels = near_ref.shape[2]
    device = lax.axis_index("row")
    own = device * row_count

    diagonal = lax.broadcasted_iota(jnp.int32, (res, res), 0) == lax.broadcasted_iota(
        jnp.int32, (res, res), 1
    )
    spread_valid = jnp.where(diagonal, valid_ref[...].astype(f32), 0.0)
    valid_column = jnp.broadcast_to(
        jnp.sum(spread_valid, axis=1, keepdims=True), (res, channels)
    )

    blocks = 2
    block_height = row_count * res
    height = blocks * block_height
    edge_weights = jnp.concatenate([w_edges[...], w_tri_gate[...]], axis=1)

    def first_row(position):
        sender = device
        for level, bit in enumerate(exchange_bits):
            sender = jnp.bitwise_xor(sender, jnp.bitwise_and(position >> level, 1) * bit)
        return sender * row_count

    for part, pairs_ref in enumerate((near_ref, far_ref)):
        steps = pairs_ref.shape[0] // (blocks * row_count)
        position = part * steps * blocks

        def norm_of(step, pairs_ref=pairs_ref, position=position):
            pairs = pairs_ref[pl.ds(step * blocks * row_count, blocks * row_count)]
            pairs = pairs.astype(f32).reshape(height, channels)
            for b in range(blocks):
                start = pl.multiple_of(first_row(position + step * blocks + b) * res, res)
                after_ref[pl.ds(start, block_height), :] = pairs[
                    b * block_height : (b + 1) * block_height
                ]
            return layer_norm(pairs, tri_norm_gain[...], tri_norm_bias[...], 1).astype(bf16)

        def edges_of(step, carry, steps=steps, position=position, norm_of=norm_of):
            normed = normed_ref[lax.rem(step, 2)]
            later = norm_of(jnp.minimum(step + 1, steps - 1))
            projected = dot(normed, edge_weights)
            pa, ga, pb, gb, gt = (
                projected[:, e * channels : (e + 1) * channels] for e in range(5)
            )
            left = sigmoid(ga) * pa
            right = sigmoid(gb) * pb
            gate = sigmoid(gt)
            for b in range(blocks):
                first = first_row(position + step * blocks + b)
                for r in range(row_count):
                    i = first + r
                    start = pl.multiple_of(i * res, res)
                    rows = slice(b * block_height + r * res, b * block_height + (r + 1) * res)
                    mask = valid_column * valid_scalars[i].astype(f32)
                    left_ref[pl.ds(start, res), :] = rounded(left[rows] * mask)
                    right_ref[pl.ds(i, res, stride=res), :] = rounded(right[rows] * mask)
                    gate_ref[pl.ds(start, res), :] = gate[rows]
            normed_ref[lax.rem(step + 1, 2)] = later
            return carry

        normed_ref[0] = norm_of(0)
        lax.fori_loop(0, steps, edges_of, 0)

    chunk = 6
    while res % chunk:
        chunk -= 1
    tall = chunk * res
    key_value = jnp.concatenate([w_key[...], w_value[...]], axis=1)

    def triangle_of(step):
        start = pl.multiple_of(step * tall, tall)
        totals = [jnp.zeros((res, channels), f32) for _ in range(chunk)]
        for k in range(res):
            right = right_ref[pl.ds(k * res, res), :]
            for r in range(chunk):
                totals[r] = totals[r] + left_ref[pl.ds(start + r * res + k, 1), :] * right
        for r in range(chunk):
            triangle_ref[lax.rem(step, 2), pl.ds(r * res, res), :] = rounded(totals[r])

    def attention_inputs_of(step):
        rows = pl.ds(pl.multiple_of(step * tall, tall), tall)
        triangle = triangle_ref[lax.rem(step, 2)]
        tri_normed = layer_norm(triangle, out_norm_gain[...], out_norm_bias[...], 1).astype(bf16)
        after_tri = after_ref[rows, :] + gate_ref[rows, :] * dot(tri_normed, w_tri_out[...])
        after_ref[rows, :] = after_tri
        att_in = layer_norm(after_tri, att_norm_gain[...], att_norm_bias[...], 1).astype(bf16)
        att_ref[rows, :] = att_in.astype(f32)
        joined = dot(att_in, key_value)
        key_ref[rows, :] = rounded(joined[:, :channels])
        value_ref[rows, :] = rounded(joined[:, channels:])

    def both_of(step, carry):
        attention_inputs_of(step - 1)
        triangle_of(step)
        return carry

    triangle_of(0)
    lax.fori_loop(1, res // chunk, both_of, 0)
    attention_inputs_of(res // chunk - 1)

    factor = 1.0 / math.sqrt(HEAD_DIM)
    head_of_row = lax.broadcasted_iota(jnp.int32, (2 * channels, channels), 0) % channels // HEAD_DIM
    head_of_column = lax.broadcasted_iota(jnp.int32, (2 * channels, channels), 1) // HEAD_DIM
    same_head = jnp.where(head_of_row == head_of_column, 1.0, 0.0).astype(bf16)
    to_head = lax.broadcasted_iota(jnp.int32, (HEADS, channels), 0)
    to_column = lax.broadcasted_iota(jnp.int32, (HEADS, channels), 1) // HEAD_DIM
    repeat_head = jnp.where(to_head == to_column, 1.0, 0.0).astype(bf16)
    wide_bias = dot(w_pair_bias[...], repeat_head).astype(bf16)

    own_start = pl.multiple_of(own * res, res)
    own_in = att_ref[pl.ds(own_start, block_height), :].astype(bf16)
    query = rounded(dot(own_in, w_query[...]))
    att_gate = sigmoid(dot(own_in, w_att_gate[...]))
    for r in range(row_count):
        column = att_ref[pl.ds(own + r, res, stride=res), :].astype(bf16)
        bias_ref[r * res : (r + 1) * res, :] = rounded(dot(column, wide_bias))

    key_chunk = 8

    def scores_of(step, maxima):
        maxima = list(maxima)
        for offset in range(key_chunk):
            k = step * key_chunk + offset
            key_mask = 1000000000.0 * (valid_scalars[k].astype(f32) - 1.0)
            keys = key_ref[pl.ds(k * res, res), :]
            for r in range(row_count):
                product = query[r * res : (r + 1) * res] * keys
                high = product.astype(bf16)
                low = (product - high.astype(f32)).astype(bf16)
                scores = dot(jnp.concatenate([high, low], axis=1), same_head) * factor
                scores = scores + bias_ref[pl.ds(r * res + k, 1), :] + key_mask
                score_ref[pl.ds((r * res + k) * res, res), :] = scores
                maxima[r] = jnp.maximum(maxima[r], scores)
        return tuple(maxima)

    lowest = jnp.full((res, channels), -jnp.inf, f32)
    maxima = lax.fori_loop(0, res // key_chunk, scores_of, (lowest,) * row_count)

    zeros = jnp.zeros((res, channels), f32)
    weigh_chunk = 16
    attended = []
    for r in range(row_count):

        def weigh(step, totals, r=r):
            total, mixed = totals
            for offset in range(weigh_chunk):
                k = step * weigh_chunk + offset
                weight = jnp.exp(score_ref[pl.ds((r * res + k) * res, res), :] - maxima[r])
                total = total + weight
                mixed = mixed + weight * value_ref[pl.ds(k * res, res), :]
            return total, mixed

        total, mixed = lax.fori_loop(0, res // weigh_chunk, weigh, (zeros, zeros))
        attended.append(mixed / total)
    gated = (jnp.concatenate(attended, axis=0) * att_gate).astype(bf16)
    after_own = after_ref[pl.ds(own_start, block_height), :]
    final = after_own + dot(gated, w_att_out[...])
    out_ref[...] = final.astype(bf16).reshape(row_count, res, channels)


def on_whole_complex(pair_rep, residue_valid, *parameters):
    row_count, res, channels = pair_rep.shape
    devices = res // row_count
    exchange_bits = []
    while devices >> (len(exchange_bits) + 1):
        exchange_bits.append(devices >> (len(exchange_bits) + 1))
    near = pair_rep
    for bit in exchange_bits:
        far = lax.ppermute(near, "row", [(d, d ^ bit) for d in range(devices)])
        if bit > 1:
            near = jnp.concatenate([near, far], axis=0)
    parameters = [p[None, :] if p.ndim == 1 else p for p in parameters]
    in_vmem = pl.BlockSpec(memory_space=pltpu.VMEM)
    in_smem = pl.BlockSpec(memory_space=pltpu.SMEM)
    pairs = res * res
    tall = pltpu.VMEM((pairs, channels), jnp.float32)
    return pl.pallas_call(
        functools.partial(whole_complex_kernel, row_count, tuple(exchange_bits)),
        out_shape=jax.ShapeDtypeStruct((row_count, res, channels), jnp.bfloat16),
        in_specs=[in_vmem, in_vmem, in_smem, in_vmem] + [in_vmem] * len(parameters),
        out_specs=in_vmem,
        scratch_shapes=[
            pltpu.VMEM((2, 2 * row_count * res, channels), jnp.bfloat16),
            tall,
            tall,
            tall,
            pltpu.VMEM((2, 6 * res, channels), jnp.float32),
            tall,
            tall,
            tall,
            tall,
            pltpu.VMEM((row_count * pairs, channels), jnp.float32),
            pltpu.VMEM((row_count * res, channels), jnp.float32),
        ],
        compiler_params=pltpu.CompilerParams(vmem_limit_bytes=40 * 1024 * 1024),
    )(near, far, residue_valid, residue_valid[None, :], *parameters)


def per_device(pair_rep, residue_valid, *parameters):
    row_count, res, channels = pair_rep.shape
    devices = res // row_count
    if res % 48 == 0 and devices in (4, 8, 16) and 40 * res * res * channels <= 32 * 1024 * 1024:
        return on_whole_complex(pair_rep, residue_valid, *parameters)
    return split_over_devices(pair_rep, residue_valid, *parameters)


def solution(mesh):
    return jax.shard_map(
        per_device,
        mesh=mesh,
        in_specs=(
            P(("groups", "row"), None, None),
            P("groups"),
            P(),
            P(),
            P(),
            P(),
            P(),
            P(),
            P(),
            P(),
            P(),
            P(),
            P(),
            P(),
            P(),
            P(),
            P(),
        ),
        out_specs=P(("groups", "row"), None, None),
        check_vma=False,
    )
```

```python
import functools
import math

import jax
import jax.numpy as jnp
from jax import lax
from jax.experimental import pallas as pl
from jax.experimental.pallas import tpu as pltpu
from jax.sharding import PartitionSpec as P

HEADS = 4
HEAD_DIM = 32


def layer_norm(values, norm_gain, norm_bias, along_axis):
    centre = values - jnp.mean(values, axis=along_axis, keepdims=True)
    spread = jnp.mean(centre * centre, axis=along_axis, keepdims=True)
    return centre * lax.rsqrt(spread + 1e-05) * norm_gain + norm_bias


def attend(query_cols, key_cols, value_cols, whole_bias, key_mask):
    factor = 1.0 / math.sqrt(HEAD_DIM)
    scores = (
        jnp.einsum("kjhd,ijhd->jhki", key_cols, query_cols, preferred_element_type=jnp.float32)
        * factor
    )
    scores = scores + whole_bias.astype(jnp.float32)[None] + key_mask[None, None, :, None]
    scores = scores - jnp.max(scores, axis=2, keepdims=True)
    exponent = jnp.exp(scores)
    weights = (exponent / jnp.sum(exponent, axis=2, keepdims=True)).astype(jnp.bfloat16)
    return jnp.einsum("jhki,kjhd->ijhd", weights, value_cols, preferred_element_type=jnp.float32)


def split_over_devices(
    pair_rep,
    residue_valid,
    tri_norm_gain,
    tri_norm_bias,
    w_edges,
    w_tri_gate,
    out_norm_gain,
    out_norm_bias,
    w_tri_out,
    att_norm_gain,
    att_norm_bias,
    w_query,
    w_key,
    w_value,
    w_att_gate,
    w_pair_bias,
    w_att_out,
):
    row_count = pair_rep.shape[0]
    res_count = pair_rep.shape[1]
    channels = pair_rep.shape[2]
    hidden_width = HEADS * HEAD_DIM
    row_start = lax.axis_index("row") * row_count
    valid_flags = residue_valid.astype(jnp.float32)
    own_valid = lax.dynamic_slice_in_dim(valid_flags, row_start, row_count)
    normed = layer_norm(pair_rep.astype(jnp.float32), tri_norm_gain, tri_norm_bias, 2).astype(
        jnp.bfloat16
    )
    projected = jnp.einsum("ikd,de->eik", normed, w_edges, preferred_element_type=jnp.float32)
    projected = projected.reshape(4, channels, row_count, res_count)
    pair_mask = (own_valid[:, None] * valid_flags[None, :])[None, :, :]
    left_edges = (jax.nn.sigmoid(projected[1]) * projected[0] * pair_mask).astype(jnp.bfloat16)
    right_edges = (jax.nn.sigmoid(projected[3]) * projected[2] * pair_mask).astype(jnp.bfloat16)
    left_cols, right_cols = (
        lax.all_to_all(left_edges, "row", split_axis=0, concat_axis=1, tiled=True),
        lax.all_to_all(right_edges, "row", split_axis=0, concat_axis=1, tiled=True),
    )
    block_product = jnp.einsum(
        "cik,cjk->cij", left_cols, right_cols, preferred_element_type=jnp.float32
    ).astype(jnp.bfloat16)
    triangle = lax.all_to_all(block_product, "row", split_axis=1, concat_axis=0, tiled=True)
    tri_normed = layer_norm(
        triangle.astype(jnp.float32), out_norm_gain[:, None, None], out_norm_bias[:, None, None], 0
    ).astype(jnp.bfloat16)
    tri_gate = jax.nn.sigmoid(
        jnp.einsum("ijc,ce->ije", normed, w_tri_gate, preferred_element_type=jnp.float32)
    )
    tri_update = jnp.einsum(
        "cij,ce->ije", tri_normed, w_tri_out, preferred_element_type=jnp.float32
    )
    after_tri = pair_rep.astype(jnp.float32) + tri_gate * tri_update
    att_in = layer_norm(after_tri, att_norm_gain, att_norm_bias, 2).astype(jnp.bfloat16)
    pair_bias = jnp.einsum(
        "kic,ch->hki", att_in, w_pair_bias, preferred_element_type=jnp.float32
    ).astype(jnp.bfloat16)
    whole_bias = lax.all_gather(pair_bias, "row", axis=1, tiled=True)
    key_mask = 1000000000.0 * (valid_flags - 1.0)
    columns = lax.all_to_all(att_in, "row", split_axis=1, concat_axis=0, tiled=True)
    all_weights = jnp.concatenate([w_query, w_key, w_value, w_att_gate], axis=1)
    joined = jnp.dot(columns.reshape(-1, channels), all_weights, preferred_element_type=jnp.float32)
    query_cols = (
        joined[:, :hidden_width].astype(jnp.bfloat16).reshape(res_count, row_count, HEADS, HEAD_DIM)
    )
    key_cols = (
        joined[:, hidden_width : 2 * hidden_width]
        .astype(jnp.bfloat16)
        .reshape(res_count, row_count, HEADS, HEAD_DIM)
    )
    value_cols = (
        joined[:, 2 * hidden_width : 3 * hidden_width]
        .astype(jnp.bfloat16)
        .reshape(res_count, row_count, HEADS, HEAD_DIM)
    )
    gate_cols = jax.nn.sigmoid(joined[:, 3 * hidden_width :]).reshape(
        res_count, row_count, hidden_width
    )
    attended = attend(query_cols, key_cols, value_cols, whole_bias, key_mask)
    gated = (attended.reshape(res_count, row_count, hidden_width) * gate_cols).astype(jnp.bfloat16)
    gated_rows = lax.all_to_all(gated, "row", split_axis=0, concat_axis=1, tiled=True)
    final = after_tri + jnp.einsum(
        "ije,ec->ijc", gated_rows, w_att_out, preferred_element_type=jnp.float32
    )
    return final.astype(jnp.bfloat16)


def sigmoid(values):
    return 0.5 * jnp.tanh(0.5 * values) + 0.5


def dot(left, right):
    return jnp.dot(left, right, preferred_element_type=jnp.float32)


def rounded(values):
    return values.astype(jnp.bfloat16).astype(jnp.float32)


def head_repeat(rows, row_of_head):
    head = lax.broadcasted_iota(jnp.int32, (rows, HEADS * HEAD_DIM), 0)
    column = lax.broadcasted_iota(jnp.int32, (rows, HEADS * HEAD_DIM), 1)
    return jnp.where(row_of_head(head) == column // HEAD_DIM, 1.0, 0.0).astype(jnp.bfloat16)


def prepare_kernel(
    pair_ref,
    valid_ref,
    tri_norm_gain,
    tri_norm_bias,
    w_edges,
    w_tri_gate,
    out_norm_gain,
    out_norm_bias,
    w_tri_out,
    att_norm_gain,
    att_norm_bias,
    w_query,
    w_key,
    w_value,
    w_att_gate,
    w_pair_bias,
    w_att_out,
    own_ref,
    valid_column_ref,
    norms_ref,
    edge_weights_ref,
    square_weights_ref,
):
    res = pair_ref.shape[1]
    channels = pair_ref.shape[2]
    own_ref[...] = pair_ref[...]
    diagonal = lax.broadcasted_iota(jnp.int32, (res, res), 0) == lax.broadcasted_iota(
        jnp.int32, (res, res), 1
    )
    spread_valid = jnp.where(diagonal, valid_ref[...].astype(jnp.float32), 0.0)
    valid_column_ref[...] = jnp.broadcast_to(
        jnp.sum(spread_valid, axis=1, keepdims=True), (res, channels)
    )
    vectors = (
        tri_norm_gain,
        tri_norm_bias,
        out_norm_gain,
        out_norm_bias,
        att_norm_gain,
        att_norm_bias,
    )
    for row, vector in enumerate(vectors):
        norms_ref[row : row + 1, :] = vector[...]
    edge_weights_ref[:, : 4 * channels] = w_edges[...]
    edge_weights_ref[:, 4 * channels :] = w_tri_gate[...]
    wide_bias = dot(w_pair_bias[...], head_repeat(HEADS, lambda head: head))
    squares = (w_tri_out, w_key, w_value, w_query, w_att_gate, w_att_out)
    for column, square in enumerate(squares):
        square_weights_ref[:, column * channels : (column + 1) * channels] = square[...]
    square_weights_ref[:, len(squares) * channels :] = wide_bias.astype(jnp.bfloat16)


def edges_kernel(
    row_count,
    senders,
    valid_scalars,
    pairs_ref,
    valid_column,
    norms,
    edge_weights,
    *refs,
):
    left_ref, right_ref, gate_ref, after_ref = refs[-4:]
    f32, bf16 = jnp.float32, jnp.bfloat16
    res = pairs_ref.shape[1]
    channels = pairs_ref.shape[2]
    device = lax.axis_index("row")
    for block, bits in enumerate(senders):
        first = jnp.bitwise_xor(device, bits) * row_count
        pairs = pairs_ref[block * row_count : (block + 1) * row_count].astype(f32)
        pairs = pairs.reshape(row_count * res, channels)
        start = pl.multiple_of(first * res, res)
        after_ref[pl.ds(start, row_count * res), :] = pairs
        normed = layer_norm(pairs, norms[0:1, :], norms[1:2, :], 1).astype(bf16)
        projected = dot(normed, edge_weights[...])
        pa, ga, pb, gb, gt = (projected[:, e * channels : (e + 1) * channels] for e in range(5))
        left = sigmoid(ga) * pa
        right = sigmoid(gb) * pb
        gate_ref[pl.ds(start, row_count * res), :] = sigmoid(gt)
        for r in range(row_count):
            i = first + r
            rows = slice(r * res, (r + 1) * res)
            mask = valid_column[...] * valid_scalars[i].astype(f32)
            left_ref[pl.ds(pl.multiple_of(i * res, res), res), :] = rounded(left[rows] * mask)
            right_ref[pl.ds(i, res, stride=res), :] = rounded(right[rows] * mask)


def triangle_kernel(
    res,
    chunk,
    norms,
    square_weights,
    left_ref,
    right_ref,
    gate_ref,
    pairs_ref,
    after_ref,
    att_ref,
    key_ref,
    value_ref,
    triangle_ref,
):
    f32, bf16 = jnp.float32, jnp.bfloat16
    channels = left_ref.shape[1]
    tall = chunk * res

    def triangle_of(step):
        start = pl.multiple_of(step * tall, tall)
        totals = [jnp.zeros((res, channels), f32) for _ in range(chunk)]
        for k in range(res):
            right = right_ref[pl.ds(k * res, res), :]
            for r in range(chunk):
                totals[r] = totals[r] + left_ref[pl.ds(start + r * res + k, 1), :] * right
        for r in range(chunk):
            triangle_ref[lax.rem(step, 2), pl.ds(r * res, res), :] = rounded(totals[r])

    def attention_inputs_of(step):
        rows = pl.ds(pl.multiple_of(step * tall, tall), tall)
        triangle = triangle_ref[lax.rem(step, 2)]
        tri_normed = layer_norm(triangle, norms[2:3, :], norms[3:4, :], 1).astype(bf16)
        update = dot(tri_normed, square_weights[:, :channels])
        after_tri = pairs_ref[rows, :] + gate_ref[rows, :] * update
        after_ref[rows, :] = after_tri
        att_in = layer_norm(after_tri, norms[4:5, :], norms[5:6, :], 1).astype(bf16)
        att_ref[rows, :] = att_in.astype(f32)
        joined = dot(att_in, square_weights[:, channels : 3 * channels])
        key_ref[rows, :] = rounded(joined[:, :channels])
        value_ref[rows, :] = rounded(joined[:, channels:])

    def both_of(step, carry):
        attention_inputs_of(step - 1)
        triangle_of(step)
        return carry

    triangle_of(0)
    lax.fori_loop(1, res // chunk, both_of, 0)
    attention_inputs_of(res // chunk - 1)


def attention_kernel(
    row_count,
    res,
    key_chunk,
    weigh_chunk,
    valid_scalars,
    square_weights,
    after_ref,
    att_ref,
    key_ref,
    value_ref,
    out_ref,
    score_ref,
    bias_ref,
):
    f32, bf16 = jnp.float32, jnp.bfloat16
    channels = key_ref.shape[1]
    own = lax.axis_index("row") * row_count
    own_start = pl.multiple_of(own * res, res)
    own_in = att_ref[pl.ds(own_start, row_count * res), :].astype(bf16)
    joined = dot(own_in, square_weights[:, 3 * channels : 5 * channels])
    query = rounded(joined[:, :channels])
    att_gate = sigmoid(joined[:, channels:])
    wide_bias = square_weights[:, 6 * channels :]
    for r in range(row_count):
        column = att_ref[pl.ds(own + r, res, stride=res), :].astype(bf16)
        bias_ref[r * res : (r + 1) * res, :] = rounded(dot(column, wide_bias))

    factor = 1.0 / math.sqrt(HEAD_DIM)
    same_head = head_repeat(2 * channels, lambda row: row % channels // HEAD_DIM)

    def scores_of(step, maxima):
        maxima = list(maxima)
        for offset in range(key_chunk):
            k = step * key_chunk + offset
            key_mask = 1000000000.0 * (valid_scalars[k].astype(f32) - 1.0)
            keys = key_ref[pl.ds(k * res, res), :]
            for r in range(row_count):
                product = query[r * res : (r + 1) * res] * keys
                high = product.astype(bf16)
                low = (product - high.astype(f32)).astype(bf16)
                scores = dot(jnp.concatenate([high, low], axis=1), same_head) * factor
                scores = scores + bias_ref[pl.ds(r * res + k, 1), :] + key_mask
                score_ref[pl.ds((r * res + k) * res, res), :] = scores
                maxima[r] = jnp.maximum(maxima[r], scores)
        return tuple(maxima)

    lowest = jnp.full((res, channels), -jnp.inf, f32)
    maxima = lax.fori_loop(0, res // key_chunk, scores_of, (lowest,) * row_count)

    zeros = jnp.zeros((res, channels), f32)
    attended = []
    for r in range(row_count):

        def weigh(step, totals, r=r):
            total, mixed = totals
            for offset in range(weigh_chunk):
                k = step * weigh_chunk + offset
                weight = jnp.exp(score_ref[pl.ds((r * res + k) * res, res), :] - maxima[r])
                total = total + weight
                mixed = mixed + weight * value_ref[pl.ds(k * res, res), :]
            return total, mixed

        total, mixed = lax.fori_loop(0, res // weigh_chunk, weigh, (zeros, zeros))
        attended.append(mixed / total)
    gated = (jnp.concatenate(attended, axis=0) * att_gate).astype(bf16)
    after_own = after_ref[pl.ds(own_start, row_count * res), :]
    final = after_own + dot(gated, square_weights[:, 5 * channels : 6 * channels])
    out_ref[...] = final.astype(bf16).reshape(row_count, res, channels)


def on_whole_complex(pair_rep, residue_valid, *parameters):
    row_count, res, channels = pair_rep.shape
    devices = res // row_count
    f32, bf16 = jnp.float32, jnp.bfloat16
    in_vmem = pl.BlockSpec(memory_space=pltpu.VMEM)
    in_smem = pl.BlockSpec(memory_space=pltpu.SMEM)
    compiler_params = pltpu.CompilerParams(vmem_limit_bytes=24 * 1024 * 1024)
    tall = jax.ShapeDtypeStruct((res * res, channels), f32)

    def exchange(values, bit):
        return lax.ppermute(values, "row", [(d, d ^ bit) for d in range(devices)])

    parameters = [p[None, :] if p.ndim == 1 else p for p in parameters]
    own, valid_column, norms, edge_weights, square_weights = pl.pallas_call(
        prepare_kernel,
        out_shape=(
            jax.ShapeDtypeStruct(pair_rep.shape, bf16),
            jax.ShapeDtypeStruct((res, channels), f32),
            jax.ShapeDtypeStruct((8, channels), f32),
            jax.ShapeDtypeStruct((channels, 5 * channels), bf16),
            jax.ShapeDtypeStruct((channels, 7 * channels), bf16),
        ),
        in_specs=[in_vmem] * (2 + len(parameters)),
        out_specs=(in_vmem,) * 5,
        compiler_params=compiler_params,
    )(pair_rep, residue_valid[None, :], *parameters)

    def edges_of(pairs, senders, edges):
        return pl.pallas_call(
            functools.partial(edges_kernel, row_count, senders),
            out_shape=(tall,) * 4,
            in_specs=[in_smem] + [in_vmem] * (4 + len(edges)),
            out_specs=(in_vmem,) * 4,
            input_output_aliases={5 + e: e for e in range(len(edges))},
            compiler_params=compiler_params,
            cost_estimate=pl.CostEstimate(
                flops=10 * pairs.size * channels, bytes_accessed=6 * 1024 * 1024, transcendentals=0
            ),
        )(residue_valid, pairs, valid_column, norms, edge_weights, *edges)

    senders = (0,)
    quarter = pair_rep
    bit = devices // 2
    while bit > 2:
        kept = own if bit == devices // 2 else quarter
        quarter = jnp.concatenate([kept, exchange(quarter, bit)], axis=0)
        senders = senders + tuple(s ^ bit for s in senders)
        bit //= 2
    beside = exchange(quarter, 2)
    across = exchange(quarter, 1)
    edges = edges_of(quarter, senders, ())
    edges = edges_of(across, tuple(s ^ 1 for s in senders), edges)
    corner = exchange(beside, 1)
    edges = edges_of(beside, tuple(s ^ 2 for s in senders), edges)
    edges = edges_of(corner, tuple(s ^ 3 for s in senders), edges)

    chunk = 6
    after_tri, att_in, keys, values = pl.pallas_call(
        functools.partial(triangle_kernel, res, chunk),
        out_shape=(tall,) * 4,
        in_specs=[in_vmem] * 6,
        out_specs=(in_vmem,) * 4,
        scratch_shapes=[pltpu.VMEM((2, chunk * res, channels), f32)],
        compiler_params=compiler_params,
    )(norms, square_weights, *edges)
    return pl.pallas_call(
        functools.partial(attention_kernel, row_count, res, 8, 16),
        out_shape=jax.ShapeDtypeStruct(pair_rep.shape, bf16),
        in_specs=[in_smem] + [in_vmem] * 5,
        out_specs=in_vmem,
        scratch_shapes=[
            pltpu.VMEM((row_count * res * res, channels), f32),
            pltpu.VMEM((row_count * res, channels), f32),
        ],
        compiler_params=compiler_params,
    )(residue_valid, square_weights, after_tri, att_in, keys, values)


def per_device(pair_rep, residue_valid, *parameters):
    row_count, res, channels = pair_rep.shape
    devices = res // row_count
    if res % 48 == 0 and devices in (4, 8, 16) and 40 * res * res * channels <= 32 * 1024 * 1024:
        return on_whole_complex(pair_rep, residue_valid, *parameters)
    return split_over_devices(pair_rep, residue_valid, *parameters)


def solution(mesh):
    return jax.shard_map(
        per_device,
        mesh=mesh,
        in_specs=(
            P(("groups", "row"), None, None),
            P("groups"),
            P(),
            P(),
            P(),
            P(),
            P(),
            P(),
            P(),
            P(),
            P(),
            P(),
            P(),
            P(),
            P(),
            P(),
            P(),
        ),
        out_specs=P(("groups", "row"), None, None),
        check_vma=False,
    )
```

```python
import functools
import math

import jax
import jax.numpy as jnp
from jax import lax
from jax.experimental import pallas as pl
from jax.experimental.pallas import tpu as pltpu
from jax.sharding import PartitionSpec as P

HEADS = 4
HEAD_DIM = 32


def layer_norm(values, norm_gain, norm_bias, along_axis):
    centre = values - jnp.mean(values, axis=along_axis, keepdims=True)
    spread = jnp.mean(centre * centre, axis=along_axis, keepdims=True)
    return centre * lax.rsqrt(spread + 1e-05) * norm_gain + norm_bias


def attend(query_cols, key_cols, value_cols, whole_bias, key_mask):
    factor = 1.0 / math.sqrt(HEAD_DIM)
    scores = (
        jnp.einsum("kjhd,ijhd->jhki", key_cols, query_cols, preferred_element_type=jnp.float32)
        * factor
    )
    scores = scores + whole_bias.astype(jnp.float32)[None] + key_mask[None, None, :, None]
    scores = scores - jnp.max(scores, axis=2, keepdims=True)
    exponent = jnp.exp(scores)
    weights = (exponent / jnp.sum(exponent, axis=2, keepdims=True)).astype(jnp.bfloat16)
    return jnp.einsum("jhki,kjhd->ijhd", weights, value_cols, preferred_element_type=jnp.float32)


def split_over_devices(
    pair_rep,
    residue_valid,
    tri_norm_gain,
    tri_norm_bias,
    w_edges,
    w_tri_gate,
    out_norm_gain,
    out_norm_bias,
    w_tri_out,
    att_norm_gain,
    att_norm_bias,
    w_query,
    w_key,
    w_value,
    w_att_gate,
    w_pair_bias,
    w_att_out,
):
    row_count = pair_rep.shape[0]
    res_count = pair_rep.shape[1]
    channels = pair_rep.shape[2]
    hidden_width = HEADS * HEAD_DIM
    row_start = lax.axis_index("row") * row_count
    valid_flags = residue_valid.astype(jnp.float32)
    own_valid = lax.dynamic_slice_in_dim(valid_flags, row_start, row_count)
    normed = layer_norm(pair_rep.astype(jnp.float32), tri_norm_gain, tri_norm_bias, 2).astype(
        jnp.bfloat16
    )
    projected = jnp.einsum("ikd,de->eik", normed, w_edges, preferred_element_type=jnp.float32)
    projected = projected.reshape(4, channels, row_count, res_count)
    pair_mask = (own_valid[:, None] * valid_flags[None, :])[None, :, :]
    left_edges = (jax.nn.sigmoid(projected[1]) * projected[0] * pair_mask).astype(jnp.bfloat16)
    right_edges = (jax.nn.sigmoid(projected[3]) * projected[2] * pair_mask).astype(jnp.bfloat16)
    left_cols, right_cols = (
        lax.all_to_all(left_edges, "row", split_axis=0, concat_axis=1, tiled=True),
        lax.all_to_all(right_edges, "row", split_axis=0, concat_axis=1, tiled=True),
    )
    block_product = jnp.einsum(
        "cik,cjk->cij", left_cols, right_cols, preferred_element_type=jnp.float32
    ).astype(jnp.bfloat16)
    triangle = lax.all_to_all(block_product, "row", split_axis=1, concat_axis=0, tiled=True)
    tri_normed = layer_norm(
        triangle.astype(jnp.float32), out_norm_gain[:, None, None], out_norm_bias[:, None, None], 0
    ).astype(jnp.bfloat16)
    tri_gate = jax.nn.sigmoid(
        jnp.einsum("ijc,ce->ije", normed, w_tri_gate, preferred_element_type=jnp.float32)
    )
    tri_update = jnp.einsum(
        "cij,ce->ije", tri_normed, w_tri_out, preferred_element_type=jnp.float32
    )
    after_tri = pair_rep.astype(jnp.float32) + tri_gate * tri_update
    att_in = layer_norm(after_tri, att_norm_gain, att_norm_bias, 2).astype(jnp.bfloat16)
    pair_bias = jnp.einsum(
        "kic,ch->hki", att_in, w_pair_bias, preferred_element_type=jnp.float32
    ).astype(jnp.bfloat16)
    whole_bias = lax.all_gather(pair_bias, "row", axis=1, tiled=True)
    key_mask = 1000000000.0 * (valid_flags - 1.0)
    columns = lax.all_to_all(att_in, "row", split_axis=1, concat_axis=0, tiled=True)
    all_weights = jnp.concatenate([w_query, w_key, w_value, w_att_gate], axis=1)
    joined = jnp.dot(columns.reshape(-1, channels), all_weights, preferred_element_type=jnp.float32)
    query_cols = (
        joined[:, :hidden_width].astype(jnp.bfloat16).reshape(res_count, row_count, HEADS, HEAD_DIM)
    )
    key_cols = (
        joined[:, hidden_width : 2 * hidden_width]
        .astype(jnp.bfloat16)
        .reshape(res_count, row_count, HEADS, HEAD_DIM)
    )
    value_cols = (
        joined[:, 2 * hidden_width : 3 * hidden_width]
        .astype(jnp.bfloat16)
        .reshape(res_count, row_count, HEADS, HEAD_DIM)
    )
    gate_cols = jax.nn.sigmoid(joined[:, 3 * hidden_width :]).reshape(
        res_count, row_count, hidden_width
    )
    attended = attend(query_cols, key_cols, value_cols, whole_bias, key_mask)
    gated = (attended.reshape(res_count, row_count, hidden_width) * gate_cols).astype(jnp.bfloat16)
    gated_rows = lax.all_to_all(gated, "row", split_axis=0, concat_axis=1, tiled=True)
    final = after_tri + jnp.einsum(
        "ije,ec->ijc", gated_rows, w_att_out, preferred_element_type=jnp.float32
    )
    return final.astype(jnp.bfloat16)


def sigmoid(values):
    return 0.5 * jnp.tanh(0.5 * values) + 0.5


def dot(left, right):
    return jnp.dot(left, right, preferred_element_type=jnp.float32)


def rounded(values):
    return values.astype(jnp.bfloat16).astype(jnp.float32)


def edges_kernel(row_count, senders, pairs_ref, valid_column, norms, weights, *refs):
    left_ref, right_ref, gate_ref, after_ref = refs[-4:]
    f32, bf16 = jnp.float32, jnp.bfloat16
    res = pairs_ref.shape[1]
    channels = pairs_ref.shape[2]
    tall = row_count * res
    pairs = pairs_ref[...].astype(f32).reshape(len(senders) * tall, channels)
    normed = layer_norm(pairs, norms[0:1, :], norms[1:2, :], 1).astype(bf16)
    column = valid_column[...]
    rows_of = [
        jnp.bitwise_xor(lax.axis_index("row"), bits) * row_count + r
        for bits in senders
        for r in range(row_count)
    ]
    masks = jnp.concatenate([column * valid_column[pl.ds(i, 1), :] for i in rows_of], axis=0)
    joined = dot(normed, weights[:, : 2 * channels])
    left = rounded(sigmoid(joined[:, channels:]) * joined[:, :channels] * masks)
    joined = dot(normed, weights[:, 2 * channels : 4 * channels])
    right = rounded(sigmoid(joined[:, channels:]) * joined[:, :channels] * masks)
    gate = sigmoid(dot(normed, weights[:, 4 * channels :]))
    for n, i in enumerate(rows_of):
        rows = slice(n * res, (n + 1) * res)
        start = pl.multiple_of(i * res, res)
        left_ref[pl.ds(start, res), :] = left[rows]
        right_ref[pl.ds(i, res, stride=res), :] = right[rows]
        gate_ref[pl.ds(start, res), :] = gate[rows]
        after_ref[pl.ds(start, res), :] = pairs[rows]


def triangle_kernel(
    res,
    chunk,
    post_chunk,
    norms,
    w_out,
    w_key,
    w_value,
    left_ref,
    right_ref,
    gate_ref,
    pairs_ref,
    after_ref,
    att_ref,
    key_ref,
    value_ref,
    triangle_ref,
):
    f32, bf16 = jnp.float32, jnp.bfloat16
    channels = left_ref.shape[1]

    def triangle_of(step, carry):
        start = pl.multiple_of(step * chunk * res, chunk * res)
        totals = [jnp.zeros((res, channels), f32) for _ in range(chunk)]
        for k in range(res):
            right = right_ref[pl.ds(k * res, res), :]
            for r in range(chunk):
                totals[r] = totals[r] + left_ref[pl.ds(start + r * res + k, 1), :] * right
        for r in range(chunk):
            triangle_ref[pl.ds(start + r * res, res), :] = rounded(totals[r])
        return carry

    lax.fori_loop(0, res // chunk, triangle_of, 0)
    key_value = jnp.concatenate([w_key[...], w_value[...]], axis=1)

    def attention_inputs_of(step, carry):
        tall = post_chunk * res
        rows = pl.ds(pl.multiple_of(step * tall, tall), tall)
        tri_normed = layer_norm(triangle_ref[rows, :], norms[2:3, :], norms[3:4, :], 1).astype(bf16)
        after_tri = pairs_ref[rows, :] + gate_ref[rows, :] * dot(tri_normed, w_out[...])
        att_in = layer_norm(after_tri, norms[4:5, :], norms[5:6, :], 1).astype(bf16)
        joined = dot(att_in, key_value)
        after_ref[rows, :] = after_tri
        att_ref[rows, :] = att_in.astype(f32)
        key_ref[rows, :] = rounded(joined[:, :channels])
        value_ref[rows, :] = rounded(joined[:, channels:])
        return carry

    lax.fori_loop(0, res // post_chunk, attention_inputs_of, 0)


def attention_kernel(
    row_count,
    res,
    key_chunk,
    weigh_chunk,
    valid_column,
    w_query,
    w_gate,
    w_out,
    head_bias,
    after_ref,
    att_ref,
    key_ref,
    value_ref,
    out_ref,
    score_ref,
    bias_ref,
):
    f32, bf16 = jnp.float32, jnp.bfloat16
    channels = key_ref.shape[1]
    own = lax.axis_index("row") * row_count
    own_start = pl.multiple_of(own * res, res)
    own_in = att_ref[pl.ds(own_start, row_count * res), :].astype(bf16)
    query = rounded(dot(own_in, w_query[...]))
    att_gate = sigmoid(dot(own_in, w_gate[...]))
    row = lax.broadcasted_iota(jnp.int32, (channels, HEADS), 0) // HEAD_DIM
    head = lax.broadcasted_iota(jnp.int32, (channels, HEADS), 1)
    repeat = jnp.where(row == head, 1.0, 0.0).astype(bf16)
    wide_bias = dot(repeat, head_bias[...]).astype(bf16)
    for r in range(row_count):
        column = att_ref[pl.ds(own + r, res, stride=res), :].astype(bf16)
        bias_ref[r * res : (r + 1) * res, :] = rounded(
            lax.dot_general(
                column, wide_bias, (((1,), (1,)), ((), ())), preferred_element_type=f32
            )
        )

    factor = 1.0 / math.sqrt(HEAD_DIM)
    row = lax.broadcasted_iota(jnp.int32, (2 * channels, channels), 0) % channels // HEAD_DIM
    column = lax.broadcasted_iota(jnp.int32, (2 * channels, channels), 1) // HEAD_DIM
    same_head = jnp.where(row == column, 1.0, 0.0).astype(bf16)

    def scores_of(step, maxima):
        maxima = list(maxima)
        products = []
        for offset in range(key_chunk):
            keys = key_ref[pl.ds((step * key_chunk + offset) * res, res), :]
            products.append(jnp.concatenate([keys] * row_count, axis=0) * query)
        product = jnp.concatenate(products, axis=0)
        high = product.astype(bf16)
        low = (product - high.astype(f32)).astype(bf16)
        scores = dot(jnp.concatenate([high, low], axis=1), same_head) * factor
        for offset in range(key_chunk):
            k = step * key_chunk + offset
            key_mask = 1000000000.0 * (valid_column[pl.ds(k, 1), :] - 1.0)
            for r in range(row_count):
                at = (offset * row_count + r) * res
                score = scores[at : at + res] + bias_ref[pl.ds(r * res + k, 1), :] + key_mask
                score_ref[pl.ds((r * res + k) * res, res), :] = score
                maxima[r] = jnp.maximum(maxima[r], score)
        return tuple(maxima)

    lowest = jnp.full((res, channels), -jnp.inf, f32)
    maxima = lax.fori_loop(0, res // key_chunk, scores_of, (lowest,) * row_count)

    zeros = jnp.zeros((res, channels), f32)
    attended = []
    for r in range(row_count):

        def weigh(step, totals, r=r):
            total, mixed = totals
            for offset in range(weigh_chunk):
                k = step * weigh_chunk + offset
                weight = jnp.exp(score_ref[pl.ds((r * res + k) * res, res), :] - maxima[r])
                total = total + weight
                mixed = mixed + weight * value_ref[pl.ds(k * res, res), :]
            return total, mixed

        total, mixed = lax.fori_loop(0, res // weigh_chunk, weigh, (zeros, zeros))
        attended.append(mixed / total)
    gated = (jnp.concatenate(attended, axis=0) * att_gate).astype(bf16)
    after_own = after_ref[pl.ds(own_start, row_count * res), :]
    final = after_own + dot(gated, w_out[...])
    out_ref[...] = final.astype(bf16).reshape(row_count, res, channels)


def on_whole_complex(
    pair_rep,
    residue_valid,
    tri_norm_gain,
    tri_norm_bias,
    w_edges,
    w_tri_gate,
    out_norm_gain,
    out_norm_bias,
    w_tri_out,
    att_norm_gain,
    att_norm_bias,
    w_query,
    w_key,
    w_value,
    w_att_gate,
    w_pair_bias,
    w_att_out,
):
    row_count, res, channels = pair_rep.shape
    devices = res // row_count
    f32, bf16 = jnp.float32, jnp.bfloat16
    in_vmem = pl.BlockSpec(memory_space=pltpu.VMEM)
    compiler_params = pltpu.CompilerParams(vmem_limit_bytes=24 * 1024 * 1024)
    tall = jax.ShapeDtypeStruct((res * res, channels), f32)

    def exchange(values, bit):
        return lax.ppermute(values, "row", [(d, d ^ bit) for d in range(devices)])

    vectors = (
        tri_norm_gain,
        tri_norm_bias,
        out_norm_gain,
        out_norm_bias,
        att_norm_gain,
        att_norm_bias,
    )
    norms = jnp.stack(vectors)
    edge_weights = jnp.concatenate([w_edges, w_tri_gate], axis=1)
    valid_column = jnp.broadcast_to(residue_valid.astype(f32)[:, None], (res, channels))

    def edges_of(pairs, senders, edges):
        return pl.pallas_call(
            functools.partial(edges_kernel, row_count, senders),
            out_shape=(tall,) * 4,
            in_specs=[in_vmem] * (4 + len(edges)),
            out_specs=(in_vmem,) * 4,
            input_output_aliases={4 + e: e for e in range(len(edges))},
            compiler_params=compiler_params,
            cost_estimate=pl.CostEstimate(
                flops=10 * pairs.size * channels, bytes_accessed=2**25, transcendentals=0
            ),
        )(pairs, valid_column, norms, edge_weights, *edges)

    senders = (0,)
    quarter = pair_rep
    bit = devices // 2
    while bit > 2:
        twice = jnp.zeros((2 * quarter.shape[0],) + quarter.shape[1:], bf16)
        kept = lax.dynamic_update_slice(twice, quarter, (0, 0, 0))
        far = exchange(quarter, bit)
        if bit == devices // 2:
            far, kept, norms, edge_weights, valid_column = lax.optimization_barrier(
                (far, kept, norms, edge_weights, valid_column)
            )
        quarter = lax.dynamic_update_slice(kept, far, (quarter.shape[0], 0, 0))
        senders = senders + tuple(s ^ bit for s in senders)
        bit //= 2
    beside = exchange(quarter, 2)
    across = exchange(quarter, 1)
    edges = edges_of(quarter, senders, ())
    edges = edges_of(across, tuple(s ^ 1 for s in senders), edges)
    beside, edges = lax.optimization_barrier((beside, edges))
    corner = exchange(beside, 1)
    edges = edges_of(beside, tuple(s ^ 2 for s in senders), edges)
    edges = edges_of(corner, tuple(s ^ 3 for s in senders), edges)

    after_tri, att_in, keys, values = pl.pallas_call(
        functools.partial(triangle_kernel, res, 6, 12),
        out_shape=(tall,) * 4,
        in_specs=[in_vmem] * 8,
        out_specs=(in_vmem,) * 4,
        scratch_shapes=[pltpu.VMEM((res * res, channels), f32)],
        compiler_params=compiler_params,
    )(norms, w_tri_out, w_key, w_value, *edges)
    return pl.pallas_call(
        functools.partial(attention_kernel, row_count, res, 8, 16),
        out_shape=jax.ShapeDtypeStruct(pair_rep.shape, bf16),
        in_specs=[in_vmem] * 9,
        out_specs=in_vmem,
        scratch_shapes=[
            pltpu.VMEM((row_count * res * res, channels), f32),
            pltpu.VMEM((row_count * res, channels), f32),
        ],
        compiler_params=compiler_params,
    )(valid_column, w_query, w_att_gate, w_att_out, w_pair_bias.T, after_tri, att_in, keys, values)


def per_device(pair_rep, residue_valid, *parameters):
    row_count, res, channels = pair_rep.shape
    devices = res // row_count
    if res % 48 == 0 and devices in (4, 8, 16) and 40 * res * res * channels <= 32 * 1024 * 1024:
        return on_whole_complex(pair_rep, residue_valid, *parameters)
    return split_over_devices(pair_rep, residue_valid, *parameters)


def solution(mesh):
    return jax.shard_map(
        per_device,
        mesh=mesh,
        in_specs=(
            P(("groups", "row"), None, None),
            P("groups"),
            P(),
            P(),
            P(),
            P(),
            P(),
            P(),
            P(),
            P(),
            P(),
            P(),
            P(),
            P(),
            P(),
            P(),
            P(),
        ),
        out_specs=P(("groups", "row"), None, None),
        check_vma=False,
    )
```

```python
import functools
import math

import jax
import jax.numpy as jnp
from jax import lax
from jax.experimental import pallas as pl
from jax.experimental.pallas import tpu as pltpu
from jax.sharding import PartitionSpec as P

HEADS = 4
HEAD_DIM = 32


def layer_norm(values, norm_gain, norm_bias, along_axis):
    centre = values - jnp.mean(values, axis=along_axis, keepdims=True)
    spread = jnp.mean(centre * centre, axis=along_axis, keepdims=True)
    return centre * lax.rsqrt(spread + 1e-05) * norm_gain + norm_bias


def attend(query_cols, key_cols, value_cols, whole_bias, key_mask):
    factor = 1.0 / math.sqrt(HEAD_DIM)
    scores = (
        jnp.einsum("kjhd,ijhd->jhki", key_cols, query_cols, preferred_element_type=jnp.float32)
        * factor
    )
    scores = scores + whole_bias.astype(jnp.float32)[None] + key_mask[None, None, :, None]
    scores = scores - jnp.max(scores, axis=2, keepdims=True)
    exponent = jnp.exp(scores)
    weights = (exponent / jnp.sum(exponent, axis=2, keepdims=True)).astype(jnp.bfloat16)
    return jnp.einsum("jhki,kjhd->ijhd", weights, value_cols, preferred_element_type=jnp.float32)


def split_over_devices(
    pair_rep,
    residue_valid,
    tri_norm_gain,
    tri_norm_bias,
    w_edges,
    w_tri_gate,
    out_norm_gain,
    out_norm_bias,
    w_tri_out,
    att_norm_gain,
    att_norm_bias,
    w_query,
    w_key,
    w_value,
    w_att_gate,
    w_pair_bias,
    w_att_out,
):
    row_count = pair_rep.shape[0]
    res_count = pair_rep.shape[1]
    channels = pair_rep.shape[2]
    hidden_width = HEADS * HEAD_DIM
    row_start = lax.axis_index("row") * row_count
    valid_flags = residue_valid.astype(jnp.float32)
    own_valid = lax.dynamic_slice_in_dim(valid_flags, row_start, row_count)
    normed = layer_norm(pair_rep.astype(jnp.float32), tri_norm_gain, tri_norm_bias, 2).astype(
        jnp.bfloat16
    )
    projected = jnp.einsum("ikd,de->eik", normed, w_edges, preferred_element_type=jnp.float32)
    projected = projected.reshape(4, channels, row_count, res_count)
    pair_mask = (own_valid[:, None] * valid_flags[None, :])[None, :, :]
    left_edges = (jax.nn.sigmoid(projected[1]) * projected[0] * pair_mask).astype(jnp.bfloat16)
    right_edges = (jax.nn.sigmoid(projected[3]) * projected[2] * pair_mask).astype(jnp.bfloat16)
    left_cols, right_cols = (
        lax.all_to_all(left_edges, "row", split_axis=0, concat_axis=1, tiled=True),
        lax.all_to_all(right_edges, "row", split_axis=0, concat_axis=1, tiled=True),
    )
    block_product = jnp.einsum(
        "cik,cjk->cij", left_cols, right_cols, preferred_element_type=jnp.float32
    ).astype(jnp.bfloat16)
    triangle = lax.all_to_all(block_product, "row", split_axis=1, concat_axis=0, tiled=True)
    tri_normed = layer_norm(
        triangle.astype(jnp.float32), out_norm_gain[:, None, None], out_norm_bias[:, None, None], 0
    ).astype(jnp.bfloat16)
    tri_gate = jax.nn.sigmoid(
        jnp.einsum("ijc,ce->ije", normed, w_tri_gate, preferred_element_type=jnp.float32)
    )
    tri_update = jnp.einsum(
        "cij,ce->ije", tri_normed, w_tri_out, preferred_element_type=jnp.float32
    )
    after_tri = pair_rep.astype(jnp.float32) + tri_gate * tri_update
    att_in = layer_norm(after_tri, att_norm_gain, att_norm_bias, 2).astype(jnp.bfloat16)
    pair_bias = jnp.einsum(
        "kic,ch->hki", att_in, w_pair_bias, preferred_element_type=jnp.float32
    ).astype(jnp.bfloat16)
    whole_bias = lax.all_gather(pair_bias, "row", axis=1, tiled=True)
    key_mask = 1000000000.0 * (valid_flags - 1.0)
    columns = lax.all_to_all(att_in, "row", split_axis=1, concat_axis=0, tiled=True)
    all_weights = jnp.concatenate([w_query, w_key, w_value, w_att_gate], axis=1)
    joined = jnp.dot(columns.reshape(-1, channels), all_weights, preferred_element_type=jnp.float32)
    query_cols = (
        joined[:, :hidden_width].astype(jnp.bfloat16).reshape(res_count, row_count, HEADS, HEAD_DIM)
    )
    key_cols = (
        joined[:, hidden_width : 2 * hidden_width]
        .astype(jnp.bfloat16)
        .reshape(res_count, row_count, HEADS, HEAD_DIM)
    )
    value_cols = (
        joined[:, 2 * hidden_width : 3 * hidden_width]
        .astype(jnp.bfloat16)
        .reshape(res_count, row_count, HEADS, HEAD_DIM)
    )
    gate_cols = jax.nn.sigmoid(joined[:, 3 * hidden_width :]).reshape(
        res_count, row_count, hidden_width
    )
    attended = attend(query_cols, key_cols, value_cols, whole_bias, key_mask)
    gated = (attended.reshape(res_count, row_count, hidden_width) * gate_cols).astype(jnp.bfloat16)
    gated_rows = lax.all_to_all(gated, "row", split_axis=0, concat_axis=1, tiled=True)
    final = after_tri + jnp.einsum(
        "ije,ec->ijc", gated_rows, w_att_out, preferred_element_type=jnp.float32
    )
    return final.astype(jnp.bfloat16)


def sigmoid(values):
    return 0.5 * jnp.tanh(0.5 * values) + 0.5


def dot(left, right):
    return jnp.dot(left, right, preferred_element_type=jnp.float32)


def rounded(values):
    return values.astype(jnp.bfloat16).astype(jnp.float32)


def edges_kernel(row_count, senders, valid_column, norms, weights, *refs):
    pair_refs = refs[: len(senders)]
    left_ref, right_ref, gate_ref, after_ref = refs[-4:]
    f32, bf16 = jnp.float32, jnp.bfloat16
    res = valid_column.shape[0]
    channels = valid_column.shape[1]
    pairs = jnp.concatenate(
        [ref[...].astype(f32).reshape(-1, channels) for ref in pair_refs], axis=0
    )
    normed = layer_norm(pairs, norms[0:1, :], norms[1:2, :], 1).astype(bf16)
    column = valid_column[...]
    rows_of = [
        jnp.bitwise_xor(lax.axis_index("row"), bits) * row_count + r
        for piece in senders
        for bits in piece
        for r in range(row_count)
    ]
    masks = jnp.concatenate([column * valid_column[pl.ds(i, 1), :] for i in rows_of], axis=0)
    joined = dot(normed, weights[:, : 2 * channels])
    left = rounded(sigmoid(joined[:, channels:]) * joined[:, :channels] * masks)
    joined = dot(normed, weights[:, 2 * channels : 4 * channels])
    right = rounded(sigmoid(joined[:, channels:]) * joined[:, :channels] * masks)
    gate = sigmoid(dot(normed, weights[:, 4 * channels :]))
    for n, i in enumerate(rows_of):
        rows = slice(n * res, (n + 1) * res)
        start = pl.multiple_of(i * res, res)
        left_ref[pl.ds(start, res), :] = left[rows]
        right_ref[pl.ds(i, res, stride=res), :] = right[rows]
        gate_ref[pl.ds(start, res), :] = gate[rows]
        after_ref[pl.ds(start, res), :] = pairs[rows]


def triangle_kernel(res, chunk, left_ref, right_ref, triangle_ref):
    channels = left_ref.shape[1]

    def triangle_of(step, carry):
        start = pl.multiple_of(step * chunk * res, chunk * res)
        totals = [jnp.zeros((res, channels), jnp.float32) for _ in range(chunk)]
        for k in range(res):
            right = right_ref[pl.ds(k * res, res), :]
            for r in range(chunk):
                totals[r] = totals[r] + left_ref[pl.ds(start + r * res + k, 1), :] * right
        for r in range(chunk):
            triangle_ref[pl.ds(start + r * res, res), :] = rounded(totals[r])
        return carry

    lax.fori_loop(0, res // chunk, triangle_of, 0)


def attention_inputs_kernel(
    res,
    chunk,
    norms,
    w_out,
    w_key,
    w_value,
    triangle_ref,
    gate_ref,
    pairs_ref,
    after_ref,
    att_ref,
    key_ref,
    value_ref,
):
    f32, bf16 = jnp.float32, jnp.bfloat16
    channels = triangle_ref.shape[1]
    key_value = jnp.concatenate([w_key[...], w_value[...]], axis=1)
    tall = chunk * res

    def inputs_of(step, carry):
        rows = pl.ds(pl.multiple_of(step * tall, tall), tall)
        triangle = triangle_ref[rows, :]
        tri_normed = layer_norm(triangle, norms[2:3, :], norms[3:4, :], 1).astype(bf16)
        after_tri = pairs_ref[rows, :] + gate_ref[rows, :] * dot(tri_normed, w_out[...])
        att_in = layer_norm(after_tri, norms[4:5, :], norms[5:6, :], 1).astype(bf16)
        joined = dot(att_in, key_value)
        after_ref[rows, :] = after_tri
        att_ref[rows, :] = att_in.astype(f32)
        key_ref[rows, :] = rounded(joined[:, :channels])
        value_ref[rows, :] = rounded(joined[:, channels:])
        return carry

    lax.fori_loop(0, res // chunk, inputs_of, 0)


def attention_kernel(
    row_count,
    res,
    key_chunk,
    valid_column,
    w_query,
    w_gate,
    w_out,
    head_bias,
    after_ref,
    att_ref,
    key_ref,
    value_ref,
    out_ref,
    score_ref,
    bias_ref,
):
    f32, bf16 = jnp.float32, jnp.bfloat16
    channels = key_ref.shape[1]
    own = lax.axis_index("row") * row_count
    own_start = pl.multiple_of(own * res, res)
    own_in = att_ref[pl.ds(own_start, row_count * res), :].astype(bf16)
    factor = 1.0 / math.sqrt(HEAD_DIM)
    query = rounded(dot(own_in, w_query[...])) * factor
    att_gate = sigmoid(dot(own_in, w_gate[...]))
    row = lax.broadcasted_iota(jnp.int32, (channels, HEADS), 0) // HEAD_DIM
    head = lax.broadcasted_iota(jnp.int32, (channels, HEADS), 1)
    repeat = jnp.where(row == head, 1.0, 0.0).astype(bf16)
    wide_bias = dot(repeat, head_bias[...]).astype(bf16)
    for r in range(row_count):
        column = att_ref[pl.ds(own + r, res, stride=res), :].astype(bf16)
        bias_ref[r * res : (r + 1) * res, :] = rounded(
            lax.dot_general(
                column, wide_bias, (((1,), (1,)), ((), ())), preferred_element_type=f32
            )
        )

    row = lax.broadcasted_iota(jnp.int32, (2 * channels, channels), 0) % channels // HEAD_DIM
    column = lax.broadcasted_iota(jnp.int32, (2 * channels, channels), 1) // HEAD_DIM
    same_head = jnp.where(row == column, 1.0, 0.0).astype(bf16)

    def scores_of(step, maxima):
        maxima = list(maxima)
        products = []
        for offset in range(key_chunk):
            keys = key_ref[pl.ds((step * key_chunk + offset) * res, res), :]
            products.append(jnp.concatenate([keys] * row_count, axis=0) * query)
        product = jnp.concatenate(products, axis=0)
        high = product.astype(bf16)
        low = (product - high.astype(f32)).astype(bf16)
        scores = dot(jnp.concatenate([high, low], axis=1), same_head)
        for offset in range(key_chunk):
            k = step * key_chunk + offset
            key_mask = 1000000000.0 * (valid_column[pl.ds(k, 1), :] - 1.0)
            for r in range(row_count):
                at = (offset * row_count + r) * res
                score = scores[at : at + res] + bias_ref[pl.ds(r * res + k, 1), :] + key_mask
                score_ref[pl.ds((r * res + k) * res, res), :] = score
                maxima[r] = jnp.maximum(maxima[r], score)
        return tuple(maxima)

    lowest = jnp.full((res, channels), -jnp.inf, f32)
    maxima = lax.fori_loop(0, res // key_chunk, scores_of, (lowest,) * row_count)

    attended = []
    for r in range(row_count):
        total = mixed = jnp.zeros((res, channels), f32)
        for k in range(res):
            weight = jnp.exp(score_ref[pl.ds((r * res + k) * res, res), :] - maxima[r])
            total = total + weight
            mixed = mixed + weight * value_ref[pl.ds(k * res, res), :]
        attended.append(mixed / total)
    gated = (jnp.concatenate(attended, axis=0) * att_gate).astype(bf16)
    after_own = after_ref[pl.ds(own_start, row_count * res), :]
    final = after_own + dot(gated, w_out[...])
    out_ref[...] = final.astype(bf16).reshape(row_count, res, channels)


def on_whole_complex(
    pair_rep,
    residue_valid,
    tri_norm_gain,
    tri_norm_bias,
    w_edges,
    w_tri_gate,
    out_norm_gain,
    out_norm_bias,
    w_tri_out,
    att_norm_gain,
    att_norm_bias,
    w_query,
    w_key,
    w_value,
    w_att_gate,
    w_pair_bias,
    w_att_out,
):
    row_count, res, channels = pair_rep.shape
    devices = res // row_count
    f32, bf16 = jnp.float32, jnp.bfloat16
    in_vmem = pl.BlockSpec(memory_space=pltpu.VMEM)
    compiler_params = pltpu.CompilerParams(vmem_limit_bytes=24 * 1024 * 1024)
    tall = jax.ShapeDtypeStruct((res * res, channels), f32)

    def exchange(values, bit):
        return lax.ppermute(values, "row", [(d, d ^ bit) for d in range(devices)])

    vectors = (
        tri_norm_gain,
        tri_norm_bias,
        out_norm_gain,
        out_norm_bias,
        att_norm_gain,
        att_norm_bias,
    )
    norms = jnp.stack(vectors)
    edge_weights = jnp.concatenate([w_edges, w_tri_gate], axis=1)
    valid_column = jnp.broadcast_to(residue_valid.astype(f32)[:, None], (res, channels))

    def edges_of(pieces, edges):
        pairs = [p for p, _ in pieces]
        senders = tuple(s for _, s in pieces)
        operands = 3 + len(pieces)
        return pl.pallas_call(
            functools.partial(edges_kernel, row_count, senders),
            out_shape=(tall,) * 4,
            in_specs=[in_vmem] * (operands + len(edges)),
            out_specs=(in_vmem,) * 4,
            input_output_aliases={operands + e: e for e in range(len(edges))},
            compiler_params=compiler_params,
            cost_estimate=pl.CostEstimate(
                flops=10 * sum(p.size for p in pairs) * channels,
                bytes_accessed=2**25,
                transcendentals=0,
            ),
        )(valid_column, norms, edge_weights, *pairs, *edges)

    senders = (0,)
    own = pair_rep
    bit = devices // 2
    while bit > 4:
        twice = jnp.zeros((2 * own.shape[0],) + own.shape[1:], bf16)
        kept = lax.dynamic_update_slice(twice, own, (0, 0, 0))
        far = exchange(own, bit)
        if bit == devices // 2:
            far, kept, norms, edge_weights = lax.optimization_barrier(
                (far, kept, norms, edge_weights)
            )
        own = lax.dynamic_update_slice(kept, far, (own.shape[0], 0, 0))
        senders = senders + tuple(s ^ bit for s in senders)
        bit //= 2

    def from_sender(bits):
        return tuple(s ^ bits for s in senders)

    diagonal = exchange(own, 6)
    beside = exchange(own, 2)
    near = exchange(own, 4)
    across = exchange(own, 1)
    edges = edges_of([(own, senders), (across, from_sender(1))], ())
    diagonal, edges = lax.optimization_barrier((diagonal, edges))
    diagonal_across = exchange(diagonal, 1)
    beside_across = exchange(beside, 1)
    edges = edges_of([(diagonal, from_sender(6)), (beside, from_sender(2))], edges)
    near, edges = lax.optimization_barrier((near, edges))
    near_across = exchange(near, 1)
    edges = edges_of(
        [
            (diagonal_across, from_sender(7)),
            (beside_across, from_sender(3)),
            (near, from_sender(4)),
        ],
        edges,
    )
    edges = edges_of([(near_across, from_sender(5))], edges)

    left, right, gate, pairs = edges
    triangle = pl.pallas_call(
        functools.partial(triangle_kernel, res, 6),
        out_shape=tall,
        in_specs=[in_vmem] * 2,
        out_specs=in_vmem,
        compiler_params=compiler_params,
    )(left, right)
    after_tri, att_in, keys, values = pl.pallas_call(
        functools.partial(attention_inputs_kernel, res, 12),
        out_shape=(tall,) * 4,
        in_specs=[in_vmem] * 7,
        out_specs=(in_vmem,) * 4,
        compiler_params=compiler_params,
    )(norms, w_tri_out, w_key, w_value, triangle, gate, pairs)
    return pl.pallas_call(
        functools.partial(attention_kernel, row_count, res, 8),
        out_shape=jax.ShapeDtypeStruct(pair_rep.shape, bf16),
        in_specs=[in_vmem] * 9,
        out_specs=in_vmem,
        scratch_shapes=[
            pltpu.VMEM((row_count * res * res, channels), f32),
            pltpu.VMEM((row_count * res, channels), f32),
        ],
        compiler_params=compiler_params,
    )(valid_column, w_query, w_att_gate, w_att_out, w_pair_bias.T, after_tri, att_in, keys, values)


def per_device(pair_rep, residue_valid, *parameters):
    row_count, res, channels = pair_rep.shape
    devices = res // row_count
    if res % 48 == 0 and devices in (8, 16) and 40 * res * res * channels <= 32 * 1024 * 1024:
        return on_whole_complex(pair_rep, residue_valid, *parameters)
    return split_over_devices(pair_rep, residue_valid, *parameters)


def solution(mesh):
    return jax.shard_map(
        per_device,
        mesh=mesh,
        in_specs=(
            P(("groups", "row"), None, None),
            P("groups"),
            P(),
            P(),
            P(),
            P(),
            P(),
            P(),
            P(),
            P(),
            P(),
            P(),
            P(),
            P(),
            P(),
            P(),
            P(),
        ),
        out_specs=P(("groups", "row"), None, None),
        check_vma=False,
    )
```

```python
import functools
import math

import jax
import jax.numpy as jnp
from jax import lax
from jax.experimental import pallas as pl
from jax.experimental.pallas import tpu as pltpu
from jax.sharding import PartitionSpec as P

HEADS = 4
HEAD_DIM = 32


def layer_norm(values, norm_gain, norm_bias, along_axis):
    centre = values - jnp.mean(values, axis=along_axis, keepdims=True)
    spread = jnp.mean(centre * centre, axis=along_axis, keepdims=True)
    return centre * lax.rsqrt(spread + 1e-05) * norm_gain + norm_bias


def attend(query_cols, key_cols, value_cols, whole_bias, key_mask):
    factor = 1.0 / math.sqrt(HEAD_DIM)
    scores = (
        jnp.einsum("kjhd,ijhd->jhki", key_cols, query_cols, preferred_element_type=jnp.float32)
        * factor
    )
    scores = scores + whole_bias.astype(jnp.float32)[None] + key_mask[None, None, :, None]
    scores = scores - jnp.max(scores, axis=2, keepdims=True)
    exponent = jnp.exp(scores)
    weights = (exponent / jnp.sum(exponent, axis=2, keepdims=True)).astype(jnp.bfloat16)
    return jnp.einsum("jhki,kjhd->ijhd", weights, value_cols, preferred_element_type=jnp.float32)


def split_over_devices(
    pair_rep,
    residue_valid,
    tri_norm_gain,
    tri_norm_bias,
    w_edges,
    w_tri_gate,
    out_norm_gain,
    out_norm_bias,
    w_tri_out,
    att_norm_gain,
    att_norm_bias,
    w_query,
    w_key,
    w_value,
    w_att_gate,
    w_pair_bias,
    w_att_out,
):
    row_count = pair_rep.shape[0]
    res_count = pair_rep.shape[1]
    channels = pair_rep.shape[2]
    hidden_width = HEADS * HEAD_DIM
    row_start = lax.axis_index("row") * row_count
    valid_flags = residue_valid.astype(jnp.float32)
    own_valid = lax.dynamic_slice_in_dim(valid_flags, row_start, row_count)
    normed = layer_norm(pair_rep.astype(jnp.float32), tri_norm_gain, tri_norm_bias, 2).astype(
        jnp.bfloat16
    )
    projected = jnp.einsum("ikd,de->eik", normed, w_edges, preferred_element_type=jnp.float32)
    projected = projected.reshape(4, channels, row_count, res_count)
    pair_mask = (own_valid[:, None] * valid_flags[None, :])[None, :, :]
    left_edges = (jax.nn.sigmoid(projected[1]) * projected[0] * pair_mask).astype(jnp.bfloat16)
    right_edges = (jax.nn.sigmoid(projected[3]) * projected[2] * pair_mask).astype(jnp.bfloat16)
    left_cols, right_cols = (
        lax.all_to_all(left_edges, "row", split_axis=0, concat_axis=1, tiled=True),
        lax.all_to_all(right_edges, "row", split_axis=0, concat_axis=1, tiled=True),
    )
    block_product = jnp.einsum(
        "cik,cjk->cij", left_cols, right_cols, preferred_element_type=jnp.float32
    ).astype(jnp.bfloat16)
    triangle = lax.all_to_all(block_product, "row", split_axis=1, concat_axis=0, tiled=True)
    tri_normed = layer_norm(
        triangle.astype(jnp.float32), out_norm_gain[:, None, None], out_norm_bias[:, None, None], 0
    ).astype(jnp.bfloat16)
    tri_gate = jax.nn.sigmoid(
        jnp.einsum("ijc,ce->ije", normed, w_tri_gate, preferred_element_type=jnp.float32)
    )
    tri_update = jnp.einsum(
        "cij,ce->ije", tri_normed, w_tri_out, preferred_element_type=jnp.float32
    )
    after_tri = pair_rep.astype(jnp.float32) + tri_gate * tri_update
    att_in = layer_norm(after_tri, att_norm_gain, att_norm_bias, 2).astype(jnp.bfloat16)
    pair_bias = jnp.einsum(
        "kic,ch->hki", att_in, w_pair_bias, preferred_element_type=jnp.float32
    ).astype(jnp.bfloat16)
    whole_bias = lax.all_gather(pair_bias, "row", axis=1, tiled=True)
    key_mask = 1000000000.0 * (valid_flags - 1.0)
    columns = lax.all_to_all(att_in, "row", split_axis=1, concat_axis=0, tiled=True)
    all_weights = jnp.concatenate([w_query, w_key, w_value, w_att_gate], axis=1)
    joined = jnp.dot(columns.reshape(-1, channels), all_weights, preferred_element_type=jnp.float32)
    query_cols = (
        joined[:, :hidden_width].astype(jnp.bfloat16).reshape(res_count, row_count, HEADS, HEAD_DIM)
    )
    key_cols = (
        joined[:, hidden_width : 2 * hidden_width]
        .astype(jnp.bfloat16)
        .reshape(res_count, row_count, HEADS, HEAD_DIM)
    )
    value_cols = (
        joined[:, 2 * hidden_width : 3 * hidden_width]
        .astype(jnp.bfloat16)
        .reshape(res_count, row_count, HEADS, HEAD_DIM)
    )
    gate_cols = jax.nn.sigmoid(joined[:, 3 * hidden_width :]).reshape(
        res_count, row_count, hidden_width
    )
    attended = attend(query_cols, key_cols, value_cols, whole_bias, key_mask)
    gated = (attended.reshape(res_count, row_count, hidden_width) * gate_cols).astype(jnp.bfloat16)
    gated_rows = lax.all_to_all(gated, "row", split_axis=0, concat_axis=1, tiled=True)
    final = after_tri + jnp.einsum(
        "ije,ec->ijc", gated_rows, w_att_out, preferred_element_type=jnp.float32
    )
    return final.astype(jnp.bfloat16)


def sigmoid(values):
    return 0.5 * jnp.tanh(0.5 * values) + 0.5


def dot(left, right):
    return jnp.dot(left, right, preferred_element_type=jnp.float32)


def rounded(values):
    return values.astype(jnp.bfloat16).astype(jnp.float32)


def chip_and_core():
    device = lax.axis_index("row")
    return lax.shift_right_logical(device, 1), jnp.bitwise_and(device, 1)


def rows_of_blocks(row_count, blocks):
    chip, _ = chip_and_core()
    return [(jnp.bitwise_xor(chip, bits), r) for bits in blocks for r in range(row_count)]


def edges_kernel(row_count, chips, pieces, valid_column, norms, weights, *refs):
    pair_refs = refs[: len(pieces)]
    left_ref, right_ref, gate_ref, pairs_ref, send_ref = refs[-5:]
    f32, bf16 = jnp.float32, jnp.bfloat16
    res, channels = valid_column.shape
    _, core = chip_and_core()
    pairs = jnp.concatenate(
        [ref[...].astype(f32).reshape(-1, channels) for ref in pair_refs], axis=0
    )
    normed = layer_norm(pairs, norms[0:1, :], norms[1:2, :], 1).astype(bf16)
    column = valid_column[...]
    rows_of = rows_of_blocks(row_count, [bits for piece in pieces for bits in piece])
    masks = jnp.concatenate(
        [
            column * valid_column[pl.ds((2 * chip + core) * row_count + r, 1), :]
            for chip, r in rows_of
        ],
        axis=0,
    )
    joined = dot(normed, weights[:, : 2 * channels])
    left = rounded(sigmoid(joined[:, channels:]) * joined[:, :channels] * masks)
    joined = dot(normed, weights[:, 2 * channels : 4 * channels])
    right = (sigmoid(joined[:, channels:]) * joined[:, :channels] * masks).astype(bf16)
    gate = sigmoid(dot(normed, weights[:, 4 * channels :]))
    for n, (chip, r) in enumerate(rows_of):
        rows = slice(n * res, (n + 1) * res)
        start = pl.multiple_of((chip * row_count + r) * res, res)
        send_ref[n] = right[rows]
        left_ref[pl.ds(start, res), :] = left[rows]
        place_right(right_ref, row_count, chips, chip, r, right[rows])
        gate_ref[pl.ds(start, res), :] = gate[rows]
        pairs_ref[pl.ds(start, res), :] = pairs[rows]


def place_right(right_ref, row_count, chips, chip, r, edges):
    right_ref[pl.ds(r * chips + chip, edges.shape[0], stride=row_count * chips), :] = edges.astype(
        jnp.float32
    )


def triangle_rows(row_count, chips, left_ref, right_ref, triangle_ref, first, count, core):
    channels = left_ref.shape[1]
    columns = row_count * chips
    res = 2 * columns
    start = pl.multiple_of(first * res, res)
    totals = [jnp.zeros((columns, channels), jnp.float32) for _ in range(count)]
    for k in range(res):
        right = right_ref[pl.ds(k * columns, columns), :]
        for n in range(count):
            totals[n] = totals[n] + left_ref[pl.ds(start + n * res + k, 1), :] * right
    for n in range(count):
        for r in range(row_count):
            triangle_ref[
                pl.ds(start + n * res + core * row_count + r, chips, stride=2 * row_count), :
            ] = rounded(totals[n][r * chips : (r + 1) * chips])


def near_triangle_kernel(row_count, chips, chunk, pieces, left_ref, right_ref, *refs):
    received, (triangle_ref, across_ref) = refs[:-2], refs[-2:]
    _, core = chip_and_core()

    def some_rows(step, carry):
        first = step * chunk
        triangle_rows(
            row_count, chips, left_ref, right_ref, triangle_ref, first, chunk, core
        )
        return carry

    for ref, blocks in zip(received, pieces):
        for n, (chip, r) in enumerate(rows_of_blocks(row_count, blocks)):
            place_right(across_ref, row_count, chips, chip, r, ref[n])
    lax.fori_loop(0, row_count * chips // chunk, some_rows, 0)


def attention_inputs_kernel(
    row_count, chips, chunk, part, pieces, norms, w_out, left_ref, gate_ref, pairs_ref, *refs
):
    f32, bf16 = jnp.float32, jnp.bfloat16
    received = refs[: len(pieces)]
    triangle_ref, across_ref, after_ref, att_ref = refs[-4:]
    _, core = chip_and_core()
    half = row_count * chips
    tall = (half // 2) * 2 * half
    for ref, blocks in zip(received, pieces):
        for n, (chip, r) in enumerate(rows_of_blocks(row_count, blocks)):
            place_right(across_ref, row_count, chips, chip, r, ref[n])

    def some_rows(step, carry):
        first = part * (half // 2) + step * chunk
        triangle_rows(
            row_count, chips, left_ref, across_ref, triangle_ref, first, chunk, 1 - core
        )
        return carry

    lax.fori_loop(0, half // 2 // chunk, some_rows, 0)
    rows = slice(part * tall, (part + 1) * tall)
    tri_normed = layer_norm(triangle_ref[rows, :], norms[2:3, :], norms[3:4, :], 1).astype(bf16)
    after_tri = pairs_ref[rows, :] + gate_ref[rows, :] * dot(tri_normed, w_out[...])
    att_in = layer_norm(after_tri, norms[4:5, :], norms[5:6, :], 1).astype(bf16)
    after_ref[...] = after_tri
    att_ref[...] = att_in


def column_bias(att_ref, row_count, keys, res, head_bias):
    bf16, channels = jnp.bfloat16, att_ref.shape[1]
    row = lax.broadcasted_iota(jnp.int32, (channels, HEADS), 0) // HEAD_DIM
    head = lax.broadcasted_iota(jnp.int32, (channels, HEADS), 1)
    repeat = jnp.where(row == head, 1.0, 0.0).astype(bf16)
    wide_bias = dot(repeat, head_bias[...]).astype(bf16)
    own = lax.axis_index("row") * row_count
    for r in range(row_count):
        column = att_ref[pl.ds(own + r, keys, stride=res), :].astype(bf16)
        yield rounded(
            lax.dot_general(
                column, wide_bias, (((1,), (1,)), ((), ())), preferred_element_type=jnp.float32
            )
        )


def scores_of_keys(row_count, chips, query, key_ref, bias_ref, valid_column, first, at, core, res):
    bf16, f32, channels = jnp.bfloat16, jnp.float32, key_ref.shape[1]
    count = row_count * chips // 2
    row = lax.broadcasted_iota(jnp.int32, (2 * channels, channels), 0) % channels // HEAD_DIM
    column = lax.broadcasted_iota(jnp.int32, (2 * channels, channels), 1) // HEAD_DIM
    same_head = jnp.where(row == column, 1.0, 0.0).astype(bf16)
    products = []
    for n in range(count):
        keys = key_ref[pl.ds(pl.multiple_of((at + n) * res, res), res), :]
        products.append(jnp.concatenate([keys] * row_count, axis=0) * query)
    product = jnp.concatenate(products, axis=0)
    high = product.astype(bf16)
    low = (product - high.astype(f32)).astype(bf16)
    scores = dot(jnp.concatenate([high, low], axis=1), same_head)
    for n in range(count):
        k = (2 * (first + n // row_count) + core) * row_count + n % row_count
        key_mask = 1000000000.0 * (valid_column[pl.ds(k, 1), :] - 1.0)
        for r in range(row_count):
            score = scores[(n * row_count + r) * res : (n * row_count + r + 1) * res]
            yield r, n, score + bias_ref[r, pl.ds(at + n, 1), :] + key_mask


def most_scores_kernel(
    row_count,
    chips,
    valid_column,
    w_query,
    w_gate,
    w_key,
    w_value,
    head_bias,
    own_att_a,
    own_att_b,
    far_att_a,
    own_after_a,
    own_after_b,
    score_ref,
    maxima_ref,
    value_ref,
    query_ref,
    gate_ref,
    after_ref,
    att_ref,
    key_ref,
    bias_ref,
):
    f32, bf16 = jnp.float32, jnp.bfloat16
    chip, core = chip_and_core()
    half = row_count * chips
    res = 2 * half
    channels = att_ref.shape[1]
    tall = half // 2 * res
    att = [ref[...] for ref in (own_att_a, own_att_b, far_att_a)]
    key_value = jnp.concatenate([w_key[...], w_value[...]], axis=1)
    for n, values in enumerate(att):
        att_ref[n * tall : (n + 1) * tall, :] = values.astype(f32)
        joined = dot(values, key_value)
        key_ref[n * tall : (n + 1) * tall, :] = rounded(joined[:, :channels])
        value_ref[n * tall : (n + 1) * tall, :] = rounded(joined[:, channels:])
    own = row_count * res
    own_in = att_ref[pl.ds(pl.multiple_of(chip * own, own), own), :].astype(bf16)
    query = rounded(dot(own_in, w_query[...])) * (1.0 / math.sqrt(HEAD_DIM))
    query_ref[...] = query
    gate_ref[...] = sigmoid(dot(own_in, w_gate[...]))
    chip_a = pl.multiple_of(jnp.minimum(chip, chips // 2 - 1) * own, own)
    chip_b = pl.multiple_of(jnp.maximum(chip - chips // 2, 0) * own, own)
    after_ref[...] = jnp.where(
        chip < chips // 2, own_after_a[pl.ds(chip_a, own), :], own_after_b[pl.ds(chip_b, own), :]
    )
    keys = 3 * half // 2
    for r, bias in enumerate(column_bias(att_ref, row_count, keys, res, head_bias)):
        bias_ref[r, :keys, :] = bias

    def scores_of(step, maxima):
        maxima = list(maxima)
        at = step * (half // 2)
        first = lax.rem(step, 2) * (chips // 2)
        sender = jnp.where(step < 2, core, 1 - core)
        for r, n, score in scores_of_keys(
            row_count, chips, query, key_ref, bias_ref, valid_column, first, at, sender, res
        ):
            start = pl.multiple_of((r * keys + at + n) * res, res)
            score_ref[pl.ds(start, res), :] = score
            maxima[r] = jnp.maximum(maxima[r], score)
        return tuple(maxima)

    lowest = jnp.full((res, channels), -jnp.inf, f32)
    maxima = lax.fori_loop(0, 3, scores_of, (lowest,) * row_count)
    for r in range(row_count):
        maxima_ref[r] = maxima[r]


def attention_kernel(
    row_count,
    chips,
    valid_column,
    w_key,
    w_value,
    w_out,
    head_bias,
    far_att_b,
    score_ref,
    maxima_ref,
    value_ref,
    query_ref,
    gate_ref,
    after_ref,
    out_ref,
    att_ref,
    key_ref,
    bias_ref,
):
    f32, bf16 = jnp.float32, jnp.bfloat16
    _, core = chip_and_core()
    half = row_count * chips
    res = 2 * half
    channels = att_ref.shape[1]
    key_value = jnp.concatenate([w_key[...], w_value[...]], axis=1)
    far_att = far_att_b[...]
    att_ref[...] = far_att.astype(f32)
    joined = dot(far_att, key_value)
    key_ref[...] = rounded(joined[:, :channels])
    last_values = rounded(joined[:, channels:])
    for r, bias in enumerate(column_bias(att_ref, row_count, half // 2, res, head_bias)):
        bias_ref[r, : half // 2, :] = bias
    maxima = [maxima_ref[r] for r in range(row_count)]
    last_scores = [[] for _ in range(row_count)]
    for r, _, score in scores_of_keys(
        row_count,
        chips,
        query_ref[...],
        key_ref,
        bias_ref,
        valid_column,
        chips // 2,
        0,
        1 - core,
        res,
    ):
        last_scores[r].append(score)
        maxima[r] = jnp.maximum(maxima[r], score)
    keys = 3 * half // 2
    attended = []
    for r in range(row_count):
        total = mixed = jnp.zeros((res, channels), f32)
        for n in range(half // 2):
            weight = jnp.exp(last_scores[r][n] - maxima[r])
            total = total + weight
            mixed = mixed + weight * last_values[n * res : (n + 1) * res]
        for n in range(keys):
            weight = jnp.exp(score_ref[(r * keys + n) * res : (r * keys + n + 1) * res] - maxima[r])
            total = total + weight
            mixed = mixed + weight * value_ref[n * res : (n + 1) * res]
        attended.append(mixed / total)
    gated = (jnp.concatenate(attended, axis=0) * gate_ref[...]).astype(bf16)
    final = after_ref[...] + dot(gated, w_out[...])
    out_ref[...] = final.astype(bf16).reshape(row_count, res, channels)


def on_whole_complex(
    pair_rep,
    residue_valid,
    tri_norm_gain,
    tri_norm_bias,
    w_edges,
    w_tri_gate,
    out_norm_gain,
    out_norm_bias,
    w_tri_out,
    att_norm_gain,
    att_norm_bias,
    w_query,
    w_key,
    w_value,
    w_att_gate,
    w_pair_bias,
    w_att_out,
):
    row_count, res, channels = pair_rep.shape
    devices = res // row_count
    chips = devices // 2
    half = res // 2
    f32, bf16 = jnp.float32, jnp.bfloat16
    in_vmem = pl.BlockSpec(memory_space=pltpu.VMEM)

    def shaped(dtype, *shape):
        return jax.ShapeDtypeStruct(shape, dtype)

    def call(kernel, outs, operands, aliases=None, scratch=(), cost=2**25):
        return pl.pallas_call(
            kernel,
            out_shape=outs,
            in_specs=[in_vmem] * len(operands),
            out_specs=jax.tree.map(lambda _: in_vmem, outs),
            input_output_aliases=aliases or {},
            scratch_shapes=list(scratch),
            compiler_params=pltpu.CompilerParams(vmem_limit_bytes=24 * 1024 * 1024),
            cost_estimate=pl.CostEstimate(flops=2**20, bytes_accessed=cost, transcendentals=0),
        )(*operands)

    def exchange(values, bit):
        return lax.ppermute(values, "row", [(d, d ^ bit) for d in range(devices)])

    vectors = (
        tri_norm_gain,
        tri_norm_bias,
        out_norm_gain,
        out_norm_bias,
        att_norm_gain,
        att_norm_bias,
    )
    norms = jnp.stack(vectors)
    edge_weights = jnp.concatenate([w_edges, w_tri_gate], axis=1)
    valid_column = jnp.broadcast_to(residue_valid.astype(f32)[:, None], (res, channels))

    kept = lax.dynamic_update_slice(
        jnp.zeros((2 * row_count, res, channels), bf16), pair_rep, (0, 0, 0)
    )
    far = exchange(pair_rep, devices // 2)
    far, kept, norms, edge_weights, valid_column = lax.optimization_barrier(
        (far, kept, norms, edge_weights, valid_column)
    )
    own = lax.dynamic_update_slice(kept, far, (row_count, 0, 0))
    own_blocks = (0, chips // 2)

    def blocks_from(bits):
        return tuple(s ^ bits for s in own_blocks)

    edge_shapes = (shaped(f32, half * res, channels),) * 4

    def edges_of(pieces, edges):
        pairs = tuple(p for p, _ in pieces)
        blocks = tuple(b for _, b in pieces)
        sent = shaped(bf16, sum(p.shape[0] for p in pairs), res, channels)
        operands = (valid_column, norms, edge_weights) + pairs + edges
        first = len(operands) - len(edges)
        *edges, right = call(
            functools.partial(edges_kernel, row_count, chips, blocks),
            edge_shapes + (sent,),
            operands,
            {first + e: e for e in range(len(edges))},
        )
        return tuple(edges), (right, sum(blocks, ()))

    diagonal = exchange(own, 6)
    beside = exchange(own, 2)
    near = exchange(own, 4)
    edges, own_right = edges_of([(own, own_blocks)], ())
    diagonal, edges = lax.optimization_barrier((diagonal, edges))
    edges, side_right = edges_of(
        [(diagonal, blocks_from(3)), (beside, blocks_from(1))], edges
    )
    near, edges = lax.optimization_barrier((near, edges))
    edges, near_right = edges_of([(near, blocks_from(2))], edges)
    received = [(exchange(right, 1), b) for right, b in (own_right, side_right, near_right)]

    left, right, gate, pairs = edges
    tall = edge_shapes[0]
    triangle, across = call(
        functools.partial(
            near_triangle_kernel, row_count, chips, half // 2, [b for _, b in received[:2]]
        ),
        (tall, tall),
        (left, right) + tuple(r for r, _ in received[:2]),
    )
    part = half // 2 * res
    piece = (shaped(f32, part, channels), shaped(bf16, part, channels))

    def inputs_of(n, fresh, triangle, across):
        operands = (norms, w_tri_out, left, gate, pairs)
        operands += tuple(r for r, _ in fresh) + (triangle, across)
        return call(
            functools.partial(
                attention_inputs_kernel, row_count, chips, half // 2, n, [b for _, b in fresh]
            ),
            (tall, tall) + piece,
            operands,
            {len(operands) - 2: 0, len(operands) - 1: 1},
        )

    triangle, across, after_a, att_a = inputs_of(0, received[2:], triangle, across)
    far_att_a = exchange(att_a, 1)
    triangle, across, after_b, att_b = inputs_of(1, [], triangle, across)
    far_att_b = exchange(att_b, 1)

    keys = 3 * half // 2
    own_shape = shaped(f32, row_count * res, channels)
    scores, maxima, values, query, att_gate, after_own = call(
        functools.partial(most_scores_kernel, row_count, chips),
        (
            shaped(f32, row_count * keys * res, channels),
            shaped(f32, row_count, res, channels),
            shaped(f32, keys * res, channels),
            own_shape,
            own_shape,
            own_shape,
        ),
        (
            valid_column,
            w_query,
            w_att_gate,
            w_key,
            w_value,
            w_pair_bias.T,
            att_a,
            att_b,
            far_att_a,
            after_a,
            after_b,
        ),
        scratch=(
            pltpu.VMEM((keys * res, channels), f32),
            pltpu.VMEM((keys * res, channels), f32),
            pltpu.VMEM((row_count, 40, channels), f32),
        ),
    )
    return call(
        functools.partial(attention_kernel, row_count, chips),
        shaped(bf16, *pair_rep.shape),
        (
            valid_column,
            w_key,
            w_value,
            w_att_out,
            w_pair_bias.T,
            far_att_b,
            scores,
            maxima,
            values,
            query,
            att_gate,
            after_own,
        ),
        scratch=(
            pltpu.VMEM((part, channels), f32),
            pltpu.VMEM((part, channels), f32),
            pltpu.VMEM((row_count, 16, channels), f32),
        ),
    )


def per_device(pair_rep, residue_valid, *parameters):
    row_count, res, channels = pair_rep.shape
    devices = res // row_count
    if res % 48 == 0 and devices == 16 and 40 * res * res * channels <= 32 * 1024 * 1024:
        return on_whole_complex(pair_rep, residue_valid, *parameters)
    return split_over_devices(pair_rep, residue_valid, *parameters)


def solution(mesh):
    return jax.shard_map(
        per_device,
        mesh=mesh,
        in_specs=(
            P(("groups", "row"), None, None),
            P("groups"),
            P(),
            P(),
            P(),
            P(),
            P(),
            P(),
            P(),
            P(),
            P(),
            P(),
            P(),
            P(),
            P(),
            P(),
            P(),
        ),
        out_specs=P(("groups", "row"), None, None),
        check_vma=False,
    )
```

```python
import functools
import math

import jax
import jax.numpy as jnp
from jax import lax
from jax.experimental import pallas as pl
from jax.experimental.pallas import tpu as pltpu
from jax.sharding import PartitionSpec as P

HEADS = 4
HEAD_DIM = 32


def layer_norm(values, norm_gain, norm_bias, along_axis):
    centre = values - jnp.mean(values, axis=along_axis, keepdims=True)
    spread = jnp.mean(centre * centre, axis=along_axis, keepdims=True)
    return centre * lax.rsqrt(spread + 1e-05) * norm_gain + norm_bias


def attend(query_cols, key_cols, value_cols, whole_bias, key_mask):
    factor = 1.0 / math.sqrt(HEAD_DIM)
    scores = (
        jnp.einsum("kjhd,ijhd->jhki", key_cols, query_cols, preferred_element_type=jnp.float32)
        * factor
    )
    scores = scores + whole_bias.astype(jnp.float32)[None] + key_mask[None, None, :, None]
    scores = scores - jnp.max(scores, axis=2, keepdims=True)
    exponent = jnp.exp(scores)
    weights = (exponent / jnp.sum(exponent, axis=2, keepdims=True)).astype(jnp.bfloat16)
    return jnp.einsum("jhki,kjhd->ijhd", weights, value_cols, preferred_element_type=jnp.float32)


def split_over_devices(
    pair_rep,
    residue_valid,
    tri_norm_gain,
    tri_norm_bias,
    w_edges,
    w_tri_gate,
    out_norm_gain,
    out_norm_bias,
    w_tri_out,
    att_norm_gain,
    att_norm_bias,
    w_query,
    w_key,
    w_value,
    w_att_gate,
    w_pair_bias,
    w_att_out,
):
    row_count = pair_rep.shape[0]
    res_count = pair_rep.shape[1]
    channels = pair_rep.shape[2]
    hidden_width = HEADS * HEAD_DIM
    row_start = lax.axis_index("row") * row_count
    valid_flags = residue_valid.astype(jnp.float32)
    own_valid = lax.dynamic_slice_in_dim(valid_flags, row_start, row_count)
    normed = layer_norm(pair_rep.astype(jnp.float32), tri_norm_gain, tri_norm_bias, 2).astype(
        jnp.bfloat16
    )
    projected = jnp.einsum("ikd,de->eik", normed, w_edges, preferred_element_type=jnp.float32)
    projected = projected.reshape(4, channels, row_count, res_count)
    pair_mask = (own_valid[:, None] * valid_flags[None, :])[None, :, :]
    left_edges = (jax.nn.sigmoid(projected[1]) * projected[0] * pair_mask).astype(jnp.bfloat16)
    right_edges = (jax.nn.sigmoid(projected[3]) * projected[2] * pair_mask).astype(jnp.bfloat16)
    left_cols, right_cols = (
        lax.all_to_all(left_edges, "row", split_axis=0, concat_axis=1, tiled=True),
        lax.all_to_all(right_edges, "row", split_axis=0, concat_axis=1, tiled=True),
    )
    block_product = jnp.einsum(
        "cik,cjk->cij", left_cols, right_cols, preferred_element_type=jnp.float32
    ).astype(jnp.bfloat16)
    triangle = lax.all_to_all(block_product, "row", split_axis=1, concat_axis=0, tiled=True)
    tri_normed = layer_norm(
        triangle.astype(jnp.float32), out_norm_gain[:, None, None], out_norm_bias[:, None, None], 0
    ).astype(jnp.bfloat16)
    tri_gate = jax.nn.sigmoid(
        jnp.einsum("ijc,ce->ije", normed, w_tri_gate, preferred_element_type=jnp.float32)
    )
    tri_update = jnp.einsum(
        "cij,ce->ije", tri_normed, w_tri_out, preferred_element_type=jnp.float32
    )
    after_tri = pair_rep.astype(jnp.float32) + tri_gate * tri_update
    att_in = layer_norm(after_tri, att_norm_gain, att_norm_bias, 2).astype(jnp.bfloat16)
    pair_bias = jnp.einsum(
        "kic,ch->hki", att_in, w_pair_bias, preferred_element_type=jnp.float32
    ).astype(jnp.bfloat16)
    whole_bias = lax.all_gather(pair_bias, "row", axis=1, tiled=True)
    key_mask = 1000000000.0 * (valid_flags - 1.0)
    columns = lax.all_to_all(att_in, "row", split_axis=1, concat_axis=0, tiled=True)
    all_weights = jnp.concatenate([w_query, w_key, w_value, w_att_gate], axis=1)
    joined = jnp.dot(columns.reshape(-1, channels), all_weights, preferred_element_type=jnp.float32)
    query_cols = (
        joined[:, :hidden_width].astype(jnp.bfloat16).reshape(res_count, row_count, HEADS, HEAD_DIM)
    )
    key_cols = (
        joined[:, hidden_width : 2 * hidden_width]
        .astype(jnp.bfloat16)
        .reshape(res_count, row_count, HEADS, HEAD_DIM)
    )
    value_cols = (
        joined[:, 2 * hidden_width : 3 * hidden_width]
        .astype(jnp.bfloat16)
        .reshape(res_count, row_count, HEADS, HEAD_DIM)
    )
    gate_cols = jax.nn.sigmoid(joined[:, 3 * hidden_width :]).reshape(
        res_count, row_count, hidden_width
    )
    attended = attend(query_cols, key_cols, value_cols, whole_bias, key_mask)
    gated = (attended.reshape(res_count, row_count, hidden_width) * gate_cols).astype(jnp.bfloat16)
    gated_rows = lax.all_to_all(gated, "row", split_axis=0, concat_axis=1, tiled=True)
    final = after_tri + jnp.einsum(
        "ije,ec->ijc", gated_rows, w_att_out, preferred_element_type=jnp.float32
    )
    return final.astype(jnp.bfloat16)


def sigmoid(values):
    return 0.5 * jnp.tanh(0.5 * values) + 0.5


def dot(left, right):
    return jnp.dot(left, right, preferred_element_type=jnp.float32)


def rounded(values):
    return values.astype(jnp.bfloat16).astype(jnp.float32)


def chip_and_core():
    device = lax.axis_index("row")
    return lax.shift_right_logical(device, 1), jnp.bitwise_and(device, 1)


def rows_of_blocks(row_count, blocks):
    chip, _ = chip_and_core()
    return [(jnp.bitwise_xor(chip, bits), r) for bits in blocks for r in range(row_count)]


def edges_kernel(row_count, chips, pieces, send_row, valid_column, norms, weights, *refs):
    pair_refs = refs[: len(pieces)]
    left_ref, right_ref, gate_ref, pairs_ref, send_ref = refs[-5:]
    f32, bf16 = jnp.float32, jnp.bfloat16
    res, channels = valid_column.shape
    _, core = chip_and_core()
    pairs = jnp.concatenate(
        [ref[...].astype(f32).reshape(-1, channels) for ref in pair_refs], axis=0
    )
    normed = layer_norm(pairs, norms[0:1, :], norms[1:2, :], 1).astype(bf16)
    column = valid_column[...]
    rows_of = rows_of_blocks(row_count, [bits for piece in pieces for bits in piece])
    masks = jnp.concatenate(
        [
            column * valid_column[pl.ds((2 * chip + core) * row_count + r, 1), :]
            for chip, r in rows_of
        ],
        axis=0,
    )
    joined = dot(normed, weights[:, : 2 * channels])
    left = rounded(sigmoid(joined[:, channels:]) * joined[:, :channels] * masks)
    joined = dot(normed, weights[:, 2 * channels : 4 * channels])
    right = (sigmoid(joined[:, channels:]) * joined[:, :channels] * masks).astype(bf16)
    gate = sigmoid(dot(normed, weights[:, 4 * channels :]))
    for n, (chip, r) in enumerate(rows_of):
        rows = slice(n * res, (n + 1) * res)
        start = pl.multiple_of((chip * row_count + r) * res, res)
        send_ref[send_row + n] = right[rows]
        left_ref[pl.ds(start, res), :] = left[rows]
        place_right(right_ref, chips, chip, r, right[rows])
        gate_ref[pl.ds(start, res), :] = gate[rows]
        pairs_ref[pl.ds(start, res), :] = pairs[rows]


def right_strides(res):
    return 3 * res + 1, 3


def place_right(right_ref, chips, chip, r, edges):
    res = edges.shape[0]
    column_stride, key_stride = right_strides(res)
    start = (r * chips + chip) * column_stride
    right_ref[pl.ds(start, res, stride=key_stride), :] = edges.astype(jnp.float32)


def triangle_rows(row_count, chips, left_ref, right_ref, triangle_ref, first, count, core):
    channels = left_ref.shape[1]
    columns = row_count * chips
    res = 2 * columns
    start = pl.multiple_of(first * res, res)
    column_stride, key_stride = right_strides(res)
    totals = [jnp.zeros((columns, channels), jnp.float32) for _ in range(count)]
    for k in range(res):
        right = right_ref[pl.ds(k * key_stride, columns, stride=column_stride), :]
        for n in range(count):
            totals[n] = totals[n] + left_ref[pl.ds(start + n * res + k, 1), :] * right
    for n in range(count):
        for r in range(row_count):
            triangle_ref[
                pl.ds(start + n * res + core * row_count + r, chips, stride=2 * row_count), :
            ] = rounded(totals[n][r * chips : (r + 1) * chips])


def near_triangle_kernel(row_count, chips, chunk, pieces, left_ref, right_ref, *refs):
    received, (triangle_ref, across_ref) = refs[:-2], refs[-2:]
    _, core = chip_and_core()

    def some_rows(step, carry):
        first = step * chunk
        triangle_rows(
            row_count, chips, left_ref, right_ref, triangle_ref, first, chunk, core
        )
        return carry

    for ref, blocks in zip(received, pieces):
        for n, (chip, r) in enumerate(rows_of_blocks(row_count, blocks)):
            place_right(across_ref, chips, chip, r, ref[n])
    lax.fori_loop(0, row_count * chips // chunk, some_rows, 0)


def attention_inputs_kernel(
    row_count, chips, chunk, part, pieces, norms, w_out, left_ref, gate_ref, pairs_ref, *refs
):
    f32, bf16 = jnp.float32, jnp.bfloat16
    received = refs[: len(pieces)]
    triangle_ref, across_ref, after_ref, att_ref = refs[-4:]
    _, core = chip_and_core()
    half = row_count * chips
    tall = (half // 2) * 2 * half
    for ref, blocks in zip(received, pieces):
        for n, (chip, r) in enumerate(rows_of_blocks(row_count, blocks)):
            place_right(across_ref, chips, chip, r, ref[n])

    def some_rows(step, carry):
        first = part * (half // 2) + step * chunk
        triangle_rows(
            row_count, chips, left_ref, across_ref, triangle_ref, first, chunk, 1 - core
        )
        return carry

    lax.fori_loop(0, half // 2 // chunk, some_rows, 0)
    rows = slice(part * tall, (part + 1) * tall)
    tri_normed = layer_norm(triangle_ref[rows, :], norms[2:3, :], norms[3:4, :], 1).astype(bf16)
    after_tri = pairs_ref[rows, :] + gate_ref[rows, :] * dot(tri_normed, w_out[...])
    att_in = layer_norm(after_tri, norms[4:5, :], norms[5:6, :], 1).astype(bf16)
    after_ref[...] = after_tri
    att_ref[...] = att_in


def column_bias(att_ref, row_count, keys, res, head_bias):
    bf16, channels = jnp.bfloat16, att_ref.shape[1]
    row = lax.broadcasted_iota(jnp.int32, (channels, HEADS), 0) // HEAD_DIM
    head = lax.broadcasted_iota(jnp.int32, (channels, HEADS), 1)
    repeat = jnp.where(row == head, 1.0, 0.0).astype(bf16)
    wide_bias = dot(repeat, head_bias[...]).astype(bf16)
    own = lax.axis_index("row") * row_count
    for r in range(row_count):
        column = att_ref[pl.ds(own + r, keys, stride=res), :].astype(bf16)
        yield rounded(
            lax.dot_general(
                column, wide_bias, (((1,), (1,)), ((), ())), preferred_element_type=jnp.float32
            )
        )


def partial_attention(
    row_count, chips, query, key_ref, value_ref, bias_ref, valid_column, score_ref, halves
):
    bf16, f32, channels = jnp.bfloat16, jnp.float32, key_ref.shape[1]
    res = 2 * row_count * chips
    count = row_count * chips // 2
    row = lax.broadcasted_iota(jnp.int32, (2 * channels, 2 * channels), 0) // HEAD_DIM
    column = lax.broadcasted_iota(jnp.int32, (2 * channels, 2 * channels), 1) // HEAD_DIM
    same_head = jnp.where(row == column, 1.0, 0.0).astype(bf16)
    maxima = [jnp.full((res, channels), -jnp.inf, f32) for _ in range(row_count)]
    for part, (core, first) in enumerate(halves):
        products = []
        for n in range(part * count, (part + 1) * count, 2):
            pair = [
                jnp.concatenate([key_ref[m * res : (m + 1) * res, :]] * row_count, axis=0) * query
                for m in (n, n + 1)
            ]
            products.append(jnp.concatenate([p.astype(bf16) for p in pair], axis=1))
        scores = dot(jnp.concatenate(products, axis=0), same_head)
        for n in range(count):
            k = (2 * (first + n // row_count) + core) * row_count + n % row_count
            key_mask = 1000000000.0 * (valid_column[pl.ds(k, 1), :] - 1.0)
            at = part * count + n
            lanes = slice(n % 2 * channels, (n % 2 + 1) * channels)
            for r in range(row_count):
                start = (n // 2 * row_count + r) * res
                score = scores[start : start + res, lanes] + bias_ref[r, at : at + 1, :] + key_mask
                place = (r * len(halves) * count + at) * res
                score_ref[place : place + res, :] = score
                maxima[r] = jnp.maximum(maxima[r], score)
    totals, mixed = [], []
    for r in range(row_count):
        total = mix = jnp.zeros((res, channels), f32)
        for n in range(len(halves) * count):
            start = (r * len(halves) * count + n) * res
            weight = jnp.exp(score_ref[start : start + res, :] - maxima[r])
            total = total + weight
            mix = mix + weight * value_ref[n * res : (n + 1) * res, :]
        totals.append(total)
        mixed.append(mix)
    return maxima, totals, mixed


def keys_and_values(att, w_key, w_value, att_ref, key_ref, value_ref):
    channels = att_ref.shape[1]
    key_value = jnp.concatenate([w_key[...], w_value[...]], axis=1)
    start = 0
    for values in att:
        rows = slice(start, start + values.shape[0])
        att_ref[rows, :] = values.astype(jnp.float32)
        joined = dot(values, key_value)
        key_ref[rows, :] = rounded(joined[:, :channels])
        value_ref[rows, :] = rounded(joined[:, channels:])
        start = rows.stop


def most_attention_kernel(
    row_count,
    chips,
    valid_column,
    w_query,
    w_gate,
    w_key,
    w_value,
    head_bias,
    own_att_a,
    own_att_b,
    far_att_a,
    own_after_a,
    own_after_b,
    sums_ref,
    query_ref,
    gate_ref,
    after_ref,
    att_ref,
    key_ref,
    value_ref,
    bias_ref,
    score_ref,
):
    bf16 = jnp.bfloat16
    chip, core = chip_and_core()
    res = 2 * row_count * chips
    att = [ref[...] for ref in (own_att_a, own_att_b, far_att_a)]
    keys_and_values(att, w_key, w_value, att_ref, key_ref, value_ref)
    own = row_count * res
    own_in = att_ref[pl.ds(pl.multiple_of(chip * own, own), own), :].astype(bf16)
    query = rounded(dot(own_in, w_query[...])) * (1.0 / math.sqrt(HEAD_DIM))
    query_ref[...] = query
    gate_ref[...] = sigmoid(dot(own_in, w_gate[...]))
    chip_a = pl.multiple_of(jnp.minimum(chip, chips // 2 - 1) * own, own)
    chip_b = pl.multiple_of(jnp.maximum(chip - chips // 2, 0) * own, own)
    after_ref[...] = jnp.where(
        chip < chips // 2, own_after_a[pl.ds(chip_a, own), :], own_after_b[pl.ds(chip_b, own), :]
    )
    keys = 3 * row_count * chips // 2
    for r, bias in enumerate(column_bias(att_ref, row_count, keys, res, head_bias)):
        bias_ref[r, :keys, :] = bias
    halves = ((core, 0), (core, chips // 2), (1 - core, 0))
    maxima, totals, mixed = partial_attention(
        row_count, chips, query, key_ref, value_ref, bias_ref, valid_column, score_ref, halves
    )
    for r in range(row_count):
        sums_ref[r, 0] = maxima[r]
        sums_ref[r, 1] = totals[r]
        sums_ref[r, 2] = mixed[r]


def attention_kernel(
    row_count,
    chips,
    valid_column,
    w_key,
    w_value,
    w_out,
    head_bias,
    far_att_b,
    sums_ref,
    query_ref,
    gate_ref,
    after_ref,
    out_ref,
    att_ref,
    key_ref,
    value_ref,
    bias_ref,
    score_ref,
):
    bf16 = jnp.bfloat16
    _, core = chip_and_core()
    res = 2 * row_count * chips
    channels = att_ref.shape[1]
    keys_and_values([far_att_b[...]], w_key, w_value, att_ref, key_ref, value_ref)
    keys = row_count * chips // 2
    for r, bias in enumerate(column_bias(att_ref, row_count, keys, res, head_bias)):
        bias_ref[r, :keys, :] = bias
    last = partial_attention(
        row_count,
        chips,
        query_ref[...],
        key_ref,
        value_ref,
        bias_ref,
        valid_column,
        score_ref,
        ((1 - core, chips // 2),),
    )
    attended = []
    for r, (last_maximum, last_total, last_mixed) in enumerate(zip(*last)):
        maximum = jnp.maximum(sums_ref[r, 0], last_maximum)
        most_scale = jnp.exp(sums_ref[r, 0] - maximum)
        last_scale = jnp.exp(last_maximum - maximum)
        total = sums_ref[r, 1] * most_scale + last_total * last_scale
        attended.append((sums_ref[r, 2] * most_scale + last_mixed * last_scale) / total)
    gated = (jnp.concatenate(attended, axis=0) * gate_ref[...]).astype(bf16)
    final = after_ref[...] + dot(gated, w_out[...])
    out_ref[...] = final.astype(bf16).reshape(row_count, res, channels)


def on_whole_complex(
    pair_rep,
    residue_valid,
    tri_norm_gain,
    tri_norm_bias,
    w_edges,
    w_tri_gate,
    out_norm_gain,
    out_norm_bias,
    w_tri_out,
    att_norm_gain,
    att_norm_bias,
    w_query,
    w_key,
    w_value,
    w_att_gate,
    w_pair_bias,
    w_att_out,
):
    row_count, res, channels = pair_rep.shape
    devices = res // row_count
    chips = devices // 2
    half = res // 2
    f32, bf16 = jnp.float32, jnp.bfloat16
    in_vmem = pl.BlockSpec(memory_space=pltpu.VMEM)

    def shaped(dtype, *shape):
        return jax.ShapeDtypeStruct(shape, dtype)

    def call(kernel, outs, operands, aliases=None, scratch=(), cost=2**25):
        return pl.pallas_call(
            kernel,
            out_shape=outs,
            in_specs=[in_vmem] * len(operands),
            out_specs=jax.tree.map(lambda _: in_vmem, outs),
            input_output_aliases=aliases or {},
            scratch_shapes=list(scratch),
            compiler_params=pltpu.CompilerParams(vmem_limit_bytes=24 * 1024 * 1024),
            cost_estimate=pl.CostEstimate(flops=2**20, bytes_accessed=cost, transcendentals=0),
        )(*operands)

    def exchange(values, bit):
        return lax.ppermute(values, "row", [(d, d ^ bit) for d in range(devices)])

    vectors = (
        tri_norm_gain,
        tri_norm_bias,
        out_norm_gain,
        out_norm_bias,
        att_norm_gain,
        att_norm_bias,
    )
    norms = jnp.stack(vectors)
    edge_weights = jnp.concatenate([w_edges, w_tri_gate], axis=1)
    valid_column = jnp.broadcast_to(residue_valid.astype(f32)[:, None], (res, channels))

    kept = lax.dynamic_update_slice(
        jnp.zeros((2 * row_count, res, channels), bf16), pair_rep, (0, 0, 0)
    )
    far = exchange(pair_rep, devices // 2)
    far, kept, norms, edge_weights = lax.optimization_barrier((far, kept, norms, edge_weights))
    own = lax.dynamic_update_slice(kept, far, (row_count, 0, 0))
    own_blocks = (0, chips // 2)

    def blocks_from(bits):
        return tuple(s ^ bits for s in own_blocks)

    tall = shaped(f32, half * res, channels)
    spread = shaped(f32, half * right_strides(res)[0], channels)

    def edges_of(pieces, send_row, *held):
        pairs = tuple(p for p, _ in pieces)
        blocks = tuple(b for _, b in pieces)
        operands = (valid_column, norms, edge_weights) + pairs + held
        first = len(operands) - len(held)
        return call(
            functools.partial(edges_kernel, row_count, chips, blocks, send_row),
            (tall, spread, tall, tall, shaped(bf16, 4 * row_count, res, channels)),
            operands,
            {first + e: e for e in range(len(held))},
        )

    diagonal = exchange(own, 6)
    beside = exchange(own, 2)
    near = exchange(own, 4)
    *edges, early_right = edges_of([(own, own_blocks)], 0)
    diagonal, edges = lax.optimization_barrier((diagonal, edges))
    *edges, early_right = edges_of(
        [(diagonal, blocks_from(3))], 2 * row_count, *edges, early_right
    )
    beside, edges, early_right = lax.optimization_barrier((beside, edges, early_right))
    early = (exchange(early_right, 1), own_blocks + blocks_from(3))
    *edges, late_right = edges_of(
        [(beside, blocks_from(1)), (near, blocks_from(2))], 0, *edges
    )
    late = (exchange(late_right, 1), blocks_from(1) + blocks_from(2))

    left, right, gate, pairs = edges
    triangle, across = call(
        functools.partial(near_triangle_kernel, row_count, chips, half // 2, [early[1]]),
        (tall, spread),
        (left, right, early[0]),
    )
    part = half // 2 * res
    piece = (shaped(f32, part, channels), shaped(bf16, part, channels))

    def inputs_of(n, fresh, triangle, across):
        operands = (norms, w_tri_out, left, gate, pairs)
        operands += tuple(r for r, _ in fresh) + (triangle, across)
        return call(
            functools.partial(
                attention_inputs_kernel, row_count, chips, half // 2, n, [b for _, b in fresh]
            ),
            (tall, spread) + piece,
            operands,
            {len(operands) - 2: 0, len(operands) - 1: 1},
        )

    triangle, across, after_a, att_a = inputs_of(0, [late], triangle, across)
    far_att_a = exchange(att_a, 1)
    triangle, across, after_b, att_b = inputs_of(1, [], triangle, across)
    far_att_b = exchange(att_b, 1)

    own_shape = shaped(f32, row_count * res, channels)

    def attention_scratch(keys):
        return (
            pltpu.VMEM((keys * res, channels), f32),
            pltpu.VMEM((keys * res, channels), f32),
            pltpu.VMEM((keys * res, channels), f32),
            pltpu.VMEM((row_count, 40, channels), f32),
            pltpu.VMEM((row_count * keys * res, channels), f32),
        )

    sums, query, att_gate, after_own = call(
        functools.partial(most_attention_kernel, row_count, chips),
        (shaped(f32, row_count, 3, res, channels), own_shape, own_shape, own_shape),
        (
            valid_column,
            w_query,
            w_att_gate,
            w_key,
            w_value,
            w_pair_bias.T,
            att_a,
            att_b,
            far_att_a,
            after_a,
            after_b,
        ),
        scratch=attention_scratch(3 * half // 2),
    )
    return call(
        functools.partial(attention_kernel, row_count, chips),
        shaped(bf16, *pair_rep.shape),
        (
            valid_column,
            w_key,
            w_value,
            w_att_out,
            w_pair_bias.T,
            far_att_b,
            sums,
            query,
            att_gate,
            after_own,
        ),
        scratch=attention_scratch(half // 2),
    )


def per_device(pair_rep, residue_valid, *parameters):
    row_count, res, channels = pair_rep.shape
    devices = res // row_count
    if res % 48 == 0 and devices == 16 and 40 * res * res * channels <= 32 * 1024 * 1024:
        return on_whole_complex(pair_rep, residue_valid, *parameters)
    return split_over_devices(pair_rep, residue_valid, *parameters)


def solution(mesh):
    return jax.shard_map(
        per_device,
        mesh=mesh,
        in_specs=(
            P(("groups", "row"), None, None),
            P("groups"),
            P(),
            P(),
            P(),
            P(),
            P(),
            P(),
            P(),
            P(),
            P(),
            P(),
            P(),
            P(),
            P(),
            P(),
            P(),
        ),
        out_specs=P(("groups", "row"), None, None),
        check_vma=False,
    )
```

```python
import functools
import math

import jax
import jax.numpy as jnp
from jax import lax
from jax.experimental import pallas as pl
from jax.experimental.pallas import tpu as pltpu
from jax.sharding import PartitionSpec as P

HEADS = 4
HEAD_DIM = 32


def layer_norm(values, norm_gain, norm_bias, along_axis):
    centre = values - jnp.mean(values, axis=along_axis, keepdims=True)
    spread = jnp.mean(centre * centre, axis=along_axis, keepdims=True)
    return centre * lax.rsqrt(spread + 1e-05) * norm_gain + norm_bias


def attend(query_cols, key_cols, value_cols, whole_bias, key_mask):
    factor = 1.0 / math.sqrt(HEAD_DIM)
    scores = (
        jnp.einsum("kjhd,ijhd->jhki", key_cols, query_cols, preferred_element_type=jnp.float32)
        * factor
    )
    scores = scores + whole_bias.astype(jnp.float32)[None] + key_mask[None, None, :, None]
    scores = scores - jnp.max(scores, axis=2, keepdims=True)
    exponent = jnp.exp(scores)
    weights = (exponent / jnp.sum(exponent, axis=2, keepdims=True)).astype(jnp.bfloat16)
    return jnp.einsum("jhki,kjhd->ijhd", weights, value_cols, preferred_element_type=jnp.float32)


def split_over_devices(
    pair_rep,
    residue_valid,
    tri_norm_gain,
    tri_norm_bias,
    w_edges,
    w_tri_gate,
    out_norm_gain,
    out_norm_bias,
    w_tri_out,
    att_norm_gain,
    att_norm_bias,
    w_query,
    w_key,
    w_value,
    w_att_gate,
    w_pair_bias,
    w_att_out,
):
    row_count = pair_rep.shape[0]
    res_count = pair_rep.shape[1]
    channels = pair_rep.shape[2]
    hidden_width = HEADS * HEAD_DIM
    row_start = lax.axis_index("row") * row_count
    valid_flags = residue_valid.astype(jnp.float32)
    own_valid = lax.dynamic_slice_in_dim(valid_flags, row_start, row_count)
    normed = layer_norm(pair_rep.astype(jnp.float32), tri_norm_gain, tri_norm_bias, 2).astype(
        jnp.bfloat16
    )
    projected = jnp.einsum("ikd,de->eik", normed, w_edges, preferred_element_type=jnp.float32)
    projected = projected.reshape(4, channels, row_count, res_count)
    pair_mask = (own_valid[:, None] * valid_flags[None, :])[None, :, :]
    left_edges = (jax.nn.sigmoid(projected[1]) * projected[0] * pair_mask).astype(jnp.bfloat16)
    right_edges = (jax.nn.sigmoid(projected[3]) * projected[2] * pair_mask).astype(jnp.bfloat16)
    left_cols, right_cols = (
        lax.all_to_all(left_edges, "row", split_axis=0, concat_axis=1, tiled=True),
        lax.all_to_all(right_edges, "row", split_axis=0, concat_axis=1, tiled=True),
    )
    block_product = jnp.einsum(
        "cik,cjk->cij", left_cols, right_cols, preferred_element_type=jnp.float32
    ).astype(jnp.bfloat16)
    triangle = lax.all_to_all(block_product, "row", split_axis=1, concat_axis=0, tiled=True)
    tri_normed = layer_norm(
        triangle.astype(jnp.float32), out_norm_gain[:, None, None], out_norm_bias[:, None, None], 0
    ).astype(jnp.bfloat16)
    tri_gate = jax.nn.sigmoid(
        jnp.einsum("ijc,ce->ije", normed, w_tri_gate, preferred_element_type=jnp.float32)
    )
    tri_update = jnp.einsum(
        "cij,ce->ije", tri_normed, w_tri_out, preferred_element_type=jnp.float32
    )
    after_tri = pair_rep.astype(jnp.float32) + tri_gate * tri_update
    att_in = layer_norm(after_tri, att_norm_gain, att_norm_bias, 2).astype(jnp.bfloat16)
    pair_bias = jnp.einsum(
        "kic,ch->hki", att_in, w_pair_bias, preferred_element_type=jnp.float32
    ).astype(jnp.bfloat16)
    whole_bias = lax.all_gather(pair_bias, "row", axis=1, tiled=True)
    key_mask = 1000000000.0 * (valid_flags - 1.0)
    columns = lax.all_to_all(att_in, "row", split_axis=1, concat_axis=0, tiled=True)
    all_weights = jnp.concatenate([w_query, w_key, w_value, w_att_gate], axis=1)
    joined = jnp.dot(columns.reshape(-1, channels), all_weights, preferred_element_type=jnp.float32)
    query_cols = (
        joined[:, :hidden_width].astype(jnp.bfloat16).reshape(res_count, row_count, HEADS, HEAD_DIM)
    )
    key_cols = (
        joined[:, hidden_width : 2 * hidden_width]
        .astype(jnp.bfloat16)
        .reshape(res_count, row_count, HEADS, HEAD_DIM)
    )
    value_cols = (
        joined[:, 2 * hidden_width : 3 * hidden_width]
        .astype(jnp.bfloat16)
        .reshape(res_count, row_count, HEADS, HEAD_DIM)
    )
    gate_cols = jax.nn.sigmoid(joined[:, 3 * hidden_width :]).reshape(
        res_count, row_count, hidden_width
    )
    attended = attend(query_cols, key_cols, value_cols, whole_bias, key_mask)
    gated = (attended.reshape(res_count, row_count, hidden_width) * gate_cols).astype(jnp.bfloat16)
    gated_rows = lax.all_to_all(gated, "row", split_axis=0, concat_axis=1, tiled=True)
    final = after_tri + jnp.einsum(
        "ije,ec->ijc", gated_rows, w_att_out, preferred_element_type=jnp.float32
    )
    return final.astype(jnp.bfloat16)


def sigmoid(values):
    return 0.5 * jnp.tanh(0.5 * values) + 0.5


def dot(left, right):
    return jnp.dot(left, right, preferred_element_type=jnp.float32)


def rounded(values):
    return values.astype(jnp.bfloat16).astype(jnp.float32)


def chip_and_core():
    device = lax.axis_index("row")
    return lax.shift_right_logical(device, 1), jnp.bitwise_and(device, 1)


def rows_of_blocks(row_count, blocks):
    chip, _ = chip_and_core()
    return [(jnp.bitwise_xor(chip, bits), r) for bits in blocks for r in range(row_count)]


def edges_kernel(row_count, chips, pieces, send_row, valid_column, norms, weights, *refs):
    pair_refs = refs[: len(pieces)]
    if send_row or len(pieces) > 1:
        left_ref, right_ref, gate_ref, pairs_ref, send_ref = refs[-5:]
    else:
        left_ref, right_ref, gate_ref, pairs_ref, send_ref, same_head_ref = refs[-6:]
        wide = same_head_ref.shape
        row = lax.broadcasted_iota(jnp.int32, wide, 0) // HEAD_DIM
        column = lax.broadcasted_iota(jnp.int32, wide, 1) // HEAD_DIM
        same_head_ref[...] = jnp.where(row == column, 1.0, 0.0).astype(jnp.bfloat16)
    f32, bf16 = jnp.float32, jnp.bfloat16
    res, channels = valid_column.shape
    _, core = chip_and_core()
    pairs = jnp.concatenate(
        [ref[...].astype(f32).reshape(-1, channels) for ref in pair_refs], axis=0
    )
    normed = layer_norm(pairs, norms[0:1, :], norms[1:2, :], 1).astype(bf16)
    column = valid_column[...]
    rows_of = rows_of_blocks(row_count, [bits for piece in pieces for bits in piece])
    masks = jnp.concatenate(
        [
            column * valid_column[pl.ds((2 * chip + core) * row_count + r, 1), :]
            for chip, r in rows_of
        ],
        axis=0,
    )
    joined = dot(normed, weights[:, : 2 * channels])
    left = rounded(sigmoid(joined[:, channels:]) * joined[:, :channels] * masks)
    joined = dot(normed, weights[:, 2 * channels : 4 * channels])
    right = (sigmoid(joined[:, channels:]) * joined[:, :channels] * masks).astype(bf16)
    gate = sigmoid(dot(normed, weights[:, 4 * channels :]))
    for n, (chip, r) in enumerate(rows_of):
        rows = slice(n * res, (n + 1) * res)
        start = pl.multiple_of((chip * row_count + r) * res, res)
        send_ref[send_row + n] = right[rows]
        left_ref[pl.ds(start, res), :] = left[rows]
        place_right(right_ref, chips, chip, r, right[rows])
        gate_ref[pl.ds(start, res), :] = gate[rows]
        pairs_ref[pl.ds(start, res), :] = pairs[rows]


def place_right(right_ref, chips, chip, r, edges):
    res = edges.shape[0]
    start = pl.multiple_of((r * chips + chip) * res, res)
    right_ref[pl.ds(start, res), :] = edges.astype(jnp.float32)


def sum_sublanes(parts):
    row = lax.broadcasted_iota(jnp.int32, parts[0].shape, 0)
    for shift in (1, 2, 4):
        high = jnp.bitwise_and(row, shift) > 0
        parts = [
            jnp.where(high, odd, even) + pltpu.roll(jnp.where(high, even, odd), shift, 0)
            for even, odd in zip(parts[0::2], parts[1::2])
        ]
    return parts[0]


def triangle_rows(row_count, chips, left_ref, right_ref, triangle_ref, first, count, core):
    res = 2 * row_count * chips
    start = pl.multiple_of(first * res, res)
    lefts = [left_ref[pl.ds(start + n * res, res), :] for n in range(count)]
    for r in range(row_count):
        parts = [[] for _ in range(count)]
        for chip in range(chips):
            at = (r * chips + chip) * res
            right = right_ref[at : at + res, :]
            for n in range(count):
                product = lefts[n] * right
                parts[n].append(
                    sum(product[k : k + 8] for k in range(8, res, 8)) + product[:8]
                )
        for n in range(count):
            triangle_ref[
                pl.ds(start + n * res + core * row_count + r, chips, stride=2 * row_count), :
            ] = rounded(sum_sublanes(parts[n]))


def near_triangle_kernel(row_count, chips, chunk, pieces, left_ref, right_ref, *refs):
    received, (triangle_ref, across_ref) = refs[:-2], refs[-2:]
    _, core = chip_and_core()

    def some_rows(step, carry):
        first = step * chunk
        triangle_rows(
            row_count, chips, left_ref, right_ref, triangle_ref, first, chunk, core
        )
        return carry

    for ref, blocks in zip(received, pieces):
        for n, (chip, r) in enumerate(rows_of_blocks(row_count, blocks)):
            place_right(across_ref, chips, chip, r, ref[n])
    lax.fori_loop(0, row_count * chips // chunk, some_rows, 0)


def attention_inputs(
    row_count, chips, chunk, first, norms, w_out, left_ref, gate_ref, pairs_ref, refs
):
    f32, bf16 = jnp.float32, jnp.bfloat16
    triangle_ref, across_ref, after_ref, att_ref = refs
    _, core = chip_and_core()
    half = row_count * chips
    tall = (half // 2) * 2 * half

    def some_rows(step, carry):
        triangle_rows(
            row_count,
            chips,
            left_ref,
            across_ref,
            triangle_ref,
            first + step * chunk,
            chunk,
            1 - core,
        )
        return carry

    lax.fori_loop(0, half // 2 // chunk, some_rows, 0)
    rows = pl.ds(pl.multiple_of(first * 2 * half, tall), tall)
    tri_normed = layer_norm(triangle_ref[rows, :], norms[2:3, :], norms[3:4, :], 1).astype(bf16)
    after_tri = pairs_ref[rows, :] + gate_ref[rows, :] * dot(tri_normed, w_out[...])
    att_in = layer_norm(after_tri, norms[4:5, :], norms[5:6, :], 1).astype(bf16)
    after_ref[...] = after_tri
    att_ref[...] = att_in


def first_chip(chips, part):
    chip, _ = chip_and_core()
    return jnp.bitwise_xor(jnp.bitwise_and(chip, chips // 2), part * (chips // 2))


def own_inputs_kernel(
    row_count, chips, chunk, blocks, norms, w_out, left_ref, gate_ref, pairs_ref, received, *refs
):
    for n, (chip, r) in enumerate(rows_of_blocks(row_count, blocks)):
        place_right(refs[-3], chips, chip, r, received[n])
    first = first_chip(chips, 0) * row_count
    attention_inputs(
        row_count, chips, chunk, first, norms, w_out, left_ref, gate_ref, pairs_ref, refs[-4:]
    )


def other_inputs_kernel(
    row_count,
    chips,
    chunk,
    norms,
    w_out,
    left_ref,
    gate_ref,
    pairs_ref,
    w_query,
    w_gate,
    w_key,
    w_value,
    own_att,
    own_after,
    held_triangle,
    across_ref,
    triangle_ref,
    after_ref,
    att_ref,
    query_ref,
    att_gate_ref,
    own_after_ref,
    key_ref,
    value_ref,
):
    keys_and_values([own_att[...]], w_key, w_value, key_ref, value_ref)
    chip, _ = chip_and_core()
    own = row_count * 2 * row_count * chips
    rows = pl.ds(pl.multiple_of(jnp.bitwise_and(chip, chips // 2 - 1) * own, own), own)
    own_in = own_att[rows, :]
    query_ref[...] = rounded(dot(own_in, w_query[...])) * (1.0 / math.sqrt(HEAD_DIM))
    att_gate_ref[...] = sigmoid(dot(own_in, w_gate[...]))
    own_after_ref[...] = own_after[rows, :]
    first = first_chip(chips, 1) * row_count
    refs = (triangle_ref, across_ref, after_ref, att_ref)
    attention_inputs(
        row_count, chips, chunk, first, norms, w_out, left_ref, gate_ref, pairs_ref, refs
    )


def keys_and_values(att, w_key, w_value, key_ref, value_ref):
    channels = key_ref.shape[1]
    key_value = jnp.concatenate([w_key[...], w_value[...]], axis=1)
    start = 0
    for values in att:
        rows = slice(start, start + values.shape[0])
        joined = dot(values, key_value)
        key_ref[rows, :] = rounded(joined[:, :channels])
        value_ref[rows, :] = rounded(joined[:, channels:])
        start = rows.stop


def column_bias(row_count, res, att, wide_bias, att_ref, bias_ref):
    start = 0
    for values in att:
        att_ref[start : start + values.shape[0], :] = values.astype(jnp.float32)
        start += values.shape[0]
    keys = start // res
    own = lax.axis_index("row") * row_count
    for r in range(row_count):
        column = att_ref[pl.ds(own + r, keys, stride=res), :].astype(jnp.bfloat16)
        bias_ref[r, :keys, :] = rounded(dot(column, wide_bias[...]))


def partial_attention(row_count, chips, query, parts, bias_ref, same_head, valid_column, score_ref):
    bf16, f32 = jnp.bfloat16, jnp.float32
    res = 2 * row_count * chips
    channels = valid_column.shape[1]
    count = row_count * chips // 2
    keys = len(parts) * count
    maxima = [jnp.full((res, channels), -jnp.inf, f32) for _ in range(row_count)]
    for part, (core, first, key_of, _) in enumerate(parts):
        products = []
        for n in range(0, count, 2):
            pair = [jnp.concatenate([key_of(m)] * row_count, axis=0) * query for m in (n, n + 1)]
            products.append(jnp.concatenate([p.astype(bf16) for p in pair], axis=1))
        scores = dot(jnp.concatenate(products, axis=0), same_head[...])
        for n in range(count):
            k = (2 * (first + n // row_count) + core) * row_count + n % row_count
            key_mask = 1000000000.0 * (valid_column[pl.ds(k, 1), :] - 1.0)
            at = part * count + n
            lanes = slice(n % 2 * channels, (n % 2 + 1) * channels)
            for r in range(row_count):
                start = (n // 2 * row_count + r) * res
                score = scores[start : start + res, lanes] + bias_ref[r, at : at + 1, :] + key_mask
                score_ref[(r * keys + at) * res : (r * keys + at + 1) * res, :] = score
                maxima[r] = jnp.maximum(maxima[r], score)
    totals, mixed = [], []
    for r in range(row_count):
        total = mix = jnp.zeros((res, channels), f32)
        for part, (_, _, _, value_of) in enumerate(parts):
            for n in range(count):
                start = (r * keys + part * count + n) * res
                weight = jnp.exp(score_ref[start : start + res, :] - maxima[r])
                total = total + weight
                mix = mix + weight * value_of(n)
        totals.append(total)
        mixed.append(mix)
    return maxima, totals, mixed


def most_attention_kernel(
    row_count,
    chips,
    valid_column,
    same_head,
    w_key,
    w_value,
    wide_bias,
    own_att_a,
    own_att_b,
    far_att_a,
    query_ref,
    own_key_a,
    own_value_a,
    sums_ref,
    att_ref,
    key_ref,
    value_ref,
    bias_ref,
    score_ref,
):
    _, core = chip_and_core()
    res, channels = valid_column.shape
    keys_and_values([own_att_b[...], far_att_a[...]], w_key, w_value, key_ref, value_ref)
    att = [ref[...] for ref in (own_att_a, own_att_b, far_att_a)]
    column_bias(row_count, res, att, wide_bias, att_ref, bias_ref)
    count = row_count * chips // 2

    def rows_of(ref, first):
        return lambda n: ref[(first + n) * res : (first + n + 1) * res, :]

    a, b = first_chip(chips, 0), first_chip(chips, 1)
    parts = (
        (core, a, rows_of(own_key_a, 0), rows_of(own_value_a, 0)),
        (core, b, rows_of(key_ref, 0), rows_of(value_ref, 0)),
        (1 - core, a, rows_of(key_ref, count), rows_of(value_ref, count)),
    )
    sums = partial_attention(
        row_count, chips, query_ref[...], parts, bias_ref, same_head, valid_column, score_ref
    )
    for n, each in enumerate(sums):
        for r in range(row_count):
            sums_ref[r, n] = each[r]


def attention_kernel(
    row_count,
    chips,
    valid_column,
    same_head,
    w_key,
    w_value,
    w_out,
    wide_bias,
    far_att_b,
    query_ref,
    gate_ref,
    after_ref,
    sums_ref,
    out_ref,
    att_ref,
    key_ref,
    value_ref,
    bias_ref,
    score_ref,
):
    _, core = chip_and_core()
    res, channels = valid_column.shape
    far_att = far_att_b[...]
    keys_and_values([far_att], w_key, w_value, key_ref, value_ref)
    column_bias(row_count, res, [far_att], wide_bias, att_ref, bias_ref)

    def rows_of(ref):
        return lambda n: ref[n * res : (n + 1) * res, :]

    parts = ((1 - core, first_chip(chips, 1), rows_of(key_ref), rows_of(value_ref)),)
    last = partial_attention(
        row_count, chips, query_ref[...], parts, bias_ref, same_head, valid_column, score_ref
    )
    attended = []
    for r, (last_maximum, last_total, last_mixed) in enumerate(zip(*last)):
        maximum = jnp.maximum(sums_ref[r, 0], last_maximum)
        most_scale = jnp.exp(sums_ref[r, 0] - maximum)
        last_scale = jnp.exp(last_maximum - maximum)
        total = sums_ref[r, 1] * most_scale + last_total * last_scale
        attended.append((sums_ref[r, 2] * most_scale + last_mixed * last_scale) / total)
    gated = (jnp.concatenate(attended, axis=0) * gate_ref[...]).astype(jnp.bfloat16)
    final = after_ref[...] + dot(gated, w_out[...])
    out_ref[...] = final.astype(jnp.bfloat16).reshape(row_count, res, channels)


def on_whole_complex(
    pair_rep,
    residue_valid,
    tri_norm_gain,
    tri_norm_bias,
    w_edges,
    w_tri_gate,
    out_norm_gain,
    out_norm_bias,
    w_tri_out,
    att_norm_gain,
    att_norm_bias,
    w_query,
    w_key,
    w_value,
    w_att_gate,
    w_pair_bias,
    w_att_out,
):
    row_count, res, channels = pair_rep.shape
    devices = res // row_count
    chips = devices // 2
    half = res // 2
    f32, bf16 = jnp.float32, jnp.bfloat16
    in_vmem = pl.BlockSpec(memory_space=pltpu.VMEM)

    def shaped(dtype, *shape):
        return jax.ShapeDtypeStruct(shape, dtype)

    def call(kernel, outs, operands, aliases=None, scratch=(), cost=2**25):
        return pl.pallas_call(
            kernel,
            out_shape=outs,
            in_specs=[in_vmem] * len(operands),
            out_specs=jax.tree.map(lambda _: in_vmem, outs),
            input_output_aliases=aliases or {},
            scratch_shapes=list(scratch),
            compiler_params=pltpu.CompilerParams(vmem_limit_bytes=24 * 1024 * 1024),
            cost_estimate=pl.CostEstimate(flops=2**20, bytes_accessed=cost, transcendentals=0),
        )(*operands)

    def exchange(values, bit):
        return lax.ppermute(values, "row", [(d, d ^ bit) for d in range(devices)])

    vectors = (
        tri_norm_gain,
        tri_norm_bias,
        out_norm_gain,
        out_norm_bias,
        att_norm_gain,
        att_norm_bias,
    )
    norms = jnp.stack(vectors)
    edge_weights = jnp.concatenate([w_edges, w_tri_gate], axis=1)
    valid_column = jnp.broadcast_to(residue_valid.astype(f32)[:, None], (res, channels))

    head = lax.broadcasted_iota(jnp.int32, (HEADS, channels), 0)
    head_of_channel = lax.broadcasted_iota(jnp.int32, (HEADS, channels), 1) // HEAD_DIM
    repeat = jnp.where(head == head_of_channel, 1.0, 0.0).astype(bf16)
    wide_bias = dot(w_pair_bias, repeat).astype(bf16)

    kept = lax.dynamic_update_slice(
        jnp.zeros((2 * row_count, res, channels), bf16), pair_rep, (0, 0, 0)
    )
    far = exchange(pair_rep, devices // 2)
    far, kept, norms, edge_weights = lax.optimization_barrier((far, kept, norms, edge_weights))
    own = lax.dynamic_update_slice(kept, far, (row_count, 0, 0))
    own_blocks = (0, chips // 2)

    def blocks_from(bits):
        return tuple(s ^ bits for s in own_blocks)

    tall = shaped(f32, half * res, channels)

    def edges_of(pieces, send_row, *held):
        pairs = tuple(p for p, _ in pieces)
        blocks = tuple(b for _, b in pieces)
        operands = (valid_column, norms, edge_weights) + pairs + held
        first = len(operands) - len(held)
        return call(
            functools.partial(edges_kernel, row_count, chips, blocks, send_row),
            (tall, tall, tall, tall, shaped(bf16, 4 * row_count, res, channels))
            + (() if held else (shaped(bf16, 2 * channels, 2 * channels),)),
            operands,
            {first + e: e for e in range(len(held))},
        )

    diagonal = exchange(own, 6)
    beside = exchange(own, 2)
    near = exchange(own, 4)
    *edges, early_right, same_head = edges_of([(own, own_blocks)], 0)
    diagonal, edges = lax.optimization_barrier((diagonal, edges))
    *edges, early_right = edges_of(
        [(diagonal, blocks_from(3))], 2 * row_count, *edges, early_right
    )
    beside, edges, early_right, wide_bias = lax.optimization_barrier(
        (beside, edges, early_right, wide_bias)
    )
    early = (exchange(early_right, 1), own_blocks + blocks_from(3))
    *edges, late_right = edges_of(
        [(beside, blocks_from(1)), (near, blocks_from(2))], 0, *edges
    )
    late = (exchange(late_right, 1), blocks_from(1) + blocks_from(2))

    left, right, gate, pairs = edges
    triangle, across = call(
        functools.partial(near_triangle_kernel, row_count, chips, 4, [early[1]]),
        (tall, tall),
        (left, right, early[0]),
    )
    part = half // 2 * res
    in_part, own_shape = shaped(f32, part, channels), shaped(f32, row_count * res, channels)
    att_part = shaped(bf16, part, channels)
    shared = (norms, w_tri_out, left, gate, pairs)
    triangle, across, after_a, att_a = call(
        functools.partial(own_inputs_kernel, row_count, chips, 4, late[1]),
        (tall, tall, in_part, att_part),
        shared + (late[0], triangle, across),
        {6: 0, 7: 1},
    )
    far_att_a = exchange(att_a, 1)
    _, _, att_b, query, att_gate, after_own, keys_a, values_a = call(
        functools.partial(other_inputs_kernel, row_count, chips, 4),
        (tall, in_part, att_part, own_shape, own_shape, own_shape, in_part, in_part),
        shared + (w_query, w_att_gate, w_key, w_value, att_a, after_a, triangle, across),
        {11: 0},
    )
    far_att_b = exchange(att_b, 1)

    def attention_scratch(keys, projected):
        return (
            pltpu.VMEM((keys * res, channels), f32),
            pltpu.VMEM((projected * res, channels), f32),
            pltpu.VMEM((projected * res, channels), f32),
            pltpu.VMEM((row_count, 40, channels), f32),
            pltpu.VMEM((row_count * keys * res, channels), f32),
        )

    sums = call(
        functools.partial(most_attention_kernel, row_count, chips),
        shaped(f32, row_count, 3, res, channels),
        (valid_column, same_head, w_key, w_value, wide_bias, att_a, att_b, far_att_a)
        + (query, keys_a, values_a),
        scratch=attention_scratch(3 * half // 2, half),
    )
    return call(
        functools.partial(attention_kernel, row_count, chips),
        shaped(bf16, *pair_rep.shape),
        (valid_column, same_head, w_key, w_value, w_att_out, wide_bias, far_att_b)
        + (query, att_gate, after_own, sums),
        scratch=attention_scratch(half // 2, half // 2),
    )


def per_device(pair_rep, residue_valid, *parameters):
    row_count, res, channels = pair_rep.shape
    devices = res // row_count
    if res % 48 == 0 and devices == 16 and 40 * res * res * channels <= 32 * 1024 * 1024:
        return on_whole_complex(pair_rep, residue_valid, *parameters)
    return split_over_devices(pair_rep, residue_valid, *parameters)


def solution(mesh):
    return jax.shard_map(
        per_device,
        mesh=mesh,
        in_specs=(
            P(("groups", "row"), None, None),
            P("groups"),
            P(),
            P(),
            P(),
            P(),
            P(),
            P(),
            P(),
            P(),
            P(),
            P(),
            P(),
            P(),
            P(),
            P(),
            P(),
        ),
        out_specs=P(("groups", "row"), None, None),
        check_vma=False,
    )
```

```python
import functools
import math

import jax
import jax.numpy as jnp
from jax import lax
from jax.experimental import pallas as pl
from jax.experimental.pallas import tpu as pltpu
from jax.sharding import PartitionSpec as P

HEADS = 4
HEAD_DIM = 32


def layer_norm(values, norm_gain, norm_bias, along_axis):
    centre = values - jnp.mean(values, axis=along_axis, keepdims=True)
    spread = jnp.mean(centre * centre, axis=along_axis, keepdims=True)
    return centre * lax.rsqrt(spread + 1e-05) * norm_gain + norm_bias


def attend(query_cols, key_cols, value_cols, whole_bias, key_mask):
    factor = 1.0 / math.sqrt(HEAD_DIM)
    scores = (
        jnp.einsum("kjhd,ijhd->jhki", key_cols, query_cols, preferred_element_type=jnp.float32)
        * factor
    )
    scores = scores + whole_bias.astype(jnp.float32)[None] + key_mask[None, None, :, None]
    scores = scores - jnp.max(scores, axis=2, keepdims=True)
    exponent = jnp.exp(scores)
    weights = (exponent / jnp.sum(exponent, axis=2, keepdims=True)).astype(jnp.bfloat16)
    return jnp.einsum("jhki,kjhd->ijhd", weights, value_cols, preferred_element_type=jnp.float32)


def split_over_devices(
    pair_rep,
    residue_valid,
    tri_norm_gain,
    tri_norm_bias,
    w_edges,
    w_tri_gate,
    out_norm_gain,
    out_norm_bias,
    w_tri_out,
    att_norm_gain,
    att_norm_bias,
    w_query,
    w_key,
    w_value,
    w_att_gate,
    w_pair_bias,
    w_att_out,
):
    row_count = pair_rep.shape[0]
    res_count = pair_rep.shape[1]
    channels = pair_rep.shape[2]
    hidden_width = HEADS * HEAD_DIM
    row_start = lax.axis_index("row") * row_count
    valid_flags = residue_valid.astype(jnp.float32)
    own_valid = lax.dynamic_slice_in_dim(valid_flags, row_start, row_count)
    normed = layer_norm(pair_rep.astype(jnp.float32), tri_norm_gain, tri_norm_bias, 2).astype(
        jnp.bfloat16
    )
    projected = jnp.einsum("ikd,de->eik", normed, w_edges, preferred_element_type=jnp.float32)
    projected = projected.reshape(4, channels, row_count, res_count)
    pair_mask = (own_valid[:, None] * valid_flags[None, :])[None, :, :]
    left_edges = (jax.nn.sigmoid(projected[1]) * projected[0] * pair_mask).astype(jnp.bfloat16)
    right_edges = (jax.nn.sigmoid(projected[3]) * projected[2] * pair_mask).astype(jnp.bfloat16)
    left_cols, right_cols = (
        lax.all_to_all(left_edges, "row", split_axis=0, concat_axis=1, tiled=True),
        lax.all_to_all(right_edges, "row", split_axis=0, concat_axis=1, tiled=True),
    )
    block_product = jnp.einsum(
        "cik,cjk->cij", left_cols, right_cols, preferred_element_type=jnp.float32
    ).astype(jnp.bfloat16)
    triangle = lax.all_to_all(block_product, "row", split_axis=1, concat_axis=0, tiled=True)
    tri_normed = layer_norm(
        triangle.astype(jnp.float32), out_norm_gain[:, None, None], out_norm_bias[:, None, None], 0
    ).astype(jnp.bfloat16)
    tri_gate = jax.nn.sigmoid(
        jnp.einsum("ijc,ce->ije", normed, w_tri_gate, preferred_element_type=jnp.float32)
    )
    tri_update = jnp.einsum(
        "cij,ce->ije", tri_normed, w_tri_out, preferred_element_type=jnp.float32
    )
    after_tri = pair_rep.astype(jnp.float32) + tri_gate * tri_update
    att_in = layer_norm(after_tri, att_norm_gain, att_norm_bias, 2).astype(jnp.bfloat16)
    pair_bias = jnp.einsum(
        "kic,ch->hki", att_in, w_pair_bias, preferred_element_type=jnp.float32
    ).astype(jnp.bfloat16)
    whole_bias = lax.all_gather(pair_bias, "row", axis=1, tiled=True)
    key_mask = 1000000000.0 * (valid_flags - 1.0)
    columns = lax.all_to_all(att_in, "row", split_axis=1, concat_axis=0, tiled=True)
    all_weights = jnp.concatenate([w_query, w_key, w_value, w_att_gate], axis=1)
    joined = jnp.dot(columns.reshape(-1, channels), all_weights, preferred_element_type=jnp.float32)
    query_cols = (
        joined[:, :hidden_width].astype(jnp.bfloat16).reshape(res_count, row_count, HEADS, HEAD_DIM)
    )
    key_cols = (
        joined[:, hidden_width : 2 * hidden_width]
        .astype(jnp.bfloat16)
        .reshape(res_count, row_count, HEADS, HEAD_DIM)
    )
    value_cols = (
        joined[:, 2 * hidden_width : 3 * hidden_width]
        .astype(jnp.bfloat16)
        .reshape(res_count, row_count, HEADS, HEAD_DIM)
    )
    gate_cols = jax.nn.sigmoid(joined[:, 3 * hidden_width :]).reshape(
        res_count, row_count, hidden_width
    )
    attended = attend(query_cols, key_cols, value_cols, whole_bias, key_mask)
    gated = (attended.reshape(res_count, row_count, hidden_width) * gate_cols).astype(jnp.bfloat16)
    gated_rows = lax.all_to_all(gated, "row", split_axis=0, concat_axis=1, tiled=True)
    final = after_tri + jnp.einsum(
        "ije,ec->ijc", gated_rows, w_att_out, preferred_element_type=jnp.float32
    )
    return final.astype(jnp.bfloat16)


def sigmoid(values):
    return 0.5 * jnp.tanh(0.5 * values) + 0.5


def dot(left, right):
    return jnp.dot(left, right, preferred_element_type=jnp.float32)


def rounded(values):
    return values.astype(jnp.bfloat16).astype(jnp.float32)


def chip_and_core():
    device = lax.axis_index("row")
    return lax.shift_right_logical(device, 1), jnp.bitwise_and(device, 1)


def rows_of_blocks(row_count, blocks):
    chip, _ = chip_and_core()
    return [(jnp.bitwise_xor(chip, bits), r) for bits in blocks for r in range(row_count)]


def edges_kernel(
    row_count, chips, pieces, send_row, makes_heads, valid_column, norms, weights, *refs
):
    pair_refs = refs[: len(pieces)]
    left_ref, right_ref, gate_ref, pairs_ref, send_ref = refs[-5:]
    if makes_heads:
        left_ref, right_ref, gate_ref, pairs_ref, send_ref, same_head_ref = refs[-6:]
        wide = same_head_ref.shape
        row = lax.broadcasted_iota(jnp.int32, wide, 0) // HEAD_DIM
        column = lax.broadcasted_iota(jnp.int32, wide, 1) // HEAD_DIM
        same_head_ref[...] = jnp.where(row == column, 1.0, 0.0).astype(jnp.bfloat16)
    f32, bf16 = jnp.float32, jnp.bfloat16
    res, channels = valid_column.shape
    _, core = chip_and_core()
    pairs = jnp.concatenate(
        [ref[...].astype(f32).reshape(-1, channels) for ref in pair_refs], axis=0
    )
    normed = layer_norm(pairs, norms[0:1, :], norms[1:2, :], 1).astype(bf16)
    column = valid_column[...]
    rows_of = rows_of_blocks(row_count, [bits for piece in pieces for bits in piece])
    masks = jnp.concatenate(
        [
            column * valid_column[pl.ds((2 * chip + core) * row_count + r, 1), :]
            for chip, r in rows_of
        ],
        axis=0,
    )
    joined = dot(normed, weights[:, : 2 * channels])
    left = rounded(sigmoid(joined[:, channels:]) * joined[:, :channels] * masks)
    joined = dot(normed, weights[:, 2 * channels : 4 * channels])
    right = (sigmoid(joined[:, channels:]) * joined[:, :channels] * masks).astype(bf16)
    gate = sigmoid(dot(normed, weights[:, 4 * channels :]))
    for n, (chip, r) in enumerate(rows_of):
        rows = slice(n * res, (n + 1) * res)
        start = pl.multiple_of((chip * row_count + r) * res, res)
        send_ref[send_row + n] = right[rows]
        left_ref[pl.ds(start, res), :] = left[rows]
        place_right(right_ref, chips, chip, r, right[rows])
        gate_ref[pl.ds(start, res), :] = gate[rows]
        pairs_ref[pl.ds(start, res), :] = pairs[rows]


def place_right(right_ref, chips, chip, r, edges):
    res = edges.shape[0]
    start = pl.multiple_of((r * chips + chip) * res, res)
    right_ref[pl.ds(start, res), :] = edges.astype(jnp.float32)


def sum_sublanes(parts):
    row = lax.broadcasted_iota(jnp.int32, parts[0].shape, 0)
    for shift in (1, 2, 4):
        high = jnp.bitwise_and(row, shift) > 0
        parts = [
            jnp.where(high, odd, even) + pltpu.roll(jnp.where(high, even, odd), shift, 0)
            for even, odd in zip(parts[0::2], parts[1::2])
        ]
    return parts[0]


def triangle_rows(row_count, chips, left_ref, right_ref, triangle_ref, first, count, core):
    res = 2 * row_count * chips
    start = pl.multiple_of(first * res, res)
    block = 4
    for n in range(0, count, block):
        lefts = [left_ref[pl.ds(start + m * res, res), :] for m in range(n, n + block)]
        for r in range(row_count):
            parts = [[] for _ in range(block)]
            for chip in range(chips):
                at = (r * chips + chip) * res
                right = right_ref[at : at + res, :]
                for m in range(block):
                    product = lefts[m] * right
                    parts[m].append(
                        sum(product[k : k + 8] for k in range(8, res, 8)) + product[:8]
                    )
            for m in range(block):
                place = start + (n + m) * res + core * row_count + r
                triangle_ref[pl.ds(place, chips, stride=2 * row_count), :] = rounded(
                    sum_sublanes(parts[m])
                )


def near_triangle_kernel(row_count, chips, chunk, pieces, left_ref, right_ref, *refs):
    received, (triangle_ref, across_ref) = refs[:-2], refs[-2:]
    _, core = chip_and_core()

    def some_rows(step, carry):
        first = step * chunk
        triangle_rows(
            row_count, chips, left_ref, right_ref, triangle_ref, first, chunk, core
        )
        return carry

    for ref, blocks in zip(received, pieces):
        for n, (chip, r) in enumerate(rows_of_blocks(row_count, blocks)):
            place_right(across_ref, chips, chip, r, ref[n])
    lax.fori_loop(0, row_count * chips // chunk, some_rows, 0)


def attention_inputs(
    row_count, chips, first, norms, w_out, left_ref, gate_ref, pairs_ref, refs
):
    f32, bf16 = jnp.float32, jnp.bfloat16
    triangle_ref, across_ref, after_ref, att_ref = refs
    _, core = chip_and_core()
    half = row_count * chips
    tall = (half // 2) * 2 * half

    triangle_rows(
        row_count, chips, left_ref, across_ref, triangle_ref, first, half // 2, 1 - core
    )
    rows = pl.ds(pl.multiple_of(first * 2 * half, tall), tall)
    tri_normed = layer_norm(triangle_ref[rows, :], norms[2:3, :], norms[3:4, :], 1).astype(bf16)
    after_tri = pairs_ref[rows, :] + gate_ref[rows, :] * dot(tri_normed, w_out[...])
    att_in = layer_norm(after_tri, norms[4:5, :], norms[5:6, :], 1).astype(bf16)
    after_ref[...] = after_tri
    att_ref[...] = att_in


def first_chip(chips, part):
    chip, _ = chip_and_core()
    return jnp.bitwise_xor(jnp.bitwise_and(chip, chips // 2), part * (chips // 2))


def own_inputs_kernel(
    row_count, chips, blocks, norms, w_out, left_ref, gate_ref, pairs_ref, received, *refs
):
    for n, (chip, r) in enumerate(rows_of_blocks(row_count, blocks)):
        place_right(refs[-3], chips, chip, r, received[n])
    first = first_chip(chips, 0) * row_count
    attention_inputs(
        row_count, chips, first, norms, w_out, left_ref, gate_ref, pairs_ref, refs[-4:]
    )


def other_inputs_kernel(
    row_count,
    chips,
    norms,
    w_out,
    left_ref,
    gate_ref,
    pairs_ref,
    held_triangle,
    across_ref,
    triangle_ref,
    after_ref,
    att_ref,
):
    first = first_chip(chips, 1) * row_count
    refs = (triangle_ref, across_ref, after_ref, att_ref)
    attention_inputs(
        row_count, chips, first, norms, w_out, left_ref, gate_ref, pairs_ref, refs
    )


def keys_and_values(att, w_key, w_value, key_ref, value_ref):
    channels = key_ref.shape[1]
    key_value = jnp.concatenate([w_key[...], w_value[...]], axis=1)
    start = 0
    for values in att:
        rows = slice(start, start + values.shape[0])
        joined = dot(values, key_value)
        key_ref[rows, :] = rounded(joined[:, :channels])
        value_ref[rows, :] = rounded(joined[:, channels:])
        start = rows.stop


def column_bias(row_count, res, att, wide_bias, att_ref, bias_ref):
    start = 0
    for values in att:
        att_ref[start : start + values.shape[0], :] = values.astype(jnp.float32)
        start += values.shape[0]
    keys = start // res
    own = lax.axis_index("row") * row_count
    for r in range(row_count):
        column = att_ref[pl.ds(own + r, keys, stride=res), :].astype(jnp.bfloat16)
        bias_ref[r, :keys, :] = rounded(dot(column, wide_bias[...]))


def partial_attention(row_count, chips, query, parts, bias_ref, same_head, valid_column, score_ref):
    bf16, f32 = jnp.bfloat16, jnp.float32
    res = 2 * row_count * chips
    channels = valid_column.shape[1]
    count = row_count * chips // 2
    keys = len(parts) * count
    maxima = [jnp.full((res, channels), -jnp.inf, f32) for _ in range(row_count)]
    for part, (core, first, key_of, _) in enumerate(parts):
        products = []
        for n in range(0, count, 2):
            pair = [jnp.concatenate([key_of(m)] * row_count, axis=0) * query for m in (n, n + 1)]
            products.append(jnp.concatenate([p.astype(bf16) for p in pair], axis=1))
        scores = dot(jnp.concatenate(products, axis=0), same_head[...])
        for n in range(count):
            k = (2 * (first + n // row_count) + core) * row_count + n % row_count
            key_mask = 1000000000.0 * (valid_column[pl.ds(k, 1), :] - 1.0)
            at = part * count + n
            lanes = slice(n % 2 * channels, (n % 2 + 1) * channels)
            for r in range(row_count):
                start = (n // 2 * row_count + r) * res
                score = scores[start : start + res, lanes] + bias_ref[r, at : at + 1, :] + key_mask
                score_ref[(r * keys + at) * res : (r * keys + at + 1) * res, :] = score
                maxima[r] = jnp.maximum(maxima[r], score)
    totals, mixed = [], []
    for r in range(row_count):
        total = mix = jnp.zeros((res, channels), f32)
        for part, (_, _, _, value_of) in enumerate(parts):
            for n in range(count):
                start = (r * keys + part * count + n) * res
                weight = jnp.exp(score_ref[start : start + res, :] - maxima[r])
                total = total + weight
                mix = mix + weight * value_of(n)
        totals.append(total)
        mixed.append(mix)
    return maxima, totals, mixed


def most_attention_kernel(
    row_count,
    chips,
    valid_column,
    same_head,
    w_query,
    w_gate,
    w_key,
    w_value,
    wide_bias,
    own_att_a,
    own_att_b,
    far_att_a,
    own_after,
    sums_ref,
    query_ref,
    gate_ref,
    after_ref,
    att_ref,
    key_ref,
    value_ref,
    bias_ref,
    score_ref,
):
    chip, core = chip_and_core()
    res, channels = valid_column.shape
    own = row_count * res
    rows = pl.ds(pl.multiple_of(jnp.bitwise_and(chip, chips // 2 - 1) * own, own), own)
    own_in = own_att_a[rows, :]
    query = rounded(dot(own_in, w_query[...])) * (1.0 / math.sqrt(HEAD_DIM))
    att = [ref[...] for ref in (own_att_a, own_att_b, far_att_a)]
    keys_and_values(att, w_key, w_value, key_ref, value_ref)
    column_bias(row_count, res, att, wide_bias, att_ref, bias_ref)
    count = row_count * chips // 2

    def rows_of(ref, first):
        return lambda n: ref[(first + n) * res : (first + n + 1) * res, :]

    a, b = first_chip(chips, 0), first_chip(chips, 1)
    parts = [
        (sender, first, rows_of(key_ref, n * count), rows_of(value_ref, n * count))
        for n, (sender, first) in enumerate(((core, a), (core, b), (1 - core, a)))
    ]
    sums = partial_attention(
        row_count, chips, query, parts, bias_ref, same_head, valid_column, score_ref
    )
    for n, each in enumerate(sums):
        for r in range(row_count):
            sums_ref[r, n] = each[r]
    query_ref[...] = query
    gate_ref[...] = sigmoid(dot(own_in, w_gate[...]))
    after_ref[...] = own_after[rows, :]


def attention_kernel(
    row_count,
    chips,
    valid_column,
    same_head,
    w_key,
    w_value,
    w_out,
    wide_bias,
    far_att_b,
    query_ref,
    gate_ref,
    after_ref,
    sums_ref,
    out_ref,
    att_ref,
    key_ref,
    value_ref,
    bias_ref,
    score_ref,
):
    _, core = chip_and_core()
    res, channels = valid_column.shape
    far_att = far_att_b[...]
    keys_and_values([far_att], w_key, w_value, key_ref, value_ref)
    column_bias(row_count, res, [far_att], wide_bias, att_ref, bias_ref)

    def rows_of(ref):
        return lambda n: ref[n * res : (n + 1) * res, :]

    parts = ((1 - core, first_chip(chips, 1), rows_of(key_ref), rows_of(value_ref)),)
    last = partial_attention(
        row_count, chips, query_ref[...], parts, bias_ref, same_head, valid_column, score_ref
    )
    attended = []
    for r, (last_maximum, last_total, last_mixed) in enumerate(zip(*last)):
        maximum = jnp.maximum(sums_ref[r, 0], last_maximum)
        most_scale = jnp.exp(sums_ref[r, 0] - maximum)
        last_scale = jnp.exp(last_maximum - maximum)
        total = sums_ref[r, 1] * most_scale + last_total * last_scale
        attended.append((sums_ref[r, 2] * most_scale + last_mixed * last_scale) / total)
    gated = (jnp.concatenate(attended, axis=0) * gate_ref[...]).astype(jnp.bfloat16)
    final = after_ref[...] + dot(gated, w_out[...])
    out_ref[...] = final.astype(jnp.bfloat16).reshape(row_count, res, channels)


def on_whole_complex(
    pair_rep,
    residue_valid,
    tri_norm_gain,
    tri_norm_bias,
    w_edges,
    w_tri_gate,
    out_norm_gain,
    out_norm_bias,
    w_tri_out,
    att_norm_gain,
    att_norm_bias,
    w_query,
    w_key,
    w_value,
    w_att_gate,
    w_pair_bias,
    w_att_out,
):
    row_count, res, channels = pair_rep.shape
    devices = res // row_count
    chips = devices // 2
    half = res // 2
    f32, bf16 = jnp.float32, jnp.bfloat16
    in_vmem = pl.BlockSpec(memory_space=pltpu.VMEM)

    def shaped(dtype, *shape):
        return jax.ShapeDtypeStruct(shape, dtype)

    def call(kernel, outs, operands, aliases=None, scratch=(), cost=2**25):
        return pl.pallas_call(
            kernel,
            out_shape=outs,
            in_specs=[in_vmem] * len(operands),
            out_specs=jax.tree.map(lambda _: in_vmem, outs),
            input_output_aliases=aliases or {},
            scratch_shapes=list(scratch),
            compiler_params=pltpu.CompilerParams(vmem_limit_bytes=24 * 1024 * 1024),
            cost_estimate=pl.CostEstimate(flops=2**20, bytes_accessed=cost, transcendentals=0),
        )(*operands)

    def exchange(values, bit):
        return lax.ppermute(values, "row", [(d, d ^ bit) for d in range(devices)])

    vectors = (
        tri_norm_gain,
        tri_norm_bias,
        out_norm_gain,
        out_norm_bias,
        att_norm_gain,
        att_norm_bias,
    )
    norms = jnp.stack(vectors)
    edge_weights = jnp.concatenate([w_edges, w_tri_gate], axis=1)
    valid_column = jnp.broadcast_to(residue_valid.astype(f32)[:, None], (res, channels))

    head = lax.broadcasted_iota(jnp.int32, (HEADS, channels), 0)
    head_of_channel = lax.broadcasted_iota(jnp.int32, (HEADS, channels), 1) // HEAD_DIM
    repeat = jnp.where(head == head_of_channel, 1.0, 0.0).astype(bf16)
    wide_bias = dot(w_pair_bias, repeat).astype(bf16)

    far = exchange(pair_rep, 8)
    near = exchange(pair_rep, 4)
    beside = exchange(pair_rep, 2)
    far, near, beside, norms, edge_weights = lax.optimization_barrier(
        (far, near, beside, norms, edge_weights)
    )

    tall = shaped(f32, half * res, channels)

    def edges_of(pieces, send_row, *held):
        to_send = (2 if send_row == 0 and held else 6) * row_count
        pairs = tuple(p for p, _ in pieces)
        blocks = tuple(b for _, b in pieces)
        operands = (valid_column, norms, edge_weights) + pairs + held
        first = len(operands) - len(held)
        return call(
            functools.partial(edges_kernel, row_count, chips, blocks, send_row, not held),
            (tall, tall, tall, tall, shaped(bf16, to_send, res, channels))
            + (() if held else (shaped(bf16, 2 * channels, 2 * channels),)),
            operands,
            {first + e: e for e in range(len(held))},
        )

    diagonal_far = exchange(far, 6)
    beside_more = exchange(jnp.concatenate([far, near], axis=0), 2)
    near_far = exchange(far, 4)
    *edges, early_right, same_head = edges_of(
        [(pair_rep, (0,)), (far, (4,)), (near, (2,)), (beside, (1,))], 0
    )
    diagonal_far, near_far, edges, early_right = lax.optimization_barrier(
        (diagonal_far, near_far, edges, early_right)
    )
    *edges, early_right = edges_of(
        [(diagonal_far, (7,)), (near_far, (6,))], 4 * row_count, *edges, early_right
    )
    beside_more, edges, early_right, wide_bias = lax.optimization_barrier(
        (beside_more, edges, early_right, wide_bias)
    )
    early = (exchange(early_right, 1), (0, 4, 2, 1, 7, 6))
    *edges, late_right = edges_of([(beside_more, (5, 3))], 0, *edges)
    late = (exchange(late_right, 1), (5, 3))

    left, right, gate, pairs = edges
    triangle, across = call(
        functools.partial(near_triangle_kernel, row_count, chips, half // 2, [early[1]]),
        (tall, tall),
        (left, right, early[0]),
    )
    part = half // 2 * res
    in_part, own_shape = shaped(f32, part, channels), shaped(f32, row_count * res, channels)
    att_part = shaped(bf16, part, channels)
    shared = (norms, w_tri_out, left, gate, pairs)
    triangle, across, after_a, att_a = call(
        functools.partial(own_inputs_kernel, row_count, chips, late[1]),
        (tall, tall, in_part, att_part),
        shared + (late[0], triangle, across),
        {6: 0, 7: 1},
    )
    far_att_a = exchange(att_a, 1)
    _, _, att_b = call(
        functools.partial(other_inputs_kernel, row_count, chips),
        (tall, in_part, att_part),
        shared + (triangle, across),
        {5: 0},
    )
    far_att_b = exchange(att_b, 1)

    def attention_scratch(keys, projected):
        return (
            pltpu.VMEM((keys * res, channels), f32),
            pltpu.VMEM((projected * res, channels), f32),
            pltpu.VMEM((projected * res, channels), f32),
            pltpu.VMEM((row_count, 40, channels), f32),
            pltpu.VMEM((row_count * keys * res, channels), f32),
        )

    sums, query, att_gate, after_own = call(
        functools.partial(most_attention_kernel, row_count, chips),
        (shaped(f32, row_count, 3, res, channels), own_shape, own_shape, own_shape),
        (valid_column, same_head, w_query, w_att_gate, w_key, w_value, wide_bias)
        + (att_a, att_b, far_att_a, after_a),
        scratch=attention_scratch(3 * half // 2, 3 * half // 2),
    )
    return call(
        functools.partial(attention_kernel, row_count, chips),
        shaped(bf16, *pair_rep.shape),
        (valid_column, same_head, w_key, w_value, w_att_out, wide_bias, far_att_b)
        + (query, att_gate, after_own, sums),
        scratch=attention_scratch(half // 2, half // 2),
    )


def per_device(pair_rep, residue_valid, *parameters):
    row_count, res, channels = pair_rep.shape
    devices = res // row_count
    if res % 48 == 0 and devices == 16 and 40 * res * res * channels <= 32 * 1024 * 1024:
        return on_whole_complex(pair_rep, residue_valid, *parameters)
    return split_over_devices(pair_rep, residue_valid, *parameters)


def solution(mesh):
    return jax.shard_map(
        per_device,
        mesh=mesh,
        in_specs=(
            P(("groups", "row"), None, None),
            P("groups"),
            P(),
            P(),
            P(),
            P(),
            P(),
            P(),
            P(),
            P(),
            P(),
            P(),
            P(),
            P(),
            P(),
            P(),
            P(),
        ),
        out_specs=P(("groups", "row"), None, None),
        check_vma=False,
    )
```

```python
import functools
import math

import jax
import jax.numpy as jnp
from jax import lax
from jax.experimental import pallas as pl
from jax.experimental.pallas import tpu as pltpu
from jax.sharding import PartitionSpec as P

HEADS = 4
HEAD_DIM = 32


def layer_norm(values, norm_gain, norm_bias, along_axis):
    centre = values - jnp.mean(values, axis=along_axis, keepdims=True)
    spread = jnp.mean(centre * centre, axis=along_axis, keepdims=True)
    return centre * lax.rsqrt(spread + 1e-05) * norm_gain + norm_bias


def attend(query_cols, key_cols, value_cols, whole_bias, key_mask):
    factor = 1.0 / math.sqrt(HEAD_DIM)
    scores = (
        jnp.einsum("kjhd,ijhd->jhki", key_cols, query_cols, preferred_element_type=jnp.float32)
        * factor
    )
    scores = scores + whole_bias.astype(jnp.float32)[None] + key_mask[None, None, :, None]
    scores = scores - jnp.max(scores, axis=2, keepdims=True)
    exponent = jnp.exp(scores)
    weights = (exponent / jnp.sum(exponent, axis=2, keepdims=True)).astype(jnp.bfloat16)
    return jnp.einsum("jhki,kjhd->ijhd", weights, value_cols, preferred_element_type=jnp.float32)


def split_over_devices(
    pair_rep,
    residue_valid,
    tri_norm_gain,
    tri_norm_bias,
    w_edges,
    w_tri_gate,
    out_norm_gain,
    out_norm_bias,
    w_tri_out,
    att_norm_gain,
    att_norm_bias,
    w_query,
    w_key,
    w_value,
    w_att_gate,
    w_pair_bias,
    w_att_out,
):
    row_count = pair_rep.shape[0]
    res_count = pair_rep.shape[1]
    channels = pair_rep.shape[2]
    hidden_width = HEADS * HEAD_DIM
    row_start = lax.axis_index("row") * row_count
    valid_flags = residue_valid.astype(jnp.float32)
    own_valid = lax.dynamic_slice_in_dim(valid_flags, row_start, row_count)
    normed = layer_norm(pair_rep.astype(jnp.float32), tri_norm_gain, tri_norm_bias, 2).astype(
        jnp.bfloat16
    )
    projected = jnp.einsum("ikd,de->eik", normed, w_edges, preferred_element_type=jnp.float32)
    projected = projected.reshape(4, channels, row_count, res_count)
    pair_mask = (own_valid[:, None] * valid_flags[None, :])[None, :, :]
    left_edges = (jax.nn.sigmoid(projected[1]) * projected[0] * pair_mask).astype(jnp.bfloat16)
    right_edges = (jax.nn.sigmoid(projected[3]) * projected[2] * pair_mask).astype(jnp.bfloat16)
    left_cols, right_cols = (
        lax.all_to_all(left_edges, "row", split_axis=0, concat_axis=1, tiled=True),
        lax.all_to_all(right_edges, "row", split_axis=0, concat_axis=1, tiled=True),
    )
    block_product = jnp.einsum(
        "cik,cjk->cij", left_cols, right_cols, preferred_element_type=jnp.float32
    ).astype(jnp.bfloat16)
    triangle = lax.all_to_all(block_product, "row", split_axis=1, concat_axis=0, tiled=True)
    tri_normed = layer_norm(
        triangle.astype(jnp.float32), out_norm_gain[:, None, None], out_norm_bias[:, None, None], 0
    ).astype(jnp.bfloat16)
    tri_gate = jax.nn.sigmoid(
        jnp.einsum("ijc,ce->ije", normed, w_tri_gate, preferred_element_type=jnp.float32)
    )
    tri_update = jnp.einsum(
        "cij,ce->ije", tri_normed, w_tri_out, preferred_element_type=jnp.float32
    )
    after_tri = pair_rep.astype(jnp.float32) + tri_gate * tri_update
    att_in = layer_norm(after_tri, att_norm_gain, att_norm_bias, 2).astype(jnp.bfloat16)
    pair_bias = jnp.einsum(
        "kic,ch->hki", att_in, w_pair_bias, preferred_element_type=jnp.float32
    ).astype(jnp.bfloat16)
    whole_bias = lax.all_gather(pair_bias, "row", axis=1, tiled=True)
    key_mask = 1000000000.0 * (valid_flags - 1.0)
    columns = lax.all_to_all(att_in, "row", split_axis=1, concat_axis=0, tiled=True)
    all_weights = jnp.concatenate([w_query, w_key, w_value, w_att_gate], axis=1)
    joined = jnp.dot(columns.reshape(-1, channels), all_weights, preferred_element_type=jnp.float32)
    query_cols = (
        joined[:, :hidden_width].astype(jnp.bfloat16).reshape(res_count, row_count, HEADS, HEAD_DIM)
    )
    key_cols = (
        joined[:, hidden_width : 2 * hidden_width]
        .astype(jnp.bfloat16)
        .reshape(res_count, row_count, HEADS, HEAD_DIM)
    )
    value_cols = (
        joined[:, 2 * hidden_width : 3 * hidden_width]
        .astype(jnp.bfloat16)
        .reshape(res_count, row_count, HEADS, HEAD_DIM)
    )
    gate_cols = jax.nn.sigmoid(joined[:, 3 * hidden_width :]).reshape(
        res_count, row_count, hidden_width
    )
    attended = attend(query_cols, key_cols, value_cols, whole_bias, key_mask)
    gated = (attended.reshape(res_count, row_count, hidden_width) * gate_cols).astype(jnp.bfloat16)
    gated_rows = lax.all_to_all(gated, "row", split_axis=0, concat_axis=1, tiled=True)
    final = after_tri + jnp.einsum(
        "ije,ec->ijc", gated_rows, w_att_out, preferred_element_type=jnp.float32
    )
    return final.astype(jnp.bfloat16)


def sigmoid(values):
    return 0.5 * jnp.tanh(0.5 * values) + 0.5


def dot(left, right):
    return jnp.dot(left, right, preferred_element_type=jnp.float32)


def rounded(values):
    return values.astype(jnp.bfloat16).astype(jnp.float32)


def chip_and_core():
    device = lax.axis_index("row")
    return lax.shift_right_logical(device, 1), jnp.bitwise_and(device, 1)


def rows_of_blocks(row_count, blocks):
    chip, _ = chip_and_core()
    return [(jnp.bitwise_xor(chip, bits), r) for bits in blocks for r in range(row_count)]


def edges_kernel(
    row_count, chips, pieces, send_row, makes_heads, valid_column, norms, weights, *refs
):
    pair_refs = refs[: len(pieces)]
    left_ref, right_ref, gate_ref, pairs_ref, send_ref = refs[-5:]
    if makes_heads:
        left_ref, right_ref, gate_ref, pairs_ref, send_ref, same_head_ref = refs[-6:]
        wide = same_head_ref.shape
        row = lax.broadcasted_iota(jnp.int32, wide, 0) // HEAD_DIM
        column = lax.broadcasted_iota(jnp.int32, wide, 1) // HEAD_DIM
        same_head_ref[...] = jnp.where(row == column, 1.0, 0.0).astype(jnp.bfloat16)
    f32, bf16 = jnp.float32, jnp.bfloat16
    res, channels = valid_column.shape
    _, core = chip_and_core()
    pairs = jnp.concatenate(
        [ref[...].astype(f32).reshape(-1, channels) for ref in pair_refs], axis=0
    )
    normed = layer_norm(pairs, norms[0:1, :], norms[1:2, :], 1).astype(bf16)
    column = valid_column[...]
    rows_of = rows_of_blocks(row_count, [bits for piece in pieces for bits in piece])
    masks = jnp.concatenate(
        [
            column * valid_column[pl.ds((2 * chip + core) * row_count + r, 1), :]
            for chip, r in rows_of
        ],
        axis=0,
    )
    joined = dot(normed, weights[:, : 2 * channels])
    left = rounded(sigmoid(joined[:, channels:]) * joined[:, :channels] * masks)
    joined = dot(normed, weights[:, 2 * channels : 4 * channels])
    right = (sigmoid(joined[:, channels:]) * joined[:, :channels] * masks).astype(bf16)
    gate = sigmoid(dot(normed, weights[:, 4 * channels :]))
    for n, (chip, r) in enumerate(rows_of):
        rows = slice(n * res, (n + 1) * res)
        start = pl.multiple_of((chip * row_count + r) * res, res)
        send_ref[send_row + n] = right[rows]
        left_ref[pl.ds(start, res), :] = left[rows]
        place_right(right_ref, chips, chip, r, right[rows])
        gate_ref[pl.ds(start, res), :] = gate[rows]
        pairs_ref[pl.ds(start, res), :] = pairs[rows]


def place_right(right_ref, chips, chip, r, edges):
    res = edges.shape[0]
    start = pl.multiple_of((r * chips + chip) * res, res)
    right_ref[pl.ds(start, res), :] = edges.astype(jnp.float32)


def sum_sublanes(parts):
    row = lax.broadcasted_iota(jnp.int32, parts[0].shape, 0)
    for shift in (1, 2, 4):
        high = jnp.bitwise_and(row, shift) > 0
        parts = [
            jnp.where(high, odd, even) + pltpu.roll(jnp.where(high, even, odd), shift, 0)
            for even, odd in zip(parts[0::2], parts[1::2])
        ]
    return parts[0]


def triangle_rows(
    row_count, chips, left_ref, right_ref, triangle_ref, first, count, core, triangle_first
):
    res = 2 * row_count * chips
    start = pl.multiple_of(first * res, res)
    block = 4
    for n in range(0, count, block):
        lefts = [left_ref[pl.ds(start + m * res, res), :] for m in range(n, n + block)]
        for r in range(row_count):
            parts = [[] for _ in range(block)]
            for chip in range(chips):
                at = (r * chips + chip) * res
                right = right_ref[at : at + res, :]
                for m in range(block):
                    product = lefts[m] * right
                    parts[m].append(
                        sum(product[k : k + 8] for k in range(8, res, 8)) + product[:8]
                    )
            for m in range(block):
                place = (triangle_first + n + m) * res + core * row_count + r
                triangle_ref[pl.ds(place, chips, stride=2 * row_count), :] = rounded(
                    sum_sublanes(parts[m])
                )


def near_triangle_kernel(row_count, chips, chunk, pieces, left_ref, right_ref, *refs):
    received, (triangle_ref, across_ref) = refs[:-2], refs[-2:]
    _, core = chip_and_core()

    def some_rows(step, carry):
        first = step * chunk
        triangle_rows(
            row_count, chips, left_ref, right_ref, triangle_ref, first, chunk, core, first
        )
        return carry

    for ref, blocks in zip(received, pieces):
        for n, (chip, r) in enumerate(rows_of_blocks(row_count, blocks)):
            place_right(across_ref, chips, chip, r, ref[n])
    lax.fori_loop(0, row_count * chips // chunk, some_rows, 0)


def attention_inputs(
    row_count, chips, first, norms, w_out, left_ref, gate_ref, pairs_ref, held_triangle, across_ref,
    triangle_ref,
):
    bf16 = jnp.bfloat16
    _, core = chip_and_core()
    half = row_count * chips
    tall = (half // 2) * 2 * half
    rows = pl.ds(pl.multiple_of(first * 2 * half, tall), tall)
    triangle_ref[...] = held_triangle[rows, :]
    triangle_rows(
        row_count, chips, left_ref, across_ref, triangle_ref, first, half // 2, 1 - core, 0
    )
    tri_normed = layer_norm(triangle_ref[...], norms[2:3, :], norms[3:4, :], 1).astype(bf16)
    after_tri = pairs_ref[rows, :] + gate_ref[rows, :] * dot(tri_normed, w_out[...])
    att_in = layer_norm(after_tri, norms[4:5, :], norms[5:6, :], 1).astype(bf16)
    return after_tri, att_in


def first_chip(chips, part):
    chip, _ = chip_and_core()
    return jnp.bitwise_xor(jnp.bitwise_and(chip, chips // 2), part * (chips // 2))


def own_inputs_kernel(
    row_count,
    chips,
    blocks,
    norms,
    w_out,
    left_ref,
    gate_ref,
    pairs_ref,
    received,
    triangle_ref,
    held_across,
    across_ref,
    after_ref,
    att_ref,
    scratch_ref,
):
    for n, (chip, r) in enumerate(rows_of_blocks(row_count, blocks)):
        place_right(across_ref, chips, chip, r, received[n])
    first = first_chip(chips, 0) * row_count
    refs = (left_ref, gate_ref, pairs_ref, triangle_ref, across_ref, scratch_ref)
    after_ref[...], att_ref[...] = attention_inputs(
        row_count, chips, first, norms, w_out, *refs
    )


def other_inputs_kernel(row_count, chips, norms, w_out, *refs):
    *refs, att_ref, scratch_ref = refs
    first = first_chip(chips, 1) * row_count
    _, att_ref[...] = attention_inputs(row_count, chips, first, norms, w_out, *refs, scratch_ref)


def keys_and_values(att, w_key, w_value, key_ref, value_ref):
    channels = key_ref.shape[1]
    key_value = jnp.concatenate([w_key[...], w_value[...]], axis=1)
    start = 0
    for values in att:
        rows = slice(start, start + values.shape[0])
        joined = dot(values, key_value)
        key_ref[rows, :] = rounded(joined[:, :channels])
        value_ref[rows, :] = rounded(joined[:, channels:])
        start = rows.stop


def column_bias(row_count, res, att, wide_bias, att_ref, bias_ref):
    start = 0
    for values in att:
        att_ref[start : start + values.shape[0], :] = values.astype(jnp.float32)
        start += values.shape[0]
    keys = start // res
    own = lax.axis_index("row") * row_count
    for r in range(row_count):
        column = att_ref[pl.ds(own + r, keys, stride=res), :].astype(jnp.bfloat16)
        bias_ref[r, :keys, :] = rounded(dot(column, wide_bias[...]))


def partial_attention(row_count, chips, query, parts, bias_ref, same_head, valid_column, score_ref):
    bf16, f32 = jnp.bfloat16, jnp.float32
    res = 2 * row_count * chips
    channels = valid_column.shape[1]
    count = row_count * chips // 2
    keys = len(parts) * count
    maxima = [jnp.full((res, channels), -jnp.inf, f32) for _ in range(row_count)]
    for part, (core, first, key_of, _) in enumerate(parts):
        products = []
        for n in range(0, count, 2):
            pair = [jnp.concatenate([key_of(m)] * row_count, axis=0) * query for m in (n, n + 1)]
            products.append(jnp.concatenate([p.astype(bf16) for p in pair], axis=1))
        scores = dot(jnp.concatenate(products, axis=0), same_head[...])
        for n in range(count):
            k = (2 * (first + n // row_count) + core) * row_count + n % row_count
            key_mask = 1000000000.0 * (valid_column[pl.ds(k, 1), :] - 1.0)
            at = part * count + n
            shifts = [
                (bias_ref[r, at : at + 1, :] + key_mask) * math.log2(math.e)
                for r in range(row_count)
            ]
            lanes = slice(n % 2 * channels, (n % 2 + 1) * channels)
            for r in range(row_count):
                start = (n // 2 * row_count + r) * res
                score = scores[start : start + res, lanes] + shifts[r]
                score_ref[(r * keys + at) * res : (r * keys + at + 1) * res, :] = score
                maxima[r] = jnp.maximum(maxima[r], score)
    totals, mixed = [], []
    for r in range(row_count):
        total = mix = jnp.zeros((res, channels), f32)
        for part, (_, _, _, value_of) in enumerate(parts):
            for n in range(count):
                start = (r * keys + part * count + n) * res
                weight = jnp.exp2(score_ref[start : start + res, :] - maxima[r])
                total = total + weight
                mix = mix + weight * value_of(n)
        totals.append(total)
        mixed.append(mix)
    return maxima, totals, mixed


def most_attention_kernel(
    row_count,
    chips,
    valid_column,
    same_head,
    w_query,
    w_gate,
    w_key,
    w_value,
    wide_bias,
    own_att_a,
    own_att_b,
    far_att_a,
    own_after,
    sums_ref,
    query_ref,
    gate_ref,
    after_ref,
    att_ref,
    key_ref,
    value_ref,
    bias_ref,
    score_ref,
):
    chip, core = chip_and_core()
    res, channels = valid_column.shape
    own = row_count * res
    rows = pl.ds(pl.multiple_of(jnp.bitwise_and(chip, chips // 2 - 1) * own, own), own)
    own_in = own_att_a[rows, :]
    query = rounded(dot(own_in, w_query[...])) * (math.log2(math.e) / math.sqrt(HEAD_DIM))
    att = [ref[...] for ref in (own_att_a, own_att_b, far_att_a)]
    keys_and_values(att, w_key, w_value, key_ref, value_ref)
    column_bias(row_count, res, att, wide_bias, att_ref, bias_ref)
    count = row_count * chips // 2

    def rows_of(ref, first):
        return lambda n: ref[(first + n) * res : (first + n + 1) * res, :]

    a, b = first_chip(chips, 0), first_chip(chips, 1)
    parts = [
        (sender, first, rows_of(key_ref, n * count), rows_of(value_ref, n * count))
        for n, (sender, first) in enumerate(((core, a), (core, b), (1 - core, a)))
    ]
    sums = partial_attention(
        row_count, chips, query, parts, bias_ref, same_head, valid_column, score_ref
    )
    for n, each in enumerate(sums):
        for r in range(row_count):
            sums_ref[r, n] = each[r]
    query_ref[...] = query
    gate_ref[...] = sigmoid(dot(own_in, w_gate[...]))
    after_ref[...] = own_after[rows, :]


def attention_kernel(
    row_count,
    chips,
    valid_column,
    same_head,
    w_key,
    w_value,
    w_out,
    wide_bias,
    far_att_b,
    query_ref,
    gate_ref,
    after_ref,
    sums_ref,
    out_ref,
    att_ref,
    key_ref,
    value_ref,
    bias_ref,
    score_ref,
):
    _, core = chip_and_core()
    res, channels = valid_column.shape
    far_att = far_att_b[...]
    keys_and_values([far_att], w_key, w_value, key_ref, value_ref)
    column_bias(row_count, res, [far_att], wide_bias, att_ref, bias_ref)

    def rows_of(ref):
        return lambda n: ref[n * res : (n + 1) * res, :]

    parts = ((1 - core, first_chip(chips, 1), rows_of(key_ref), rows_of(value_ref)),)
    last = partial_attention(
        row_count, chips, query_ref[...], parts, bias_ref, same_head, valid_column, score_ref
    )
    attended = []
    for r, (last_maximum, last_total, last_mixed) in enumerate(zip(*last)):
        maximum = jnp.maximum(sums_ref[r, 0], last_maximum)
        most_scale = jnp.exp2(sums_ref[r, 0] - maximum)
        last_scale = jnp.exp2(last_maximum - maximum)
        total = sums_ref[r, 1] * most_scale + last_total * last_scale
        attended.append((sums_ref[r, 2] * most_scale + last_mixed * last_scale) / total)
    gated = (jnp.concatenate(attended, axis=0) * gate_ref[...]).astype(jnp.bfloat16)
    final = after_ref[...] + dot(gated, w_out[...])
    out_ref[...] = final.astype(jnp.bfloat16).reshape(row_count, res, channels)


def on_whole_complex(
    pair_rep,
    residue_valid,
    tri_norm_gain,
    tri_norm_bias,
    w_edges,
    w_tri_gate,
    out_norm_gain,
    out_norm_bias,
    w_tri_out,
    att_norm_gain,
    att_norm_bias,
    w_query,
    w_key,
    w_value,
    w_att_gate,
    w_pair_bias,
    w_att_out,
):
    row_count, res, channels = pair_rep.shape
    devices = res // row_count
    chips = devices // 2
    half = res // 2
    f32, bf16 = jnp.float32, jnp.bfloat16
    in_vmem = pl.BlockSpec(memory_space=pltpu.VMEM)

    def shaped(dtype, *shape):
        return jax.ShapeDtypeStruct(shape, dtype)

    def call(kernel, outs, operands, aliases=None, scratch=(), cost=2**25):
        return pl.pallas_call(
            kernel,
            out_shape=outs,
            in_specs=[in_vmem] * len(operands),
            out_specs=jax.tree.map(lambda _: in_vmem, outs),
            input_output_aliases=aliases or {},
            scratch_shapes=list(scratch),
            compiler_params=pltpu.CompilerParams(vmem_limit_bytes=24 * 1024 * 1024),
            cost_estimate=pl.CostEstimate(flops=2**20, bytes_accessed=cost, transcendentals=0),
        )(*operands)

    def exchange(values, bit):
        return lax.ppermute(values, "row", [(d, d ^ bit) for d in range(devices)])

    vectors = (
        tri_norm_gain,
        tri_norm_bias,
        out_norm_gain,
        out_norm_bias,
        att_norm_gain,
        att_norm_bias,
    )
    norms = jnp.stack(vectors)
    edge_weights = jnp.concatenate([w_edges, w_tri_gate], axis=1)
    valid_column = jnp.broadcast_to(residue_valid.astype(f32)[:, None], (res, channels))

    head = lax.broadcasted_iota(jnp.int32, (HEADS, channels), 0)
    head_of_channel = lax.broadcasted_iota(jnp.int32, (HEADS, channels), 1) // HEAD_DIM
    repeat = jnp.where(head == head_of_channel, 1.0, 0.0).astype(bf16)
    wide_bias = dot(w_pair_bias, repeat).astype(bf16)

    kept = lax.dynamic_update_slice(
        jnp.zeros((2 * row_count, res, channels), bf16), pair_rep, (0, 0, 0)
    )
    far = exchange(pair_rep, devices // 2)
    far, kept, norms, edge_weights = lax.optimization_barrier((far, kept, norms, edge_weights))
    own = lax.dynamic_update_slice(kept, far, (row_count, 0, 0))
    own_blocks = (0, chips // 2)

    def blocks_from(bits):
        return tuple(s ^ bits for s in own_blocks)

    tall = shaped(f32, half * res, channels)

    def edges_of(pieces, send_row, *held):
        pairs = tuple(p for p, _ in pieces)
        blocks = tuple(b for _, b in pieces)
        operands = (valid_column, norms, edge_weights) + pairs + held
        first = len(operands) - len(held)
        return call(
            functools.partial(edges_kernel, row_count, chips, blocks, send_row, not held),
            (tall, tall, tall, tall, shaped(bf16, 4 * row_count, res, channels))
            + (() if held else (shaped(bf16, 2 * channels, 2 * channels),)),
            operands,
            {first + e: e for e in range(len(held))},
        )

    diagonal = exchange(own, 6)
    beside = exchange(own, 2)
    near = exchange(own, 4)
    *edges, early_right, same_head = edges_of([(own, own_blocks)], 0)
    diagonal, edges = lax.optimization_barrier((diagonal, edges))
    *edges, early_right = edges_of(
        [(diagonal, blocks_from(3))], 2 * row_count, *edges, early_right
    )
    beside, edges, early_right, wide_bias = lax.optimization_barrier(
        (beside, edges, early_right, wide_bias)
    )
    early = (exchange(early_right, 1), own_blocks + blocks_from(3))
    *edges, late_right = edges_of(
        [(beside, blocks_from(1)), (near, blocks_from(2))], 0, *edges
    )
    late = (exchange(late_right, 1), blocks_from(1) + blocks_from(2))

    left, right, gate, pairs = edges
    triangle, across = call(
        functools.partial(near_triangle_kernel, row_count, chips, half // 2, [early[1]]),
        (tall, tall),
        (left, right, early[0]),
    )
    part = half // 2 * res
    in_part, own_shape = shaped(f32, part, channels), shaped(f32, row_count * res, channels)
    att_part = shaped(bf16, part, channels)
    shared = (norms, w_tri_out, left, gate, pairs)
    scratch = (pltpu.VMEM((part, channels), f32),)
    across, after_a, att_a = call(
        functools.partial(own_inputs_kernel, row_count, chips, late[1]),
        (tall, in_part, att_part),
        shared + (late[0], triangle, across),
        {7: 0},
        scratch=scratch,
    )
    far_att_a = exchange(att_a, 1)
    att_b = call(
        functools.partial(other_inputs_kernel, row_count, chips),
        att_part,
        shared + (triangle, across),
        scratch=scratch,
    )
    far_att_b = exchange(att_b, 1)

    def attention_scratch(keys, projected):
        return (
            pltpu.VMEM((keys * res, channels), f32),
            pltpu.VMEM((projected * res, channels), f32),
            pltpu.VMEM((projected * res, channels), f32),
            pltpu.VMEM((row_count, 40, channels), f32),
            pltpu.VMEM((row_count * keys * res, channels), f32),
        )

    sums, query, att_gate, after_own = call(
        functools.partial(most_attention_kernel, row_count, chips),
        (shaped(f32, row_count, 3, res, channels), own_shape, own_shape, own_shape),
        (valid_column, same_head, w_query, w_att_gate, w_key, w_value, wide_bias)
        + (att_a, att_b, far_att_a, after_a),
        scratch=attention_scratch(3 * half // 2, 3 * half // 2),
    )
    return call(
        functools.partial(attention_kernel, row_count, chips),
        shaped(bf16, *pair_rep.shape),
        (valid_column, same_head, w_key, w_value, w_att_out, wide_bias, far_att_b)
        + (query, att_gate, after_own, sums),
        scratch=attention_scratch(half // 2, half // 2),
    )


def per_device(pair_rep, residue_valid, *parameters):
    row_count, res, channels = pair_rep.shape
    devices = res // row_count
    if res % 48 == 0 and devices == 16 and 40 * res * res * channels <= 32 * 1024 * 1024:
        return on_whole_complex(pair_rep, residue_valid, *parameters)
    return split_over_devices(pair_rep, residue_valid, *parameters)


def solution(mesh):
    return jax.shard_map(
        per_device,
        mesh=mesh,
        in_specs=(
            P(("groups", "row"), None, None),
            P("groups"),
            P(),
            P(),
            P(),
            P(),
            P(),
            P(),
            P(),
            P(),
            P(),
            P(),
            P(),
            P(),
            P(),
            P(),
            P(),
        ),
        out_specs=P(("groups", "row"), None, None),
        check_vma=False,
    )
```

```python
import functools
import math

import jax
import jax.numpy as jnp
from jax import lax
from jax.experimental import pallas as pl
from jax.experimental.pallas import tpu as pltpu
from jax.sharding import PartitionSpec as P

HEADS = 4
HEAD_DIM = 32


def layer_norm(values, norm_gain, norm_bias, along_axis):
    centre = values - jnp.mean(values, axis=along_axis, keepdims=True)
    spread = jnp.mean(centre * centre, axis=along_axis, keepdims=True)
    return centre * lax.rsqrt(spread + 1e-05) * norm_gain + norm_bias


def attend(query_cols, key_cols, value_cols, whole_bias, key_mask):
    factor = 1.0 / math.sqrt(HEAD_DIM)
    scores = (
        jnp.einsum("kjhd,ijhd->jhki", key_cols, query_cols, preferred_element_type=jnp.float32)
        * factor
    )
    scores = scores + whole_bias.astype(jnp.float32)[None] + key_mask[None, None, :, None]
    scores = scores - jnp.max(scores, axis=2, keepdims=True)
    exponent = jnp.exp(scores)
    weights = (exponent / jnp.sum(exponent, axis=2, keepdims=True)).astype(jnp.bfloat16)
    return jnp.einsum("jhki,kjhd->ijhd", weights, value_cols, preferred_element_type=jnp.float32)


def split_over_devices(
    pair_rep,
    residue_valid,
    tri_norm_gain,
    tri_norm_bias,
    w_edges,
    w_tri_gate,
    out_norm_gain,
    out_norm_bias,
    w_tri_out,
    att_norm_gain,
    att_norm_bias,
    w_query,
    w_key,
    w_value,
    w_att_gate,
    w_pair_bias,
    w_att_out,
):
    row_count = pair_rep.shape[0]
    res_count = pair_rep.shape[1]
    channels = pair_rep.shape[2]
    hidden_width = HEADS * HEAD_DIM
    row_start = lax.axis_index("row") * row_count
    valid_flags = residue_valid.astype(jnp.float32)
    own_valid = lax.dynamic_slice_in_dim(valid_flags, row_start, row_count)
    normed = layer_norm(pair_rep.astype(jnp.float32), tri_norm_gain, tri_norm_bias, 2).astype(
        jnp.bfloat16
    )
    projected = jnp.einsum("ikd,de->eik", normed, w_edges, preferred_element_type=jnp.float32)
    projected = projected.reshape(4, channels, row_count, res_count)
    pair_mask = (own_valid[:, None] * valid_flags[None, :])[None, :, :]
    left_edges = (jax.nn.sigmoid(projected[1]) * projected[0] * pair_mask).astype(jnp.bfloat16)
    right_edges = (jax.nn.sigmoid(projected[3]) * projected[2] * pair_mask).astype(jnp.bfloat16)
    left_cols, right_cols = (
        lax.all_to_all(left_edges, "row", split_axis=0, concat_axis=1, tiled=True),
        lax.all_to_all(right_edges, "row", split_axis=0, concat_axis=1, tiled=True),
    )
    block_product = jnp.einsum(
        "cik,cjk->cij", left_cols, right_cols, preferred_element_type=jnp.float32
    ).astype(jnp.bfloat16)
    triangle = lax.all_to_all(block_product, "row", split_axis=1, concat_axis=0, tiled=True)
    tri_normed = layer_norm(
        triangle.astype(jnp.float32), out_norm_gain[:, None, None], out_norm_bias[:, None, None], 0
    ).astype(jnp.bfloat16)
    tri_gate = jax.nn.sigmoid(
        jnp.einsum("ijc,ce->ije", normed, w_tri_gate, preferred_element_type=jnp.float32)
    )
    tri_update = jnp.einsum(
        "cij,ce->ije", tri_normed, w_tri_out, preferred_element_type=jnp.float32
    )
    after_tri = pair_rep.astype(jnp.float32) + tri_gate * tri_update
    att_in = layer_norm(after_tri, att_norm_gain, att_norm_bias, 2).astype(jnp.bfloat16)
    pair_bias = jnp.einsum(
        "kic,ch->hki", att_in, w_pair_bias, preferred_element_type=jnp.float32
    ).astype(jnp.bfloat16)
    whole_bias = lax.all_gather(pair_bias, "row", axis=1, tiled=True)
    key_mask = 1000000000.0 * (valid_flags - 1.0)
    columns = lax.all_to_all(att_in, "row", split_axis=1, concat_axis=0, tiled=True)
    all_weights = jnp.concatenate([w_query, w_key, w_value, w_att_gate], axis=1)
    joined = jnp.dot(columns.reshape(-1, channels), all_weights, preferred_element_type=jnp.float32)
    query_cols = (
        joined[:, :hidden_width].astype(jnp.bfloat16).reshape(res_count, row_count, HEADS, HEAD_DIM)
    )
    key_cols = (
        joined[:, hidden_width : 2 * hidden_width]
        .astype(jnp.bfloat16)
        .reshape(res_count, row_count, HEADS, HEAD_DIM)
    )
    value_cols = (
        joined[:, 2 * hidden_width : 3 * hidden_width]
        .astype(jnp.bfloat16)
        .reshape(res_count, row_count, HEADS, HEAD_DIM)
    )
    gate_cols = jax.nn.sigmoid(joined[:, 3 * hidden_width :]).reshape(
        res_count, row_count, hidden_width
    )
    attended = attend(query_cols, key_cols, value_cols, whole_bias, key_mask)
    gated = (attended.reshape(res_count, row_count, hidden_width) * gate_cols).astype(jnp.bfloat16)
    gated_rows = lax.all_to_all(gated, "row", split_axis=0, concat_axis=1, tiled=True)
    final = after_tri + jnp.einsum(
        "ije,ec->ijc", gated_rows, w_att_out, preferred_element_type=jnp.float32
    )
    return final.astype(jnp.bfloat16)


def sigmoid(values):
    return 0.5 * jnp.tanh(0.5 * values) + 0.5


def dot(left, right):
    return jnp.dot(left, right, preferred_element_type=jnp.float32)


def rounded(values):
    return values.astype(jnp.bfloat16).astype(jnp.float32)


def chip_and_core():
    device = lax.axis_index("row")
    return lax.shift_right_logical(device, 1), jnp.bitwise_and(device, 1)


def rows_of_blocks(row_count, blocks):
    chip, _ = chip_and_core()
    return [(jnp.bitwise_xor(chip, bits), r) for bits in blocks for r in range(row_count)]


def edges_kernel(
    row_count, chips, pieces, send_row, makes_heads, valid_column, norms, weights, *refs
):
    pairs_ref_in = refs[0]
    left_ref, right_ref, gate_ref, pairs_ref, send_ref = refs[-5:]
    if makes_heads:
        left_ref, right_ref, gate_ref, pairs_ref, send_ref, same_head_ref = refs[-6:]
        wide = same_head_ref.shape
        row = lax.broadcasted_iota(jnp.int32, wide, 0) // HEAD_DIM
        column = lax.broadcasted_iota(jnp.int32, wide, 1) // HEAD_DIM
        same_head_ref[...] = jnp.where(row == column, 1.0, 0.0).astype(jnp.bfloat16)
    f32, bf16 = jnp.float32, jnp.bfloat16
    res, channels = valid_column.shape
    _, core = chip_and_core()
    own_place = jnp.bitwise_and(lax.shift_right_logical(lax.axis_index("row"), 1), 3)
    pairs = []
    for piece in pieces:
        rows = len(piece) * row_count
        place = 0 if makes_heads else jnp.bitwise_xor(own_place, piece[0])
        pairs.append(pairs_ref_in[pl.ds(place * rows, rows)].astype(f32).reshape(-1, channels))
    pairs = jnp.concatenate(pairs, axis=0)
    normed = layer_norm(pairs, norms[0:1, :], norms[1:2, :], 1).astype(bf16)
    column = valid_column[...]
    rows_of = rows_of_blocks(row_count, [bits for piece in pieces for bits in piece])
    masks = jnp.concatenate(
        [
            column * valid_column[pl.ds((2 * chip + core) * row_count + r, 1), :]
            for chip, r in rows_of
        ],
        axis=0,
    )
    joined = dot(normed, weights[:, : 2 * channels])
    left = rounded(sigmoid(joined[:, channels:]) * joined[:, :channels] * masks)
    joined = dot(normed, weights[:, 2 * channels : 4 * channels])
    right = (sigmoid(joined[:, channels:]) * joined[:, :channels] * masks).astype(bf16)
    gate = sigmoid(dot(normed, weights[:, 4 * channels :]))
    for n, (chip, r) in enumerate(rows_of):
        rows = slice(n * res, (n + 1) * res)
        start = pl.multiple_of((chip * row_count + r) * res, res)
        send_ref[send_row + n] = right[rows]
        left_ref[pl.ds(start, res), :] = left[rows]
        place_right(right_ref, chips, chip, r, right[rows])
        gate_ref[pl.ds(start, res), :] = gate[rows]
        pairs_ref[pl.ds(start, res), :] = pairs[rows]


def place_right(right_ref, chips, chip, r, edges):
    res = edges.shape[0]
    start = pl.multiple_of((r * chips + chip) * res, res)
    right_ref[pl.ds(start, res), :] = edges.astype(jnp.float32)


def sum_sublanes(parts):
    row = lax.broadcasted_iota(jnp.int32, parts[0].shape, 0)
    for shift in (1, 2, 4):
        high = jnp.bitwise_and(row, shift) > 0
        parts = [
            jnp.where(high, odd, even) + pltpu.roll(jnp.where(high, even, odd), shift, 0)
            for even, odd in zip(parts[0::2], parts[1::2])
        ]
    return parts[0]


def triangle_rows(
    row_count, chips, left_ref, right_ref, triangle_ref, first, count, core, triangle_first
):
    res = 2 * row_count * chips
    start = pl.multiple_of(first * res, res)
    block = 4
    for n in range(0, count, block):
        lefts = [left_ref[pl.ds(start + m * res, res), :] for m in range(n, n + block)]
        for r in range(row_count):
            parts = [[] for _ in range(block)]
            for chip in range(chips):
                at = (r * chips + chip) * res
                right = right_ref[at : at + res, :]
                for m in range(block):
                    product = lefts[m] * right
                    parts[m].append(
                        sum(product[k : k + 8] for k in range(8, res, 8)) + product[:8]
                    )
            for m in range(block):
                place = (triangle_first + n + m) * res + core * row_count + r
                triangle_ref[pl.ds(place, chips, stride=2 * row_count), :] = rounded(
                    sum_sublanes(parts[m])
                )


def near_triangle_kernel(row_count, chips, chunk, pieces, left_ref, right_ref, *refs):
    received, (triangle_ref, across_ref) = refs[:-2], refs[-2:]
    _, core = chip_and_core()

    def some_rows(step, carry):
        first = step * chunk
        triangle_rows(
            row_count, chips, left_ref, right_ref, triangle_ref, first, chunk, core, first
        )
        return carry

    for ref, blocks in zip(received, pieces):
        for n, (chip, r) in enumerate(rows_of_blocks(row_count, blocks)):
            place_right(across_ref, chips, chip, r, ref[n])
    lax.fori_loop(0, row_count * chips // chunk, some_rows, 0)


def attention_inputs(
    row_count, chips, first, norms, w_out, left_ref, gate_ref, pairs_ref, held_triangle, across_ref,
    triangle_ref,
):
    bf16 = jnp.bfloat16
    _, core = chip_and_core()
    half = row_count * chips
    tall = (half // 2) * 2 * half
    rows = pl.ds(pl.multiple_of(first * 2 * half, tall), tall)
    triangle_ref[...] = held_triangle[rows, :]
    triangle_rows(
        row_count, chips, left_ref, across_ref, triangle_ref, first, half // 2, 1 - core, 0
    )
    tri_normed = layer_norm(triangle_ref[...], norms[2:3, :], norms[3:4, :], 1).astype(bf16)
    after_tri = pairs_ref[rows, :] + gate_ref[rows, :] * dot(tri_normed, w_out[...])
    att_in = layer_norm(after_tri, norms[4:5, :], norms[5:6, :], 1).astype(bf16)
    return after_tri, att_in


def first_chip(chips, part):
    chip, _ = chip_and_core()
    return jnp.bitwise_xor(jnp.bitwise_and(chip, chips // 2), part * (chips // 2))


def own_inputs_kernel(
    row_count,
    chips,
    blocks,
    norms,
    w_out,
    left_ref,
    gate_ref,
    pairs_ref,
    received,
    triangle_ref,
    held_across,
    across_ref,
    after_ref,
    att_ref,
    scratch_ref,
):
    for n, (chip, r) in enumerate(rows_of_blocks(row_count, blocks)):
        place_right(across_ref, chips, chip, r, received[n])
    first = first_chip(chips, 0) * row_count
    refs = (left_ref, gate_ref, pairs_ref, triangle_ref, across_ref, scratch_ref)
    after_ref[...], att_ref[...] = attention_inputs(
        row_count, chips, first, norms, w_out, *refs
    )


def other_inputs_kernel(row_count, chips, norms, w_out, *refs):
    *refs, att_ref, scratch_ref = refs
    first = first_chip(chips, 1) * row_count
    _, att_ref[...] = attention_inputs(row_count, chips, first, norms, w_out, *refs, scratch_ref)


def keys_and_values(att, w_key, w_value, key_ref, value_ref):
    channels = key_ref.shape[1]
    key_value = jnp.concatenate([w_key[...], w_value[...]], axis=1)
    start = 0
    for values in att:
        rows = slice(start, start + values.shape[0])
        joined = dot(values, key_value)
        key_ref[rows, :] = rounded(joined[:, :channels])
        value_ref[rows, :] = rounded(joined[:, channels:])
        start = rows.stop


def column_bias(row_count, res, att, wide_bias, att_ref, bias_ref):
    start = 0
    for values in att:
        att_ref[start : start + values.shape[0], :] = values.astype(jnp.float32)
        start += values.shape[0]
    keys = start // res
    own = lax.axis_index("row") * row_count
    for r in range(row_count):
        column = att_ref[pl.ds(own + r, keys, stride=res), :].astype(jnp.bfloat16)
        bias_ref[r, :keys, :] = rounded(dot(column, wide_bias[...]))


def partial_attention(row_count, chips, query, parts, bias_ref, same_head, valid_column, score_ref):
    bf16, f32 = jnp.bfloat16, jnp.float32
    res = 2 * row_count * chips
    channels = valid_column.shape[1]
    count = row_count * chips // 2
    keys = len(parts) * count
    maxima = [jnp.full((res, channels), -jnp.inf, f32) for _ in range(row_count)]
    for part, (core, first, key_of, _) in enumerate(parts):
        products = []
        for n in range(0, count, 2):
            pair = [jnp.concatenate([key_of(m)] * row_count, axis=0) * query for m in (n, n + 1)]
            products.append(jnp.concatenate([p.astype(bf16) for p in pair], axis=1))
        scores = dot(jnp.concatenate(products, axis=0), same_head[...])
        for n in range(count):
            k = (2 * (first + n // row_count) + core) * row_count + n % row_count
            key_mask = 1000000000.0 * (valid_column[pl.ds(k, 1), :] - 1.0)
            at = part * count + n
            shifts = [
                (bias_ref[r, at : at + 1, :] + key_mask) * math.log2(math.e)
                for r in range(row_count)
            ]
            lanes = slice(n % 2 * channels, (n % 2 + 1) * channels)
            for r in range(row_count):
                start = (n // 2 * row_count + r) * res
                score = scores[start : start + res, lanes] + shifts[r]
                score_ref[(r * keys + at) * res : (r * keys + at + 1) * res, :] = score
                maxima[r] = jnp.maximum(maxima[r], score)
    totals, mixed = [], []
    for r in range(row_count):
        total = mix = jnp.zeros((res, channels), f32)
        for part, (_, _, _, value_of) in enumerate(parts):
            for n in range(count):
                start = (r * keys + part * count + n) * res
                weight = jnp.exp2(score_ref[start : start + res, :] - maxima[r])
                total = total + weight
                mix = mix + weight * value_of(n)
        totals.append(total)
        mixed.append(mix)
    return maxima, totals, mixed


def most_attention_kernel(
    row_count,
    chips,
    valid_column,
    same_head,
    w_query,
    w_gate,
    w_key,
    w_value,
    wide_bias,
    own_att_a,
    own_att_b,
    far_att_a,
    own_after,
    sums_ref,
    query_ref,
    gate_ref,
    after_ref,
    att_ref,
    key_ref,
    value_ref,
    bias_ref,
    score_ref,
):
    chip, core = chip_and_core()
    res, channels = valid_column.shape
    own = row_count * res
    rows = pl.ds(pl.multiple_of(jnp.bitwise_and(chip, chips // 2 - 1) * own, own), own)
    own_in = own_att_a[rows, :]
    query = rounded(dot(own_in, w_query[...])) * (math.log2(math.e) / math.sqrt(HEAD_DIM))
    att = [ref[...] for ref in (own_att_a, own_att_b, far_att_a)]
    keys_and_values(att, w_key, w_value, key_ref, value_ref)
    column_bias(row_count, res, att, wide_bias, att_ref, bias_ref)
    count = row_count * chips // 2

    def rows_of(ref, first):
        return lambda n: ref[(first + n) * res : (first + n + 1) * res, :]

    a, b = first_chip(chips, 0), first_chip(chips, 1)
    parts = [
        (sender, first, rows_of(key_ref, n * count), rows_of(value_ref, n * count))
        for n, (sender, first) in enumerate(((core, a), (core, b), (1 - core, a)))
    ]
    sums = partial_attention(
        row_count, chips, query, parts, bias_ref, same_head, valid_column, score_ref
    )
    for n, each in enumerate(sums):
        for r in range(row_count):
            sums_ref[r, n] = each[r]
    query_ref[...] = query
    gate_ref[...] = sigmoid(dot(own_in, w_gate[...]))
    after_ref[...] = own_after[rows, :]


def attention_kernel(
    row_count,
    chips,
    valid_column,
    same_head,
    w_key,
    w_value,
    w_out,
    wide_bias,
    far_att_b,
    query_ref,
    gate_ref,
    after_ref,
    sums_ref,
    out_ref,
    att_ref,
    key_ref,
    value_ref,
    bias_ref,
    score_ref,
):
    _, core = chip_and_core()
    res, channels = valid_column.shape
    far_att = far_att_b[...]
    keys_and_values([far_att], w_key, w_value, key_ref, value_ref)
    column_bias(row_count, res, [far_att], wide_bias, att_ref, bias_ref)

    def rows_of(ref):
        return lambda n: ref[n * res : (n + 1) * res, :]

    parts = ((1 - core, first_chip(chips, 1), rows_of(key_ref), rows_of(value_ref)),)
    last = partial_attention(
        row_count, chips, query_ref[...], parts, bias_ref, same_head, valid_column, score_ref
    )
    attended = []
    for r, (last_maximum, last_total, last_mixed) in enumerate(zip(*last)):
        maximum = jnp.maximum(sums_ref[r, 0], last_maximum)
        most_scale = jnp.exp2(sums_ref[r, 0] - maximum)
        last_scale = jnp.exp2(last_maximum - maximum)
        total = sums_ref[r, 1] * most_scale + last_total * last_scale
        attended.append((sums_ref[r, 2] * most_scale + last_mixed * last_scale) / total)
    gated = (jnp.concatenate(attended, axis=0) * gate_ref[...]).astype(jnp.bfloat16)
    final = after_ref[...] + dot(gated, w_out[...])
    out_ref[...] = final.astype(jnp.bfloat16).reshape(row_count, res, channels)


def on_whole_complex(
    pair_rep,
    residue_valid,
    tri_norm_gain,
    tri_norm_bias,
    w_edges,
    w_tri_gate,
    out_norm_gain,
    out_norm_bias,
    w_tri_out,
    att_norm_gain,
    att_norm_bias,
    w_query,
    w_key,
    w_value,
    w_att_gate,
    w_pair_bias,
    w_att_out,
):
    row_count, res, channels = pair_rep.shape
    devices = res // row_count
    chips = devices // 2
    half = res // 2
    f32, bf16 = jnp.float32, jnp.bfloat16
    in_vmem = pl.BlockSpec(memory_space=pltpu.VMEM)

    def shaped(dtype, *shape):
        return jax.ShapeDtypeStruct(shape, dtype)

    def call(kernel, outs, operands, aliases=None, scratch=(), cost=2**25):
        return pl.pallas_call(
            kernel,
            out_shape=outs,
            in_specs=[in_vmem] * len(operands),
            out_specs=jax.tree.map(lambda _: in_vmem, outs),
            input_output_aliases=aliases or {},
            scratch_shapes=list(scratch),
            compiler_params=pltpu.CompilerParams(vmem_limit_bytes=24 * 1024 * 1024),
            cost_estimate=pl.CostEstimate(flops=2**20, bytes_accessed=cost, transcendentals=0),
        )(*operands)

    def exchange(values, bit):
        return lax.ppermute(values, "row", [(d, d ^ bit) for d in range(devices)])

    vectors = (
        tri_norm_gain,
        tri_norm_bias,
        out_norm_gain,
        out_norm_bias,
        att_norm_gain,
        att_norm_bias,
    )
    norms = jnp.stack(vectors)
    edge_weights = jnp.concatenate([w_edges, w_tri_gate], axis=1)
    valid_column = jnp.broadcast_to(residue_valid.astype(f32)[:, None], (res, channels))

    head = lax.broadcasted_iota(jnp.int32, (HEADS, channels), 0)
    head_of_channel = lax.broadcasted_iota(jnp.int32, (HEADS, channels), 1) // HEAD_DIM
    repeat = jnp.where(head == head_of_channel, 1.0, 0.0).astype(bf16)
    wide_bias = dot(w_pair_bias, repeat).astype(bf16)

    kept = lax.dynamic_update_slice(
        jnp.zeros((2 * row_count, res, channels), bf16), pair_rep, (0, 0, 0)
    )
    far = exchange(pair_rep, devices // 2)
    far, kept, norms, edge_weights = lax.optimization_barrier((far, kept, norms, edge_weights))
    own = lax.dynamic_update_slice(kept, far, (row_count, 0, 0))
    own_blocks = (0, chips // 2)

    def blocks_from(bits):
        return tuple(s ^ bits for s in own_blocks)

    tall = shaped(f32, half * res, channels)

    def edges_of(pairs, blocks, send_row, *held):
        operands = (valid_column, norms, edge_weights, pairs) + held
        first = len(operands) - len(held)
        sent = sum(len(b) for b in blocks) * row_count
        return call(
            functools.partial(edges_kernel, row_count, chips, blocks, send_row, not held),
            (tall, tall, tall, tall, shaped(bf16, sent, res, channels))
            + (() if held else (shaped(bf16, 2 * channels, 2 * channels),)),
            operands,
            {first + e: e for e in range(len(held))},
        )

    groups = [
        [far_bit + 2 * place + core for place in range(4)]
        for far_bit in range(0, devices, 8)
        for core in range(2)
    ]
    gathered = lax.all_to_all(
        jnp.concatenate([own] * 4, axis=0),
        "row",
        split_axis=0,
        concat_axis=0,
        axis_index_groups=groups,
        tiled=True,
    )
    *edges, early_right, same_head = edges_of(own, (own_blocks,), 0)
    edges, wide_bias = lax.optimization_barrier((edges, wide_bias))
    early = (exchange(early_right, 1), own_blocks)
    new_blocks = tuple(blocks_from(bits) for bits in (1, 2, 3))
    *edges, late_right = edges_of(gathered, new_blocks, 0, *edges)
    late = (exchange(late_right, 1), sum(new_blocks, ()))

    left, right, gate, pairs = edges
    triangle, across = call(
        functools.partial(near_triangle_kernel, row_count, chips, half // 2, [early[1]]),
        (tall, tall),
        (left, right, early[0]),
    )
    part = half // 2 * res
    in_part, own_shape = shaped(f32, part, channels), shaped(f32, row_count * res, channels)
    att_part = shaped(bf16, part, channels)
    shared = (norms, w_tri_out, left, gate, pairs)
    scratch = (pltpu.VMEM((part, channels), f32),)
    across, after_a, att_a = call(
        functools.partial(own_inputs_kernel, row_count, chips, late[1]),
        (tall, in_part, att_part),
        shared + (late[0], triangle, across),
        {7: 0},
        scratch=scratch,
    )
    far_att_a = exchange(att_a, 1)
    att_b = call(
        functools.partial(other_inputs_kernel, row_count, chips),
        att_part,
        shared + (triangle, across),
        scratch=scratch,
    )
    far_att_b = exchange(att_b, 1)

    def attention_scratch(keys, projected):
        return (
            pltpu.VMEM((keys * res, channels), f32),
            pltpu.VMEM((projected * res, channels), f32),
            pltpu.VMEM((projected * res, channels), f32),
            pltpu.VMEM((row_count, 40, channels), f32),
            pltpu.VMEM((row_count * keys * res, channels), f32),
        )

    sums, query, att_gate, after_own = call(
        functools.partial(most_attention_kernel, row_count, chips),
        (shaped(f32, row_count, 3, res, channels), own_shape, own_shape, own_shape),
        (valid_column, same_head, w_query, w_att_gate, w_key, w_value, wide_bias)
        + (att_a, att_b, far_att_a, after_a),
        scratch=attention_scratch(3 * half // 2, 3 * half // 2),
    )
    return call(
        functools.partial(attention_kernel, row_count, chips),
        shaped(bf16, *pair_rep.shape),
        (valid_column, same_head, w_key, w_value, w_att_out, wide_bias, far_att_b)
        + (query, att_gate, after_own, sums),
        scratch=attention_scratch(half // 2, half // 2),
    )


def per_device(pair_rep, residue_valid, *parameters):
    row_count, res, channels = pair_rep.shape
    devices = res // row_count
    if res % 48 == 0 and devices == 16 and 40 * res * res * channels <= 32 * 1024 * 1024:
        return on_whole_complex(pair_rep, residue_valid, *parameters)
    return split_over_devices(pair_rep, residue_valid, *parameters)


def solution(mesh):
    return jax.shard_map(
        per_device,
        mesh=mesh,
        in_specs=(
            P(("groups", "row"), None, None),
            P("groups"),
            P(),
            P(),
            P(),
            P(),
            P(),
            P(),
            P(),
            P(),
            P(),
            P(),
            P(),
            P(),
            P(),
            P(),
            P(),
        ),
        out_specs=P(("groups", "row"), None, None),
        check_vma=False,
    )
```

```python
import functools
import math

import jax
import jax.numpy as jnp
from jax import lax
from jax.experimental import pallas as pl
from jax.experimental.pallas import tpu as pltpu
from jax.sharding import PartitionSpec as P

HEADS = 4
HEAD_DIM = 32


def layer_norm(values, norm_gain, norm_bias, along_axis):
    centre = values - jnp.mean(values, axis=along_axis, keepdims=True)
    spread = jnp.mean(centre * centre, axis=along_axis, keepdims=True)
    return centre * lax.rsqrt(spread + 1e-05) * norm_gain + norm_bias


def attend(query_cols, key_cols, value_cols, whole_bias, key_mask):
    factor = 1.0 / math.sqrt(HEAD_DIM)
    scores = (
        jnp.einsum("kjhd,ijhd->jhki", key_cols, query_cols, preferred_element_type=jnp.float32)
        * factor
    )
    scores = scores + whole_bias.astype(jnp.float32)[None] + key_mask[None, None, :, None]
    scores = scores - jnp.max(scores, axis=2, keepdims=True)
    exponent = jnp.exp(scores)
    weights = (exponent / jnp.sum(exponent, axis=2, keepdims=True)).astype(jnp.bfloat16)
    return jnp.einsum("jhki,kjhd->ijhd", weights, value_cols, preferred_element_type=jnp.float32)


def split_over_devices(
    pair_rep,
    residue_valid,
    tri_norm_gain,
    tri_norm_bias,
    w_edges,
    w_tri_gate,
    out_norm_gain,
    out_norm_bias,
    w_tri_out,
    att_norm_gain,
    att_norm_bias,
    w_query,
    w_key,
    w_value,
    w_att_gate,
    w_pair_bias,
    w_att_out,
):
    row_count = pair_rep.shape[0]
    res_count = pair_rep.shape[1]
    channels = pair_rep.shape[2]
    hidden_width = HEADS * HEAD_DIM
    row_start = lax.axis_index("row") * row_count
    valid_flags = residue_valid.astype(jnp.float32)
    own_valid = lax.dynamic_slice_in_dim(valid_flags, row_start, row_count)
    normed = layer_norm(pair_rep.astype(jnp.float32), tri_norm_gain, tri_norm_bias, 2).astype(
        jnp.bfloat16
    )
    projected = jnp.einsum("ikd,de->eik", normed, w_edges, preferred_element_type=jnp.float32)
    projected = projected.reshape(4, channels, row_count, res_count)
    pair_mask = (own_valid[:, None] * valid_flags[None, :])[None, :, :]
    left_edges = (jax.nn.sigmoid(projected[1]) * projected[0] * pair_mask).astype(jnp.bfloat16)
    right_edges = (jax.nn.sigmoid(projected[3]) * projected[2] * pair_mask).astype(jnp.bfloat16)
    left_cols, right_cols = (
        lax.all_to_all(left_edges, "row", split_axis=0, concat_axis=1, tiled=True),
        lax.all_to_all(right_edges, "row", split_axis=0, concat_axis=1, tiled=True),
    )
    block_product = jnp.einsum(
        "cik,cjk->cij", left_cols, right_cols, preferred_element_type=jnp.float32
    ).astype(jnp.bfloat16)
    triangle = lax.all_to_all(block_product, "row", split_axis=1, concat_axis=0, tiled=True)
    tri_normed = layer_norm(
        triangle.astype(jnp.float32), out_norm_gain[:, None, None], out_norm_bias[:, None, None], 0
    ).astype(jnp.bfloat16)
    tri_gate = jax.nn.sigmoid(
        jnp.einsum("ijc,ce->ije", normed, w_tri_gate, preferred_element_type=jnp.float32)
    )
    tri_update = jnp.einsum(
        "cij,ce->ije", tri_normed, w_tri_out, preferred_element_type=jnp.float32
    )
    after_tri = pair_rep.astype(jnp.float32) + tri_gate * tri_update
    att_in = layer_norm(after_tri, att_norm_gain, att_norm_bias, 2).astype(jnp.bfloat16)
    pair_bias = jnp.einsum(
        "kic,ch->hki", att_in, w_pair_bias, preferred_element_type=jnp.float32
    ).astype(jnp.bfloat16)
    whole_bias = lax.all_gather(pair_bias, "row", axis=1, tiled=True)
    key_mask = 1000000000.0 * (valid_flags - 1.0)
    columns = lax.all_to_all(att_in, "row", split_axis=1, concat_axis=0, tiled=True)
    all_weights = jnp.concatenate([w_query, w_key, w_value, w_att_gate], axis=1)
    joined = jnp.dot(columns.reshape(-1, channels), all_weights, preferred_element_type=jnp.float32)
    query_cols = (
        joined[:, :hidden_width].astype(jnp.bfloat16).reshape(res_count, row_count, HEADS, HEAD_DIM)
    )
    key_cols = (
        joined[:, hidden_width : 2 * hidden_width]
        .astype(jnp.bfloat16)
        .reshape(res_count, row_count, HEADS, HEAD_DIM)
    )
    value_cols = (
        joined[:, 2 * hidden_width : 3 * hidden_width]
        .astype(jnp.bfloat16)
        .reshape(res_count, row_count, HEADS, HEAD_DIM)
    )
    gate_cols = jax.nn.sigmoid(joined[:, 3 * hidden_width :]).reshape(
        res_count, row_count, hidden_width
    )
    attended = attend(query_cols, key_cols, value_cols, whole_bias, key_mask)
    gated = (attended.reshape(res_count, row_count, hidden_width) * gate_cols).astype(jnp.bfloat16)
    gated_rows = lax.all_to_all(gated, "row", split_axis=0, concat_axis=1, tiled=True)
    final = after_tri + jnp.einsum(
        "ije,ec->ijc", gated_rows, w_att_out, preferred_element_type=jnp.float32
    )
    return final.astype(jnp.bfloat16)


def sigmoid(values):
    return 0.5 * jnp.tanh(0.5 * values) + 0.5


def row_norm(values, norm_gain, norm_bias):
    count = values.shape[1]
    centre = values - jnp.sum(values, axis=1, keepdims=True) * (1.0 / count)
    squares = jnp.sum(centre * centre, axis=1, keepdims=True)
    return centre * lax.rsqrt(squares + 1e-05 * count) * (norm_gain * count**0.5) + norm_bias


def dot(left, right):
    return jnp.dot(left, right, preferred_element_type=jnp.float32)


def rounded(values):
    return values.astype(jnp.bfloat16).astype(jnp.float32)


def chip_and_core():
    device = lax.axis_index("row")
    return lax.shift_right_logical(device, 1), jnp.bitwise_and(device, 1)


def rows_of_blocks(row_count, blocks):
    chip, _ = chip_and_core()
    return [(jnp.bitwise_xor(chip, bits), r) for bits in blocks for r in range(row_count)]


def edges_kernel(
    row_count, chips, pieces, send_row, makes_heads, valid_column, norms, weights, *refs
):
    pair_refs = refs[: len(pieces)]
    left_ref, right_ref, gate_ref, pairs_ref, send_ref = refs[-5:]
    if makes_heads:
        left_ref, right_ref, gate_ref, pairs_ref, send_ref, same_head_ref = refs[-6:]
        wide = same_head_ref.shape
        row = lax.broadcasted_iota(jnp.int32, wide, 0) // HEAD_DIM
        column = lax.broadcasted_iota(jnp.int32, wide, 1) // HEAD_DIM
        same_head_ref[...] = jnp.where(row == column, 1.0, 0.0).astype(jnp.bfloat16)
    f32, bf16 = jnp.float32, jnp.bfloat16
    res, channels = valid_column.shape
    _, core = chip_and_core()
    pairs = jnp.concatenate(
        [ref[...].astype(f32).reshape(-1, channels) for ref in pair_refs], axis=0
    )
    normed = row_norm(pairs, norms[0:1, :], norms[1:2, :]).astype(bf16)
    column = 0.5 * valid_column[...]
    rows_of = rows_of_blocks(row_count, [bits for piece in pieces for bits in piece])
    masks = jnp.concatenate(
        [
            column * valid_column[pl.ds((2 * chip + core) * row_count + r, 1), :]
            for chip, r in rows_of
        ],
        axis=0,
    )
    joined = dot(normed, weights[:, : 2 * channels])
    left = rounded((jnp.tanh(joined[:, channels:]) + 1.0) * joined[:, :channels] * masks)
    joined = dot(normed, weights[:, 2 * channels : 4 * channels])
    right = ((jnp.tanh(joined[:, channels:]) + 1.0) * joined[:, :channels] * masks).astype(bf16)
    gate = 0.5 * jnp.tanh(dot(normed, weights[:, 4 * channels :])) + 0.5
    for n, (chip, r) in enumerate(rows_of):
        rows = slice(n * res, (n + 1) * res)
        start = pl.multiple_of((chip * row_count + r) * res, res)
        send_ref[send_row + n] = right[rows]
        left_ref[pl.ds(start, res), :] = left[rows]
        place_right(right_ref, chips, chip, r, right[rows])
        gate_ref[pl.ds(start, res), :] = gate[rows]
        pairs_ref[pl.ds(start, res), :] = pairs[rows]


def place_right(right_ref, chips, chip, r, edges):
    res = edges.shape[0]
    start = pl.multiple_of((r * chips + chip) * res, res)
    right_ref[pl.ds(start, res), :] = edges.astype(jnp.float32)


def sum_sublanes(parts):
    row = lax.broadcasted_iota(jnp.int32, parts[0].shape, 0)
    for shift in (1, 2, 4):
        high = jnp.bitwise_and(row, shift) > 0
        parts = [
            jnp.where(high, odd, even) + pltpu.roll(jnp.where(high, even, odd), shift, 0)
            for even, odd in zip(parts[0::2], parts[1::2])
        ]
    return parts[0]


def triangle_rows(
    row_count, chips, left_ref, right_ref, triangle_ref, first, count, core, triangle_first
):
    res = 2 * row_count * chips
    start = pl.multiple_of(first * res, res)
    block = 4
    for n in range(0, count, block):
        lefts = [left_ref[pl.ds(start + m * res, res), :] for m in range(n, n + block)]
        for r in range(row_count):
            parts = [[] for _ in range(block)]
            for chip in range(chips):
                at = (r * chips + chip) * res
                right = right_ref[at : at + res, :]
                for m in range(block):
                    product = lefts[m] * right
                    parts[m].append(
                        sum(product[k : k + 8] for k in range(8, res, 8)) + product[:8]
                    )
            for m in range(block):
                place = (triangle_first + n + m) * res + core * row_count + r
                triangle_ref[pl.ds(place, chips, stride=2 * row_count), :] = rounded(
                    sum_sublanes(parts[m])
                )


def near_triangle_kernel(row_count, chips, chunk, pieces, left_ref, right_ref, *refs):
    received, (triangle_ref, across_ref) = refs[:-2], refs[-2:]
    _, core = chip_and_core()

    def some_rows(step, carry):
        first = step * chunk
        triangle_rows(
            row_count, chips, left_ref, right_ref, triangle_ref, first, chunk, core, first
        )
        return carry

    for ref, blocks in zip(received, pieces):
        for n, (chip, r) in enumerate(rows_of_blocks(row_count, blocks)):
            place_right(across_ref, chips, chip, r, ref[n])
    lax.fori_loop(0, row_count * chips // chunk, some_rows, 0)


def attention_inputs(
    row_count, chips, first, norms, w_out, left_ref, gate_ref, pairs_ref, held_triangle, across_ref,
    triangle_ref,
):
    bf16 = jnp.bfloat16
    _, core = chip_and_core()
    half = row_count * chips
    tall = (half // 2) * 2 * half
    rows = pl.ds(pl.multiple_of(first * 2 * half, tall), tall)
    triangle_ref[...] = held_triangle[rows, :]
    triangle_rows(
        row_count, chips, left_ref, across_ref, triangle_ref, first, half // 2, 1 - core, 0
    )
    tri_normed = row_norm(triangle_ref[...], norms[2:3, :], norms[3:4, :]).astype(bf16)
    after_tri = pairs_ref[rows, :] + gate_ref[rows, :] * dot(tri_normed, w_out[...])
    att_in = row_norm(after_tri, norms[4:5, :], norms[5:6, :]).astype(bf16)
    return after_tri, att_in


def first_chip(chips, part):
    chip, _ = chip_and_core()
    return jnp.bitwise_xor(jnp.bitwise_and(chip, chips // 2), part * (chips // 2))


def own_inputs_kernel(
    row_count,
    chips,
    blocks,
    norms,
    w_out,
    left_ref,
    gate_ref,
    pairs_ref,
    received,
    triangle_ref,
    held_across,
    across_ref,
    after_ref,
    att_ref,
    scratch_ref,
):
    for n, (chip, r) in enumerate(rows_of_blocks(row_count, blocks)):
        place_right(across_ref, chips, chip, r, received[n])
    first = first_chip(chips, 0) * row_count
    refs = (left_ref, gate_ref, pairs_ref, triangle_ref, across_ref, scratch_ref)
    after_ref[...], att_ref[...] = attention_inputs(
        row_count, chips, first, norms, w_out, *refs
    )


def other_inputs_kernel(row_count, chips, norms, w_out, *refs):
    *refs, att_ref, scratch_ref = refs
    first = first_chip(chips, 1) * row_count
    _, att_ref[...] = attention_inputs(row_count, chips, first, norms, w_out, *refs, scratch_ref)


def keys_and_values(att, w_key, w_value, key_ref, value_ref):
    channels = key_ref.shape[1]
    key_value = jnp.concatenate([w_key[...], w_value[...]], axis=1)
    start = 0
    for values in att:
        rows = slice(start, start + values.shape[0])
        joined = dot(values, key_value)
        key_ref[rows, :] = joined[:, :channels]
        value_ref[rows, :] = joined[:, channels:]
        start = rows.stop


def column_bias(row_count, res, att, wide_bias, att_ref, bias_ref):
    start = 0
    for values in att:
        att_ref[start : start + values.shape[0], :] = values.astype(jnp.float32)
        start += values.shape[0]
    keys = start // res
    own = lax.axis_index("row") * row_count
    height = -(-keys // 8) * 8
    columns = []
    for r in range(row_count):
        column = att_ref[pl.ds(own + r, keys, stride=res), :]
        columns.append(jnp.concatenate([column, jnp.zeros((height - keys, column.shape[1]), jnp.float32)]))
    columns = jnp.concatenate(columns, axis=0).astype(jnp.bfloat16)
    bias = rounded(dot(columns, wide_bias[...]))
    for r in range(row_count):
        bias_ref[r, :height, :] = bias[r * height : (r + 1) * height]


def partial_attention(row_count, chips, query, parts, bias_ref, same_head, valid_column, score_ref):
    bf16, f32 = jnp.bfloat16, jnp.float32
    res = 2 * row_count * chips
    channels = valid_column.shape[1]
    count = row_count * chips // 2
    keys = len(parts) * count
    maxima = [jnp.full((res, channels), -jnp.inf, f32) for _ in range(row_count)]
    for part, (core, first, key_of, _) in enumerate(parts):
        products = []
        for n in range(0, count, 2):
            pair = [jnp.concatenate([key_of(m)] * row_count, axis=0) * query for m in (n, n + 1)]
            products.append(jnp.concatenate([p.astype(bf16) for p in pair], axis=1))
        scores = dot(jnp.concatenate(products, axis=0), same_head[...])
        for n in range(count):
            k = (2 * (first + n // row_count) + core) * row_count + n % row_count
            key_mask = 1000000000.0 * (valid_column[pl.ds(k, 1), :] - 1.0)
            at = part * count + n
            shifts = [
                (bias_ref[r, at : at + 1, :] + key_mask) * math.log2(math.e)
                for r in range(row_count)
            ]
            lanes = slice(n % 2 * channels, (n % 2 + 1) * channels)
            for r in range(row_count):
                start = (n // 2 * row_count + r) * res
                score = scores[start : start + res, lanes] + shifts[r]
                score_ref[(r * keys + at) * res : (r * keys + at + 1) * res, :] = score
                maxima[r] = jnp.maximum(maxima[r], score)
    totals, mixed = [], []
    for r in range(row_count):
        total = mix = jnp.zeros((res, channels), f32)
        for part, (_, _, _, value_of) in enumerate(parts):
            for n in range(count):
                start = (r * keys + part * count + n) * res
                weight = jnp.exp2(score_ref[start : start + res, :] - maxima[r])
                total = total + weight
                mix = mix + weight * value_of(n)
        totals.append(total)
        mixed.append(mix)
    return maxima, totals, mixed


def most_attention_kernel(
    row_count,
    chips,
    valid_column,
    same_head,
    w_query,
    w_gate,
    w_key,
    w_value,
    wide_bias,
    own_att_a,
    own_att_b,
    far_att_a,
    own_after,
    sums_ref,
    query_ref,
    gate_ref,
    after_ref,
    att_ref,
    key_ref,
    value_ref,
    bias_ref,
    score_ref,
):
    chip, core = chip_and_core()
    res, channels = valid_column.shape
    own = row_count * res
    rows = pl.ds(pl.multiple_of(jnp.bitwise_and(chip, chips // 2 - 1) * own, own), own)
    own_in = own_att_a[rows, :]
    query = rounded(dot(own_in, w_query[...])) * (math.log2(math.e) / math.sqrt(HEAD_DIM))
    att = [ref[...] for ref in (own_att_a, own_att_b, far_att_a)]
    keys_and_values(att, w_key, w_value, key_ref, value_ref)
    column_bias(row_count, res, att, wide_bias, att_ref, bias_ref)
    count = row_count * chips // 2

    def rows_of(ref, first):
        return lambda n: ref[(first + n) * res : (first + n + 1) * res, :]

    a, b = first_chip(chips, 0), first_chip(chips, 1)
    parts = [
        (sender, first, rows_of(key_ref, n * count), rows_of(value_ref, n * count))
        for n, (sender, first) in enumerate(((core, a), (core, b), (1 - core, a)))
    ]
    sums = partial_attention(
        row_count, chips, query, parts, bias_ref, same_head, valid_column, score_ref
    )
    for n, each in enumerate(sums):
        for r in range(row_count):
            sums_ref[r, n] = each[r]
    query_ref[...] = query
    gate_ref[...] = sigmoid(dot(own_in, w_gate[...]))
    after_ref[...] = own_after[rows, :]


def attention_kernel(
    row_count,
    chips,
    valid_column,
    same_head,
    w_key,
    w_value,
    w_out,
    wide_bias,
    far_att_b,
    query_ref,
    gate_ref,
    after_ref,
    sums_ref,
    out_ref,
    att_ref,
    key_ref,
    value_ref,
    bias_ref,
    score_ref,
):
    _, core = chip_and_core()
    res, channels = valid_column.shape
    far_att = far_att_b[...]
    keys_and_values([far_att], w_key, w_value, key_ref, value_ref)
    column_bias(row_count, res, [far_att], wide_bias, att_ref, bias_ref)

    def rows_of(ref):
        return lambda n: ref[n * res : (n + 1) * res, :]

    parts = ((1 - core, first_chip(chips, 1), rows_of(key_ref), rows_of(value_ref)),)
    last = partial_attention(
        row_count, chips, query_ref[...], parts, bias_ref, same_head, valid_column, score_ref
    )
    attended = []
    for r, (last_maximum, last_total, last_mixed) in enumerate(zip(*last)):
        maximum = jnp.maximum(sums_ref[r, 0], last_maximum)
        most_scale = jnp.exp2(sums_ref[r, 0] - maximum)
        last_scale = jnp.exp2(last_maximum - maximum)
        total = sums_ref[r, 1] * most_scale + last_total * last_scale
        attended.append((sums_ref[r, 2] * most_scale + last_mixed * last_scale) / total)
    gated = (jnp.concatenate(attended, axis=0) * gate_ref[...]).astype(jnp.bfloat16)
    final = after_ref[...] + dot(gated, w_out[...])
    out_ref[...] = final.astype(jnp.bfloat16).reshape(row_count, res, channels)


def on_whole_complex(
    pair_rep,
    residue_valid,
    tri_norm_gain,
    tri_norm_bias,
    w_edges,
    w_tri_gate,
    out_norm_gain,
    out_norm_bias,
    w_tri_out,
    att_norm_gain,
    att_norm_bias,
    w_query,
    w_key,
    w_value,
    w_att_gate,
    w_pair_bias,
    w_att_out,
):
    row_count, res, channels = pair_rep.shape
    devices = res // row_count
    chips = devices // 2
    half = res // 2
    f32, bf16 = jnp.float32, jnp.bfloat16
    in_vmem = pl.BlockSpec(memory_space=pltpu.VMEM)

    def shaped(dtype, *shape):
        return jax.ShapeDtypeStruct(shape, dtype)

    def call(kernel, outs, operands, aliases=None, scratch=(), cost=2**25):
        return pl.pallas_call(
            kernel,
            out_shape=outs,
            in_specs=[in_vmem] * len(operands),
            out_specs=jax.tree.map(lambda _: in_vmem, outs),
            input_output_aliases=aliases or {},
            scratch_shapes=list(scratch),
            compiler_params=pltpu.CompilerParams(vmem_limit_bytes=24 * 1024 * 1024),
            cost_estimate=pl.CostEstimate(flops=2**20, bytes_accessed=cost, transcendentals=0),
        )(*operands)

    def exchange(values, bit):
        return lax.ppermute(values, "row", [(d, d ^ bit) for d in range(devices)])

    vectors = (
        tri_norm_gain,
        tri_norm_bias,
        out_norm_gain,
        out_norm_bias,
        att_norm_gain,
        att_norm_bias,
    )
    norms = jnp.stack(vectors)
    is_gate = lax.broadcasted_iota(jnp.int32, (1, 5 * channels), 1) // channels
    halves = jnp.where((is_gate == 0) | (is_gate == 2), 1.0, 0.5).astype(bf16)
    edge_weights = jnp.concatenate([w_edges, w_tri_gate], axis=1) * halves
    valid_column = jnp.broadcast_to(residue_valid.astype(f32)[:, None], (res, channels))

    head = lax.broadcasted_iota(jnp.int32, (HEADS, channels), 0)
    head_of_channel = lax.broadcasted_iota(jnp.int32, (HEADS, channels), 1) // HEAD_DIM
    repeat = jnp.where(head == head_of_channel, 1.0, 0.0).astype(bf16)
    wide_bias = dot(w_pair_bias, repeat).astype(bf16)

    kept = lax.dynamic_update_slice(
        jnp.zeros((2 * row_count, res, channels), bf16), pair_rep, (0, 0, 0)
    )
    far = exchange(pair_rep, devices // 2)
    far, kept, norms, edge_weights = lax.optimization_barrier((far, kept, norms, edge_weights))
    own = lax.dynamic_update_slice(kept, far, (row_count, 0, 0))
    own_blocks = (0, chips // 2)

    def blocks_from(bits):
        return tuple(s ^ bits for s in own_blocks)

    tall = shaped(f32, half * res, channels)

    def edges_of(pieces, send_row, *held):
        pairs = tuple(p for p, _ in pieces)
        blocks = tuple(b for _, b in pieces)
        operands = (valid_column, norms, edge_weights) + pairs + held
        first = len(operands) - len(held)
        return call(
            functools.partial(edges_kernel, row_count, chips, blocks, send_row, not held),
            (tall, tall, tall, tall, shaped(bf16, 4 * row_count, res, channels))
            + (() if held else (shaped(bf16, 2 * channels, 2 * channels),)),
            operands,
            {first + e: e for e in range(len(held))},
        )

    diagonal = exchange(own, 6)
    beside = exchange(own, 2)
    near = exchange(own, 4)
    *edges, early_right, same_head = edges_of([(own, own_blocks)], 0)
    diagonal, edges = lax.optimization_barrier((diagonal, edges))
    *edges, early_right = edges_of(
        [(diagonal, blocks_from(3))], 2 * row_count, *edges, early_right
    )
    beside, edges, early_right, wide_bias = lax.optimization_barrier(
        (beside, edges, early_right, wide_bias)
    )
    early = (exchange(early_right, 1), own_blocks + blocks_from(3))
    *edges, late_right = edges_of(
        [(beside, blocks_from(1)), (near, blocks_from(2))], 0, *edges
    )
    late = (exchange(late_right, 1), blocks_from(1) + blocks_from(2))

    left, right, gate, pairs = edges
    triangle, across = call(
        functools.partial(near_triangle_kernel, row_count, chips, half // 2, [early[1]]),
        (tall, tall),
        (left, right, early[0]),
    )
    part = half // 2 * res
    in_part, own_shape = shaped(f32, part, channels), shaped(f32, row_count * res, channels)
    att_part = shaped(bf16, part, channels)
    shared = (norms, w_tri_out, left, gate, pairs)
    scratch = (pltpu.VMEM((part, channels), f32),)
    across, after_a, att_a = call(
        functools.partial(own_inputs_kernel, row_count, chips, late[1]),
        (tall, in_part, att_part),
        shared + (late[0], triangle, across),
        {7: 0},
        scratch=scratch,
    )
    far_att_a = exchange(att_a, 1)
    att_b = call(
        functools.partial(other_inputs_kernel, row_count, chips),
        att_part,
        shared + (triangle, across),
        scratch=scratch,
    )
    far_att_b = exchange(att_b, 1)

    def attention_scratch(keys, projected):
        return (
            pltpu.VMEM((keys * res, channels), f32),
            pltpu.VMEM((projected * res, channels), f32),
            pltpu.VMEM((projected * res, channels), f32),
            pltpu.VMEM((row_count, 40, channels), f32),
            pltpu.VMEM((row_count * keys * res, channels), f32),
        )

    sums, query, att_gate, after_own = call(
        functools.partial(most_attention_kernel, row_count, chips),
        (shaped(f32, row_count, 3, res, channels), own_shape, own_shape, own_shape),
        (valid_column, same_head, w_query, w_att_gate, w_key, w_value, wide_bias)
        + (att_a, att_b, far_att_a, after_a),
        scratch=attention_scratch(3 * half // 2, 3 * half // 2),
    )
    return call(
        functools.partial(attention_kernel, row_count, chips),
        shaped(bf16, *pair_rep.shape),
        (valid_column, same_head, w_key, w_value, w_att_out, wide_bias, far_att_b)
        + (query, att_gate, after_own, sums),
        scratch=attention_scratch(half // 2, half // 2),
    )


def per_device(pair_rep, residue_valid, *parameters):
    row_count, res, channels = pair_rep.shape
    devices = res // row_count
    if res % 48 == 0 and devices == 16 and 40 * res * res * channels <= 32 * 1024 * 1024:
        return on_whole_complex(pair_rep, residue_valid, *parameters)
    return split_over_devices(pair_rep, residue_valid, *parameters)


def solution(mesh):
    return jax.shard_map(
        per_device,
        mesh=mesh,
        in_specs=(
            P(("groups", "row"), None, None),
            P("groups"),
            P(),
            P(),
            P(),
            P(),
            P(),
            P(),
            P(),
            P(),
            P(),
            P(),
            P(),
            P(),
            P(),
            P(),
            P(),
        ),
        out_specs=P(("groups", "row"), None, None),
        check_vma=False,
    )
```

```python
import functools
import math

import jax
import jax.numpy as jnp
from jax import lax
from jax.experimental import pallas as pl
from jax.experimental.pallas import tpu as pltpu
from jax.sharding import PartitionSpec as P

HEADS = 4
HEAD_DIM = 32


def layer_norm(values, norm_gain, norm_bias, along_axis):
    centre = values - jnp.mean(values, axis=along_axis, keepdims=True)
    spread = jnp.mean(centre * centre, axis=along_axis, keepdims=True)
    return centre * lax.rsqrt(spread + 1e-05) * norm_gain + norm_bias


def attend(query_cols, key_cols, value_cols, whole_bias, key_mask):
    factor = 1.0 / math.sqrt(HEAD_DIM)
    scores = (
        jnp.einsum("kjhd,ijhd->jhki", key_cols, query_cols, preferred_element_type=jnp.float32)
        * factor
    )
    scores = scores + whole_bias.astype(jnp.float32)[None] + key_mask[None, None, :, None]
    scores = scores - jnp.max(scores, axis=2, keepdims=True)
    exponent = jnp.exp(scores)
    weights = (exponent / jnp.sum(exponent, axis=2, keepdims=True)).astype(jnp.bfloat16)
    return jnp.einsum("jhki,kjhd->ijhd", weights, value_cols, preferred_element_type=jnp.float32)


def split_over_devices(
    pair_rep,
    residue_valid,
    tri_norm_gain,
    tri_norm_bias,
    w_edges,
    w_tri_gate,
    out_norm_gain,
    out_norm_bias,
    w_tri_out,
    att_norm_gain,
    att_norm_bias,
    w_query,
    w_key,
    w_value,
    w_att_gate,
    w_pair_bias,
    w_att_out,
):
    row_count = pair_rep.shape[0]
    res_count = pair_rep.shape[1]
    channels = pair_rep.shape[2]
    hidden_width = HEADS * HEAD_DIM
    row_start = lax.axis_index("row") * row_count
    valid_flags = residue_valid.astype(jnp.float32)
    own_valid = lax.dynamic_slice_in_dim(valid_flags, row_start, row_count)
    normed = layer_norm(pair_rep.astype(jnp.float32), tri_norm_gain, tri_norm_bias, 2).astype(
        jnp.bfloat16
    )
    projected = jnp.einsum("ikd,de->eik", normed, w_edges, preferred_element_type=jnp.float32)
    projected = projected.reshape(4, channels, row_count, res_count)
    pair_mask = (own_valid[:, None] * valid_flags[None, :])[None, :, :]
    left_edges = (jax.nn.sigmoid(projected[1]) * projected[0] * pair_mask).astype(jnp.bfloat16)
    right_edges = (jax.nn.sigmoid(projected[3]) * projected[2] * pair_mask).astype(jnp.bfloat16)
    left_cols, right_cols = (
        lax.all_to_all(left_edges, "row", split_axis=0, concat_axis=1, tiled=True),
        lax.all_to_all(right_edges, "row", split_axis=0, concat_axis=1, tiled=True),
    )
    block_product = jnp.einsum(
        "cik,cjk->cij", left_cols, right_cols, preferred_element_type=jnp.float32
    ).astype(jnp.bfloat16)
    triangle = lax.all_to_all(block_product, "row", split_axis=1, concat_axis=0, tiled=True)
    tri_normed = layer_norm(
        triangle.astype(jnp.float32), out_norm_gain[:, None, None], out_norm_bias[:, None, None], 0
    ).astype(jnp.bfloat16)
    tri_gate = jax.nn.sigmoid(
        jnp.einsum("ijc,ce->ije", normed, w_tri_gate, preferred_element_type=jnp.float32)
    )
    tri_update = jnp.einsum(
        "cij,ce->ije", tri_normed, w_tri_out, preferred_element_type=jnp.float32
    )
    after_tri = pair_rep.astype(jnp.float32) + tri_gate * tri_update
    att_in = layer_norm(after_tri, att_norm_gain, att_norm_bias, 2).astype(jnp.bfloat16)
    pair_bias = jnp.einsum(
        "kic,ch->hki", att_in, w_pair_bias, preferred_element_type=jnp.float32
    ).astype(jnp.bfloat16)
    whole_bias = lax.all_gather(pair_bias, "row", axis=1, tiled=True)
    key_mask = 1000000000.0 * (valid_flags - 1.0)
    columns = lax.all_to_all(att_in, "row", split_axis=1, concat_axis=0, tiled=True)
    all_weights = jnp.concatenate([w_query, w_key, w_value, w_att_gate], axis=1)
    joined = jnp.dot(columns.reshape(-1, channels), all_weights, preferred_element_type=jnp.float32)
    query_cols = (
        joined[:, :hidden_width].astype(jnp.bfloat16).reshape(res_count, row_count, HEADS, HEAD_DIM)
    )
    key_cols = (
        joined[:, hidden_width : 2 * hidden_width]
        .astype(jnp.bfloat16)
        .reshape(res_count, row_count, HEADS, HEAD_DIM)
    )
    value_cols = (
        joined[:, 2 * hidden_width : 3 * hidden_width]
        .astype(jnp.bfloat16)
        .reshape(res_count, row_count, HEADS, HEAD_DIM)
    )
    gate_cols = jax.nn.sigmoid(joined[:, 3 * hidden_width :]).reshape(
        res_count, row_count, hidden_width
    )
    attended = attend(query_cols, key_cols, value_cols, whole_bias, key_mask)
    gated = (attended.reshape(res_count, row_count, hidden_width) * gate_cols).astype(jnp.bfloat16)
    gated_rows = lax.all_to_all(gated, "row", split_axis=0, concat_axis=1, tiled=True)
    final = after_tri + jnp.einsum(
        "ije,ec->ijc", gated_rows, w_att_out, preferred_element_type=jnp.float32
    )
    return final.astype(jnp.bfloat16)


def sigmoid(values):
    return 0.5 * jnp.tanh(0.5 * values) + 0.5


def row_norm(values, norm_gain, norm_bias):
    count = values.shape[1]
    centre = values - jnp.sum(values, axis=1, keepdims=True) * (1.0 / count)
    squares = jnp.sum(centre * centre, axis=1, keepdims=True)
    return centre * lax.rsqrt(squares + 1e-05 * count) * (norm_gain * count**0.5) + norm_bias


def dot(left, right):
    return jnp.dot(left, right, preferred_element_type=jnp.float32)


def rounded(values):
    return values.astype(jnp.bfloat16).astype(jnp.float32)


def chip_and_core():
    device = lax.axis_index("row")
    return lax.shift_right_logical(device, 1), jnp.bitwise_and(device, 1)


def rows_of_blocks(row_count, blocks):
    chip, _ = chip_and_core()
    return [(jnp.bitwise_xor(chip, bits), r) for bits in blocks for r in range(row_count)]


def edges_kernel(
    row_count, chips, pieces, send_row, makes_heads, valid_column, norms, weights, *refs
):
    pair_refs = refs[: len(pieces)]
    left_ref, right_ref, gate_ref, pairs_ref, send_ref = refs[-5:]
    if makes_heads:
        left_ref, right_ref, gate_ref, pairs_ref, send_ref, same_head_ref = refs[-6:]
        wide = same_head_ref.shape
        row = lax.broadcasted_iota(jnp.int32, wide, 0) // HEAD_DIM
        column = lax.broadcasted_iota(jnp.int32, wide, 1) // HEAD_DIM
        same_head_ref[...] = jnp.where(row == column, 1.0, 0.0).astype(jnp.bfloat16)
    f32, bf16 = jnp.float32, jnp.bfloat16
    res, channels = valid_column.shape
    _, core = chip_and_core()
    pairs = jnp.concatenate(
        [ref[...].astype(f32).reshape(-1, channels) for ref in pair_refs], axis=0
    )
    normed = row_norm(pairs, norms[0:1, :], norms[1:2, :]).astype(bf16)
    column = 0.5 * valid_column[...]
    rows_of = rows_of_blocks(row_count, [bits for piece in pieces for bits in piece])
    masks = jnp.concatenate(
        [
            column * valid_column[pl.ds((2 * chip + core) * row_count + r, 1), :]
            for chip, r in rows_of
        ],
        axis=0,
    )
    joined = dot(normed, weights[:, : 2 * channels])
    left = rounded((jnp.tanh(joined[:, channels:]) + 1.0) * joined[:, :channels] * masks)
    joined = dot(normed, weights[:, 2 * channels : 4 * channels])
    right = ((jnp.tanh(joined[:, channels:]) + 1.0) * joined[:, :channels] * masks).astype(bf16)
    gate = 0.5 * jnp.tanh(dot(normed, weights[:, 4 * channels :])) + 0.5
    for n, (chip, r) in enumerate(rows_of):
        rows = slice(n * res, (n + 1) * res)
        start = pl.multiple_of((chip * row_count + r) * res, res)
        send_ref[send_row + n] = right[rows]
        left_ref[pl.ds(start, res), :] = left[rows]
        place_right(right_ref, chips, chip, r, right[rows])
        gate_ref[pl.ds(start, res), :] = gate[rows]
        pairs_ref[pl.ds(start, res), :] = pairs[rows]


def place_right(right_ref, chips, chip, r, edges):
    res = edges.shape[0]
    start = pl.multiple_of((r * chips + chip) * res, res)
    right_ref[pl.ds(start, res), :] = edges.astype(jnp.float32)


def sum_sublanes(parts):
    row = lax.broadcasted_iota(jnp.int32, parts[0].shape, 0)
    for shift in (1, 2, 4):
        high = jnp.bitwise_and(row, shift) > 0
        parts = [
            jnp.where(high, odd, even) + pltpu.roll(jnp.where(high, even, odd), shift, 0)
            for even, odd in zip(parts[0::2], parts[1::2])
        ]
    return parts[0]


def triangle_rows(
    row_count, chips, left_ref, right_ref, triangle_ref, first, count, core, triangle_first
):
    res = 2 * row_count * chips
    start = pl.multiple_of(first * res, res)
    block = 4
    for n in range(0, count, block):
        lefts = [left_ref[pl.ds(start + m * res, res), :] for m in range(n, n + block)]
        for r in range(row_count):
            parts = [[] for _ in range(block)]
            for chip in range(chips):
                at = (r * chips + chip) * res
                right = right_ref[at : at + res, :]
                for m in range(block):
                    product = lefts[m] * right
                    parts[m].append(
                        sum(product[k : k + 8] for k in range(8, res, 8)) + product[:8]
                    )
            for m in range(block):
                place = (triangle_first + n + m) * res + core * row_count + r
                triangle_ref[pl.ds(place, chips, stride=2 * row_count), :] = rounded(
                    sum_sublanes(parts[m])
                )


def near_triangle_kernel(row_count, chips, chunk, left_ref, right_ref, triangle_ref):
    _, core = chip_and_core()

    def some_rows(step, carry):
        first = step * chunk
        triangle_rows(
            row_count, chips, left_ref, right_ref, triangle_ref, first, chunk, core, first
        )
        return carry

    lax.fori_loop(0, row_count * chips // chunk, some_rows, 0)


def attention_inputs(
    row_count, chips, first, norms, w_out, left_ref, gate_ref, pairs_ref, held_triangle, across_ref,
    triangle_ref,
):
    bf16 = jnp.bfloat16
    _, core = chip_and_core()
    half = row_count * chips
    tall = (half // 2) * 2 * half
    rows = pl.ds(pl.multiple_of(first * 2 * half, tall), tall)
    triangle_ref[...] = held_triangle[rows, :]
    triangle_rows(
        row_count, chips, left_ref, across_ref, triangle_ref, first, half // 2, 1 - core, 0
    )
    tri_normed = row_norm(triangle_ref[...], norms[2:3, :], norms[3:4, :]).astype(bf16)
    after_tri = pairs_ref[rows, :] + gate_ref[rows, :] * dot(tri_normed, w_out[...])
    att_in = row_norm(after_tri, norms[4:5, :], norms[5:6, :]).astype(bf16)
    return after_tri, att_in


def first_chip(chips, part):
    chip, _ = chip_and_core()
    return jnp.bitwise_xor(jnp.bitwise_and(chip, chips // 2), part * (chips // 2))


def own_inputs_kernel(
    row_count,
    chips,
    blocks,
    norms,
    w_out,
    left_ref,
    gate_ref,
    pairs_ref,
    early,
    late,
    triangle_ref,
    across_ref,
    after_ref,
    att_ref,
    scratch_ref,
):
    for received, senders in zip((early, late), blocks):
        for n, (chip, r) in enumerate(rows_of_blocks(row_count, senders)):
            place_right(across_ref, chips, chip, r, received[n])
    first = first_chip(chips, 0) * row_count
    refs = (left_ref, gate_ref, pairs_ref, triangle_ref, across_ref, scratch_ref)
    after_ref[...], att_ref[...] = attention_inputs(
        row_count, chips, first, norms, w_out, *refs
    )


def other_inputs_kernel(row_count, chips, norms, w_out, *refs):
    *refs, att_ref, scratch_ref = refs
    first = first_chip(chips, 1) * row_count
    _, att_ref[...] = attention_inputs(row_count, chips, first, norms, w_out, *refs, scratch_ref)


def keys_and_values(att, w_key, w_value, key_ref, value_ref):
    channels = key_ref.shape[1]
    key_value = jnp.concatenate([w_key[...], w_value[...]], axis=1)
    start = 0
    for values in att:
        rows = slice(start, start + values.shape[0])
        joined = dot(values, key_value)
        key_ref[rows, :] = rounded(joined[:, :channels])
        value_ref[rows, :] = rounded(joined[:, channels:])
        start = rows.stop


def column_bias(row_count, res, att, wide_bias, att_ref, bias_ref):
    start = 0
    for values in att:
        att_ref[start : start + values.shape[0], :] = values.astype(jnp.float32)
        start += values.shape[0]
    keys = start // res
    own = lax.axis_index("row") * row_count
    height = -(-keys // 8) * 8
    columns = []
    for r in range(row_count):
        column = att_ref[pl.ds(own + r, keys, stride=res), :]
        columns.append(jnp.concatenate([column, jnp.zeros((height - keys, column.shape[1]), jnp.float32)]))
    columns = jnp.concatenate(columns, axis=0).astype(jnp.bfloat16)
    bias = rounded(dot(columns, wide_bias[...]))
    for r in range(row_count):
        bias_ref[r, :height, :] = bias[r * height : (r + 1) * height]


def partial_attention(
    row_count, chips, query, parts, bias_ref, same_head, valid_column, sums
):
    bf16 = jnp.bfloat16
    res = 2 * row_count * chips
    channels = valid_column.shape[1]
    count = row_count * chips // 2
    for part, (core, first, key_of, value_of) in enumerate(parts):
        products = []
        for n in range(0, count, 2):
            pair = [jnp.concatenate([key_of(m)] * row_count, axis=0) * query for m in (n, n + 1)]
            products.append(jnp.concatenate([p.astype(bf16) for p in pair], axis=1))
        scores = dot(jnp.concatenate(products, axis=0), same_head[...])

        def score_of(n, r):
            start = (n // 2 * row_count + r) * res
            lanes = slice(n % 2 * channels, (n % 2 + 1) * channels)
            k = (2 * (first + n // row_count) + core) * row_count + n % row_count
            key_mask = 1000000000.0 * (valid_column[pl.ds(k, 1), :] - 1.0)
            at = part * count + n
            shift = (bias_ref[r, at : at + 1, :] + key_mask) * math.log2(math.e)
            return scores[start : start + res, lanes] + shift

        later = []
        for r, (maximum, total, mixed) in enumerate(sums):
            highest = score_of(0, r)
            for n in range(1, count):
                highest = jnp.maximum(highest, score_of(n, r))
            if maximum is None:
                maximum, total, mixed = highest, 0.0, 0.0
            else:
                highest = jnp.maximum(highest, maximum)
                scale = jnp.exp2(maximum - highest)
                maximum, total, mixed = highest, total * scale, mixed * scale
            for n in range(count):
                weight = jnp.exp2(score_of(n, r) - maximum)
                total = total + weight
                mixed = mixed + weight * value_of(n)
            later.append((maximum, total, mixed))
        sums = later
    return sums


def most_attention_kernel(
    row_count,
    chips,
    valid_column,
    same_head,
    w_query,
    w_gate,
    w_key,
    w_value,
    wide_bias,
    own_att_a,
    own_att_b,
    far_att_a,
    own_after,
    sums_ref,
    query_ref,
    gate_ref,
    after_ref,
    att_ref,
    key_ref,
    value_ref,
    bias_ref,
):
    chip, core = chip_and_core()
    res, channels = valid_column.shape
    own = row_count * res
    rows = pl.ds(pl.multiple_of(jnp.bitwise_and(chip, chips // 2 - 1) * own, own), own)
    own_in = own_att_a[rows, :]
    query = rounded(dot(own_in, w_query[...])) * (math.log2(math.e) / math.sqrt(HEAD_DIM))
    att = [ref[...] for ref in (own_att_a, own_att_b, far_att_a)]
    keys_and_values(att, w_key, w_value, key_ref, value_ref)
    column_bias(row_count, res, att, wide_bias, att_ref, bias_ref)
    count = row_count * chips // 2

    def rows_of(ref, first):
        return lambda n: ref[(first + n) * res : (first + n + 1) * res, :]

    a, b = first_chip(chips, 0), first_chip(chips, 1)
    parts = [
        (sender, first, rows_of(key_ref, n * count), rows_of(value_ref, n * count))
        for n, (sender, first) in enumerate(((core, a), (core, b), (1 - core, a)))
    ]
    none = [(None, None, None)] * row_count
    sums = partial_attention(
        row_count, chips, query, parts, bias_ref, same_head, valid_column, none
    )
    for r in range(row_count):
        for n, each in enumerate(sums[r]):
            sums_ref[r, n] = each
    query_ref[...] = query
    gate_ref[...] = sigmoid(dot(own_in, w_gate[...]))
    after_ref[...] = own_after[rows, :]


def attention_kernel(
    row_count,
    chips,
    valid_column,
    same_head,
    w_key,
    w_value,
    w_out,
    wide_bias,
    far_att_b,
    query_ref,
    gate_ref,
    after_ref,
    sums_ref,
    out_ref,
    att_ref,
    key_ref,
    value_ref,
    bias_ref,
):
    _, core = chip_and_core()
    res, channels = valid_column.shape
    far_att = far_att_b[...]
    keys_and_values([far_att], w_key, w_value, key_ref, value_ref)
    column_bias(row_count, res, [far_att], wide_bias, att_ref, bias_ref)

    def rows_of(ref):
        return lambda n: ref[n * res : (n + 1) * res, :]

    parts = ((1 - core, first_chip(chips, 1), rows_of(key_ref), rows_of(value_ref)),)
    sums = [tuple(sums_ref[r, n] for n in range(3)) for r in range(row_count)]
    sums = partial_attention(
        row_count, chips, query_ref[...], parts, bias_ref, same_head, valid_column, sums
    )
    attended = [mixed / total for _, total, mixed in sums]
    gated = (jnp.concatenate(attended, axis=0) * gate_ref[...]).astype(jnp.bfloat16)
    final = after_ref[...] + dot(gated, w_out[...])
    out_ref[...] = final.astype(jnp.bfloat16).reshape(row_count, res, channels)


def on_whole_complex(
    pair_rep,
    residue_valid,
    tri_norm_gain,
    tri_norm_bias,
    w_edges,
    w_tri_gate,
    out_norm_gain,
    out_norm_bias,
    w_tri_out,
    att_norm_gain,
    att_norm_bias,
    w_query,
    w_key,
    w_value,
    w_att_gate,
    w_pair_bias,
    w_att_out,
):
    row_count, res, channels = pair_rep.shape
    devices = res // row_count
    chips = devices // 2
    half = res // 2
    f32, bf16 = jnp.float32, jnp.bfloat16
    in_vmem = pl.BlockSpec(memory_space=pltpu.VMEM)

    def shaped(dtype, *shape):
        return jax.ShapeDtypeStruct(shape, dtype)

    def call(kernel, outs, operands, aliases=None, scratch=(), cost=2**25):
        return pl.pallas_call(
            kernel,
            out_shape=outs,
            in_specs=[in_vmem] * len(operands),
            out_specs=jax.tree.map(lambda _: in_vmem, outs),
            input_output_aliases=aliases or {},
            scratch_shapes=list(scratch),
            compiler_params=pltpu.CompilerParams(vmem_limit_bytes=24 * 1024 * 1024),
            cost_estimate=pl.CostEstimate(flops=2**20, bytes_accessed=cost, transcendentals=0),
        )(*operands)

    def exchange(values, bit):
        return lax.ppermute(values, "row", [(d, d ^ bit) for d in range(devices)])

    vectors = (
        tri_norm_gain,
        tri_norm_bias,
        out_norm_gain,
        out_norm_bias,
        att_norm_gain,
        att_norm_bias,
    )
    norms = jnp.stack(vectors)
    is_gate = lax.broadcasted_iota(jnp.int32, (1, 5 * channels), 1) // channels
    halves = jnp.where((is_gate == 0) | (is_gate == 2), 1.0, 0.5).astype(bf16)
    edge_weights = jnp.concatenate([w_edges, w_tri_gate], axis=1) * halves
    valid_column = jnp.broadcast_to(residue_valid.astype(f32)[:, None], (res, channels))

    head = lax.broadcasted_iota(jnp.int32, (HEADS, channels), 0)
    head_of_channel = lax.broadcasted_iota(jnp.int32, (HEADS, channels), 1) // HEAD_DIM
    repeat = jnp.where(head == head_of_channel, 1.0, 0.0).astype(bf16)
    wide_bias = dot(w_pair_bias, repeat).astype(bf16)

    kept = lax.dynamic_update_slice(
        jnp.zeros((2 * row_count, res, channels), bf16), pair_rep, (0, 0, 0)
    )
    far = exchange(pair_rep, devices // 2)
    far, kept, norms, edge_weights = lax.optimization_barrier((far, kept, norms, edge_weights))
    own = lax.dynamic_update_slice(kept, far, (row_count, 0, 0))
    own_blocks = (0, chips // 2)

    def blocks_from(bits):
        return tuple(s ^ bits for s in own_blocks)

    tall = shaped(f32, half * res, channels)

    def edges_of(pieces, send_row, *held):
        pairs = tuple(p for p, _ in pieces)
        blocks = tuple(b for _, b in pieces)
        sent = (2 if held and send_row == 0 else 6) * row_count
        operands = (valid_column, norms, edge_weights) + pairs + held
        first = len(operands) - len(held)
        return call(
            functools.partial(edges_kernel, row_count, chips, blocks, send_row, not held),
            (tall, tall, tall, tall, shaped(bf16, sent, res, channels))
            + (() if held else (shaped(bf16, 2 * channels, 2 * channels),)),
            operands,
            {first + e: e for e in range(len(held))},
        )

    diagonal = exchange(own, 6)
    beside = exchange(own, 2)
    near = exchange(own, 4)
    *edges, early_right, same_head = edges_of([(own, own_blocks)], 0)
    diagonal, edges = lax.optimization_barrier((diagonal, edges))
    *edges, early_right = edges_of(
        [(diagonal, blocks_from(3))], 2 * row_count, *edges, early_right
    )
    beside, edges, wide_bias = lax.optimization_barrier((beside, edges, wide_bias))
    *edges, early_right = edges_of([(beside, blocks_from(1))], 4 * row_count, *edges, early_right)
    near, edges, early_right = lax.optimization_barrier((near, edges, early_right))
    early = (exchange(early_right, 1), own_blocks + blocks_from(3) + blocks_from(1))
    *edges, late_right = edges_of([(near, blocks_from(2))], 0, *edges)
    late = (exchange(late_right, 1), blocks_from(2))

    left, right, gate, pairs = edges
    triangle = call(
        functools.partial(near_triangle_kernel, row_count, chips, half // 2), tall, (left, right)
    )
    part = half // 2 * res
    in_part, own_shape = shaped(f32, part, channels), shaped(f32, row_count * res, channels)
    att_part = shaped(bf16, part, channels)
    shared = (norms, w_tri_out, left, gate, pairs)
    scratch = (pltpu.VMEM((part, channels), f32),)
    across, after_a, att_a = call(
        functools.partial(own_inputs_kernel, row_count, chips, (early[1], late[1])),
        (tall, in_part, att_part),
        shared + (early[0], late[0], triangle),
        scratch=scratch,
    )
    far_att_a = exchange(att_a, 1)
    att_b = call(
        functools.partial(other_inputs_kernel, row_count, chips),
        att_part,
        shared + (triangle, across),
        scratch=scratch,
    )
    far_att_b = exchange(att_b, 1)

    def attention_scratch(keys, projected):
        return (
            pltpu.VMEM((keys * res, channels), f32),
            pltpu.VMEM((projected * res, channels), f32),
            pltpu.VMEM((projected * res, channels), f32),
            pltpu.VMEM((row_count, 40, channels), f32),
        )

    sums, query, att_gate, after_own = call(
        functools.partial(most_attention_kernel, row_count, chips),
        (shaped(f32, row_count, 3, res, channels), own_shape, own_shape, own_shape),
        (valid_column, same_head, w_query, w_att_gate, w_key, w_value, wide_bias)
        + (att_a, att_b, far_att_a, after_a),
        scratch=attention_scratch(3 * half // 2, 3 * half // 2),
    )
    return call(
        functools.partial(attention_kernel, row_count, chips),
        shaped(bf16, *pair_rep.shape),
        (valid_column, same_head, w_key, w_value, w_att_out, wide_bias, far_att_b)
        + (query, att_gate, after_own, sums),
        scratch=attention_scratch(half // 2, half // 2),
    )


def per_device(pair_rep, residue_valid, *parameters):
    row_count, res, channels = pair_rep.shape
    devices = res // row_count
    if res % 48 == 0 and devices == 16 and 40 * res * res * channels <= 32 * 1024 * 1024:
        return on_whole_complex(pair_rep, residue_valid, *parameters)
    return split_over_devices(pair_rep, residue_valid, *parameters)


def solution(mesh):
    return jax.shard_map(
        per_device,
        mesh=mesh,
        in_specs=(
            P(("groups", "row"), None, None),
            P("groups"),
            P(),
            P(),
            P(),
            P(),
            P(),
            P(),
            P(),
            P(),
            P(),
            P(),
            P(),
            P(),
            P(),
            P(),
            P(),
        ),
        out_specs=P(("groups", "row"), None, None),
        check_vma=False,
    )
```

```python
import functools
import math

import jax
import jax.numpy as jnp
from jax import lax
from jax.experimental import pallas as pl
from jax.experimental.pallas import tpu as pltpu
from jax.sharding import PartitionSpec as P

HEADS = 4
HEAD_DIM = 32


def layer_norm(values, norm_gain, norm_bias, along_axis):
    centre = values - jnp.mean(values, axis=along_axis, keepdims=True)
    spread = jnp.mean(centre * centre, axis=along_axis, keepdims=True)
    return centre * lax.rsqrt(spread + 1e-05) * norm_gain + norm_bias


def attend(query_cols, key_cols, value_cols, whole_bias, key_mask):
    factor = 1.0 / math.sqrt(HEAD_DIM)
    scores = (
        jnp.einsum("kjhd,ijhd->jhki", key_cols, query_cols, preferred_element_type=jnp.float32)
        * factor
    )
    scores = scores + whole_bias.astype(jnp.float32)[None] + key_mask[None, None, :, None]
    scores = scores - jnp.max(scores, axis=2, keepdims=True)
    exponent = jnp.exp(scores)
    weights = (exponent / jnp.sum(exponent, axis=2, keepdims=True)).astype(jnp.bfloat16)
    return jnp.einsum("jhki,kjhd->ijhd", weights, value_cols, preferred_element_type=jnp.float32)


def split_over_devices(
    pair_rep,
    residue_valid,
    tri_norm_gain,
    tri_norm_bias,
    w_edges,
    w_tri_gate,
    out_norm_gain,
    out_norm_bias,
    w_tri_out,
    att_norm_gain,
    att_norm_bias,
    w_query,
    w_key,
    w_value,
    w_att_gate,
    w_pair_bias,
    w_att_out,
):
    row_count = pair_rep.shape[0]
    res_count = pair_rep.shape[1]
    channels = pair_rep.shape[2]
    hidden_width = HEADS * HEAD_DIM
    row_start = lax.axis_index("row") * row_count
    valid_flags = residue_valid.astype(jnp.float32)
    own_valid = lax.dynamic_slice_in_dim(valid_flags, row_start, row_count)
    normed = layer_norm(pair_rep.astype(jnp.float32), tri_norm_gain, tri_norm_bias, 2).astype(
        jnp.bfloat16
    )
    projected = jnp.einsum("ikd,de->eik", normed, w_edges, preferred_element_type=jnp.float32)
    projected = projected.reshape(4, channels, row_count, res_count)
    pair_mask = (own_valid[:, None] * valid_flags[None, :])[None, :, :]
    left_edges = (jax.nn.sigmoid(projected[1]) * projected[0] * pair_mask).astype(jnp.bfloat16)
    right_edges = (jax.nn.sigmoid(projected[3]) * projected[2] * pair_mask).astype(jnp.bfloat16)
    left_cols, right_cols = (
        lax.all_to_all(left_edges, "row", split_axis=0, concat_axis=1, tiled=True),
        lax.all_to_all(right_edges, "row", split_axis=0, concat_axis=1, tiled=True),
    )
    block_product = jnp.einsum(
        "cik,cjk->cij", left_cols, right_cols, preferred_element_type=jnp.float32
    ).astype(jnp.bfloat16)
    triangle = lax.all_to_all(block_product, "row", split_axis=1, concat_axis=0, tiled=True)
    tri_normed = layer_norm(
        triangle.astype(jnp.float32), out_norm_gain[:, None, None], out_norm_bias[:, None, None], 0
    ).astype(jnp.bfloat16)
    tri_gate = jax.nn.sigmoid(
        jnp.einsum("ijc,ce->ije", normed, w_tri_gate, preferred_element_type=jnp.float32)
    )
    tri_update = jnp.einsum(
        "cij,ce->ije", tri_normed, w_tri_out, preferred_element_type=jnp.float32
    )
    after_tri = pair_rep.astype(jnp.float32) + tri_gate * tri_update
    att_in = layer_norm(after_tri, att_norm_gain, att_norm_bias, 2).astype(jnp.bfloat16)
    pair_bias = jnp.einsum(
        "kic,ch->hki", att_in, w_pair_bias, preferred_element_type=jnp.float32
    ).astype(jnp.bfloat16)
    whole_bias = lax.all_gather(pair_bias, "row", axis=1, tiled=True)
    key_mask = 1000000000.0 * (valid_flags - 1.0)
    columns = lax.all_to_all(att_in, "row", split_axis=1, concat_axis=0, tiled=True)
    all_weights = jnp.concatenate([w_query, w_key, w_value, w_att_gate], axis=1)
    joined = jnp.dot(columns.reshape(-1, channels), all_weights, preferred_element_type=jnp.float32)
    query_cols = (
        joined[:, :hidden_width].astype(jnp.bfloat16).reshape(res_count, row_count, HEADS, HEAD_DIM)
    )
    key_cols = (
        joined[:, hidden_width : 2 * hidden_width]
        .astype(jnp.bfloat16)
        .reshape(res_count, row_count, HEADS, HEAD_DIM)
    )
    value_cols = (
        joined[:, 2 * hidden_width : 3 * hidden_width]
        .astype(jnp.bfloat16)
        .reshape(res_count, row_count, HEADS, HEAD_DIM)
    )
    gate_cols = jax.nn.sigmoid(joined[:, 3 * hidden_width :]).reshape(
        res_count, row_count, hidden_width
    )
    attended = attend(query_cols, key_cols, value_cols, whole_bias, key_mask)
    gated = (attended.reshape(res_count, row_count, hidden_width) * gate_cols).astype(jnp.bfloat16)
    gated_rows = lax.all_to_all(gated, "row", split_axis=0, concat_axis=1, tiled=True)
    final = after_tri + jnp.einsum(
        "ije,ec->ijc", gated_rows, w_att_out, preferred_element_type=jnp.float32
    )
    return final.astype(jnp.bfloat16)


def sigmoid(values):
    return 0.5 * jnp.tanh(0.5 * values) + 0.5


def row_norm(values, norm_gain, norm_bias):
    count = values.shape[1]
    centre = values - jnp.sum(values, axis=1, keepdims=True) * (1.0 / count)
    squares = jnp.sum(centre * centre, axis=1, keepdims=True)
    return centre * lax.rsqrt(squares + 1e-05 * count) * (norm_gain * count**0.5) + norm_bias


def dot(left, right):
    return jnp.dot(left, right, preferred_element_type=jnp.float32)


def rounded(values):
    return values.astype(jnp.bfloat16).astype(jnp.float32)


def chip_and_core():
    device = lax.axis_index("row")
    return lax.shift_right_logical(device, 1), jnp.bitwise_and(device, 1)


def rows_of_blocks(row_count, blocks):
    chip, _ = chip_and_core()
    return [(jnp.bitwise_xor(chip, bits), r) for bits in blocks for r in range(row_count)]


def edges_kernel(
    row_count, chips, pieces, send_row, makes_heads, valid_column, norms, weights, *refs
):
    pair_refs = refs[: len(pieces)]
    left_ref, right_ref, gate_ref, pairs_ref, send_ref = refs[-5:]
    if makes_heads:
        left_ref, right_ref, gate_ref, pairs_ref, send_ref, same_head_ref = refs[-6:]
        wide = same_head_ref.shape
        row = lax.broadcasted_iota(jnp.int32, wide, 0) // HEAD_DIM
        column = lax.broadcasted_iota(jnp.int32, wide, 1) // HEAD_DIM
        same_head_ref[...] = jnp.where(row == column, 1.0, 0.0).astype(jnp.bfloat16)
    f32, bf16 = jnp.float32, jnp.bfloat16
    res, channels = valid_column.shape
    _, core = chip_and_core()
    pairs = jnp.concatenate(
        [ref[...].astype(f32).reshape(-1, channels) for ref in pair_refs], axis=0
    )
    normed = row_norm(pairs, norms[0:1, :], norms[1:2, :]).astype(bf16)
    column = 0.5 * valid_column[...]
    rows_of = rows_of_blocks(row_count, [bits for piece in pieces for bits in piece])
    masks = jnp.concatenate(
        [
            column * valid_column[pl.ds((2 * chip + core) * row_count + r, 1), :]
            for chip, r in rows_of
        ],
        axis=0,
    )
    joined = dot(normed, weights[:, : 2 * channels])
    left = ((jnp.tanh(joined[:, channels:]) + 1.0) * joined[:, :channels] * masks).astype(bf16)
    joined = dot(normed, weights[:, 2 * channels : 4 * channels])
    right = ((jnp.tanh(joined[:, channels:]) + 1.0) * joined[:, :channels] * masks).astype(bf16)
    gate = 0.5 * jnp.tanh(dot(normed, weights[:, 4 * channels :])) + 0.5
    for n, (chip, r) in enumerate(rows_of):
        rows = slice(n * res, (n + 1) * res)
        start = pl.multiple_of((chip * row_count + r) * res, res)
        send_ref[send_row + n] = right[rows]
        left_ref[pl.ds(start, res), :] = left[rows]
        place_right(right_ref, chips, chip, r, right[rows])
        gate_ref[pl.ds(start, res), :] = gate[rows]
        pairs_ref[pl.ds(start, res), :] = pairs[rows]


def place_right(right_ref, chips, chip, r, edges):
    res = edges.shape[0]
    start = pl.multiple_of((r * chips + chip) * res, res)
    right_ref[pl.ds(start, res), :] = edges


def sum_sublanes(parts):
    row = lax.broadcasted_iota(jnp.int32, parts[0].shape, 0)
    for shift in (1, 2, 4):
        high = jnp.bitwise_and(row, shift) > 0
        parts = [
            jnp.where(high, odd, even) + pltpu.roll(jnp.where(high, even, odd), shift, 0)
            for even, odd in zip(parts[0::2], parts[1::2])
        ]
    return parts[0]


def triangle_rows(
    row_count, chips, left_ref, right_ref, triangle_ref, first, count, core, triangle_first
):
    res = 2 * row_count * chips
    start = pl.multiple_of(first * res, res)
    block = 4
    for n in range(0, count, block):
        lefts = [left_ref[pl.ds(start + m * res, res), :] for m in range(n, n + block)]
        for r in range(row_count):
            parts = [[] for _ in range(block)]
            for chip in range(chips):
                at = (r * chips + chip) * res
                right = right_ref[at : at + res, :]
                for m in range(block):
                    product = lefts[m] * right
                    third = res // 3
                    some = product[:third] + product[third : 2 * third] + product[2 * third :]
                    some = some.astype(jnp.float32)
                    parts[m].append(sum((some[k : k + 8] for k in range(8, third, 8)), some[:8]))
            for m in range(block):
                place = (triangle_first + n + m) * res + core * row_count + r
                triangle_ref[pl.ds(place, chips, stride=2 * row_count), :] = sum_sublanes(parts[m])


def near_triangle_kernel(row_count, chips, chunk, left_ref, right_ref, triangle_ref):
    _, core = chip_and_core()

    def some_rows(step, carry):
        first = step * chunk
        triangle_rows(
            row_count, chips, left_ref, right_ref, triangle_ref, first, chunk, core, first
        )
        return carry

    lax.fori_loop(0, row_count * chips // chunk, some_rows, 0)


def attention_inputs(
    row_count, chips, first, norms, w_out, left_ref, gate_ref, pairs_ref, held_triangle, across_ref,
    triangle_ref,
):
    bf16 = jnp.bfloat16
    _, core = chip_and_core()
    half = row_count * chips
    tall = (half // 2) * 2 * half
    rows = pl.ds(pl.multiple_of(first * 2 * half, tall), tall)
    triangle_ref[...] = held_triangle[rows, :]
    triangle_rows(
        row_count, chips, left_ref, across_ref, triangle_ref, first, half // 2, 1 - core, 0
    )
    tri_normed = row_norm(triangle_ref[...], norms[2:3, :], norms[3:4, :]).astype(bf16)
    after_tri = pairs_ref[rows, :] + gate_ref[rows, :] * dot(tri_normed, w_out[...])
    att_in = row_norm(after_tri, norms[4:5, :], norms[5:6, :]).astype(bf16)
    return after_tri, att_in


def first_chip(chips, part):
    chip, _ = chip_and_core()
    return jnp.bitwise_xor(jnp.bitwise_and(chip, chips // 2), part * (chips // 2))


def own_inputs_kernel(
    row_count,
    chips,
    blocks,
    norms,
    w_out,
    left_ref,
    gate_ref,
    pairs_ref,
    early,
    late,
    triangle_ref,
    across_ref,
    after_ref,
    att_ref,
    scratch_ref,
):
    for received, senders in zip((early, late), blocks):
        for n, (chip, r) in enumerate(rows_of_blocks(row_count, senders)):
            place_right(across_ref, chips, chip, r, received[n])
    first = first_chip(chips, 0) * row_count
    refs = (left_ref, gate_ref, pairs_ref, triangle_ref, across_ref, scratch_ref)
    after_ref[...], att_ref[...] = attention_inputs(
        row_count, chips, first, norms, w_out, *refs
    )


def other_inputs_kernel(row_count, chips, norms, w_out, *refs):
    *refs, att_ref, scratch_ref = refs
    first = first_chip(chips, 1) * row_count
    _, att_ref[...] = attention_inputs(row_count, chips, first, norms, w_out, *refs, scratch_ref)


def keys_and_values(att, w_key, w_value, key_ref, value_ref):
    channels = key_ref.shape[1]
    key_value = jnp.concatenate([w_key[...], w_value[...]], axis=1)
    start = 0
    for values in att:
        rows = slice(start, start + values.shape[0])
        joined = dot(values, key_value)
        key_ref[rows, :] = rounded(joined[:, :channels])
        value_ref[rows, :] = rounded(joined[:, channels:])
        start = rows.stop


def column_bias(row_count, res, att, wide_bias, att_ref, bias_ref):
    start = 0
    for values in att:
        att_ref[start : start + values.shape[0], :] = values.astype(jnp.float32)
        start += values.shape[0]
    keys = start // res
    own = lax.axis_index("row") * row_count
    height = -(-keys // 8) * 8
    columns = []
    for r in range(row_count):
        column = att_ref[pl.ds(own + r, keys, stride=res), :]
        columns.append(jnp.concatenate([column, jnp.zeros((height - keys, column.shape[1]), jnp.float32)]))
    columns = jnp.concatenate(columns, axis=0).astype(jnp.bfloat16)
    bias = rounded(dot(columns, wide_bias[...]))
    for r in range(row_count):
        bias_ref[r, :height, :] = bias[r * height : (r + 1) * height]


def partial_attention(
    row_count, chips, query, parts, bias_ref, same_head, valid_column, sums
):
    bf16 = jnp.bfloat16
    res = 2 * row_count * chips
    channels = valid_column.shape[1]
    count = row_count * chips // 2
    for part, (core, first, key_of, value_of) in enumerate(parts):
        scores = []
        for r in range(row_count):
            own_query = query[r * res : (r + 1) * res]
            products = [(key_of(n) * own_query).astype(bf16) for n in range(count)]
            pairs = [jnp.concatenate(products[n : n + 2], axis=1) for n in range(0, count, 2)]
            scores.append(dot(jnp.concatenate(pairs, axis=0), same_head[...]))

        def score_of(n, r):
            lanes = slice(n % 2 * channels, (n % 2 + 1) * channels)
            k = (2 * (first + n // row_count) + core) * row_count + n % row_count
            key_mask = 1000000000.0 * (valid_column[pl.ds(k, 1), :] - 1.0)
            at = part * count + n
            shift = (bias_ref[r, at : at + 1, :] + key_mask) * math.log2(math.e)
            return scores[r][n // 2 * res : (n // 2 + 1) * res, lanes] + shift

        later = []
        for r, (maximum, total, mixed) in enumerate(sums):
            highest = score_of(0, r)
            for n in range(1, count):
                highest = jnp.maximum(highest, score_of(n, r))
            if maximum is None:
                maximum, total, mixed = highest, 0.0, 0.0
            else:
                highest = jnp.maximum(highest, maximum)
                scale = jnp.exp2(maximum - highest)
                maximum, total, mixed = highest, total * scale, mixed * scale
            for n in range(count):
                weight = jnp.exp2(score_of(n, r) - maximum)
                total = total + weight
                mixed = mixed + weight * value_of(n)
            later.append((maximum, total, mixed))
        sums = later
    return sums


def most_attention_kernel(
    row_count,
    chips,
    valid_column,
    same_head,
    w_query,
    w_gate,
    w_key,
    w_value,
    wide_bias,
    own_att_a,
    own_att_b,
    far_att_a,
    own_after,
    sums_ref,
    query_ref,
    gate_ref,
    after_ref,
    att_ref,
    key_ref,
    value_ref,
    bias_ref,
):
    chip, core = chip_and_core()
    res, channels = valid_column.shape
    own = row_count * res
    rows = pl.ds(pl.multiple_of(jnp.bitwise_and(chip, chips // 2 - 1) * own, own), own)
    own_in = own_att_a[rows, :]
    query = rounded(dot(own_in, w_query[...])) * (math.log2(math.e) / math.sqrt(HEAD_DIM))
    att = [ref[...] for ref in (own_att_a, own_att_b, far_att_a)]
    keys_and_values(att, w_key, w_value, key_ref, value_ref)
    column_bias(row_count, res, att, wide_bias, att_ref, bias_ref)
    count = row_count * chips // 2

    def rows_of(ref, first):
        return lambda n: ref[(first + n) * res : (first + n + 1) * res, :]

    a, b = first_chip(chips, 0), first_chip(chips, 1)
    parts = [
        (sender, first, rows_of(key_ref, n * count), rows_of(value_ref, n * count))
        for n, (sender, first) in enumerate(((core, a), (core, b), (1 - core, a)))
    ]
    none = [(None, None, None)] * row_count
    sums = partial_attention(
        row_count, chips, query, parts, bias_ref, same_head, valid_column, none
    )
    for r in range(row_count):
        for n, each in enumerate(sums[r]):
            sums_ref[r, n] = each
    query_ref[...] = query
    gate_ref[...] = sigmoid(dot(own_in, w_gate[...]))
    after_ref[...] = own_after[rows, :]


def attention_kernel(
    row_count,
    chips,
    valid_column,
    same_head,
    w_key,
    w_value,
    w_out,
    wide_bias,
    far_att_b,
    query_ref,
    gate_ref,
    after_ref,
    sums_ref,
    out_ref,
    att_ref,
    key_ref,
    value_ref,
    bias_ref,
):
    _, core = chip_and_core()
    res, channels = valid_column.shape
    far_att = far_att_b[...]
    keys_and_values([far_att], w_key, w_value, key_ref, value_ref)
    column_bias(row_count, res, [far_att], wide_bias, att_ref, bias_ref)

    def rows_of(ref):
        return lambda n: ref[n * res : (n + 1) * res, :]

    parts = ((1 - core, first_chip(chips, 1), rows_of(key_ref), rows_of(value_ref)),)
    sums = [tuple(sums_ref[r, n] for n in range(3)) for r in range(row_count)]
    sums = partial_attention(
        row_count, chips, query_ref[...], parts, bias_ref, same_head, valid_column, sums
    )
    attended = [mixed / total for _, total, mixed in sums]
    gated = (jnp.concatenate(attended, axis=0) * gate_ref[...]).astype(jnp.bfloat16)
    final = after_ref[...] + dot(gated, w_out[...])
    out_ref[...] = final.astype(jnp.bfloat16).reshape(row_count, res, channels)


def on_whole_complex(
    pair_rep,
    residue_valid,
    tri_norm_gain,
    tri_norm_bias,
    w_edges,
    w_tri_gate,
    out_norm_gain,
    out_norm_bias,
    w_tri_out,
    att_norm_gain,
    att_norm_bias,
    w_query,
    w_key,
    w_value,
    w_att_gate,
    w_pair_bias,
    w_att_out,
):
    row_count, res, channels = pair_rep.shape
    devices = res // row_count
    chips = devices // 2
    half = res // 2
    f32, bf16 = jnp.float32, jnp.bfloat16
    in_vmem = pl.BlockSpec(memory_space=pltpu.VMEM)

    def shaped(dtype, *shape):
        return jax.ShapeDtypeStruct(shape, dtype)

    def call(kernel, outs, operands, aliases=None, scratch=(), cost=2**25):
        return pl.pallas_call(
            kernel,
            out_shape=outs,
            in_specs=[in_vmem] * len(operands),
            out_specs=jax.tree.map(lambda _: in_vmem, outs),
            input_output_aliases=aliases or {},
            scratch_shapes=list(scratch),
            compiler_params=pltpu.CompilerParams(vmem_limit_bytes=24 * 1024 * 1024),
            cost_estimate=pl.CostEstimate(flops=2**20, bytes_accessed=cost, transcendentals=0),
        )(*operands)

    def exchange(values, bit):
        return lax.ppermute(values, "row", [(d, d ^ bit) for d in range(devices)])

    vectors = (
        tri_norm_gain,
        tri_norm_bias,
        out_norm_gain,
        out_norm_bias,
        att_norm_gain,
        att_norm_bias,
    )
    norms = jnp.stack(vectors)
    is_gate = lax.broadcasted_iota(jnp.int32, (1, 5 * channels), 1) // channels
    halves = jnp.where((is_gate == 0) | (is_gate == 2), 1.0, 0.5).astype(bf16)
    edge_weights = jnp.concatenate([w_edges, w_tri_gate], axis=1) * halves
    valid_column = jnp.broadcast_to(residue_valid.astype(f32)[:, None], (res, channels))

    head = lax.broadcasted_iota(jnp.int32, (HEADS, channels), 0)
    head_of_channel = lax.broadcasted_iota(jnp.int32, (HEADS, channels), 1) // HEAD_DIM
    repeat = jnp.where(head == head_of_channel, 1.0, 0.0).astype(bf16)
    wide_bias = dot(w_pair_bias, repeat).astype(bf16)

    kept = lax.dynamic_update_slice(
        jnp.zeros((2 * row_count, res, channels), bf16), pair_rep, (0, 0, 0)
    )
    far = exchange(pair_rep, devices // 2)
    far, kept, norms, edge_weights = lax.optimization_barrier((far, kept, norms, edge_weights))
    own = lax.dynamic_update_slice(kept, far, (row_count, 0, 0))
    own_blocks = (0, chips // 2)

    def blocks_from(bits):
        return tuple(s ^ bits for s in own_blocks)

    tall = shaped(f32, half * res, channels)
    edge = shaped(bf16, half * res, channels)

    def edges_of(pieces, send_row, *held):
        pairs = tuple(p for p, _ in pieces)
        blocks = tuple(b for _, b in pieces)
        sent = (2 if held and send_row == 0 else 6) * row_count
        operands = (valid_column, norms, edge_weights) + pairs + held
        first = len(operands) - len(held)
        return call(
            functools.partial(edges_kernel, row_count, chips, blocks, send_row, not held),
            (edge, edge, tall, tall, shaped(bf16, sent, res, channels))
            + (() if held else (shaped(bf16, 2 * channels, 2 * channels),)),
            operands,
            {first + e: e for e in range(len(held))},
        )

    diagonal = exchange(own, 6)
    beside = exchange(own, 2)
    near = exchange(own, 4)
    *edges, early_right, same_head = edges_of([(own, own_blocks)], 0)
    diagonal, edges = lax.optimization_barrier((diagonal, edges))
    *edges, early_right = edges_of(
        [(diagonal, blocks_from(3))], 2 * row_count, *edges, early_right
    )
    beside, edges, wide_bias = lax.optimization_barrier((beside, edges, wide_bias))
    *edges, early_right = edges_of([(beside, blocks_from(1))], 4 * row_count, *edges, early_right)
    near, edges, early_right = lax.optimization_barrier((near, edges, early_right))
    early = (exchange(early_right, 1), own_blocks + blocks_from(3) + blocks_from(1))
    *edges, late_right = edges_of([(near, blocks_from(2))], 0, *edges)
    late = (exchange(late_right, 1), blocks_from(2))

    left, right, gate, pairs = edges
    triangle = call(
        functools.partial(near_triangle_kernel, row_count, chips, half // 2), tall, (left, right)
    )
    part = half // 2 * res
    in_part, own_shape = shaped(f32, part, channels), shaped(f32, row_count * res, channels)
    att_part = shaped(bf16, part, channels)
    shared = (norms, w_tri_out, left, gate, pairs)
    scratch = (pltpu.VMEM((part, channels), f32),)
    across, after_a, att_a = call(
        functools.partial(own_inputs_kernel, row_count, chips, (early[1], late[1])),
        (edge, in_part, att_part),
        shared + (early[0], late[0], triangle),
        scratch=scratch,
    )
    far_att_a = exchange(att_a, 1)
    att_b = call(
        functools.partial(other_inputs_kernel, row_count, chips),
        att_part,
        shared + (triangle, across),
        scratch=scratch,
    )
    far_att_b = exchange(att_b, 1)

    def attention_scratch(keys, projected):
        return (
            pltpu.VMEM((keys * res, channels), f32),
            pltpu.VMEM((projected * res, channels), f32),
            pltpu.VMEM((projected * res, channels), f32),
            pltpu.VMEM((row_count, 40, channels), f32),
        )

    sums, query, att_gate, after_own = call(
        functools.partial(most_attention_kernel, row_count, chips),
        (shaped(f32, row_count, 3, res, channels), own_shape, own_shape, own_shape),
        (valid_column, same_head, w_query, w_att_gate, w_key, w_value, wide_bias)
        + (att_a, att_b, far_att_a, after_a),
        scratch=attention_scratch(3 * half // 2, 3 * half // 2),
    )
    return call(
        functools.partial(attention_kernel, row_count, chips),
        shaped(bf16, *pair_rep.shape),
        (valid_column, same_head, w_key, w_value, w_att_out, wide_bias, far_att_b)
        + (query, att_gate, after_own, sums),
        scratch=attention_scratch(half // 2, half // 2),
    )


def per_device(pair_rep, residue_valid, *parameters):
    row_count, res, channels = pair_rep.shape
    devices = res // row_count
    if res % 48 == 0 and devices == 16 and 40 * res * res * channels <= 32 * 1024 * 1024:
        return on_whole_complex(pair_rep, residue_valid, *parameters)
    return split_over_devices(pair_rep, residue_valid, *parameters)


def solution(mesh):
    return jax.shard_map(
        per_device,
        mesh=mesh,
        in_specs=(
            P(("groups", "row"), None, None),
            P("groups"),
            P(),
            P(),
            P(),
            P(),
            P(),
            P(),
            P(),
            P(),
            P(),
            P(),
            P(),
            P(),
            P(),
            P(),
            P(),
        ),
        out_specs=P(("groups", "row"), None, None),
        check_vma=False,
    )
```

```python
import functools
import math

import jax
import jax.numpy as jnp
from jax import lax
from jax.experimental import pallas as pl
from jax.experimental.pallas import tpu as pltpu
from jax.sharding import PartitionSpec as P

HEADS = 4
HEAD_DIM = 32


def layer_norm(values, norm_gain, norm_bias, along_axis):
    centre = values - jnp.mean(values, axis=along_axis, keepdims=True)
    spread = jnp.mean(centre * centre, axis=along_axis, keepdims=True)
    return centre * lax.rsqrt(spread + 1e-05) * norm_gain + norm_bias


def attend(query_cols, key_cols, value_cols, whole_bias, key_mask):
    factor = 1.0 / math.sqrt(HEAD_DIM)
    scores = (
        jnp.einsum("kjhd,ijhd->jhki", key_cols, query_cols, preferred_element_type=jnp.float32)
        * factor
    )
    scores = scores + whole_bias.astype(jnp.float32)[None] + key_mask[None, None, :, None]
    scores = scores - jnp.max(scores, axis=2, keepdims=True)
    exponent = jnp.exp(scores)
    weights = (exponent / jnp.sum(exponent, axis=2, keepdims=True)).astype(jnp.bfloat16)
    return jnp.einsum("jhki,kjhd->ijhd", weights, value_cols, preferred_element_type=jnp.float32)


def split_over_devices(
    pair_rep,
    residue_valid,
    tri_norm_gain,
    tri_norm_bias,
    w_edges,
    w_tri_gate,
    out_norm_gain,
    out_norm_bias,
    w_tri_out,
    att_norm_gain,
    att_norm_bias,
    w_query,
    w_key,
    w_value,
    w_att_gate,
    w_pair_bias,
    w_att_out,
):
    row_count = pair_rep.shape[0]
    res_count = pair_rep.shape[1]
    channels = pair_rep.shape[2]
    hidden_width = HEADS * HEAD_DIM
    row_start = lax.axis_index("row") * row_count
    valid_flags = residue_valid.astype(jnp.float32)
    own_valid = lax.dynamic_slice_in_dim(valid_flags, row_start, row_count)
    normed = layer_norm(pair_rep.astype(jnp.float32), tri_norm_gain, tri_norm_bias, 2).astype(
        jnp.bfloat16
    )
    projected = jnp.einsum("ikd,de->eik", normed, w_edges, preferred_element_type=jnp.float32)
    projected = projected.reshape(4, channels, row_count, res_count)
    pair_mask = (own_valid[:, None] * valid_flags[None, :])[None, :, :]
    left_edges = (jax.nn.sigmoid(projected[1]) * projected[0] * pair_mask).astype(jnp.bfloat16)
    right_edges = (jax.nn.sigmoid(projected[3]) * projected[2] * pair_mask).astype(jnp.bfloat16)
    left_cols, right_cols = (
        lax.all_to_all(left_edges, "row", split_axis=0, concat_axis=1, tiled=True),
        lax.all_to_all(right_edges, "row", split_axis=0, concat_axis=1, tiled=True),
    )
    block_product = jnp.einsum(
        "cik,cjk->cij", left_cols, right_cols, preferred_element_type=jnp.float32
    ).astype(jnp.bfloat16)
    triangle = lax.all_to_all(block_product, "row", split_axis=1, concat_axis=0, tiled=True)
    tri_normed = layer_norm(
        triangle.astype(jnp.float32), out_norm_gain[:, None, None], out_norm_bias[:, None, None], 0
    ).astype(jnp.bfloat16)
    tri_gate = jax.nn.sigmoid(
        jnp.einsum("ijc,ce->ije", normed, w_tri_gate, preferred_element_type=jnp.float32)
    )
    tri_update = jnp.einsum(
        "cij,ce->ije", tri_normed, w_tri_out, preferred_element_type=jnp.float32
    )
    after_tri = pair_rep.astype(jnp.float32) + tri_gate * tri_update
    att_in = layer_norm(after_tri, att_norm_gain, att_norm_bias, 2).astype(jnp.bfloat16)
    pair_bias = jnp.einsum(
        "kic,ch->hki", att_in, w_pair_bias, preferred_element_type=jnp.float32
    ).astype(jnp.bfloat16)
    whole_bias = lax.all_gather(pair_bias, "row", axis=1, tiled=True)
    key_mask = 1000000000.0 * (valid_flags - 1.0)
    columns = lax.all_to_all(att_in, "row", split_axis=1, concat_axis=0, tiled=True)
    all_weights = jnp.concatenate([w_query, w_key, w_value, w_att_gate], axis=1)
    joined = jnp.dot(columns.reshape(-1, channels), all_weights, preferred_element_type=jnp.float32)
    query_cols = (
        joined[:, :hidden_width].astype(jnp.bfloat16).reshape(res_count, row_count, HEADS, HEAD_DIM)
    )
    key_cols = (
        joined[:, hidden_width : 2 * hidden_width]
        .astype(jnp.bfloat16)
        .reshape(res_count, row_count, HEADS, HEAD_DIM)
    )
    value_cols = (
        joined[:, 2 * hidden_width : 3 * hidden_width]
        .astype(jnp.bfloat16)
        .reshape(res_count, row_count, HEADS, HEAD_DIM)
    )
    gate_cols = jax.nn.sigmoid(joined[:, 3 * hidden_width :]).reshape(
        res_count, row_count, hidden_width
    )
    attended = attend(query_cols, key_cols, value_cols, whole_bias, key_mask)
    gated = (attended.reshape(res_count, row_count, hidden_width) * gate_cols).astype(jnp.bfloat16)
    gated_rows = lax.all_to_all(gated, "row", split_axis=0, concat_axis=1, tiled=True)
    final = after_tri + jnp.einsum(
        "ije,ec->ijc", gated_rows, w_att_out, preferred_element_type=jnp.float32
    )
    return final.astype(jnp.bfloat16)


def sigmoid(values):
    return 0.5 * jnp.tanh(0.5 * values) + 0.5


def row_norm(values, norm_gain, norm_bias):
    count = values.shape[1]
    centre = values - jnp.sum(values, axis=1, keepdims=True) * (1.0 / count)
    squares = jnp.sum(centre * centre, axis=1, keepdims=True)
    return centre * lax.rsqrt(squares + 1e-05 * count) * (norm_gain * count**0.5) + norm_bias


def dot(left, right):
    return jnp.dot(left, right, preferred_element_type=jnp.float32)


def rounded(values):
    return values.astype(jnp.bfloat16).astype(jnp.float32)


def chip_and_core():
    device = lax.axis_index("row")
    return lax.shift_right_logical(device, 1), jnp.bitwise_and(device, 1)


def rows_of_blocks(row_count, blocks):
    chip, _ = chip_and_core()
    return [(jnp.bitwise_xor(chip, bits), r) for bits in blocks for r in range(row_count)]


def edges_kernel(
    row_count, chips, pieces, send_row, makes_heads, valid_column, norms, weights, *refs
):
    pair_refs = refs[: len(pieces)]
    left_ref, right_ref, gate_ref, pairs_ref, send_ref = refs[-5:]
    if makes_heads:
        left_ref, right_ref, gate_ref, pairs_ref, send_ref, same_head_ref = refs[-6:]
        wide = same_head_ref.shape
        row = lax.broadcasted_iota(jnp.int32, wide, 0) // HEAD_DIM
        column = lax.broadcasted_iota(jnp.int32, wide, 1) // HEAD_DIM
        same_head_ref[...] = jnp.where(row == column, 1.0, 0.0).astype(jnp.bfloat16)
    f32, bf16 = jnp.float32, jnp.bfloat16
    res, channels = valid_column.shape
    _, core = chip_and_core()
    pairs = jnp.concatenate(
        [ref[...].astype(f32).reshape(-1, channels) for ref in pair_refs], axis=0
    )
    normed = row_norm(pairs, norms[0:1, :], norms[1:2, :]).astype(bf16)
    column = 0.5 * valid_column[...]
    rows_of = rows_of_blocks(row_count, [bits for piece in pieces for bits in piece])
    masks = jnp.concatenate(
        [
            column * valid_column[pl.ds((2 * chip + core) * row_count + r, 1), :]
            for chip, r in rows_of
        ],
        axis=0,
    )
    joined = dot(normed, weights[:, : 2 * channels])
    left = rounded((jnp.tanh(joined[:, channels:]) + 1.0) * joined[:, :channels] * masks)
    joined = dot(normed, weights[:, 2 * channels : 4 * channels])
    right = ((jnp.tanh(joined[:, channels:]) + 1.0) * joined[:, :channels] * masks).astype(bf16)
    gate = 0.5 * jnp.tanh(dot(normed, weights[:, 4 * channels :])) + 0.5
    for n, (chip, r) in enumerate(rows_of):
        rows = slice(n * res, (n + 1) * res)
        start = pl.multiple_of((chip * row_count + r) * res, res)
        send_ref[send_row + n] = right[rows]
        left_ref[pl.ds(start, res), :] = left[rows]
        place_right(right_ref, chips, chip, r, right[rows])
        gate_ref[pl.ds(start, res), :] = gate[rows]
        pairs_ref[pl.ds(start, res), :] = pairs[rows]


def place_right(right_ref, chips, chip, r, edges):
    res = edges.shape[0]
    start = pl.multiple_of((r * chips + chip) * res, res)
    right_ref[pl.ds(start, res), :] = edges.astype(jnp.float32)


def join(even, odd, shift):
    high = jnp.bitwise_and(lax.broadcasted_iota(jnp.int32, even.shape, 0), shift) > 0
    return jnp.where(high, odd, even) + pltpu.roll(jnp.where(high, even, odd), shift, 0)


def triangle_rows(
    row_count, chips, left_ref, right_ref, triangle_ref, first, count, core, triangle_first
):
    res = 2 * row_count * chips
    start = pl.multiple_of(first * res, res)
    block = 4
    for n in range(0, count, block):
        lefts = [left_ref[pl.ds(start + m * res, res), :] for m in range(n, n + block)]
        for r in range(row_count):
            sums = [[] for _ in range(block)]
            for chip in range(chips):
                at = (r * chips + chip) * res
                right = right_ref[at : at + res, :]
                for m in range(block):
                    product = lefts[m] * right
                    part = sum((product[k : k + 8] for k in range(8, res, 8)), product[:8])
                    shift = 1
                    while chip & shift:
                        part = join(sums[m].pop(), part, shift)
                        shift *= 2
                    sums[m].append(part)
            for m in range(block):
                place = (triangle_first + n + m) * res + core * row_count + r
                triangle_ref[pl.ds(place, chips, stride=2 * row_count), :] = rounded(sums[m][0])


def near_triangle_kernel(row_count, chips, chunk, left_ref, right_ref, triangle_ref):
    _, core = chip_and_core()

    def some_rows(step, carry):
        first = step * chunk
        triangle_rows(
            row_count, chips, left_ref, right_ref, triangle_ref, first, chunk, core, first
        )
        return carry

    lax.fori_loop(0, row_count * chips // chunk, some_rows, 0)


def attention_inputs(
    row_count, chips, first, norms, w_out, left_ref, gate_ref, pairs_ref, held_triangle, across_ref,
    triangle_ref,
):
    bf16 = jnp.bfloat16
    _, core = chip_and_core()
    half = row_count * chips
    tall = (half // 2) * 2 * half
    rows = pl.ds(pl.multiple_of(first * 2 * half, tall), tall)
    triangle_ref[...] = held_triangle[rows, :]
    triangle_rows(
        row_count, chips, left_ref, across_ref, triangle_ref, first, half // 2, 1 - core, 0
    )
    tri_normed = row_norm(triangle_ref[...], norms[2:3, :], norms[3:4, :]).astype(bf16)
    after_tri = pairs_ref[rows, :] + gate_ref[rows, :] * dot(tri_normed, w_out[...])
    att_in = row_norm(after_tri, norms[4:5, :], norms[5:6, :]).astype(bf16)
    return after_tri, att_in


def first_chip(chips, part):
    chip, _ = chip_and_core()
    return jnp.bitwise_xor(jnp.bitwise_and(chip, chips // 2), part * (chips // 2))


def own_inputs_kernel(
    row_count,
    chips,
    blocks,
    norms,
    w_out,
    left_ref,
    gate_ref,
    pairs_ref,
    early,
    late,
    triangle_ref,
    across_ref,
    after_ref,
    att_ref,
    scratch_ref,
):
    for received, senders in zip((early, late), blocks):
        for n, (chip, r) in enumerate(rows_of_blocks(row_count, senders)):
            place_right(across_ref, chips, chip, r, received[n])
    first = first_chip(chips, 0) * row_count
    refs = (left_ref, gate_ref, pairs_ref, triangle_ref, across_ref, scratch_ref)
    after_ref[...], att_ref[...] = attention_inputs(
        row_count, chips, first, norms, w_out, *refs
    )


def other_inputs_kernel(row_count, chips, norms, w_out, *refs):
    *refs, att_ref, scratch_ref = refs
    first = first_chip(chips, 1) * row_count
    _, att_ref[...] = attention_inputs(row_count, chips, first, norms, w_out, *refs, scratch_ref)


def keys_and_values(att, w_key, w_value, key_ref, value_ref):
    channels = key_ref.shape[1]
    key_value = jnp.concatenate([w_key[...], w_value[...]], axis=1)
    start = 0
    for values in att:
        rows = slice(start, start + values.shape[0])
        joined = dot(values, key_value)
        key_ref[rows, :] = rounded(joined[:, :channels])
        value_ref[rows, :] = rounded(joined[:, channels:])
        start = rows.stop


def column_bias(row_count, res, att, wide_bias, att_ref, bias_ref):
    start = 0
    for values in att:
        att_ref[start : start + values.shape[0], :] = values.astype(jnp.float32)
        start += values.shape[0]
    keys = start // res
    own = lax.axis_index("row") * row_count
    height = -(-keys // 8) * 8
    columns = []
    for r in range(row_count):
        column = att_ref[pl.ds(own + r, keys, stride=res), :]
        columns.append(jnp.concatenate([column, jnp.zeros((height - keys, column.shape[1]), jnp.float32)]))
    columns = jnp.concatenate(columns, axis=0).astype(jnp.bfloat16)
    bias = rounded(dot(columns, wide_bias[...]))
    for r in range(row_count):
        bias_ref[r, :height, :] = bias[r * height : (r + 1) * height]


def partial_attention(
    row_count, chips, query, parts, bias_ref, same_head, valid_column, sums
):
    bf16 = jnp.bfloat16
    res = 2 * row_count * chips
    channels = valid_column.shape[1]
    count = row_count * chips // 2
    for part, (core, first, key_of, value_of) in enumerate(parts):
        scores = []
        for r in range(row_count):
            own_query = query[r * res : (r + 1) * res]
            products = [(key_of(n) * own_query).astype(bf16) for n in range(count)]
            pairs = [jnp.concatenate(products[n : n + 2], axis=1) for n in range(0, count, 2)]
            scores.append(dot(jnp.concatenate(pairs, axis=0), same_head[...]))

        def score_of(n, r):
            lanes = slice(n % 2 * channels, (n % 2 + 1) * channels)
            k = (2 * (first + n // row_count) + core) * row_count + n % row_count
            key_mask = 1000000000.0 * (valid_column[pl.ds(k, 1), :] - 1.0)
            at = part * count + n
            shift = (bias_ref[r, at : at + 1, :] + key_mask) * math.log2(math.e)
            return scores[r][n // 2 * res : (n // 2 + 1) * res, lanes] + shift

        later = []
        for r, (maximum, total, mixed) in enumerate(sums):
            highest = score_of(0, r)
            for n in range(1, count):
                highest = jnp.maximum(highest, score_of(n, r))
            if maximum is None:
                maximum, total, mixed = highest, 0.0, 0.0
            else:
                highest = jnp.maximum(highest, maximum)
                scale = jnp.exp2(maximum - highest)
                maximum, total, mixed = highest, total * scale, mixed * scale
            for n in range(count):
                weight = jnp.exp2(score_of(n, r) - maximum)
                total = total + weight
                mixed = mixed + weight * value_of(n)
            later.append((maximum, total, mixed))
        sums = later
    return sums


def most_attention_kernel(
    row_count,
    chips,
    valid_column,
    same_head,
    w_query,
    w_gate,
    w_key,
    w_value,
    wide_bias,
    own_att_a,
    own_att_b,
    far_att_a,
    own_after,
    sums_ref,
    query_ref,
    gate_ref,
    after_ref,
    att_ref,
    key_ref,
    value_ref,
    bias_ref,
):
    chip, core = chip_and_core()
    res, channels = valid_column.shape
    own = row_count * res
    rows = pl.ds(pl.multiple_of(jnp.bitwise_and(chip, chips // 2 - 1) * own, own), own)
    own_in = own_att_a[rows, :]
    query = rounded(dot(own_in, w_query[...])) * (math.log2(math.e) / math.sqrt(HEAD_DIM))
    att = [ref[...] for ref in (own_att_a, own_att_b, far_att_a)]
    keys_and_values(att, w_key, w_value, key_ref, value_ref)
    column_bias(row_count, res, att, wide_bias, att_ref, bias_ref)
    count = row_count * chips // 2

    def rows_of(ref, first):
        return lambda n: ref[(first + n) * res : (first + n + 1) * res, :]

    a, b = first_chip(chips, 0), first_chip(chips, 1)
    parts = [
        (sender, first, rows_of(key_ref, n * count), rows_of(value_ref, n * count))
        for n, (sender, first) in enumerate(((core, a), (core, b), (1 - core, a)))
    ]
    none = [(None, None, None)] * row_count
    sums = partial_attention(
        row_count, chips, query, parts, bias_ref, same_head, valid_column, none
    )
    for r in range(row_count):
        for n, each in enumerate(sums[r]):
            sums_ref[r, n] = each
    query_ref[...] = query
    gate_ref[...] = sigmoid(dot(own_in, w_gate[...]))
    after_ref[...] = own_after[rows, :]


def attention_kernel(
    row_count,
    chips,
    valid_column,
    same_head,
    w_key,
    w_value,
    w_out,
    wide_bias,
    far_att_b,
    query_ref,
    gate_ref,
    after_ref,
    sums_ref,
    out_ref,
    att_ref,
    key_ref,
    value_ref,
    bias_ref,
):
    _, core = chip_and_core()
    res, channels = valid_column.shape
    far_att = far_att_b[...]
    keys_and_values([far_att], w_key, w_value, key_ref, value_ref)
    column_bias(row_count, res, [far_att], wide_bias, att_ref, bias_ref)

    def rows_of(ref):
        return lambda n: ref[n * res : (n + 1) * res, :]

    parts = ((1 - core, first_chip(chips, 1), rows_of(key_ref), rows_of(value_ref)),)
    sums = [tuple(sums_ref[r, n] for n in range(3)) for r in range(row_count)]
    sums = partial_attention(
        row_count, chips, query_ref[...], parts, bias_ref, same_head, valid_column, sums
    )
    attended = [mixed / total for _, total, mixed in sums]
    gated = (jnp.concatenate(attended, axis=0) * gate_ref[...]).astype(jnp.bfloat16)
    final = after_ref[...] + dot(gated, w_out[...])
    out_ref[...] = final.astype(jnp.bfloat16).reshape(row_count, res, channels)


def on_whole_complex(
    pair_rep,
    residue_valid,
    tri_norm_gain,
    tri_norm_bias,
    w_edges,
    w_tri_gate,
    out_norm_gain,
    out_norm_bias,
    w_tri_out,
    att_norm_gain,
    att_norm_bias,
    w_query,
    w_key,
    w_value,
    w_att_gate,
    w_pair_bias,
    w_att_out,
):
    row_count, res, channels = pair_rep.shape
    devices = res // row_count
    chips = devices // 2
    half = res // 2
    f32, bf16 = jnp.float32, jnp.bfloat16
    in_vmem = pl.BlockSpec(memory_space=pltpu.VMEM)

    def shaped(dtype, *shape):
        return jax.ShapeDtypeStruct(shape, dtype)

    def call(kernel, outs, operands, aliases=None, scratch=(), cost=2**25):
        return pl.pallas_call(
            kernel,
            out_shape=outs,
            in_specs=[in_vmem] * len(operands),
            out_specs=jax.tree.map(lambda _: in_vmem, outs),
            input_output_aliases=aliases or {},
            scratch_shapes=list(scratch),
            compiler_params=pltpu.CompilerParams(vmem_limit_bytes=24 * 1024 * 1024),
            cost_estimate=pl.CostEstimate(flops=2**20, bytes_accessed=cost, transcendentals=0),
        )(*operands)

    def exchange(values, bit):
        return lax.ppermute(values, "row", [(d, d ^ bit) for d in range(devices)])

    vectors = (
        tri_norm_gain,
        tri_norm_bias,
        out_norm_gain,
        out_norm_bias,
        att_norm_gain,
        att_norm_bias,
    )
    norms = jnp.stack(vectors)
    is_gate = lax.broadcasted_iota(jnp.int32, (1, 5 * channels), 1) // channels
    halves = jnp.where((is_gate == 0) | (is_gate == 2), 1.0, 0.5).astype(bf16)
    edge_weights = jnp.concatenate([w_edges, w_tri_gate], axis=1) * halves
    valid_column = jnp.broadcast_to(residue_valid.astype(f32)[:, None], (res, channels))

    head = lax.broadcasted_iota(jnp.int32, (HEADS, channels), 0)
    head_of_channel = lax.broadcasted_iota(jnp.int32, (HEADS, channels), 1) // HEAD_DIM
    repeat = jnp.where(head == head_of_channel, 1.0, 0.0).astype(bf16)
    wide_bias = dot(w_pair_bias, repeat).astype(bf16)

    kept = lax.dynamic_update_slice(
        jnp.zeros((2 * row_count, res, channels), bf16), pair_rep, (0, 0, 0)
    )
    far = exchange(pair_rep, devices // 2)
    far, kept, norms, edge_weights = lax.optimization_barrier((far, kept, norms, edge_weights))
    own = lax.dynamic_update_slice(kept, far, (row_count, 0, 0))
    own_blocks = (0, chips // 2)

    def blocks_from(bits):
        return tuple(s ^ bits for s in own_blocks)

    tall = shaped(f32, half * res, channels)

    def edges_of(pieces, send_row, *held):
        pairs = tuple(p for p, _ in pieces)
        blocks = tuple(b for _, b in pieces)
        sent = (2 if held and send_row == 0 else 6) * row_count
        operands = (valid_column, norms, edge_weights) + pairs + held
        first = len(operands) - len(held)
        return call(
            functools.partial(edges_kernel, row_count, chips, blocks, send_row, not held),
            (tall, tall, tall, tall, shaped(bf16, sent, res, channels))
            + (() if held else (shaped(bf16, 2 * channels, 2 * channels),)),
            operands,
            {first + e: e for e in range(len(held))},
        )

    diagonal = exchange(own, 6)
    beside = exchange(own, 2)
    near = exchange(own, 4)
    *edges, early_right, same_head = edges_of([(own, own_blocks)], 0)
    diagonal, edges = lax.optimization_barrier((diagonal, edges))
    *edges, early_right = edges_of(
        [(diagonal, blocks_from(3))], 2 * row_count, *edges, early_right
    )
    beside, edges, wide_bias = lax.optimization_barrier((beside, edges, wide_bias))
    *edges, early_right = edges_of([(beside, blocks_from(1))], 4 * row_count, *edges, early_right)
    near, edges, early_right = lax.optimization_barrier((near, edges, early_right))
    early = (exchange(early_right, 1), own_blocks + blocks_from(3) + blocks_from(1))
    *edges, late_right = edges_of([(near, blocks_from(2))], 0, *edges)
    late = (exchange(late_right, 1), blocks_from(2))

    left, right, gate, pairs = edges
    triangle = call(
        functools.partial(near_triangle_kernel, row_count, chips, half // 2), tall, (left, right)
    )
    part = half // 2 * res
    in_part, own_shape = shaped(f32, part, channels), shaped(f32, row_count * res, channels)
    att_part = shaped(bf16, part, channels)
    shared = (norms, w_tri_out, left, gate, pairs)
    scratch = (pltpu.VMEM((part, channels), f32),)
    across, after_a, att_a = call(
        functools.partial(own_inputs_kernel, row_count, chips, (early[1], late[1])),
        (tall, in_part, att_part),
        shared + (early[0], late[0], triangle),
        scratch=scratch,
    )
    far_att_a = exchange(att_a, 1)
    att_b = call(
        functools.partial(other_inputs_kernel, row_count, chips),
        att_part,
        shared + (triangle, across),
        scratch=scratch,
    )
    far_att_b = exchange(att_b, 1)

    def attention_scratch(keys, projected):
        return (
            pltpu.VMEM((keys * res, channels), f32),
            pltpu.VMEM((projected * res, channels), f32),
            pltpu.VMEM((projected * res, channels), f32),
            pltpu.VMEM((row_count, 40, channels), f32),
        )

    sums, query, att_gate, after_own = call(
        functools.partial(most_attention_kernel, row_count, chips),
        (shaped(f32, row_count, 3, res, channels), own_shape, own_shape, own_shape),
        (valid_column, same_head, w_query, w_att_gate, w_key, w_value, wide_bias)
        + (att_a, att_b, far_att_a, after_a),
        scratch=attention_scratch(3 * half // 2, 3 * half // 2),
    )
    return call(
        functools.partial(attention_kernel, row_count, chips),
        shaped(bf16, *pair_rep.shape),
        (valid_column, same_head, w_key, w_value, w_att_out, wide_bias, far_att_b)
        + (query, att_gate, after_own, sums),
        scratch=attention_scratch(half // 2, half // 2),
    )


def per_device(pair_rep, residue_valid, *parameters):
    row_count, res, channels = pair_rep.shape
    devices = res // row_count
    if res % 48 == 0 and devices == 16 and 40 * res * res * channels <= 32 * 1024 * 1024:
        return on_whole_complex(pair_rep, residue_valid, *parameters)
    return split_over_devices(pair_rep, residue_valid, *parameters)


def solution(mesh):
    return jax.shard_map(
        per_device,
        mesh=mesh,
        in_specs=(
            P(("groups", "row"), None, None),
            P("groups"),
            P(),
            P(),
            P(),
            P(),
            P(),
            P(),
            P(),
            P(),
            P(),
            P(),
            P(),
            P(),
            P(),
            P(),
            P(),
        ),
        out_specs=P(("groups", "row"), None, None),
        check_vma=False,
    )
```

```python
import functools
import math

import jax
import jax.numpy as jnp
from jax import lax
from jax.experimental import pallas as pl
from jax.experimental.pallas import tpu as pltpu
from jax.sharding import PartitionSpec as P

HEADS = 4
HEAD_DIM = 32


def layer_norm(values, norm_gain, norm_bias, along_axis):
    centre = values - jnp.mean(values, axis=along_axis, keepdims=True)
    spread = jnp.mean(centre * centre, axis=along_axis, keepdims=True)
    return centre * lax.rsqrt(spread + 1e-05) * norm_gain + norm_bias


def attend(query_cols, key_cols, value_cols, whole_bias, key_mask):
    factor = 1.0 / math.sqrt(HEAD_DIM)
    scores = (
        jnp.einsum("kjhd,ijhd->jhki", key_cols, query_cols, preferred_element_type=jnp.float32)
        * factor
    )
    scores = scores + whole_bias.astype(jnp.float32)[None] + key_mask[None, None, :, None]
    scores = scores - jnp.max(scores, axis=2, keepdims=True)
    exponent = jnp.exp(scores)
    weights = (exponent / jnp.sum(exponent, axis=2, keepdims=True)).astype(jnp.bfloat16)
    return jnp.einsum("jhki,kjhd->ijhd", weights, value_cols, preferred_element_type=jnp.float32)


def split_over_devices(
    pair_rep,
    residue_valid,
    tri_norm_gain,
    tri_norm_bias,
    w_edges,
    w_tri_gate,
    out_norm_gain,
    out_norm_bias,
    w_tri_out,
    att_norm_gain,
    att_norm_bias,
    w_query,
    w_key,
    w_value,
    w_att_gate,
    w_pair_bias,
    w_att_out,
):
    row_count = pair_rep.shape[0]
    res_count = pair_rep.shape[1]
    channels = pair_rep.shape[2]
    hidden_width = HEADS * HEAD_DIM
    row_start = lax.axis_index("row") * row_count
    valid_flags = residue_valid.astype(jnp.float32)
    own_valid = lax.dynamic_slice_in_dim(valid_flags, row_start, row_count)
    normed = layer_norm(pair_rep.astype(jnp.float32), tri_norm_gain, tri_norm_bias, 2).astype(
        jnp.bfloat16
    )
    projected = jnp.einsum("ikd,de->eik", normed, w_edges, preferred_element_type=jnp.float32)
    projected = projected.reshape(4, channels, row_count, res_count)
    pair_mask = (own_valid[:, None] * valid_flags[None, :])[None, :, :]
    left_edges = (jax.nn.sigmoid(projected[1]) * projected[0] * pair_mask).astype(jnp.bfloat16)
    right_edges = (jax.nn.sigmoid(projected[3]) * projected[2] * pair_mask).astype(jnp.bfloat16)
    left_cols, right_cols = (
        lax.all_to_all(left_edges, "row", split_axis=0, concat_axis=1, tiled=True),
        lax.all_to_all(right_edges, "row", split_axis=0, concat_axis=1, tiled=True),
    )
    block_product = jnp.einsum(
        "cik,cjk->cij", left_cols, right_cols, preferred_element_type=jnp.float32
    ).astype(jnp.bfloat16)
    triangle = lax.all_to_all(block_product, "row", split_axis=1, concat_axis=0, tiled=True)
    tri_normed = layer_norm(
        triangle.astype(jnp.float32), out_norm_gain[:, None, None], out_norm_bias[:, None, None], 0
    ).astype(jnp.bfloat16)
    tri_gate = jax.nn.sigmoid(
        jnp.einsum("ijc,ce->ije", normed, w_tri_gate, preferred_element_type=jnp.float32)
    )
    tri_update = jnp.einsum(
        "cij,ce->ije", tri_normed, w_tri_out, preferred_element_type=jnp.float32
    )
    after_tri = pair_rep.astype(jnp.float32) + tri_gate * tri_update
    att_in = layer_norm(after_tri, att_norm_gain, att_norm_bias, 2).astype(jnp.bfloat16)
    pair_bias = jnp.einsum(
        "kic,ch->hki", att_in, w_pair_bias, preferred_element_type=jnp.float32
    ).astype(jnp.bfloat16)
    whole_bias = lax.all_gather(pair_bias, "row", axis=1, tiled=True)
    key_mask = 1000000000.0 * (valid_flags - 1.0)
    columns = lax.all_to_all(att_in, "row", split_axis=1, concat_axis=0, tiled=True)
    all_weights = jnp.concatenate([w_query, w_key, w_value, w_att_gate], axis=1)
    joined = jnp.dot(columns.reshape(-1, channels), all_weights, preferred_element_type=jnp.float32)
    query_cols = (
        joined[:, :hidden_width].astype(jnp.bfloat16).reshape(res_count, row_count, HEADS, HEAD_DIM)
    )
    key_cols = (
        joined[:, hidden_width : 2 * hidden_width]
        .astype(jnp.bfloat16)
        .reshape(res_count, row_count, HEADS, HEAD_DIM)
    )
    value_cols = (
        joined[:, 2 * hidden_width : 3 * hidden_width]
        .astype(jnp.bfloat16)
        .reshape(res_count, row_count, HEADS, HEAD_DIM)
    )
    gate_cols = jax.nn.sigmoid(joined[:, 3 * hidden_width :]).reshape(
        res_count, row_count, hidden_width
    )
    attended = attend(query_cols, key_cols, value_cols, whole_bias, key_mask)
    gated = (attended.reshape(res_count, row_count, hidden_width) * gate_cols).astype(jnp.bfloat16)
    gated_rows = lax.all_to_all(gated, "row", split_axis=0, concat_axis=1, tiled=True)
    final = after_tri + jnp.einsum(
        "ije,ec->ijc", gated_rows, w_att_out, preferred_element_type=jnp.float32
    )
    return final.astype(jnp.bfloat16)


def sigmoid(values):
    return 0.5 * jnp.tanh(0.5 * values) + 0.5


def row_norm(values, norm_gain, norm_bias):
    count = values.shape[1]
    centre = values - jnp.sum(values, axis=1, keepdims=True) * (1.0 / count)
    squares = jnp.sum(centre * centre, axis=1, keepdims=True)
    return centre * lax.rsqrt(squares + 1e-05 * count) * (norm_gain * count**0.5) + norm_bias


def dot(left, right):
    return jnp.dot(left, right, preferred_element_type=jnp.float32)


def rounded(values):
    return values.astype(jnp.bfloat16).astype(jnp.float32)


def chip_and_core():
    device = lax.axis_index("row")
    return lax.shift_right_logical(device, 1), jnp.bitwise_and(device, 1)


def rows_of_blocks(row_count, blocks):
    chip, _ = chip_and_core()
    return [(jnp.bitwise_xor(chip, bits), r) for bits in blocks for r in range(row_count)]


def edges_kernel(
    row_count, chips, pieces, send_row, makes_heads, valid_column, norms, weights, *refs
):
    pair_refs = refs[: len(pieces)]
    left_ref, right_ref, gate_ref, pairs_ref, send_ref = refs[-5:]
    if makes_heads:
        left_ref, right_ref, gate_ref, pairs_ref, send_ref, same_head_ref = refs[-6:]
        wide = same_head_ref.shape
        row = lax.broadcasted_iota(jnp.int32, wide, 0) // HEAD_DIM
        column = lax.broadcasted_iota(jnp.int32, wide, 1) // HEAD_DIM
        same_head_ref[...] = jnp.where(row == column, 1.0, 0.0).astype(jnp.bfloat16)
    f32, bf16 = jnp.float32, jnp.bfloat16
    res, channels = valid_column.shape
    _, core = chip_and_core()
    pairs = jnp.concatenate(
        [ref[...].astype(f32).reshape(-1, channels) for ref in pair_refs], axis=0
    )
    normed = row_norm(pairs, norms[0:1, :], norms[1:2, :]).astype(bf16)
    column = 0.5 * valid_column[...]
    rows_of = rows_of_blocks(row_count, [bits for piece in pieces for bits in piece])
    masks = jnp.concatenate(
        [
            column * valid_column[pl.ds((2 * chip + core) * row_count + r, 1), :]
            for chip, r in rows_of
        ],
        axis=0,
    )
    joined = dot(normed, weights[:, : 2 * channels])
    left = rounded((jnp.tanh(joined[:, channels:]) + 1.0) * joined[:, :channels] * masks)
    joined = dot(normed, weights[:, 2 * channels : 4 * channels])
    right = ((jnp.tanh(joined[:, channels:]) + 1.0) * joined[:, :channels] * masks).astype(bf16)
    gate = 0.5 * jnp.tanh(dot(normed, weights[:, 4 * channels :])) + 0.5
    for n, (chip, r) in enumerate(rows_of):
        rows = slice(n * res, (n + 1) * res)
        start = pl.multiple_of((chip * row_count + r) * res, res)
        send_ref[send_row + n] = right[rows]
        left_ref[pl.ds(start, res), :] = left[rows]
        place_right(right_ref, chips, chip, r, right[rows])
        gate_ref[pl.ds(start, res), :] = gate[rows]
        pairs_ref[pl.ds(start, res), :] = pairs[rows]


def place_right(right_ref, chips, chip, r, edges):
    res = edges.shape[0]
    start = pl.multiple_of((r * chips + chip) * res, res)
    right_ref[pl.ds(start, res), :] = edges.astype(jnp.float32)


def join(even, odd, shift):
    high = jnp.bitwise_and(lax.broadcasted_iota(jnp.int32, even.shape, 0), shift) > 0
    return jnp.where(high, odd, even) + pltpu.roll(jnp.where(high, even, odd), shift, 0)


def triangle_rows(
    row_count, chips, left_ref, right_ref, triangle_ref, first, count, core, triangle_first
):
    res = 2 * row_count * chips
    start = pl.multiple_of(first * res, res)
    block = 4
    for n in range(0, count, block):
        lefts = [left_ref[pl.ds(start + m * res, res), :] for m in range(n, n + block)]
        for r in range(row_count):
            sums = [[] for _ in range(block)]
            for chip in range(chips):
                at = (r * chips + chip) * res
                right = right_ref[at : at + res, :]
                for m in range(block):
                    product = lefts[m] * right
                    part = sum((product[k : k + 8] for k in range(8, res, 8)), product[:8])
                    shift = 1
                    while chip & shift:
                        part = join(sums[m].pop(), part, shift)
                        shift *= 2
                    sums[m].append(part)
            for m in range(block):
                place = (triangle_first + n + m) * res + core * row_count + r
                triangle_ref[pl.ds(place, chips, stride=2 * row_count), :] = rounded(sums[m][0])


def near_triangle_kernel(row_count, chips, chunk, pieces, left_ref, right_ref, *refs):
    received, (triangle_ref, across_ref) = refs[:-2], refs[-2:]
    _, core = chip_and_core()

    def some_rows(step, carry):
        first = step * chunk
        triangle_rows(
            row_count, chips, left_ref, right_ref, triangle_ref, first, chunk, core, first
        )
        return carry

    for ref, blocks in zip(received, pieces):
        for n, (chip, r) in enumerate(rows_of_blocks(row_count, blocks)):
            place_right(across_ref, chips, chip, r, ref[n])
    lax.fori_loop(0, row_count * chips // chunk, some_rows, 0)


def attention_inputs(
    row_count, chips, first, norms, w_out, left_ref, gate_ref, pairs_ref, held_triangle, across_ref,
    triangle_ref,
):
    bf16 = jnp.bfloat16
    _, core = chip_and_core()
    half = row_count * chips
    tall = (half // 2) * 2 * half
    rows = pl.ds(pl.multiple_of(first * 2 * half, tall), tall)
    triangle_ref[...] = held_triangle[rows, :]
    triangle_rows(
        row_count, chips, left_ref, across_ref, triangle_ref, first, half // 2, 1 - core, 0
    )
    tri_normed = row_norm(triangle_ref[...], norms[2:3, :], norms[3:4, :]).astype(bf16)
    after_tri = pairs_ref[rows, :] + gate_ref[rows, :] * dot(tri_normed, w_out[...])
    att_in = row_norm(after_tri, norms[4:5, :], norms[5:6, :]).astype(bf16)
    return after_tri, att_in


def first_chip(chips, part):
    chip, _ = chip_and_core()
    return jnp.bitwise_xor(jnp.bitwise_and(chip, chips // 2), part * (chips // 2))


def own_inputs_kernel(
    row_count,
    chips,
    blocks,
    norms,
    w_out,
    left_ref,
    gate_ref,
    pairs_ref,
    received,
    triangle_ref,
    held_across,
    across_ref,
    after_ref,
    att_ref,
    scratch_ref,
):
    for n, (chip, r) in enumerate(rows_of_blocks(row_count, blocks)):
        place_right(across_ref, chips, chip, r, received[n])
    first = first_chip(chips, 0) * row_count
    refs = (left_ref, gate_ref, pairs_ref, triangle_ref, across_ref, scratch_ref)
    after_ref[...], att_ref[...] = attention_inputs(
        row_count, chips, first, norms, w_out, *refs
    )


def other_inputs_kernel(row_count, chips, norms, w_out, *refs):
    *refs, att_ref, scratch_ref = refs
    first = first_chip(chips, 1) * row_count
    _, att_ref[...] = attention_inputs(row_count, chips, first, norms, w_out, *refs, scratch_ref)


def keys_and_values(att, w_key, w_value, key_ref, value_ref):
    channels = key_ref.shape[1]
    key_value = jnp.concatenate([w_key[...], w_value[...]], axis=1)
    start = 0
    for values in att:
        rows = slice(start, start + values.shape[0])
        joined = dot(values, key_value)
        key_ref[rows, :] = rounded(joined[:, :channels])
        value_ref[rows, :] = rounded(joined[:, channels:])
        start = rows.stop


def column_bias(row_count, res, att, wide_bias, att_ref, bias_ref):
    start = 0
    for values in att:
        att_ref[start : start + values.shape[0], :] = values.astype(jnp.float32)
        start += values.shape[0]
    keys = start // res
    own = lax.axis_index("row") * row_count
    height = -(-keys // 8) * 8
    columns = [att_ref[pl.ds(own + r, height, stride=res), :] for r in range(row_count)]
    columns = jnp.concatenate(columns, axis=0).astype(jnp.bfloat16)
    bias = rounded(dot(columns, wide_bias[...]))
    for r in range(row_count):
        bias_ref[r, :height, :] = bias[r * height : (r + 1) * height]


def partial_attention(
    row_count, chips, query, parts, bias_ref, same_head, valid_column, sums, together
):
    bf16 = jnp.bfloat16
    res = 2 * row_count * chips
    channels = valid_column.shape[1]
    count = row_count * chips // 2
    for part, (core, first, key_of, value_of) in enumerate(parts):
        products = []
        for r in range(row_count):
            own_query = query[r * res : (r + 1) * res]
            row = [(key_of(n) * own_query).astype(bf16) for n in range(count)]
            pairs = [jnp.concatenate(row[n : n + 2], axis=1) for n in range(0, count, 2)]
            products.append(jnp.concatenate(pairs, axis=0))
        if together:
            scores = dot(jnp.concatenate(products, axis=0), same_head[...])
            tall = count // 2 * res
            scores = [scores[r * tall : (r + 1) * tall] for r in range(row_count)]
        else:
            scores = [dot(product, same_head[...]) for product in products]

        def score_of(n, r):
            lanes = slice(n % 2 * channels, (n % 2 + 1) * channels)
            k = (2 * (first + n // row_count) + core) * row_count + n % row_count
            key_mask = 1000000000.0 * (valid_column[pl.ds(k, 1), :] - 1.0)
            at = part * count + n
            shift = (bias_ref[r, at : at + 1, :] + key_mask) * math.log2(math.e)
            return scores[r][n // 2 * res : (n // 2 + 1) * res, lanes] + shift

        later = []
        for r, (maximum, total, mixed) in enumerate(sums):
            highest = score_of(0, r)
            for n in range(1, count):
                highest = jnp.maximum(highest, score_of(n, r))
            if maximum is None:
                maximum, total, mixed = highest, 0.0, 0.0
            else:
                highest = jnp.maximum(highest, maximum)
                scale = jnp.exp2(maximum - highest)
                maximum, total, mixed = highest, total * scale, mixed * scale
            for n in range(count):
                weight = jnp.exp2(score_of(n, r) - maximum)
                total = total + weight
                mixed = mixed + weight * value_of(n)
            later.append((maximum, total, mixed))
        sums = later
    return sums


def most_attention_kernel(
    row_count,
    chips,
    valid_column,
    same_head,
    w_query,
    w_gate,
    w_key,
    w_value,
    wide_bias,
    own_att_a,
    own_att_b,
    far_att_a,
    own_after,
    sums_ref,
    query_ref,
    gate_ref,
    after_ref,
    att_ref,
    key_ref,
    value_ref,
    bias_ref,
):
    chip, core = chip_and_core()
    res, channels = valid_column.shape
    own = row_count * res
    rows = pl.ds(pl.multiple_of(jnp.bitwise_and(chip, chips // 2 - 1) * own, own), own)
    own_in = own_att_a[rows, :]
    query = rounded(dot(own_in, w_query[...])) * (math.log2(math.e) / math.sqrt(HEAD_DIM))
    att = [ref[...] for ref in (own_att_a, own_att_b, far_att_a)]
    keys_and_values(att, w_key, w_value, key_ref, value_ref)
    column_bias(row_count, res, att, wide_bias, att_ref, bias_ref)
    count = row_count * chips // 2

    def rows_of(ref, first):
        return lambda n: ref[(first + n) * res : (first + n + 1) * res, :]

    a, b = first_chip(chips, 0), first_chip(chips, 1)
    parts = [
        (sender, first, rows_of(key_ref, n * count), rows_of(value_ref, n * count))
        for n, (sender, first) in enumerate(((core, a), (core, b), (1 - core, a)))
    ]
    none = [(None, None, None)] * row_count
    sums = partial_attention(
        row_count, chips, query, parts, bias_ref, same_head, valid_column, none, True
    )
    for r in range(row_count):
        for n, each in enumerate(sums[r]):
            sums_ref[r, n] = each
    query_ref[...] = query
    gate_ref[...] = sigmoid(dot(own_in, w_gate[...]))
    after_ref[...] = own_after[rows, :]


def attention_kernel(
    row_count,
    chips,
    valid_column,
    same_head,
    w_key,
    w_value,
    w_out,
    wide_bias,
    far_att_b,
    query_ref,
    gate_ref,
    after_ref,
    sums_ref,
    out_ref,
    att_ref,
    key_ref,
    value_ref,
    bias_ref,
):
    _, core = chip_and_core()
    res, channels = valid_column.shape
    far_att = far_att_b[...]
    keys_and_values([far_att], w_key, w_value, key_ref, value_ref)
    column_bias(row_count, res, [far_att], wide_bias, att_ref, bias_ref)

    def rows_of(ref):
        return lambda n: ref[n * res : (n + 1) * res, :]

    parts = ((1 - core, first_chip(chips, 1), rows_of(key_ref), rows_of(value_ref)),)
    sums = [tuple(sums_ref[r, n] for n in range(3)) for r in range(row_count)]
    sums = partial_attention(
        row_count, chips, query_ref[...], parts, bias_ref, same_head, valid_column, sums, False
    )
    attended = [mixed / total for _, total, mixed in sums]
    gated = (jnp.concatenate(attended, axis=0) * gate_ref[...]).astype(jnp.bfloat16)
    final = after_ref[...] + dot(gated, w_out[...])
    out_ref[...] = final.astype(jnp.bfloat16).reshape(row_count, res, channels)


def on_whole_complex(
    pair_rep,
    residue_valid,
    tri_norm_gain,
    tri_norm_bias,
    w_edges,
    w_tri_gate,
    out_norm_gain,
    out_norm_bias,
    w_tri_out,
    att_norm_gain,
    att_norm_bias,
    w_query,
    w_key,
    w_value,
    w_att_gate,
    w_pair_bias,
    w_att_out,
):
    row_count, res, channels = pair_rep.shape
    devices = res // row_count
    chips = devices // 2
    half = res // 2
    f32, bf16 = jnp.float32, jnp.bfloat16
    in_vmem = pl.BlockSpec(memory_space=pltpu.VMEM)

    def shaped(dtype, *shape):
        return jax.ShapeDtypeStruct(shape, dtype)

    def call(kernel, outs, operands, aliases=None, scratch=(), cost=2**25):
        return pl.pallas_call(
            kernel,
            out_shape=outs,
            in_specs=[in_vmem] * len(operands),
            out_specs=jax.tree.map(lambda _: in_vmem, outs),
            input_output_aliases=aliases or {},
            scratch_shapes=list(scratch),
            compiler_params=pltpu.CompilerParams(vmem_limit_bytes=24 * 1024 * 1024),
            cost_estimate=pl.CostEstimate(flops=2**20, bytes_accessed=cost, transcendentals=0),
        )(*operands)

    def exchange(values, bit):
        return lax.ppermute(values, "row", [(d, d ^ bit) for d in range(devices)])

    vectors = (
        tri_norm_gain,
        tri_norm_bias,
        out_norm_gain,
        out_norm_bias,
        att_norm_gain,
        att_norm_bias,
    )
    norms = jnp.stack(vectors)
    is_gate = lax.broadcasted_iota(jnp.int32, (1, 5 * channels), 1) // channels
    halves = jnp.where((is_gate == 0) | (is_gate == 2), 1.0, 0.5).astype(bf16)
    edge_weights = jnp.concatenate([w_edges, w_tri_gate], axis=1) * halves
    valid_column = jnp.broadcast_to(residue_valid.astype(f32)[:, None], (res, channels))

    head = lax.broadcasted_iota(jnp.int32, (HEADS, channels), 0)
    head_of_channel = lax.broadcasted_iota(jnp.int32, (HEADS, channels), 1) // HEAD_DIM
    repeat = jnp.where(head == head_of_channel, 1.0, 0.0).astype(bf16)
    wide_bias = dot(w_pair_bias, repeat).astype(bf16)

    kept = lax.dynamic_update_slice(
        jnp.zeros((2 * row_count, res, channels), bf16), pair_rep, (0, 0, 0)
    )
    far = exchange(pair_rep, devices // 2)
    far, kept, norms, edge_weights = lax.optimization_barrier((far, kept, norms, edge_weights))
    own = lax.dynamic_update_slice(kept, far, (row_count, 0, 0))
    own_blocks = (0, chips // 2)

    def blocks_from(bits):
        return tuple(s ^ bits for s in own_blocks)

    tall = shaped(f32, half * res, channels)

    def edges_of(pieces, send_row, *held):
        pairs = tuple(p for p, _ in pieces)
        blocks = tuple(b for _, b in pieces)
        operands = (valid_column, norms, edge_weights) + pairs + held
        first = len(operands) - len(held)
        return call(
            functools.partial(edges_kernel, row_count, chips, blocks, send_row, not held),
            (tall, tall, tall, tall, shaped(bf16, 4 * row_count, res, channels))
            + (() if held else (shaped(bf16, 2 * channels, 2 * channels),)),
            operands,
            {first + e: e for e in range(len(held))},
        )

    diagonal = exchange(own, 6)
    beside = exchange(own, 2)
    near = exchange(own, 4)
    *edges, early_right, same_head = edges_of([(own, own_blocks)], 0)
    diagonal, edges = lax.optimization_barrier((diagonal, edges))
    *edges, early_right = edges_of(
        [(diagonal, blocks_from(3))], 2 * row_count, *edges, early_right
    )
    beside, edges, early_right, wide_bias = lax.optimization_barrier(
        (beside, edges, early_right, wide_bias)
    )
    early = (exchange(early_right, 1), own_blocks + blocks_from(3))
    *edges, late_right = edges_of(
        [(beside, blocks_from(1)), (near, blocks_from(2))], 0, *edges
    )
    late = (exchange(late_right, 1), blocks_from(1) + blocks_from(2))

    left, right, gate, pairs = edges
    triangle, across = call(
        functools.partial(near_triangle_kernel, row_count, chips, half // 2, [early[1]]),
        (tall, tall),
        (left, right, early[0]),
    )
    part = half // 2 * res
    in_part, own_shape = shaped(f32, part, channels), shaped(f32, row_count * res, channels)
    att_part = shaped(bf16, part, channels)
    shared = (norms, w_tri_out, left, gate, pairs)
    scratch = (pltpu.VMEM((part, channels), f32),)
    across, after_a, att_a = call(
        functools.partial(own_inputs_kernel, row_count, chips, late[1]),
        (tall, in_part, att_part),
        shared + (late[0], triangle, across),
        {7: 0},
        scratch=scratch,
    )
    far_att_a = exchange(att_a, 1)
    att_b = call(
        functools.partial(other_inputs_kernel, row_count, chips),
        att_part,
        shared + (triangle, across),
        scratch=scratch,
    )
    far_att_b = exchange(att_b, 1)

    def attention_scratch(keys, projected):
        return (
            pltpu.VMEM((-(-keys // 8) * 8 * res, channels), f32),
            pltpu.VMEM((projected * res, channels), f32),
            pltpu.VMEM((projected * res, channels), f32),
            pltpu.VMEM((row_count, 40, channels), f32),
        )

    sums, query, att_gate, after_own = call(
        functools.partial(most_attention_kernel, row_count, chips),
        (shaped(f32, row_count, 3, res, channels), own_shape, own_shape, own_shape),
        (valid_column, same_head, w_query, w_att_gate, w_key, w_value, wide_bias)
        + (att_a, att_b, far_att_a, after_a),
        scratch=attention_scratch(3 * half // 2, 3 * half // 2),
    )
    return call(
        functools.partial(attention_kernel, row_count, chips),
        shaped(bf16, *pair_rep.shape),
        (valid_column, same_head, w_key, w_value, w_att_out, wide_bias, far_att_b)
        + (query, att_gate, after_own, sums),
        scratch=attention_scratch(half // 2, half // 2),
    )


def per_device(pair_rep, residue_valid, *parameters):
    row_count, res, channels = pair_rep.shape
    devices = res // row_count
    if res % 48 == 0 and devices == 16 and 40 * res * res * channels <= 32 * 1024 * 1024:
        return on_whole_complex(pair_rep, residue_valid, *parameters)
    return split_over_devices(pair_rep, residue_valid, *parameters)


def solution(mesh):
    return jax.shard_map(
        per_device,
        mesh=mesh,
        in_specs=(
            P(("groups", "row"), None, None),
            P("groups"),
            P(),
            P(),
            P(),
            P(),
            P(),
            P(),
            P(),
            P(),
            P(),
            P(),
            P(),
            P(),
            P(),
            P(),
            P(),
        ),
        out_specs=P(("groups", "row"), None, None),
        check_vma=False,
    )
```

```python
import functools
import math

import jax
import jax.numpy as jnp
from jax import lax
from jax.experimental import pallas as pl
from jax.experimental.pallas import tpu as pltpu
from jax.sharding import PartitionSpec as P

HEADS = 4
HEAD_DIM = 32


def layer_norm(values, norm_gain, norm_bias, along_axis):
    centre = values - jnp.mean(values, axis=along_axis, keepdims=True)
    spread = jnp.mean(centre * centre, axis=along_axis, keepdims=True)
    return centre * lax.rsqrt(spread + 1e-05) * norm_gain + norm_bias


def attend(query_cols, key_cols, value_cols, whole_bias, key_mask):
    factor = 1.0 / math.sqrt(HEAD_DIM)
    scores = (
        jnp.einsum("kjhd,ijhd->jhki", key_cols, query_cols, preferred_element_type=jnp.float32)
        * factor
    )
    scores = scores + whole_bias.astype(jnp.float32)[None] + key_mask[None, None, :, None]
    scores = scores - jnp.max(scores, axis=2, keepdims=True)
    exponent = jnp.exp(scores)
    weights = (exponent / jnp.sum(exponent, axis=2, keepdims=True)).astype(jnp.bfloat16)
    return jnp.einsum("jhki,kjhd->ijhd", weights, value_cols, preferred_element_type=jnp.float32)


def split_over_devices(
    pair_rep,
    residue_valid,
    tri_norm_gain,
    tri_norm_bias,
    w_edges,
    w_tri_gate,
    out_norm_gain,
    out_norm_bias,
    w_tri_out,
    att_norm_gain,
    att_norm_bias,
    w_query,
    w_key,
    w_value,
    w_att_gate,
    w_pair_bias,
    w_att_out,
):
    row_count = pair_rep.shape[0]
    res_count = pair_rep.shape[1]
    channels = pair_rep.shape[2]
    hidden_width = HEADS * HEAD_DIM
    row_start = lax.axis_index("row") * row_count
    valid_flags = residue_valid.astype(jnp.float32)
    own_valid = lax.dynamic_slice_in_dim(valid_flags, row_start, row_count)
    normed = layer_norm(pair_rep.astype(jnp.float32), tri_norm_gain, tri_norm_bias, 2).astype(
        jnp.bfloat16
    )
    projected = jnp.einsum("ikd,de->eik", normed, w_edges, preferred_element_type=jnp.float32)
    projected = projected.reshape(4, channels, row_count, res_count)
    pair_mask = (own_valid[:, None] * valid_flags[None, :])[None, :, :]
    left_edges = (jax.nn.sigmoid(projected[1]) * projected[0] * pair_mask).astype(jnp.bfloat16)
    right_edges = (jax.nn.sigmoid(projected[3]) * projected[2] * pair_mask).astype(jnp.bfloat16)
    left_cols, right_cols = (
        lax.all_to_all(left_edges, "row", split_axis=0, concat_axis=1, tiled=True),
        lax.all_to_all(right_edges, "row", split_axis=0, concat_axis=1, tiled=True),
    )
    block_product = jnp.einsum(
        "cik,cjk->cij", left_cols, right_cols, preferred_element_type=jnp.float32
    ).astype(jnp.bfloat16)
    triangle = lax.all_to_all(block_product, "row", split_axis=1, concat_axis=0, tiled=True)
    tri_normed = layer_norm(
        triangle.astype(jnp.float32), out_norm_gain[:, None, None], out_norm_bias[:, None, None], 0
    ).astype(jnp.bfloat16)
    tri_gate = jax.nn.sigmoid(
        jnp.einsum("ijc,ce->ije", normed, w_tri_gate, preferred_element_type=jnp.float32)
    )
    tri_update = jnp.einsum(
        "cij,ce->ije", tri_normed, w_tri_out, preferred_element_type=jnp.float32
    )
    after_tri = pair_rep.astype(jnp.float32) + tri_gate * tri_update
    att_in = layer_norm(after_tri, att_norm_gain, att_norm_bias, 2).astype(jnp.bfloat16)
    pair_bias = jnp.einsum(
        "kic,ch->hki", att_in, w_pair_bias, preferred_element_type=jnp.float32
    ).astype(jnp.bfloat16)
    whole_bias = lax.all_gather(pair_bias, "row", axis=1, tiled=True)
    key_mask = 1000000000.0 * (valid_flags - 1.0)
    columns = lax.all_to_all(att_in, "row", split_axis=1, concat_axis=0, tiled=True)
    all_weights = jnp.concatenate([w_query, w_key, w_value, w_att_gate], axis=1)
    joined = jnp.dot(columns.reshape(-1, channels), all_weights, preferred_element_type=jnp.float32)
    query_cols = (
        joined[:, :hidden_width].astype(jnp.bfloat16).reshape(res_count, row_count, HEADS, HEAD_DIM)
    )
    key_cols = (
        joined[:, hidden_width : 2 * hidden_width]
        .astype(jnp.bfloat16)
        .reshape(res_count, row_count, HEADS, HEAD_DIM)
    )
    value_cols = (
        joined[:, 2 * hidden_width : 3 * hidden_width]
        .astype(jnp.bfloat16)
        .reshape(res_count, row_count, HEADS, HEAD_DIM)
    )
    gate_cols = jax.nn.sigmoid(joined[:, 3 * hidden_width :]).reshape(
        res_count, row_count, hidden_width
    )
    attended = attend(query_cols, key_cols, value_cols, whole_bias, key_mask)
    gated = (attended.reshape(res_count, row_count, hidden_width) * gate_cols).astype(jnp.bfloat16)
    gated_rows = lax.all_to_all(gated, "row", split_axis=0, concat_axis=1, tiled=True)
    final = after_tri + jnp.einsum(
        "ije,ec->ijc", gated_rows, w_att_out, preferred_element_type=jnp.float32
    )
    return final.astype(jnp.bfloat16)


def sigmoid(values):
    return 0.5 * jnp.tanh(0.5 * values) + 0.5


def row_norm(values, norm_gain, norm_bias):
    count = values.shape[1]
    centre = values - jnp.sum(values, axis=1, keepdims=True) * (1.0 / count)
    squares = jnp.sum(centre * centre, axis=1, keepdims=True)
    return centre * lax.rsqrt(squares + 1e-05 * count) * (norm_gain * count**0.5) + norm_bias


def dot(left, right):
    return jnp.dot(left, right, preferred_element_type=jnp.float32)


def rounded(values):
    return values.astype(jnp.bfloat16).astype(jnp.float32)


def chip_and_core():
    device = lax.axis_index("row")
    return lax.shift_right_logical(device, 1), jnp.bitwise_and(device, 1)


def rows_of_blocks(row_count, blocks):
    chip, _ = chip_and_core()
    return [(jnp.bitwise_xor(chip, bits), r) for bits in blocks for r in range(row_count)]


def edges_kernel(
    row_count, chips, pieces, send_row, makes_heads, valid_column, norms, weights, *refs
):
    pair_refs = refs[: len(pieces)]
    left_ref, right_ref, gate_ref, pairs_ref, send_ref = refs[-5:]
    if makes_heads:
        left_ref, right_ref, gate_ref, pairs_ref, send_ref, same_head_ref = refs[-6:]
        wide = same_head_ref.shape
        row = lax.broadcasted_iota(jnp.int32, wide, 0) // HEAD_DIM
        column = lax.broadcasted_iota(jnp.int32, wide, 1) // HEAD_DIM
        same_head_ref[...] = jnp.where(row == column, 1.0, 0.0).astype(jnp.bfloat16)
    f32, bf16 = jnp.float32, jnp.bfloat16
    res, channels = valid_column.shape
    _, core = chip_and_core()
    pairs = jnp.concatenate(
        [ref[...].astype(f32).reshape(-1, channels) for ref in pair_refs], axis=0
    )
    normed = row_norm(pairs, norms[0:1, :], norms[1:2, :]).astype(bf16)
    column = 0.5 * valid_column[...]
    rows_of = rows_of_blocks(row_count, [bits for piece in pieces for bits in piece])
    masks = jnp.concatenate(
        [
            column * valid_column[pl.ds((2 * chip + core) * row_count + r, 1), :]
            for chip, r in rows_of
        ],
        axis=0,
    )
    joined = dot(normed, weights[:, : 2 * channels])
    left = rounded((jnp.tanh(joined[:, channels:]) + 1.0) * joined[:, :channels] * masks)
    joined = dot(normed, weights[:, 2 * channels : 4 * channels])
    right = ((jnp.tanh(joined[:, channels:]) + 1.0) * joined[:, :channels] * masks).astype(bf16)
    gate = 0.5 * jnp.tanh(dot(normed, weights[:, 4 * channels :])) + 0.5
    for n, (chip, r) in enumerate(rows_of):
        rows = slice(n * res, (n + 1) * res)
        start = pl.multiple_of((chip * row_count + r) * res, res)
        send_ref[send_row + n] = right[rows]
        left_ref[pl.ds(start, res), :] = left[rows]
        place_right(right_ref, chips, chip, r, right[rows])
        gate_ref[pl.ds(start, res), :] = gate[rows]
        pairs_ref[pl.ds(start, res), :] = pairs[rows]


def place_right(right_ref, chips, chip, r, edges):
    res = edges.shape[0]
    start = pl.multiple_of((r * chips + chip) * res, res)
    right_ref[pl.ds(start, res), :] = edges.astype(jnp.float32)


def join(even, odd, shift):
    high = jnp.bitwise_and(lax.broadcasted_iota(jnp.int32, even.shape, 0), shift) > 0
    return jnp.where(high, odd, even) + pltpu.roll(jnp.where(high, even, odd), shift, 0)


def triangle_rows(
    row_count, chips, left_ref, right_ref, triangle_ref, first, count, core, triangle_first
):
    res = 2 * row_count * chips
    start = pl.multiple_of(first * res, res)
    block = 4
    for n in range(0, count, block):
        lefts = [left_ref[pl.ds(start + m * res, res), :] for m in range(n, n + block)]
        for r in range(row_count):
            sums = [[] for _ in range(block)]
            for chip in range(chips):
                at = (r * chips + chip) * res
                right = right_ref[at : at + res, :]
                for m in range(block):
                    product = lefts[m] * right
                    part = sum((product[k : k + 8] for k in range(8, res, 8)), product[:8])
                    shift = 1
                    while chip & shift:
                        part = join(sums[m].pop(), part, shift)
                        shift *= 2
                    sums[m].append(part)
            for m in range(block):
                place = (triangle_first + n + m) * res + core * row_count + r
                triangle_ref[pl.ds(place, chips, stride=2 * row_count), :] = rounded(sums[m][0])


def near_triangle_kernel(row_count, chips, chunk, pieces, left_ref, right_ref, *refs):
    received, (triangle_ref, across_ref) = refs[:-2], refs[-2:]
    _, core = chip_and_core()

    def some_rows(step, carry):
        first = step * chunk
        triangle_rows(
            row_count, chips, left_ref, right_ref, triangle_ref, first, chunk, core, first
        )
        return carry

    for ref, blocks in zip(received, pieces):
        for n, (chip, r) in enumerate(rows_of_blocks(row_count, blocks)):
            place_right(across_ref, chips, chip, r, ref[n])
    lax.fori_loop(0, row_count * chips // chunk, some_rows, 0)


def attention_inputs(
    row_count,
    chips,
    first,
    norms,
    w_out,
    left_ref,
    gate_ref,
    pairs_ref,
    held_triangle,
    across_ref,
    after_ref,
    att_ref,
    scratch_refs,
):
    bf16 = jnp.bfloat16
    _, core = chip_and_core()
    half = row_count * chips
    res = 2 * half
    count = half // 2 // len(scratch_refs)
    tall = count * res

    def rest_of_triangle(n):
        start = first + n * count
        rows = pl.ds(pl.multiple_of(start * res, tall), tall)
        scratch_refs[n][...] = held_triangle[rows, :]
        triangle_rows(
            row_count, chips, left_ref, across_ref, scratch_refs[n], start, count, 1 - core, 0
        )

    def inputs_of(n):
        rows = pl.ds(pl.multiple_of((first + n * count) * res, tall), tall)
        tri_normed = row_norm(scratch_refs[n][...], norms[2:3, :], norms[3:4, :]).astype(bf16)
        after_tri = pairs_ref[rows, :] + gate_ref[rows, :] * dot(tri_normed, w_out[...])
        att_in = row_norm(after_tri, norms[4:5, :], norms[5:6, :]).astype(bf16)
        if after_ref is not None:
            after_ref[n * tall : (n + 1) * tall, :] = after_tri
        att_ref[n * tall : (n + 1) * tall, :] = att_in

    rest_of_triangle(0)
    for n in range(1, len(scratch_refs)):
        rest_of_triangle(n)
        inputs_of(n - 1)
    inputs_of(len(scratch_refs) - 1)


def first_chip(chips, part):
    chip, _ = chip_and_core()
    return jnp.bitwise_xor(jnp.bitwise_and(chip, chips // 2), part * (chips // 2))


def own_inputs_kernel(
    row_count,
    chips,
    blocks,
    norms,
    w_out,
    left_ref,
    gate_ref,
    pairs_ref,
    received,
    triangle_ref,
    held_across,
    across_ref,
    after_ref,
    att_ref,
    *scratch_refs,
):
    for n, (chip, r) in enumerate(rows_of_blocks(row_count, blocks)):
        place_right(across_ref, chips, chip, r, received[n])
    first = first_chip(chips, 0) * row_count
    refs = (left_ref, gate_ref, pairs_ref, triangle_ref, across_ref, after_ref, att_ref)
    attention_inputs(row_count, chips, first, norms, w_out, *refs, scratch_refs)


def other_inputs_kernel(row_count, chips, norms, w_out, *refs):
    refs, att_ref, scratch_refs = refs[:5], refs[5], refs[6:]
    first = first_chip(chips, 1) * row_count
    attention_inputs(row_count, chips, first, norms, w_out, *refs, None, att_ref, scratch_refs)


def keys_and_values(att, w_key, w_value, key_ref, value_ref):
    channels = key_ref.shape[1]
    key_value = jnp.concatenate([w_key[...], w_value[...]], axis=1)
    start = 0
    for values in att:
        rows = slice(start, start + values.shape[0])
        joined = dot(values, key_value)
        key_ref[rows, :] = rounded(joined[:, :channels])
        value_ref[rows, :] = rounded(joined[:, channels:])
        start = rows.stop


def column_bias(row_count, res, att, wide_bias, att_ref, bias_ref):
    start = 0
    for values in att:
        att_ref[start : start + values.shape[0], :] = values.astype(jnp.float32)
        start += values.shape[0]
    keys = start // res
    own = lax.axis_index("row") * row_count
    height = -(-keys // 8) * 8
    columns = [att_ref[pl.ds(own + r, height, stride=res), :] for r in range(row_count)]
    columns = jnp.concatenate(columns, axis=0).astype(jnp.bfloat16)
    bias = rounded(dot(columns, wide_bias[...]))
    for r in range(row_count):
        bias_ref[r, :height, :] = bias[r * height : (r + 1) * height]


def partial_attention(
    row_count, chips, query, parts, bias_ref, same_head, valid_column, sums, together
):
    bf16 = jnp.bfloat16
    res = 2 * row_count * chips
    channels = valid_column.shape[1]
    count = row_count * chips // 2
    for part, (core, first, key_of, value_of) in enumerate(parts):
        products = []
        for r in range(row_count):
            own_query = query[r * res : (r + 1) * res]
            row = [(key_of(n) * own_query).astype(bf16) for n in range(count)]
            pairs = [jnp.concatenate(row[n : n + 2], axis=1) for n in range(0, count, 2)]
            products.append(jnp.concatenate(pairs, axis=0))
        if together:
            scores = dot(jnp.concatenate(products, axis=0), same_head[...])
            tall = count // 2 * res
            scores = [scores[r * tall : (r + 1) * tall] for r in range(row_count)]
        else:
            scores = [dot(product, same_head[...]) for product in products]

        def score_of(n, r):
            lanes = slice(n % 2 * channels, (n % 2 + 1) * channels)
            k = (2 * (first + n // row_count) + core) * row_count + n % row_count
            key_mask = 1000000000.0 * (valid_column[pl.ds(k, 1), :] - 1.0)
            at = part * count + n
            shift = (bias_ref[r, at : at + 1, :] + key_mask) * math.log2(math.e)
            return scores[r][n // 2 * res : (n // 2 + 1) * res, lanes] + shift

        later = []
        for r, (maximum, total, mixed) in enumerate(sums):
            highest = score_of(0, r)
            for n in range(1, count):
                highest = jnp.maximum(highest, score_of(n, r))
            if maximum is None:
                maximum, total, mixed = highest, 0.0, 0.0
            else:
                highest = jnp.maximum(highest, maximum)
                scale = jnp.exp2(maximum - highest)
                maximum, total, mixed = highest, total * scale, mixed * scale
            for n in range(count):
                weight = jnp.exp2(score_of(n, r) - maximum)
                total = total + weight
                mixed = mixed + weight * value_of(n)
            later.append((maximum, total, mixed))
        sums = later
    return sums


def most_attention_kernel(
    row_count,
    chips,
    valid_column,
    same_head,
    w_query,
    w_gate,
    w_key,
    w_value,
    wide_bias,
    own_att_a,
    own_att_b,
    far_att_a,
    own_after,
    sums_ref,
    query_ref,
    gate_ref,
    after_ref,
    att_ref,
    key_ref,
    value_ref,
    bias_ref,
):
    chip, core = chip_and_core()
    res, channels = valid_column.shape
    own = row_count * res
    rows = pl.ds(pl.multiple_of(jnp.bitwise_and(chip, chips // 2 - 1) * own, own), own)
    own_in = own_att_a[rows, :]
    query = rounded(dot(own_in, w_query[...])) * (math.log2(math.e) / math.sqrt(HEAD_DIM))
    att = [ref[...] for ref in (own_att_a, own_att_b, far_att_a)]
    keys_and_values(att, w_key, w_value, key_ref, value_ref)
    column_bias(row_count, res, att, wide_bias, att_ref, bias_ref)
    count = row_count * chips // 2

    def rows_of(ref, first):
        return lambda n: ref[(first + n) * res : (first + n + 1) * res, :]

    a, b = first_chip(chips, 0), first_chip(chips, 1)
    parts = [
        (sender, first, rows_of(key_ref, n * count), rows_of(value_ref, n * count))
        for n, (sender, first) in enumerate(((core, a), (core, b), (1 - core, a)))
    ]
    none = [(None, None, None)] * row_count
    sums = partial_attention(
        row_count, chips, query, parts, bias_ref, same_head, valid_column, none, True
    )
    for r in range(row_count):
        for n, each in enumerate(sums[r]):
            sums_ref[r, n] = each
    query_ref[...] = query
    gate_ref[...] = sigmoid(dot(own_in, w_gate[...]))
    after_ref[...] = own_after[rows, :]


def attention_kernel(
    row_count,
    chips,
    valid_column,
    same_head,
    w_key,
    w_value,
    w_out,
    wide_bias,
    far_att_b,
    query_ref,
    gate_ref,
    after_ref,
    sums_ref,
    out_ref,
    att_ref,
    key_ref,
    value_ref,
    bias_ref,
):
    _, core = chip_and_core()
    res, channels = valid_column.shape
    far_att = far_att_b[...]
    keys_and_values([far_att], w_key, w_value, key_ref, value_ref)
    column_bias(row_count, res, [far_att], wide_bias, att_ref, bias_ref)

    def rows_of(ref):
        return lambda n: ref[n * res : (n + 1) * res, :]

    parts = ((1 - core, first_chip(chips, 1), rows_of(key_ref), rows_of(value_ref)),)
    sums = [tuple(sums_ref[r, n] for n in range(3)) for r in range(row_count)]
    sums = partial_attention(
        row_count, chips, query_ref[...], parts, bias_ref, same_head, valid_column, sums, False
    )
    attended = [mixed / total for _, total, mixed in sums]
    gated = (jnp.concatenate(attended, axis=0) * gate_ref[...]).astype(jnp.bfloat16)
    final = after_ref[...] + dot(gated, w_out[...])
    out_ref[...] = final.astype(jnp.bfloat16).reshape(row_count, res, channels)


def on_whole_complex(
    pair_rep,
    residue_valid,
    tri_norm_gain,
    tri_norm_bias,
    w_edges,
    w_tri_gate,
    out_norm_gain,
    out_norm_bias,
    w_tri_out,
    att_norm_gain,
    att_norm_bias,
    w_query,
    w_key,
    w_value,
    w_att_gate,
    w_pair_bias,
    w_att_out,
):
    row_count, res, channels = pair_rep.shape
    devices = res // row_count
    chips = devices // 2
    half = res // 2
    f32, bf16 = jnp.float32, jnp.bfloat16
    in_vmem = pl.BlockSpec(memory_space=pltpu.VMEM)

    def shaped(dtype, *shape):
        return jax.ShapeDtypeStruct(shape, dtype)

    def call(kernel, outs, operands, aliases=None, scratch=(), cost=2**25):
        return pl.pallas_call(
            kernel,
            out_shape=outs,
            in_specs=[in_vmem] * len(operands),
            out_specs=jax.tree.map(lambda _: in_vmem, outs),
            input_output_aliases=aliases or {},
            scratch_shapes=list(scratch),
            compiler_params=pltpu.CompilerParams(vmem_limit_bytes=24 * 1024 * 1024),
            cost_estimate=pl.CostEstimate(flops=2**20, bytes_accessed=cost, transcendentals=0),
        )(*operands)

    def exchange(values, bit):
        return lax.ppermute(values, "row", [(d, d ^ bit) for d in range(devices)])

    vectors = (
        tri_norm_gain,
        tri_norm_bias,
        out_norm_gain,
        out_norm_bias,
        att_norm_gain,
        att_norm_bias,
    )
    norms = jnp.stack(vectors)
    is_gate = lax.broadcasted_iota(jnp.int32, (1, 5 * channels), 1) // channels
    halves = jnp.where((is_gate == 0) | (is_gate == 2), 1.0, 0.5).astype(bf16)
    edge_weights = jnp.concatenate([w_edges, w_tri_gate], axis=1) * halves
    valid_column = jnp.broadcast_to(residue_valid.astype(f32)[:, None], (res, channels))

    head = lax.broadcasted_iota(jnp.int32, (HEADS, channels), 0)
    head_of_channel = lax.broadcasted_iota(jnp.int32, (HEADS, channels), 1) // HEAD_DIM
    repeat = jnp.where(head == head_of_channel, 1.0, 0.0).astype(bf16)
    wide_bias = dot(w_pair_bias, repeat).astype(bf16)

    kept = lax.dynamic_update_slice(
        jnp.zeros((2 * row_count, res, channels), bf16), pair_rep, (0, 0, 0)
    )
    far = exchange(pair_rep, devices // 2)
    far, kept, norms, edge_weights = lax.optimization_barrier((far, kept, norms, edge_weights))
    own = lax.dynamic_update_slice(kept, far, (row_count, 0, 0))
    own_blocks = (0, chips // 2)

    def blocks_from(bits):
        return tuple(s ^ bits for s in own_blocks)

    tall = shaped(f32, half * res, channels)

    def edges_of(pieces, send_row, *held):
        pairs = tuple(p for p, _ in pieces)
        blocks = tuple(b for _, b in pieces)
        operands = (valid_column, norms, edge_weights) + pairs + held
        first = len(operands) - len(held)
        return call(
            functools.partial(edges_kernel, row_count, chips, blocks, send_row, not held),
            (tall, tall, tall, tall, shaped(bf16, 4 * row_count, res, channels))
            + (() if held else (shaped(bf16, 2 * channels, 2 * channels),)),
            operands,
            {first + e: e for e in range(len(held))},
        )

    diagonal = exchange(own, 6)
    beside = exchange(own, 2)
    near = exchange(own, 4)
    *edges, early_right, same_head = edges_of([(own, own_blocks)], 0)
    diagonal, edges = lax.optimization_barrier((diagonal, edges))
    *edges, early_right = edges_of(
        [(diagonal, blocks_from(3))], 2 * row_count, *edges, early_right
    )
    beside, edges, early_right, wide_bias = lax.optimization_barrier(
        (beside, edges, early_right, wide_bias)
    )
    early = (exchange(early_right, 1), own_blocks + blocks_from(3))
    *edges, late_right = edges_of(
        [(beside, blocks_from(1)), (near, blocks_from(2))], 0, *edges
    )
    late = (exchange(late_right, 1), blocks_from(1) + blocks_from(2))

    left, right, gate, pairs = edges
    triangle, across = call(
        functools.partial(near_triangle_kernel, row_count, chips, half // 2, [early[1]]),
        (tall, tall),
        (left, right, early[0]),
    )
    part = half // 2 * res
    in_part, own_shape = shaped(f32, part, channels), shaped(f32, row_count * res, channels)
    att_part = shaped(bf16, part, channels)
    shared = (norms, w_tri_out, left, gate, pairs)
    scratch = (pltpu.VMEM((part // 3, channels), f32),) * 3
    across, after_a, att_a = call(
        functools.partial(own_inputs_kernel, row_count, chips, late[1]),
        (tall, in_part, att_part),
        shared + (late[0], triangle, across),
        {7: 0},
        scratch=scratch,
    )
    far_att_a = exchange(att_a, 1)
    att_b = call(
        functools.partial(other_inputs_kernel, row_count, chips),
        att_part,
        shared + (triangle, across),
        scratch=scratch,
    )
    far_att_b = exchange(att_b, 1)

    def attention_scratch(keys, projected):
        return (
            pltpu.VMEM((-(-keys // 8) * 8 * res, channels), f32),
            pltpu.VMEM((projected * res, channels), f32),
            pltpu.VMEM((projected * res, channels), f32),
            pltpu.VMEM((row_count, 40, channels), f32),
        )

    sums, query, att_gate, after_own = call(
        functools.partial(most_attention_kernel, row_count, chips),
        (shaped(f32, row_count, 3, res, channels), own_shape, own_shape, own_shape),
        (valid_column, same_head, w_query, w_att_gate, w_key, w_value, wide_bias)
        + (att_a, att_b, far_att_a, after_a),
        scratch=attention_scratch(3 * half // 2, 3 * half // 2),
    )
    return call(
        functools.partial(attention_kernel, row_count, chips),
        shaped(bf16, *pair_rep.shape),
        (valid_column, same_head, w_key, w_value, w_att_out, wide_bias, far_att_b)
        + (query, att_gate, after_own, sums),
        scratch=attention_scratch(half // 2, half // 2),
    )


def per_device(pair_rep, residue_valid, *parameters):
    row_count, res, channels = pair_rep.shape
    devices = res // row_count
    if res % 48 == 0 and devices == 16 and 40 * res * res * channels <= 32 * 1024 * 1024:
        return on_whole_complex(pair_rep, residue_valid, *parameters)
    return split_over_devices(pair_rep, residue_valid, *parameters)


def solution(mesh):
    return jax.shard_map(
        per_device,
        mesh=mesh,
        in_specs=(
            P(("groups", "row"), None, None),
            P("groups"),
            P(),
            P(),
            P(),
            P(),
            P(),
            P(),
            P(),
            P(),
            P(),
            P(),
            P(),
            P(),
            P(),
            P(),
            P(),
        ),
        out_specs=P(("groups", "row"), None, None),
        check_vma=False,
    )
```

```python
import functools
import math

import jax
import jax.numpy as jnp
from jax import lax
from jax.experimental import pallas as pl
from jax.experimental.pallas import tpu as pltpu
from jax.sharding import PartitionSpec as P

HEADS = 4
HEAD_DIM = 32


def layer_norm(values, norm_gain, norm_bias, along_axis):
    centre = values - jnp.mean(values, axis=along_axis, keepdims=True)
    spread = jnp.mean(centre * centre, axis=along_axis, keepdims=True)
    return centre * lax.rsqrt(spread + 1e-05) * norm_gain + norm_bias


def attend(query_cols, key_cols, value_cols, whole_bias, key_mask):
    factor = 1.0 / math.sqrt(HEAD_DIM)
    scores = (
        jnp.einsum("kjhd,ijhd->jhki", key_cols, query_cols, preferred_element_type=jnp.float32)
        * factor
    )
    scores = scores + whole_bias.astype(jnp.float32)[None] + key_mask[None, None, :, None]
    scores = scores - jnp.max(scores, axis=2, keepdims=True)
    exponent = jnp.exp(scores)
    weights = (exponent / jnp.sum(exponent, axis=2, keepdims=True)).astype(jnp.bfloat16)
    return jnp.einsum("jhki,kjhd->ijhd", weights, value_cols, preferred_element_type=jnp.float32)


def split_over_devices(
    pair_rep,
    residue_valid,
    tri_norm_gain,
    tri_norm_bias,
    w_edges,
    w_tri_gate,
    out_norm_gain,
    out_norm_bias,
    w_tri_out,
    att_norm_gain,
    att_norm_bias,
    w_query,
    w_key,
    w_value,
    w_att_gate,
    w_pair_bias,
    w_att_out,
):
    row_count = pair_rep.shape[0]
    res_count = pair_rep.shape[1]
    channels = pair_rep.shape[2]
    hidden_width = HEADS * HEAD_DIM
    row_start = lax.axis_index("row") * row_count
    valid_flags = residue_valid.astype(jnp.float32)
    own_valid = lax.dynamic_slice_in_dim(valid_flags, row_start, row_count)
    normed = layer_norm(pair_rep.astype(jnp.float32), tri_norm_gain, tri_norm_bias, 2).astype(
        jnp.bfloat16
    )
    projected = jnp.einsum("ikd,de->eik", normed, w_edges, preferred_element_type=jnp.float32)
    projected = projected.reshape(4, channels, row_count, res_count)
    pair_mask = (own_valid[:, None] * valid_flags[None, :])[None, :, :]
    left_edges = (jax.nn.sigmoid(projected[1]) * projected[0] * pair_mask).astype(jnp.bfloat16)
    right_edges = (jax.nn.sigmoid(projected[3]) * projected[2] * pair_mask).astype(jnp.bfloat16)
    left_cols, right_cols = (
        lax.all_to_all(left_edges, "row", split_axis=0, concat_axis=1, tiled=True),
        lax.all_to_all(right_edges, "row", split_axis=0, concat_axis=1, tiled=True),
    )
    block_product = jnp.einsum(
        "cik,cjk->cij", left_cols, right_cols, preferred_element_type=jnp.float32
    ).astype(jnp.bfloat16)
    triangle = lax.all_to_all(block_product, "row", split_axis=1, concat_axis=0, tiled=True)
    tri_normed = layer_norm(
        triangle.astype(jnp.float32), out_norm_gain[:, None, None], out_norm_bias[:, None, None], 0
    ).astype(jnp.bfloat16)
    tri_gate = jax.nn.sigmoid(
        jnp.einsum("ijc,ce->ije", normed, w_tri_gate, preferred_element_type=jnp.float32)
    )
    tri_update = jnp.einsum(
        "cij,ce->ije", tri_normed, w_tri_out, preferred_element_type=jnp.float32
    )
    after_tri = pair_rep.astype(jnp.float32) + tri_gate * tri_update
    att_in = layer_norm(after_tri, att_norm_gain, att_norm_bias, 2).astype(jnp.bfloat16)
    pair_bias = jnp.einsum(
        "kic,ch->hki", att_in, w_pair_bias, preferred_element_type=jnp.float32
    ).astype(jnp.bfloat16)
    whole_bias = lax.all_gather(pair_bias, "row", axis=1, tiled=True)
    key_mask = 1000000000.0 * (valid_flags - 1.0)
    columns = lax.all_to_all(att_in, "row", split_axis=1, concat_axis=0, tiled=True)
    all_weights = jnp.concatenate([w_query, w_key, w_value, w_att_gate], axis=1)
    joined = jnp.dot(columns.reshape(-1, channels), all_weights, preferred_element_type=jnp.float32)
    query_cols = (
        joined[:, :hidden_width].astype(jnp.bfloat16).reshape(res_count, row_count, HEADS, HEAD_DIM)
    )
    key_cols = (
        joined[:, hidden_width : 2 * hidden_width]
        .astype(jnp.bfloat16)
        .reshape(res_count, row_count, HEADS, HEAD_DIM)
    )
    value_cols = (
        joined[:, 2 * hidden_width : 3 * hidden_width]
        .astype(jnp.bfloat16)
        .reshape(res_count, row_count, HEADS, HEAD_DIM)
    )
    gate_cols = jax.nn.sigmoid(joined[:, 3 * hidden_width :]).reshape(
        res_count, row_count, hidden_width
    )
    attended = attend(query_cols, key_cols, value_cols, whole_bias, key_mask)
    gated = (attended.reshape(res_count, row_count, hidden_width) * gate_cols).astype(jnp.bfloat16)
    gated_rows = lax.all_to_all(gated, "row", split_axis=0, concat_axis=1, tiled=True)
    final = after_tri + jnp.einsum(
        "ije,ec->ijc", gated_rows, w_att_out, preferred_element_type=jnp.float32
    )
    return final.astype(jnp.bfloat16)


def sigmoid(values):
    return 0.5 * jnp.tanh(0.5 * values) + 0.5


def row_norm(values, norm_gain, norm_bias):
    count = values.shape[1]
    centre = values - jnp.sum(values, axis=1, keepdims=True) * (1.0 / count)
    squares = jnp.sum(centre * centre, axis=1, keepdims=True)
    return centre * lax.rsqrt(squares + 1e-05 * count) * (norm_gain * count**0.5) + norm_bias


def dot(left, right):
    return jnp.dot(left, right, preferred_element_type=jnp.float32)


def rounded(values):
    return values.astype(jnp.bfloat16).astype(jnp.float32)


def chip_and_core():
    device = lax.axis_index("row")
    return lax.shift_right_logical(device, 1), jnp.bitwise_and(device, 1)


def rows_of_blocks(row_count, blocks):
    chip, _ = chip_and_core()
    return [(jnp.bitwise_xor(chip, bits), r) for bits in blocks for r in range(row_count)]


def edges_kernel(
    row_count, chips, pieces, send_row, makes_heads, valid_column, norms, weights, *refs
):
    pair_refs = refs[: len(pieces)]
    left_ref, right_ref, gate_ref, pairs_ref, send_ref = refs[-5:]
    if makes_heads:
        left_ref, right_ref, gate_ref, pairs_ref, send_ref, same_head_ref = refs[-6:]
        wide = same_head_ref.shape
        row = lax.broadcasted_iota(jnp.int32, wide, 0) // HEAD_DIM
        column = lax.broadcasted_iota(jnp.int32, wide, 1) // HEAD_DIM
        same_head_ref[...] = jnp.where(row == column, 1.0, 0.0).astype(jnp.bfloat16)
    f32, bf16 = jnp.float32, jnp.bfloat16
    res, channels = valid_column.shape
    _, core = chip_and_core()
    pairs = jnp.concatenate(
        [ref[...].astype(f32).reshape(-1, channels) for ref in pair_refs], axis=0
    )
    normed = row_norm(pairs, norms[0:1, :], norms[1:2, :]).astype(bf16)
    column = 0.5 * valid_column[...]
    rows_of = rows_of_blocks(row_count, [bits for piece in pieces for bits in piece])
    masks = jnp.concatenate(
        [
            column * valid_column[pl.ds((2 * chip + core) * row_count + r, 1), :]
            for chip, r in rows_of
        ],
        axis=0,
    )
    joined = dot(normed, weights[:, : 2 * channels])
    left = rounded((jnp.tanh(joined[:, channels:]) + 1.0) * joined[:, :channels] * masks)
    joined = dot(normed, weights[:, 2 * channels : 4 * channels])
    right = ((jnp.tanh(joined[:, channels:]) + 1.0) * joined[:, :channels] * masks).astype(bf16)
    gate = 0.5 * jnp.tanh(dot(normed, weights[:, 4 * channels :])) + 0.5
    for n, (chip, r) in enumerate(rows_of):
        rows = slice(n * res, (n + 1) * res)
        start = pl.multiple_of((chip * row_count + r) * res, res)
        send_ref[send_row + n] = right[rows]
        left_ref[pl.ds(start, res), :] = left[rows]
        place_right(right_ref, chips, chip, r, right[rows])
        gate_ref[pl.ds(start, res), :] = gate[rows]
        pairs_ref[pl.ds(start, res), :] = pairs[rows]


def place_right(right_ref, chips, chip, r, edges):
    res = edges.shape[0]
    start = pl.multiple_of((r * chips + chip) * res, res)
    right_ref[pl.ds(start, res), :] = edges.astype(jnp.float32)


def join(even, odd, shift):
    high = jnp.bitwise_and(lax.broadcasted_iota(jnp.int32, even.shape, 0), shift) > 0
    return jnp.where(high, odd, even) + pltpu.roll(jnp.where(high, even, odd), shift, 0)


def triangle_rows(
    row_count, chips, left_ref, right_ref, triangle_ref, first, count, core, triangle_first
):
    res = 2 * row_count * chips
    start = pl.multiple_of(first * res, res)
    block = 4
    for n in range(0, count, block):
        lefts = [left_ref[pl.ds(start + m * res, res), :] for m in range(n, n + block)]
        for r in range(row_count):
            sums = [[] for _ in range(block)]
            for chip in range(chips):
                at = (r * chips + chip) * res
                right = right_ref[at : at + res, :]
                for m in range(block):
                    product = lefts[m] * right
                    part = sum((product[k : k + 8] for k in range(8, res, 8)), product[:8])
                    shift = 1
                    while chip & shift:
                        part = join(sums[m].pop(), part, shift)
                        shift *= 2
                    sums[m].append(part)
            for m in range(block):
                place = (triangle_first + n + m) * res + core * row_count + r
                triangle_ref[pl.ds(place, chips, stride=2 * row_count), :] = rounded(sums[m][0])


def near_triangle_kernel(row_count, chips, chunk, pieces, left_ref, right_ref, *refs):
    received, (triangle_ref, across_ref) = refs[:-2], refs[-2:]
    _, core = chip_and_core()

    def some_rows(step, carry):
        first = step * chunk
        triangle_rows(
            row_count, chips, left_ref, right_ref, triangle_ref, first, chunk, core, first
        )
        return carry

    for ref, blocks in zip(received, pieces):
        for n, (chip, r) in enumerate(rows_of_blocks(row_count, blocks)):
            place_right(across_ref, chips, chip, r, ref[n])
    lax.fori_loop(0, row_count * chips // chunk, some_rows, 0)


def attention_inputs(
    row_count, chips, first, norms, w_out, left_ref, gate_ref, pairs_ref, held_triangle, across_ref,
    triangle_ref,
):
    bf16 = jnp.bfloat16
    _, core = chip_and_core()
    half = row_count * chips
    tall = (half // 2) * 2 * half
    rows = pl.ds(pl.multiple_of(first * 2 * half, tall), tall)
    triangle_ref[...] = held_triangle[rows, :]
    triangle_rows(
        row_count, chips, left_ref, across_ref, triangle_ref, first, half // 2, 1 - core, 0
    )
    tri_normed = row_norm(triangle_ref[...], norms[2:3, :], norms[3:4, :]).astype(bf16)
    after_tri = pairs_ref[rows, :] + gate_ref[rows, :] * dot(tri_normed, w_out[...])
    att_in = row_norm(after_tri, norms[4:5, :], norms[5:6, :]).astype(bf16)
    return after_tri, att_in


def first_chip(chips, part):
    chip, _ = chip_and_core()
    return jnp.bitwise_xor(jnp.bitwise_and(chip, chips // 2), part * (chips // 2))


def own_inputs_kernel(
    row_count,
    chips,
    blocks,
    norms,
    w_out,
    left_ref,
    gate_ref,
    pairs_ref,
    received,
    triangle_ref,
    held_across,
    across_ref,
    after_ref,
    att_ref,
    scratch_ref,
):
    for n, (chip, r) in enumerate(rows_of_blocks(row_count, blocks)):
        place_right(across_ref, chips, chip, r, received[n])
    first = first_chip(chips, 0) * row_count
    refs = (left_ref, gate_ref, pairs_ref, triangle_ref, across_ref, scratch_ref)
    after_ref[...], att_ref[...] = attention_inputs(
        row_count, chips, first, norms, w_out, *refs
    )


def other_inputs_kernel(row_count, chips, norms, w_out, *refs):
    *refs, att_ref, scratch_ref = refs
    first = first_chip(chips, 1) * row_count
    _, att_ref[...] = attention_inputs(row_count, chips, first, norms, w_out, *refs, scratch_ref)


def keys_and_values(att, w_key, w_value, key_ref, value_ref):
    channels = key_ref.shape[1]
    key_value = jnp.concatenate([w_key[...], w_value[...]], axis=1)
    start = 0
    for values in att:
        rows = slice(start, start + values.shape[0])
        joined = dot(values, key_value)
        key_ref[rows, :] = rounded(joined[:, :channels])
        value_ref[rows, :] = rounded(joined[:, channels:])
        start = rows.stop


def column_bias(row_count, res, att, wide_bias, att_ref, bias_ref):
    start = 0
    for values in att:
        att_ref[start : start + values.shape[0], :] = values.astype(jnp.float32)
        start += values.shape[0]
    keys = start // res
    own = lax.axis_index("row") * row_count
    height = -(-keys // 8) * 8
    columns = [att_ref[pl.ds(own + r, height, stride=res), :] for r in range(row_count)]
    columns = jnp.concatenate(columns, axis=0).astype(jnp.bfloat16)
    bias = rounded(dot(columns, wide_bias[...]))
    for r in range(row_count):
        bias_ref[r, :height, :] = bias[r * height : (r + 1) * height]


def partial_attention(
    row_count, chips, query, parts, bias_ref, same_head, valid_column, sums, together
):
    bf16 = jnp.bfloat16
    res = 2 * row_count * chips
    channels = valid_column.shape[1]
    count = row_count * chips // 2
    for part, (core, first, key_of, value_of) in enumerate(parts):
        products = []
        for r in range(row_count):
            own_query = query[r * res : (r + 1) * res]
            row = [(key_of(n) * own_query).astype(bf16) for n in range(count)]
            pairs = [jnp.concatenate(row[n : n + 2], axis=1) for n in range(0, count, 2)]
            products.append(jnp.concatenate(pairs, axis=0))
        if together:
            scores = dot(jnp.concatenate(products, axis=0), same_head[...])
            tall = count // 2 * res
            scores = [scores[r * tall : (r + 1) * tall] for r in range(row_count)]
        else:
            scores = [dot(product, same_head[...]) for product in products]

        def score_of(n, r):
            lanes = slice(n % 2 * channels, (n % 2 + 1) * channels)
            k = (2 * (first + n // row_count) + core) * row_count + n % row_count
            key_mask = 1000000000.0 * (valid_column[pl.ds(k, 1), :] - 1.0)
            at = part * count + n
            shift = (bias_ref[r, at : at + 1, :] + key_mask) * math.log2(math.e)
            return scores[r][n // 2 * res : (n // 2 + 1) * res, lanes] + shift

        later = []
        for r, (maximum, total, mixed) in enumerate(sums):
            highest = score_of(0, r)
            for n in range(1, count):
                highest = jnp.maximum(highest, score_of(n, r))
            if maximum is None:
                maximum, total, mixed = highest, 0.0, 0.0
            else:
                highest = jnp.maximum(highest, maximum)
                scale = jnp.exp2(maximum - highest)
                maximum, total, mixed = highest, total * scale, mixed * scale
            for n in range(count):
                weight = jnp.exp2(score_of(n, r) - maximum)
                total = total + weight
                mixed = mixed + weight * value_of(n)
            later.append((maximum, total, mixed))
        sums = later
    return sums


def most_attention_kernel(
    row_count,
    chips,
    valid_column,
    same_head,
    w_query,
    w_gate,
    w_key,
    w_value,
    wide_bias,
    own_att_a,
    own_att_b,
    far_att_a,
    own_after,
    sums_ref,
    query_ref,
    gate_ref,
    after_ref,
    att_ref,
    key_ref,
    value_ref,
    bias_ref,
):
    chip, core = chip_and_core()
    res, channels = valid_column.shape
    own = row_count * res
    rows = pl.ds(pl.multiple_of(jnp.bitwise_and(chip, chips // 2 - 1) * own, own), own)
    own_in = own_att_a[rows, :]
    query = rounded(dot(own_in, w_query[...])) * (math.log2(math.e) / math.sqrt(HEAD_DIM))
    att = [ref[...] for ref in (own_att_a, own_att_b, far_att_a)]
    keys_and_values(att, w_key, w_value, key_ref, value_ref)
    column_bias(row_count, res, att, wide_bias, att_ref, bias_ref)
    count = row_count * chips // 2

    def rows_of(ref, first):
        return lambda n: ref[(first + n) * res : (first + n + 1) * res, :]

    a, b = first_chip(chips, 0), first_chip(chips, 1)
    parts = [
        (sender, first, rows_of(key_ref, n * count), rows_of(value_ref, n * count))
        for n, (sender, first) in enumerate(((core, a), (core, b), (1 - core, a)))
    ]
    none = [(None, None, None)] * row_count
    sums = partial_attention(
        row_count, chips, query, parts, bias_ref, same_head, valid_column, none, True
    )
    for r in range(row_count):
        for n, each in enumerate(sums[r]):
            sums_ref[r, n] = each
    query_ref[...] = query
    gate_ref[...] = sigmoid(dot(own_in, w_gate[...]))
    after_ref[...] = own_after[rows, :]


def attention_kernel(
    row_count,
    chips,
    valid_column,
    same_head,
    w_key,
    w_value,
    w_out,
    wide_bias,
    far_att_b,
    query_ref,
    gate_ref,
    after_ref,
    sums_ref,
    out_ref,
    att_ref,
    key_ref,
    value_ref,
    bias_ref,
):
    _, core = chip_and_core()
    res, channels = valid_column.shape
    far_att = far_att_b[...]
    keys_and_values([far_att], w_key, w_value, key_ref, value_ref)
    column_bias(row_count, res, [far_att], wide_bias, att_ref, bias_ref)

    def rows_of(ref):
        return lambda n: ref[n * res : (n + 1) * res, :]

    parts = ((1 - core, first_chip(chips, 1), rows_of(key_ref), rows_of(value_ref)),)
    sums = [tuple(sums_ref[r, n] for n in range(3)) for r in range(row_count)]
    sums = partial_attention(
        row_count, chips, query_ref[...], parts, bias_ref, same_head, valid_column, sums, False
    )
    attended = [mixed / total for _, total, mixed in sums]
    gated = (jnp.concatenate(attended, axis=0) * gate_ref[...]).astype(jnp.bfloat16)
    final = after_ref[...] + dot(gated, w_out[...])
    out_ref[...] = final.astype(jnp.bfloat16).reshape(row_count, res, channels)


def on_whole_complex(
    pair_rep,
    residue_valid,
    tri_norm_gain,
    tri_norm_bias,
    w_edges,
    w_tri_gate,
    out_norm_gain,
    out_norm_bias,
    w_tri_out,
    att_norm_gain,
    att_norm_bias,
    w_query,
    w_key,
    w_value,
    w_att_gate,
    w_pair_bias,
    w_att_out,
):
    row_count, res, channels = pair_rep.shape
    devices = res // row_count
    chips = devices // 2
    half = res // 2
    f32, bf16 = jnp.float32, jnp.bfloat16
    in_vmem = pl.BlockSpec(memory_space=pltpu.VMEM)

    def shaped(dtype, *shape):
        return jax.ShapeDtypeStruct(shape, dtype)

    def call(kernel, outs, operands, aliases=None, scratch=(), cost=2**25):
        return pl.pallas_call(
            kernel,
            out_shape=outs,
            in_specs=[in_vmem] * len(operands),
            out_specs=jax.tree.map(lambda _: in_vmem, outs),
            input_output_aliases=aliases or {},
            scratch_shapes=list(scratch),
            compiler_params=pltpu.CompilerParams(vmem_limit_bytes=24 * 1024 * 1024),
            cost_estimate=pl.CostEstimate(flops=2**20, bytes_accessed=cost, transcendentals=0),
        )(*operands)

    def exchange(values, bit):
        return lax.ppermute(values, "row", [(d, d ^ bit) for d in range(devices)])

    vectors = (
        tri_norm_gain,
        tri_norm_bias,
        out_norm_gain,
        out_norm_bias,
        att_norm_gain,
        att_norm_bias,
    )
    norms = jnp.stack(vectors)
    is_gate = lax.broadcasted_iota(jnp.int32, (1, 5 * channels), 1) // channels
    halves = jnp.where((is_gate == 0) | (is_gate == 2), 1.0, 0.5).astype(bf16)
    edge_weights = jnp.concatenate([w_edges, w_tri_gate], axis=1) * halves
    valid_column = jnp.broadcast_to(residue_valid.astype(f32)[:, None], (res, channels))

    head = lax.broadcasted_iota(jnp.int32, (HEADS, channels), 0)
    head_of_channel = lax.broadcasted_iota(jnp.int32, (HEADS, channels), 1) // HEAD_DIM
    repeat = jnp.where(head == head_of_channel, 1.0, 0.0).astype(bf16)
    wide_bias = dot(w_pair_bias, repeat).astype(bf16)

    kept = lax.dynamic_update_slice(
        jnp.zeros((2 * row_count, res, channels), bf16), pair_rep, (0, 0, 0)
    )
    far = exchange(pair_rep, devices // 2)
    near_own = exchange(pair_rep, 4)
    far, near_own, kept, norms, edge_weights = lax.optimization_barrier(
        (far, near_own, kept, norms, edge_weights)
    )
    own = lax.dynamic_update_slice(kept, far, (row_count, 0, 0))
    own_blocks = (0, chips // 2)

    def blocks_from(bits):
        return tuple(s ^ bits for s in own_blocks)

    tall = shaped(f32, half * res, channels)

    def edges_of(pieces, send_row, *held):
        pairs = tuple(p for p, _ in pieces)
        blocks = tuple(b for _, b in pieces)
        sent = (3 if held and send_row == 0 else 5) * row_count
        operands = (valid_column, norms, edge_weights) + pairs + held
        first = len(operands) - len(held)
        return call(
            functools.partial(edges_kernel, row_count, chips, blocks, send_row, not held),
            (tall, tall, tall, tall, shaped(bf16, sent, res, channels))
            + (() if held else (shaped(bf16, 2 * channels, 2 * channels),)),
            operands,
            {first + e: e for e in range(len(held))},
        )

    diagonal = exchange(own, 6)
    beside = exchange(own, 2)
    near_far = exchange(far, 4)
    *edges, early_right, same_head = edges_of([(own, own_blocks), (near_own, (2,))], 0)
    diagonal, edges, early_right = lax.optimization_barrier((diagonal, edges, early_right))
    *edges, early_right = edges_of(
        [(diagonal, blocks_from(3))], 3 * row_count, *edges, early_right
    )
    beside, edges, early_right, wide_bias = lax.optimization_barrier(
        (beside, edges, early_right, wide_bias)
    )
    early = (exchange(early_right, 1), own_blocks + (2,) + blocks_from(3))
    *edges, late_right = edges_of([(beside, blocks_from(1)), (near_far, (6,))], 0, *edges)
    late = (exchange(late_right, 1), blocks_from(1) + (6,))

    left, right, gate, pairs = edges
    triangle, across = call(
        functools.partial(near_triangle_kernel, row_count, chips, half // 2, [early[1]]),
        (tall, tall),
        (left, right, early[0]),
    )
    part = half // 2 * res
    in_part, own_shape = shaped(f32, part, channels), shaped(f32, row_count * res, channels)
    att_part = shaped(bf16, part, channels)
    shared = (norms, w_tri_out, left, gate, pairs)
    scratch = (pltpu.VMEM((part, channels), f32),)
    across, after_a, att_a = call(
        functools.partial(own_inputs_kernel, row_count, chips, late[1]),
        (tall, in_part, att_part),
        shared + (late[0], triangle, across),
        {7: 0},
        scratch=scratch,
    )
    far_att_a = exchange(att_a, 1)
    att_b = call(
        functools.partial(other_inputs_kernel, row_count, chips),
        att_part,
        shared + (triangle, across),
        scratch=scratch,
    )
    far_att_b = exchange(att_b, 1)

    def attention_scratch(keys, projected):
        return (
            pltpu.VMEM((-(-keys // 8) * 8 * res, channels), f32),
            pltpu.VMEM((projected * res, channels), f32),
            pltpu.VMEM((projected * res, channels), f32),
            pltpu.VMEM((row_count, 40, channels), f32),
        )

    sums, query, att_gate, after_own = call(
        functools.partial(most_attention_kernel, row_count, chips),
        (shaped(f32, row_count, 3, res, channels), own_shape, own_shape, own_shape),
        (valid_column, same_head, w_query, w_att_gate, w_key, w_value, wide_bias)
        + (att_a, att_b, far_att_a, after_a),
        scratch=attention_scratch(3 * half // 2, 3 * half // 2),
    )
    return call(
        functools.partial(attention_kernel, row_count, chips),
        shaped(bf16, *pair_rep.shape),
        (valid_column, same_head, w_key, w_value, w_att_out, wide_bias, far_att_b)
        + (query, att_gate, after_own, sums),
        scratch=attention_scratch(half // 2, half // 2),
    )


def per_device(pair_rep, residue_valid, *parameters):
    row_count, res, channels = pair_rep.shape
    devices = res // row_count
    if res % 48 == 0 and devices == 16 and 40 * res * res * channels <= 32 * 1024 * 1024:
        return on_whole_complex(pair_rep, residue_valid, *parameters)
    return split_over_devices(pair_rep, residue_valid, *parameters)


def solution(mesh):
    return jax.shard_map(
        per_device,
        mesh=mesh,
        in_specs=(
            P(("groups", "row"), None, None),
            P("groups"),
            P(),
            P(),
            P(),
            P(),
            P(),
            P(),
            P(),
            P(),
            P(),
            P(),
            P(),
            P(),
            P(),
            P(),
            P(),
        ),
        out_specs=P(("groups", "row"), None, None),
        check_vma=False,
    )
```

```python
import functools
import math

import jax
import jax.numpy as jnp
from jax import lax
from jax.experimental import pallas as pl
from jax.experimental.pallas import tpu as pltpu
from jax.sharding import PartitionSpec as P

HEADS = 4
HEAD_DIM = 32


def layer_norm(values, norm_gain, norm_bias, along_axis):
    centre = values - jnp.mean(values, axis=along_axis, keepdims=True)
    spread = jnp.mean(centre * centre, axis=along_axis, keepdims=True)
    return centre * lax.rsqrt(spread + 1e-05) * norm_gain + norm_bias


def attend(query_cols, key_cols, value_cols, whole_bias, key_mask):
    factor = 1.0 / math.sqrt(HEAD_DIM)
    scores = (
        jnp.einsum("kjhd,ijhd->jhki", key_cols, query_cols, preferred_element_type=jnp.float32)
        * factor
    )
    scores = scores + whole_bias.astype(jnp.float32)[None] + key_mask[None, None, :, None]
    scores = scores - jnp.max(scores, axis=2, keepdims=True)
    exponent = jnp.exp(scores)
    weights = (exponent / jnp.sum(exponent, axis=2, keepdims=True)).astype(jnp.bfloat16)
    return jnp.einsum("jhki,kjhd->ijhd", weights, value_cols, preferred_element_type=jnp.float32)


def split_over_devices(
    pair_rep,
    residue_valid,
    tri_norm_gain,
    tri_norm_bias,
    w_edges,
    w_tri_gate,
    out_norm_gain,
    out_norm_bias,
    w_tri_out,
    att_norm_gain,
    att_norm_bias,
    w_query,
    w_key,
    w_value,
    w_att_gate,
    w_pair_bias,
    w_att_out,
):
    row_count = pair_rep.shape[0]
    res_count = pair_rep.shape[1]
    channels = pair_rep.shape[2]
    hidden_width = HEADS * HEAD_DIM
    row_start = lax.axis_index("row") * row_count
    valid_flags = residue_valid.astype(jnp.float32)
    own_valid = lax.dynamic_slice_in_dim(valid_flags, row_start, row_count)
    normed = layer_norm(pair_rep.astype(jnp.float32), tri_norm_gain, tri_norm_bias, 2).astype(
        jnp.bfloat16
    )
    projected = jnp.einsum("ikd,de->eik", normed, w_edges, preferred_element_type=jnp.float32)
    projected = projected.reshape(4, channels, row_count, res_count)
    pair_mask = (own_valid[:, None] * valid_flags[None, :])[None, :, :]
    left_edges = (jax.nn.sigmoid(projected[1]) * projected[0] * pair_mask).astype(jnp.bfloat16)
    right_edges = (jax.nn.sigmoid(projected[3]) * projected[2] * pair_mask).astype(jnp.bfloat16)
    left_cols, right_cols = (
        lax.all_to_all(left_edges, "row", split_axis=0, concat_axis=1, tiled=True),
        lax.all_to_all(right_edges, "row", split_axis=0, concat_axis=1, tiled=True),
    )
    block_product = jnp.einsum(
        "cik,cjk->cij", left_cols, right_cols, preferred_element_type=jnp.float32
    ).astype(jnp.bfloat16)
    triangle = lax.all_to_all(block_product, "row", split_axis=1, concat_axis=0, tiled=True)
    tri_normed = layer_norm(
        triangle.astype(jnp.float32), out_norm_gain[:, None, None], out_norm_bias[:, None, None], 0
    ).astype(jnp.bfloat16)
    tri_gate = jax.nn.sigmoid(
        jnp.einsum("ijc,ce->ije", normed, w_tri_gate, preferred_element_type=jnp.float32)
    )
    tri_update = jnp.einsum(
        "cij,ce->ije", tri_normed, w_tri_out, preferred_element_type=jnp.float32
    )
    after_tri = pair_rep.astype(jnp.float32) + tri_gate * tri_update
    att_in = layer_norm(after_tri, att_norm_gain, att_norm_bias, 2).astype(jnp.bfloat16)
    pair_bias = jnp.einsum(
        "kic,ch->hki", att_in, w_pair_bias, preferred_element_type=jnp.float32
    ).astype(jnp.bfloat16)
    whole_bias = lax.all_gather(pair_bias, "row", axis=1, tiled=True)
    key_mask = 1000000000.0 * (valid_flags - 1.0)
    columns = lax.all_to_all(att_in, "row", split_axis=1, concat_axis=0, tiled=True)
    all_weights = jnp.concatenate([w_query, w_key, w_value, w_att_gate], axis=1)
    joined = jnp.dot(columns.reshape(-1, channels), all_weights, preferred_element_type=jnp.float32)
    query_cols = (
        joined[:, :hidden_width].astype(jnp.bfloat16).reshape(res_count, row_count, HEADS, HEAD_DIM)
    )
    key_cols = (
        joined[:, hidden_width : 2 * hidden_width]
        .astype(jnp.bfloat16)
        .reshape(res_count, row_count, HEADS, HEAD_DIM)
    )
    value_cols = (
        joined[:, 2 * hidden_width : 3 * hidden_width]
        .astype(jnp.bfloat16)
        .reshape(res_count, row_count, HEADS, HEAD_DIM)
    )
    gate_cols = jax.nn.sigmoid(joined[:, 3 * hidden_width :]).reshape(
        res_count, row_count, hidden_width
    )
    attended = attend(query_cols, key_cols, value_cols, whole_bias, key_mask)
    gated = (attended.reshape(res_count, row_count, hidden_width) * gate_cols).astype(jnp.bfloat16)
    gated_rows = lax.all_to_all(gated, "row", split_axis=0, concat_axis=1, tiled=True)
    final = after_tri + jnp.einsum(
        "ije,ec->ijc", gated_rows, w_att_out, preferred_element_type=jnp.float32
    )
    return final.astype(jnp.bfloat16)


def sigmoid(values):
    return 0.5 * jnp.tanh(0.5 * values) + 0.5


def row_norm(values, norm_gain, norm_bias):
    count = values.shape[1]
    centre = values - jnp.sum(values, axis=1, keepdims=True) * (1.0 / count)
    squares = jnp.sum(centre * centre, axis=1, keepdims=True)
    return centre * lax.rsqrt(squares + 1e-05 * count) * (norm_gain * count**0.5) + norm_bias


def dot(left, right):
    return jnp.dot(left, right, preferred_element_type=jnp.float32)


def rounded(values):
    return values.astype(jnp.bfloat16).astype(jnp.float32)


def chip_and_core():
    device = lax.axis_index("row")
    return lax.shift_right_logical(device, 1), jnp.bitwise_and(device, 1)


def rows_of_blocks(row_count, blocks):
    chip, _ = chip_and_core()
    return [(jnp.bitwise_xor(chip, bits), r) for bits in blocks for r in range(row_count)]


def edges_kernel(
    row_count, chips, pieces, send_row, makes_heads, valid_column, norms, weights, *refs
):
    pair_refs = refs[: len(pieces)]
    left_ref, right_ref, gate_ref, pairs_ref, send_ref = refs[-5:]
    if makes_heads:
        left_ref, right_ref, gate_ref, pairs_ref, send_ref, same_head_ref = refs[-6:]
        wide = same_head_ref.shape
        row = lax.broadcasted_iota(jnp.int32, wide, 0) // HEAD_DIM
        column = lax.broadcasted_iota(jnp.int32, wide, 1) // HEAD_DIM
        same_head_ref[...] = jnp.where(row == column, 1.0, 0.0).astype(jnp.bfloat16)
    f32, bf16 = jnp.float32, jnp.bfloat16
    res, channels = valid_column.shape
    _, core = chip_and_core()
    pairs = jnp.concatenate(
        [ref[...].astype(f32).reshape(-1, channels) for ref in pair_refs], axis=0
    )
    normed = row_norm(pairs, norms[0:1, :], norms[1:2, :]).astype(bf16)
    column = 0.5 * valid_column[...]
    rows_of = rows_of_blocks(row_count, [bits for piece in pieces for bits in piece])
    masks = jnp.concatenate(
        [
            column * valid_column[pl.ds((2 * chip + core) * row_count + r, 1), :]
            for chip, r in rows_of
        ],
        axis=0,
    )
    joined = dot(normed, weights[:, : 2 * channels])
    left = rounded((jnp.tanh(joined[:, channels:]) + 1.0) * joined[:, :channels] * masks)
    joined = dot(normed, weights[:, 2 * channels : 4 * channels])
    right = ((jnp.tanh(joined[:, channels:]) + 1.0) * joined[:, :channels] * masks).astype(bf16)
    gate = 0.5 * jnp.tanh(dot(normed, weights[:, 4 * channels :])) + 0.5
    for n, (chip, r) in enumerate(rows_of):
        rows = slice(n * res, (n + 1) * res)
        start = pl.multiple_of((chip * row_count + r) * res, res)
        send_ref[send_row + n] = right[rows]
        left_ref[pl.ds(start, res), :] = left[rows]
        place_right(right_ref, chips, chip, r, right[rows])
        gate_ref[pl.ds(start, res), :] = gate[rows]
        pairs_ref[pl.ds(start, res), :] = pairs[rows]


def place_right(right_ref, chips, chip, r, edges):
    res = edges.shape[0]
    start = pl.multiple_of((r * chips + chip) * res, res)
    right_ref[pl.ds(start, res), :] = edges.astype(jnp.float32)


def join(even, odd, shift):
    high = jnp.bitwise_and(lax.broadcasted_iota(jnp.int32, even.shape, 0), shift) > 0
    return jnp.where(high, odd, even) + pltpu.roll(jnp.where(high, even, odd), shift, 0)


def triangle_rows(
    row_count, chips, left_ref, right_ref, triangle_ref, first, count, core, triangle_first
):
    res = 2 * row_count * chips
    start = pl.multiple_of(first * res, res)
    block = 4
    for n in range(0, count, block):
        lefts = [left_ref[pl.ds(start + m * res, res), :] for m in range(n, n + block)]
        for r in range(row_count):
            sums = [[] for _ in range(block)]
            for chip in range(chips):
                at = (r * chips + chip) * res
                right = right_ref[at : at + res, :]
                for m in range(block):
                    product = lefts[m] * right
                    part = sum((product[k : k + 8] for k in range(8, res, 8)), product[:8])
                    shift = 1
                    while chip & shift:
                        part = join(sums[m].pop(), part, shift)
                        shift *= 2
                    sums[m].append(part)
            for m in range(block):
                place = (triangle_first + n + m) * res + core * row_count + r
                triangle_ref[pl.ds(place, chips, stride=2 * row_count), :] = rounded(sums[m][0])


def near_triangle_kernel(row_count, chips, chunk, pieces, left_ref, right_ref, *refs):
    received, (triangle_ref, across_ref) = refs[:-2], refs[-2:]
    _, core = chip_and_core()

    def some_rows(step, carry):
        first = step * chunk
        triangle_rows(
            row_count, chips, left_ref, right_ref, triangle_ref, first, chunk, core, first
        )
        return carry

    for ref, blocks in zip(received, pieces):
        for n, (chip, r) in enumerate(rows_of_blocks(row_count, blocks)):
            place_right(across_ref, chips, chip, r, ref[n])
    lax.fori_loop(0, row_count * chips // chunk, some_rows, 0)


def attention_inputs(
    row_count, chips, first, norms, w_out, left_ref, gate_ref, pairs_ref, held_triangle, across_ref,
    triangle_ref,
):
    bf16 = jnp.bfloat16
    _, core = chip_and_core()
    half = row_count * chips
    tall = (half // 2) * 2 * half
    rows = pl.ds(pl.multiple_of(first * 2 * half, tall), tall)
    triangle_ref[...] = held_triangle[rows, :]
    triangle_rows(
        row_count, chips, left_ref, across_ref, triangle_ref, first, half // 2, 1 - core, 0
    )
    tri_normed = row_norm(triangle_ref[...], norms[2:3, :], norms[3:4, :]).astype(bf16)
    after_tri = pairs_ref[rows, :] + gate_ref[rows, :] * dot(tri_normed, w_out[...])
    att_in = row_norm(after_tri, norms[4:5, :], norms[5:6, :]).astype(bf16)
    return after_tri, att_in


def first_chip(chips, part):
    chip, _ = chip_and_core()
    return jnp.bitwise_xor(jnp.bitwise_and(chip, chips // 2), part * (chips // 2))


def own_inputs_kernel(
    row_count,
    chips,
    blocks,
    norms,
    w_out,
    left_ref,
    gate_ref,
    pairs_ref,
    received,
    triangle_ref,
    held_across,
    across_ref,
    after_ref,
    att_ref,
    scratch_ref,
):
    for n, (chip, r) in enumerate(rows_of_blocks(row_count, blocks)):
        place_right(across_ref, chips, chip, r, received[n])
    first = first_chip(chips, 0) * row_count
    refs = (left_ref, gate_ref, pairs_ref, triangle_ref, across_ref, scratch_ref)
    after_ref[...], att_ref[...] = attention_inputs(
        row_count, chips, first, norms, w_out, *refs
    )


def other_inputs_kernel(row_count, chips, norms, w_out, *refs):
    *refs, att_ref, scratch_ref = refs
    first = first_chip(chips, 1) * row_count
    _, att_ref[...] = attention_inputs(row_count, chips, first, norms, w_out, *refs, scratch_ref)


def keys_and_values(att, w_key, w_value, key_ref, value_ref):
    channels = key_ref.shape[1]
    key_value = jnp.concatenate([w_key[...], w_value[...]], axis=1)
    start = 0
    for values in att:
        rows = slice(start, start + values.shape[0])
        joined = dot(values, key_value)
        key_ref[rows, :] = rounded(joined[:, :channels])
        value_ref[rows, :] = rounded(joined[:, channels:])
        start = rows.stop


def column_bias(row_count, res, att, wide_bias, att_ref, bias_ref):
    start = 0
    for values in att:
        att_ref[start : start + values.shape[0], :] = values.astype(jnp.float32)
        start += values.shape[0]
    keys = start // res
    own = lax.axis_index("row") * row_count
    height = -(-keys // 8) * 8
    columns = [att_ref[pl.ds(own + r, height, stride=res), :] for r in range(row_count)]
    columns = jnp.concatenate(columns, axis=0).astype(jnp.bfloat16)
    bias = rounded(dot(columns, wide_bias[...]))
    for r in range(row_count):
        bias_ref[r, :height, :] = bias[r * height : (r + 1) * height]


def partial_attention(
    row_count, chips, query, parts, bias_ref, same_head, valid_column, sums, together
):
    bf16 = jnp.bfloat16
    res = 2 * row_count * chips
    channels = valid_column.shape[1]
    count = row_count * chips // 2
    for part, (core, first, key_of, value_of) in enumerate(parts):
        products = []
        for r in range(row_count):
            own_query = query[r * res : (r + 1) * res]
            row = [(key_of(n) * own_query).astype(bf16) for n in range(count)]
            pairs = [jnp.concatenate(row[n : n + 2], axis=1) for n in range(0, count, 2)]
            products.append(jnp.concatenate(pairs, axis=0))
        if together:
            scores = dot(jnp.concatenate(products, axis=0), same_head[...])
            tall = count // 2 * res
            scores = [scores[r * tall : (r + 1) * tall] for r in range(row_count)]
        else:
            scores = [dot(product, same_head[...]) for product in products]

        def score_of(n, r):
            lanes = slice(n % 2 * channels, (n % 2 + 1) * channels)
            k = (2 * (first + n // row_count) + core) * row_count + n % row_count
            key_mask = 1000000000.0 * (valid_column[pl.ds(k, 1), :] - 1.0)
            at = part * count + n
            shift = (bias_ref[r, at : at + 1, :] + key_mask) * math.log2(math.e)
            return scores[r][n // 2 * res : (n // 2 + 1) * res, lanes] + shift

        later = []
        for r, (maximum, total, mixed) in enumerate(sums):
            highest = score_of(0, r)
            for n in range(1, count):
                highest = jnp.maximum(highest, score_of(n, r))
            if maximum is None:
                maximum, total, mixed = highest, 0.0, 0.0
            else:
                highest = jnp.maximum(highest, maximum)
                scale = jnp.exp2(maximum - highest)
                maximum, total, mixed = highest, total * scale, mixed * scale
            for n in range(count):
                weight = jnp.exp2(score_of(n, r) - maximum)
                total = total + weight
                mixed = mixed + weight * value_of(n)
            later.append((maximum, total, mixed))
        sums = later
    return sums


def most_attention_kernel(
    row_count,
    chips,
    valid_column,
    same_head,
    w_query,
    w_gate,
    w_key,
    w_value,
    wide_bias,
    own_att_a,
    own_att_b,
    far_att_a,
    own_after,
    sums_ref,
    query_ref,
    gate_ref,
    after_ref,
    att_ref,
    key_ref,
    value_ref,
    bias_ref,
):
    chip, core = chip_and_core()
    res, channels = valid_column.shape
    own = row_count * res
    rows = pl.ds(pl.multiple_of(jnp.bitwise_and(chip, chips // 2 - 1) * own, own), own)
    own_in = own_att_a[rows, :]
    query = rounded(dot(own_in, w_query[...])) * (math.log2(math.e) / math.sqrt(HEAD_DIM))
    att = [ref[...] for ref in (own_att_a, own_att_b, far_att_a)]
    keys_and_values(att, w_key, w_value, key_ref, value_ref)
    column_bias(row_count, res, att, wide_bias, att_ref, bias_ref)
    count = row_count * chips // 2

    def rows_of(ref, first):
        return lambda n: ref[(first + n) * res : (first + n + 1) * res, :]

    a, b = first_chip(chips, 0), first_chip(chips, 1)
    parts = [
        (sender, first, rows_of(key_ref, n * count), rows_of(value_ref, n * count))
        for n, (sender, first) in enumerate(((core, a), (core, b), (1 - core, a)))
    ]
    none = [(None, None, None)] * row_count
    sums = partial_attention(
        row_count, chips, query, parts, bias_ref, same_head, valid_column, none, True
    )
    for r in range(row_count):
        for n, each in enumerate(sums[r]):
            sums_ref[r, n] = each
    query_ref[...] = query
    gate_ref[...] = sigmoid(dot(own_in, w_gate[...]))
    after_ref[...] = own_after[rows, :]


def attention_kernel(
    row_count,
    chips,
    valid_column,
    same_head,
    w_key,
    w_value,
    w_out,
    wide_bias,
    far_att_b,
    query_ref,
    gate_ref,
    after_ref,
    sums_ref,
    out_ref,
    att_ref,
    key_ref,
    value_ref,
    bias_ref,
):
    _, core = chip_and_core()
    res, channels = valid_column.shape
    far_att = far_att_b[...]
    keys_and_values([far_att], w_key, w_value, key_ref, value_ref)
    column_bias(row_count, res, [far_att], wide_bias, att_ref, bias_ref)

    def rows_of(ref):
        return lambda n: ref[n * res : (n + 1) * res, :]

    parts = ((1 - core, first_chip(chips, 1), rows_of(key_ref), rows_of(value_ref)),)
    sums = [tuple(sums_ref[r, n] for n in range(3)) for r in range(row_count)]
    sums = partial_attention(
        row_count, chips, query_ref[...], parts, bias_ref, same_head, valid_column, sums, False
    )
    attended = [mixed / total for _, total, mixed in sums]
    gated = (jnp.concatenate(attended, axis=0) * gate_ref[...]).astype(jnp.bfloat16)
    final = after_ref[...] + dot(gated, w_out[...])
    out_ref[...] = final.astype(jnp.bfloat16).reshape(row_count, res, channels)


def on_whole_complex(
    pair_rep,
    residue_valid,
    tri_norm_gain,
    tri_norm_bias,
    w_edges,
    w_tri_gate,
    out_norm_gain,
    out_norm_bias,
    w_tri_out,
    att_norm_gain,
    att_norm_bias,
    w_query,
    w_key,
    w_value,
    w_att_gate,
    w_pair_bias,
    w_att_out,
):
    row_count, res, channels = pair_rep.shape
    devices = res // row_count
    chips = devices // 2
    half = res // 2
    f32, bf16 = jnp.float32, jnp.bfloat16
    in_vmem = pl.BlockSpec(memory_space=pltpu.VMEM)

    def shaped(dtype, *shape):
        return jax.ShapeDtypeStruct(shape, dtype)

    def call(kernel, outs, operands, aliases=None, scratch=(), cost=2**25):
        return pl.pallas_call(
            kernel,
            out_shape=outs,
            in_specs=[in_vmem] * len(operands),
            out_specs=jax.tree.map(lambda _: in_vmem, outs),
            input_output_aliases=aliases or {},
            scratch_shapes=list(scratch),
            compiler_params=pltpu.CompilerParams(vmem_limit_bytes=24 * 1024 * 1024),
            cost_estimate=pl.CostEstimate(flops=2**20, bytes_accessed=cost, transcendentals=0),
        )(*operands)

    def exchange(values, bit):
        return lax.ppermute(values, "row", [(d, d ^ bit) for d in range(devices)])

    vectors = (
        tri_norm_gain,
        tri_norm_bias,
        out_norm_gain,
        out_norm_bias,
        att_norm_gain,
        att_norm_bias,
    )
    norms = jnp.stack(vectors)
    is_gate = lax.broadcasted_iota(jnp.int32, (1, 5 * channels), 1) // channels
    halves = jnp.where((is_gate == 0) | (is_gate == 2), 1.0, 0.5).astype(bf16)
    edge_weights = jnp.concatenate([w_edges, w_tri_gate], axis=1) * halves
    valid_column = jnp.broadcast_to(residue_valid.astype(f32)[:, None], (res, channels))

    head = lax.broadcasted_iota(jnp.int32, (HEADS, channels), 0)
    head_of_channel = lax.broadcasted_iota(jnp.int32, (HEADS, channels), 1) // HEAD_DIM
    repeat = jnp.where(head == head_of_channel, 1.0, 0.0).astype(bf16)
    wide_bias = dot(w_pair_bias, repeat).astype(bf16)

    kept = lax.dynamic_update_slice(
        jnp.zeros((2 * row_count, res, channels), bf16), pair_rep, (0, 0, 0)
    )
    far = exchange(pair_rep, devices // 2)
    far, kept, norms, edge_weights = lax.optimization_barrier((far, kept, norms, edge_weights))
    own = lax.dynamic_update_slice(kept, far, (row_count, 0, 0))
    own_blocks = (0, chips // 2)

    def blocks_from(bits):
        return tuple(s ^ bits for s in own_blocks)

    tall = shaped(f32, half * res, channels)

    def edges_of(pieces, send_row, *held):
        pairs = tuple(p for p, _ in pieces)
        blocks = tuple(b for _, b in pieces)
        operands = (valid_column, norms, edge_weights) + pairs + held
        first = len(operands) - len(held)
        return call(
            functools.partial(edges_kernel, row_count, chips, blocks, send_row, not held),
            (tall, tall, tall, tall, shaped(bf16, 4 * row_count, res, channels))
            + (() if held else (shaped(bf16, 2 * channels, 2 * channels),)),
            operands,
            {first + e: e for e in range(len(held))},
        )

    diagonal = exchange(own, 6)
    near = exchange(own, 4)
    beside = exchange(own, 2)
    *edges, early_right, same_head = edges_of([(own, own_blocks)], 0)
    diagonal, edges = lax.optimization_barrier((diagonal, edges))
    *edges, early_right = edges_of(
        [(diagonal, blocks_from(3))], 2 * row_count, *edges, early_right
    )
    near, edges, early_right, wide_bias = lax.optimization_barrier(
        (near, edges, early_right, wide_bias)
    )
    early = (exchange(early_right, 1), own_blocks + blocks_from(3))
    *edges, late_right = edges_of(
        [(near, blocks_from(2)), (beside, blocks_from(1))], 0, *edges
    )
    late = (exchange(late_right, 1), blocks_from(2) + blocks_from(1))

    left, right, gate, pairs = edges
    triangle, across = call(
        functools.partial(near_triangle_kernel, row_count, chips, half // 2, [early[1]]),
        (tall, tall),
        (left, right, early[0]),
    )
    part = half // 2 * res
    in_part, own_shape = shaped(f32, part, channels), shaped(f32, row_count * res, channels)
    att_part = shaped(bf16, part, channels)
    shared = (norms, w_tri_out, left, gate, pairs)
    scratch = (pltpu.VMEM((part, channels), f32),)
    across, after_a, att_a = call(
        functools.partial(own_inputs_kernel, row_count, chips, late[1]),
        (tall, in_part, att_part),
        shared + (late[0], triangle, across),
        {7: 0},
        scratch=scratch,
    )
    far_att_a = exchange(att_a, 1)
    att_b = call(
        functools.partial(other_inputs_kernel, row_count, chips),
        att_part,
        shared + (triangle, across),
        scratch=scratch,
    )
    far_att_b = exchange(att_b, 1)

    def attention_scratch(keys, projected):
        return (
            pltpu.VMEM((-(-keys // 8) * 8 * res, channels), f32),
            pltpu.VMEM((projected * res, channels), f32),
            pltpu.VMEM((projected * res, channels), f32),
            pltpu.VMEM((row_count, 40, channels), f32),
        )

    sums, query, att_gate, after_own = call(
        functools.partial(most_attention_kernel, row_count, chips),
        (shaped(f32, row_count, 3, res, channels), own_shape, own_shape, own_shape),
        (valid_column, same_head, w_query, w_att_gate, w_key, w_value, wide_bias)
        + (att_a, att_b, far_att_a, after_a),
        scratch=attention_scratch(3 * half // 2, 3 * half // 2),
    )
    return call(
        functools.partial(attention_kernel, row_count, chips),
        shaped(bf16, *pair_rep.shape),
        (valid_column, same_head, w_key, w_value, w_att_out, wide_bias, far_att_b)
        + (query, att_gate, after_own, sums),
        scratch=attention_scratch(half // 2, half // 2),
    )


def per_device(pair_rep, residue_valid, *parameters):
    row_count, res, channels = pair_rep.shape
    devices = res // row_count
    if res % 48 == 0 and devices == 16 and 40 * res * res * channels <= 32 * 1024 * 1024:
        return on_whole_complex(pair_rep, residue_valid, *parameters)
    return split_over_devices(pair_rep, residue_valid, *parameters)


def solution(mesh):
    return jax.shard_map(
        per_device,
        mesh=mesh,
        in_specs=(
            P(("groups", "row"), None, None),
            P("groups"),
            P(),
            P(),
            P(),
            P(),
            P(),
            P(),
            P(),
            P(),
            P(),
            P(),
            P(),
            P(),
            P(),
            P(),
            P(),
        ),
        out_specs=P(("groups", "row"), None, None),
        check_vma=False,
    )
```

```python
import functools
import math

import jax
import jax.numpy as jnp
from jax import lax
from jax.experimental import pallas as pl
from jax.experimental.pallas import tpu as pltpu
from jax.sharding import PartitionSpec as P

HEADS = 4
HEAD_DIM = 32


def layer_norm(values, norm_gain, norm_bias, along_axis):
    centre = values - jnp.mean(values, axis=along_axis, keepdims=True)
    spread = jnp.mean(centre * centre, axis=along_axis, keepdims=True)
    return centre * lax.rsqrt(spread + 1e-05) * norm_gain + norm_bias


def attend(query_cols, key_cols, value_cols, whole_bias, key_mask):
    factor = 1.0 / math.sqrt(HEAD_DIM)
    scores = (
        jnp.einsum("kjhd,ijhd->jhki", key_cols, query_cols, preferred_element_type=jnp.float32)
        * factor
    )
    scores = scores + whole_bias.astype(jnp.float32)[None] + key_mask[None, None, :, None]
    scores = scores - jnp.max(scores, axis=2, keepdims=True)
    exponent = jnp.exp(scores)
    weights = (exponent / jnp.sum(exponent, axis=2, keepdims=True)).astype(jnp.bfloat16)
    return jnp.einsum("jhki,kjhd->ijhd", weights, value_cols, preferred_element_type=jnp.float32)


def split_over_devices(
    pair_rep,
    residue_valid,
    tri_norm_gain,
    tri_norm_bias,
    w_edges,
    w_tri_gate,
    out_norm_gain,
    out_norm_bias,
    w_tri_out,
    att_norm_gain,
    att_norm_bias,
    w_query,
    w_key,
    w_value,
    w_att_gate,
    w_pair_bias,
    w_att_out,
):
    row_count = pair_rep.shape[0]
    res_count = pair_rep.shape[1]
    channels = pair_rep.shape[2]
    hidden_width = HEADS * HEAD_DIM
    row_start = lax.axis_index("row") * row_count
    valid_flags = residue_valid.astype(jnp.float32)
    own_valid = lax.dynamic_slice_in_dim(valid_flags, row_start, row_count)
    normed = layer_norm(pair_rep.astype(jnp.float32), tri_norm_gain, tri_norm_bias, 2).astype(
        jnp.bfloat16
    )
    projected = jnp.einsum("ikd,de->eik", normed, w_edges, preferred_element_type=jnp.float32)
    projected = projected.reshape(4, channels, row_count, res_count)
    pair_mask = (own_valid[:, None] * valid_flags[None, :])[None, :, :]
    left_edges = (jax.nn.sigmoid(projected[1]) * projected[0] * pair_mask).astype(jnp.bfloat16)
    right_edges = (jax.nn.sigmoid(projected[3]) * projected[2] * pair_mask).astype(jnp.bfloat16)
    left_cols, right_cols = (
        lax.all_to_all(left_edges, "row", split_axis=0, concat_axis=1, tiled=True),
        lax.all_to_all(right_edges, "row", split_axis=0, concat_axis=1, tiled=True),
    )
    block_product = jnp.einsum(
        "cik,cjk->cij", left_cols, right_cols, preferred_element_type=jnp.float32
    ).astype(jnp.bfloat16)
    triangle = lax.all_to_all(block_product, "row", split_axis=1, concat_axis=0, tiled=True)
    tri_normed = layer_norm(
        triangle.astype(jnp.float32), out_norm_gain[:, None, None], out_norm_bias[:, None, None], 0
    ).astype(jnp.bfloat16)
    tri_gate = jax.nn.sigmoid(
        jnp.einsum("ijc,ce->ije", normed, w_tri_gate, preferred_element_type=jnp.float32)
    )
    tri_update = jnp.einsum(
        "cij,ce->ije", tri_normed, w_tri_out, preferred_element_type=jnp.float32
    )
    after_tri = pair_rep.astype(jnp.float32) + tri_gate * tri_update
    att_in = layer_norm(after_tri, att_norm_gain, att_norm_bias, 2).astype(jnp.bfloat16)
    pair_bias = jnp.einsum(
        "kic,ch->hki", att_in, w_pair_bias, preferred_element_type=jnp.float32
    ).astype(jnp.bfloat16)
    whole_bias = lax.all_gather(pair_bias, "row", axis=1, tiled=True)
    key_mask = 1000000000.0 * (valid_flags - 1.0)
    columns = lax.all_to_all(att_in, "row", split_axis=1, concat_axis=0, tiled=True)
    all_weights = jnp.concatenate([w_query, w_key, w_value, w_att_gate], axis=1)
    joined = jnp.dot(columns.reshape(-1, channels), all_weights, preferred_element_type=jnp.float32)
    query_cols = (
        joined[:, :hidden_width].astype(jnp.bfloat16).reshape(res_count, row_count, HEADS, HEAD_DIM)
    )
    key_cols = (
        joined[:, hidden_width : 2 * hidden_width]
        .astype(jnp.bfloat16)
        .reshape(res_count, row_count, HEADS, HEAD_DIM)
    )
    value_cols = (
        joined[:, 2 * hidden_width : 3 * hidden_width]
        .astype(jnp.bfloat16)
        .reshape(res_count, row_count, HEADS, HEAD_DIM)
    )
    gate_cols = jax.nn.sigmoid(joined[:, 3 * hidden_width :]).reshape(
        res_count, row_count, hidden_width
    )
    attended = attend(query_cols, key_cols, value_cols, whole_bias, key_mask)
    gated = (attended.reshape(res_count, row_count, hidden_width) * gate_cols).astype(jnp.bfloat16)
    gated_rows = lax.all_to_all(gated, "row", split_axis=0, concat_axis=1, tiled=True)
    final = after_tri + jnp.einsum(
        "ije,ec->ijc", gated_rows, w_att_out, preferred_element_type=jnp.float32
    )
    return final.astype(jnp.bfloat16)


def sigmoid(values):
    return 0.5 * jnp.tanh(0.5 * values) + 0.5


def row_norm(values, norm_gain, norm_bias):
    count = values.shape[1]
    centre = values - jnp.sum(values, axis=1, keepdims=True) * (1.0 / count)
    squares = jnp.sum(centre * centre, axis=1, keepdims=True)
    return centre * lax.rsqrt(squares + 1e-05 * count) * (norm_gain * count**0.5) + norm_bias


def dot(left, right):
    return jnp.dot(left, right, preferred_element_type=jnp.float32)


def rounded(values):
    return values.astype(jnp.bfloat16).astype(jnp.float32)


def chip_and_core():
    device = lax.axis_index("row")
    return lax.shift_right_logical(device, 1), jnp.bitwise_and(device, 1)


def rows_of_blocks(row_count, blocks):
    chip, _ = chip_and_core()
    return [(jnp.bitwise_xor(chip, bits), r) for bits in blocks for r in range(row_count)]


def edges_kernel(
    row_count, chips, pieces, send_row, makes_heads, valid_column, norms, weights, *refs
):
    pair_refs = refs[: len(pieces)]
    left_ref, right_ref, gate_ref, pairs_ref, send_ref = refs[-5:]
    if makes_heads:
        left_ref, right_ref, gate_ref, pairs_ref, send_ref, same_head_ref = refs[-6:]
        wide = same_head_ref.shape
        row = lax.broadcasted_iota(jnp.int32, wide, 0) // HEAD_DIM
        column = lax.broadcasted_iota(jnp.int32, wide, 1) // HEAD_DIM
        same_head_ref[...] = jnp.where(row == column, 1.0, 0.0).astype(jnp.bfloat16)
    f32, bf16 = jnp.float32, jnp.bfloat16
    res, channels = valid_column.shape
    _, core = chip_and_core()
    pairs = jnp.concatenate(
        [ref[...].astype(f32).reshape(-1, channels) for ref in pair_refs], axis=0
    )
    normed = row_norm(pairs, norms[0:1, :], norms[1:2, :]).astype(bf16)
    column = 0.5 * valid_column[...]
    rows_of = rows_of_blocks(row_count, [bits for piece in pieces for bits in piece])
    masks = jnp.concatenate(
        [
            column * valid_column[pl.ds((2 * chip + core) * row_count + r, 1), :]
            for chip, r in rows_of
        ],
        axis=0,
    )
    joined = dot(normed, weights[:, : 2 * channels])
    left = rounded((jnp.tanh(joined[:, channels:]) + 1.0) * joined[:, :channels] * masks)
    joined = dot(normed, weights[:, 2 * channels : 4 * channels])
    right = ((jnp.tanh(joined[:, channels:]) + 1.0) * joined[:, :channels] * masks).astype(bf16)
    gate = 0.5 * jnp.tanh(dot(normed, weights[:, 4 * channels :])) + 0.5
    for n, (chip, r) in enumerate(rows_of):
        rows = slice(n * res, (n + 1) * res)
        start = pl.multiple_of((chip * row_count + r) * res, res)
        send_ref[send_row + n] = right[rows]
        left_ref[pl.ds(start, res), :] = left[rows]
        place_right(right_ref, chips, chip, r, right[rows])
        gate_ref[pl.ds(start, res), :] = gate[rows]
        pairs_ref[pl.ds(start, res), :] = pairs[rows]


def place_right(right_ref, chips, chip, r, edges):
    res = edges.shape[0]
    start = pl.multiple_of((r * chips + chip) * res, res)
    right_ref[pl.ds(start, res), :] = edges.astype(jnp.float32)


def join(even, odd, shift):
    high = jnp.bitwise_and(lax.broadcasted_iota(jnp.int32, even.shape, 0), shift) > 0
    return jnp.where(high, odd, even) + pltpu.roll(jnp.where(high, even, odd), shift, 0)


def triangle_rows(
    row_count, chips, left_ref, right_ref, triangle_ref, first, count, core, triangle_first
):
    res = 2 * row_count * chips
    start = pl.multiple_of(first * res, res)
    block = 4
    for n in range(0, count, block):
        lefts = [left_ref[pl.ds(start + m * res, res), :] for m in range(n, n + block)]
        for r in range(row_count):
            sums = [[] for _ in range(block)]
            for chip in range(chips):
                at = (r * chips + chip) * res
                right = right_ref[at : at + res, :]
                for m in range(block):
                    product = lefts[m] * right
                    part = sum((product[k : k + 8] for k in range(8, res, 8)), product[:8])
                    shift = 1
                    while chip & shift:
                        part = join(sums[m].pop(), part, shift)
                        shift *= 2
                    sums[m].append(part)
            for m in range(block):
                place = (triangle_first + n + m) * res + core * row_count + r
                triangle_ref[pl.ds(place, chips, stride=2 * row_count), :] = rounded(sums[m][0])


def near_triangle_kernel(row_count, chips, chunk, pieces, left_ref, right_ref, *refs):
    received, (triangle_ref, across_ref) = refs[:-2], refs[-2:]
    _, core = chip_and_core()

    def some_rows(step, carry):
        first = step * chunk
        triangle_rows(
            row_count, chips, left_ref, right_ref, triangle_ref, first, chunk, core, first
        )
        return carry

    for ref, blocks in zip(received, pieces):
        for n, (chip, r) in enumerate(rows_of_blocks(row_count, blocks)):
            place_right(across_ref, chips, chip, r, ref[n])
    lax.fori_loop(0, row_count * chips // chunk, some_rows, 0)


def attention_inputs(
    row_count, chips, first, norms, w_out, left_ref, gate_ref, pairs_ref, held_triangle, across_ref,
    triangle_ref,
):
    bf16 = jnp.bfloat16
    _, core = chip_and_core()
    half = row_count * chips
    tall = (half // 2) * 2 * half
    rows = pl.ds(pl.multiple_of(first * 2 * half, tall), tall)
    triangle_ref[...] = held_triangle[rows, :]
    triangle_rows(
        row_count, chips, left_ref, across_ref, triangle_ref, first, half // 2, 1 - core, 0
    )
    tri_normed = row_norm(triangle_ref[...], norms[2:3, :], norms[3:4, :]).astype(bf16)
    after_tri = pairs_ref[rows, :] + gate_ref[rows, :] * dot(tri_normed, w_out[...])
    att_in = row_norm(after_tri, norms[4:5, :], norms[5:6, :]).astype(bf16)
    return after_tri, att_in


def first_chip(chips, part):
    chip, _ = chip_and_core()
    return jnp.bitwise_xor(jnp.bitwise_and(chip, chips // 2), part * (chips // 2))


def own_inputs_kernel(
    row_count,
    chips,
    blocks,
    norms,
    w_out,
    left_ref,
    gate_ref,
    pairs_ref,
    received,
    triangle_ref,
    held_across,
    across_ref,
    after_ref,
    att_ref,
    scratch_ref,
):
    for n, (chip, r) in enumerate(rows_of_blocks(row_count, blocks)):
        place_right(across_ref, chips, chip, r, received[n])
    first = first_chip(chips, 0) * row_count
    refs = (left_ref, gate_ref, pairs_ref, triangle_ref, across_ref, scratch_ref)
    after_ref[...], att_ref[...] = attention_inputs(
        row_count, chips, first, norms, w_out, *refs
    )


def other_inputs_kernel(row_count, chips, norms, w_out, *refs):
    *refs, att_ref, scratch_ref = refs
    first = first_chip(chips, 1) * row_count
    _, att_ref[...] = attention_inputs(row_count, chips, first, norms, w_out, *refs, scratch_ref)


def keys_and_values(att, w_key, w_value, key_ref, value_ref):
    channels = key_ref.shape[1]
    key_value = jnp.concatenate([w_key[...], w_value[...]], axis=1)
    start = 0
    for values in att:
        rows = slice(start, start + values.shape[0])
        joined = dot(values, key_value)
        key_ref[rows, :] = rounded(joined[:, :channels])
        value_ref[rows, :] = rounded(joined[:, channels:])
        start = rows.stop


def column_bias(row_count, res, att, wide_bias, att_ref, bias_ref):
    start = 0
    for values in att:
        att_ref[start : start + values.shape[0], :] = values.astype(jnp.float32)
        start += values.shape[0]
    keys = start // res
    own = lax.axis_index("row") * row_count
    height = -(-keys // 8) * 8
    columns = [att_ref[pl.ds(own + r, height, stride=res), :] for r in range(row_count)]
    columns = jnp.concatenate(columns, axis=0).astype(jnp.bfloat16)
    bias = rounded(dot(columns, wide_bias[...]))
    for r in range(row_count):
        bias_ref[r, :height, :] = bias[r * height : (r + 1) * height]


def partial_attention(
    row_count, chips, query, parts, bias_ref, same_head, valid_column, sums, together
):
    bf16 = jnp.bfloat16
    res = 2 * row_count * chips
    channels = valid_column.shape[1]
    count = row_count * chips // 2
    for part, (core, first, key_of, value_of) in enumerate(parts):
        products = []
        for r in range(row_count):
            own_query = query[r * res : (r + 1) * res]
            row = [(key_of(n) * own_query).astype(bf16) for n in range(count)]
            pairs = [jnp.concatenate(row[n : n + 2], axis=1) for n in range(0, count, 2)]
            products.append(jnp.concatenate(pairs, axis=0))
        if together:
            scores = dot(jnp.concatenate(products, axis=0), same_head[...])
            tall = count // 2 * res
            scores = [scores[r * tall : (r + 1) * tall] for r in range(row_count)]
        else:
            scores = [dot(product, same_head[...]) for product in products]

        def score_of(n, r):
            lanes = slice(n % 2 * channels, (n % 2 + 1) * channels)
            k = (2 * (first + n // row_count) + core) * row_count + n % row_count
            key_mask = 1000000000.0 * (valid_column[pl.ds(k, 1), :] - 1.0)
            at = part * count + n
            shift = (bias_ref[r, at : at + 1, :] + key_mask) * math.log2(math.e)
            return scores[r][n // 2 * res : (n // 2 + 1) * res, lanes] + shift

        later = []
        for r, (maximum, total, mixed) in enumerate(sums):
            highest = score_of(0, r)
            for n in range(1, count):
                highest = jnp.maximum(highest, score_of(n, r))
            if maximum is None:
                maximum, total, mixed = highest, 0.0, 0.0
            else:
                highest = jnp.maximum(highest, maximum)
                scale = jnp.exp2(maximum - highest)
                maximum, total, mixed = highest, total * scale, mixed * scale
            for n in range(count):
                weight = jnp.exp2(score_of(n, r) - maximum)
                total = total + weight
                mixed = mixed + weight * value_of(n)
            later.append((maximum, total, mixed))
        sums = later
    return sums


def most_attention_kernel(
    row_count,
    chips,
    valid_column,
    same_head,
    w_query,
    w_gate,
    w_key,
    w_value,
    wide_bias,
    own_att_a,
    own_att_b,
    far_att_a,
    own_after,
    sums_ref,
    query_ref,
    gate_ref,
    after_ref,
    att_ref,
    key_ref,
    value_ref,
    bias_ref,
):
    chip, core = chip_and_core()
    res, channels = valid_column.shape
    own = row_count * res
    rows = pl.ds(pl.multiple_of(jnp.bitwise_and(chip, chips // 2 - 1) * own, own), own)
    own_in = own_att_a[rows, :]
    query = rounded(dot(own_in, w_query[...])) * (math.log2(math.e) / math.sqrt(HEAD_DIM))
    att = [ref[...] for ref in (own_att_a, own_att_b, far_att_a)]
    keys_and_values(att, w_key, w_value, key_ref, value_ref)
    column_bias(row_count, res, att, wide_bias, att_ref, bias_ref)
    count = row_count * chips // 2

    def rows_of(ref, first):
        return lambda n: ref[(first + n) * res : (first + n + 1) * res, :]

    a, b = first_chip(chips, 0), first_chip(chips, 1)
    parts = [
        (sender, first, rows_of(key_ref, n * count), rows_of(value_ref, n * count))
        for n, (sender, first) in enumerate(((core, a), (core, b), (1 - core, a)))
    ]
    none = [(None, None, None)] * row_count
    sums = partial_attention(
        row_count, chips, query, parts, bias_ref, same_head, valid_column, none, True
    )
    for r in range(row_count):
        for n, each in enumerate(sums[r]):
            sums_ref[r, n] = each
    query_ref[...] = query
    gate_ref[...] = sigmoid(dot(own_in, w_gate[...]))
    after_ref[...] = own_after[rows, :]


def attention_kernel(
    row_count,
    chips,
    valid_column,
    same_head,
    w_key,
    w_value,
    w_out,
    wide_bias,
    far_att_b,
    query_ref,
    gate_ref,
    after_ref,
    sums_ref,
    out_ref,
    att_ref,
    key_ref,
    value_ref,
    bias_ref,
):
    _, core = chip_and_core()
    res, channels = valid_column.shape
    far_att = far_att_b[...]
    keys_and_values([far_att], w_key, w_value, key_ref, value_ref)
    column_bias(row_count, res, [far_att], wide_bias, att_ref, bias_ref)

    def rows_of(ref):
        return lambda n: ref[n * res : (n + 1) * res, :]

    parts = ((1 - core, first_chip(chips, 1), rows_of(key_ref), rows_of(value_ref)),)
    sums = [tuple(sums_ref[r, n] for n in range(3)) for r in range(row_count)]
    sums = partial_attention(
        row_count, chips, query_ref[...], parts, bias_ref, same_head, valid_column, sums, False
    )
    attended = [mixed / total for _, total, mixed in sums]
    gated = (jnp.concatenate(attended, axis=0) * gate_ref[...]).astype(jnp.bfloat16)
    final = after_ref[...] + dot(gated, w_out[...])
    out_ref[...] = final.astype(jnp.bfloat16).reshape(row_count, res, channels)


def on_whole_complex(
    pair_rep,
    residue_valid,
    tri_norm_gain,
    tri_norm_bias,
    w_edges,
    w_tri_gate,
    out_norm_gain,
    out_norm_bias,
    w_tri_out,
    att_norm_gain,
    att_norm_bias,
    w_query,
    w_key,
    w_value,
    w_att_gate,
    w_pair_bias,
    w_att_out,
):
    row_count, res, channels = pair_rep.shape
    devices = res // row_count
    chips = devices // 2
    half = res // 2
    f32, bf16 = jnp.float32, jnp.bfloat16
    in_vmem = pl.BlockSpec(memory_space=pltpu.VMEM)

    def shaped(dtype, *shape):
        return jax.ShapeDtypeStruct(shape, dtype)

    def call(kernel, outs, operands, aliases=None, scratch=(), cost=2**25):
        return pl.pallas_call(
            kernel,
            out_shape=outs,
            in_specs=[in_vmem] * len(operands),
            out_specs=jax.tree.map(lambda _: in_vmem, outs),
            input_output_aliases=aliases or {},
            scratch_shapes=list(scratch),
            compiler_params=pltpu.CompilerParams(vmem_limit_bytes=24 * 1024 * 1024),
            cost_estimate=pl.CostEstimate(flops=2**20, bytes_accessed=cost, transcendentals=0),
        )(*operands)

    def exchange(values, bit):
        return lax.ppermute(values, "row", [(d, d ^ bit) for d in range(devices)])

    vectors = (
        tri_norm_gain,
        tri_norm_bias,
        out_norm_gain,
        out_norm_bias,
        att_norm_gain,
        att_norm_bias,
    )
    norms = jnp.stack(vectors)
    is_gate = lax.broadcasted_iota(jnp.int32, (1, 5 * channels), 1) // channels
    halves = jnp.where((is_gate == 0) | (is_gate == 2), 1.0, 0.5).astype(bf16)
    edge_weights = jnp.concatenate([w_edges, w_tri_gate], axis=1) * halves
    valid_column = jnp.broadcast_to(residue_valid.astype(f32)[:, None], (res, channels))

    head = lax.broadcasted_iota(jnp.int32, (HEADS, channels), 0)
    head_of_channel = lax.broadcasted_iota(jnp.int32, (HEADS, channels), 1) // HEAD_DIM
    repeat = jnp.where(head == head_of_channel, 1.0, 0.0).astype(bf16)
    wide_bias = dot(w_pair_bias, repeat).astype(bf16)

    kept = lax.dynamic_update_slice(
        jnp.zeros((2 * row_count, res, channels), bf16), pair_rep, (0, 0, 0)
    )
    far = exchange(pair_rep, devices // 2)
    far, kept, norms, edge_weights = lax.optimization_barrier((far, kept, norms, edge_weights))
    own = lax.dynamic_update_slice(kept, far, (row_count, 0, 0))
    own_blocks = (0, chips // 2)

    def blocks_from(bits):
        return tuple(s ^ bits for s in own_blocks)

    tall = shaped(f32, half * res, channels)

    def edges_of(pieces, send_row, *held):
        pairs = tuple(p for p, _ in pieces)
        blocks = tuple(b for _, b in pieces)
        operands = (valid_column, norms, edge_weights) + pairs + held
        first = len(operands) - len(held)
        return call(
            functools.partial(edges_kernel, row_count, chips, blocks, send_row, not held),
            (tall, tall, tall, tall, shaped(bf16, 4 * row_count, res, channels))
            + (() if held else (shaped(bf16, 2 * channels, 2 * channels),)),
            operands,
            {first + e: e for e in range(len(held))},
        )

    beside = exchange(own, 2)
    diagonal = exchange(own, 6)
    near = exchange(own, 4)
    *edges, early_right, same_head = edges_of([(own, own_blocks)], 0)
    beside, edges = lax.optimization_barrier((beside, edges))
    *edges, early_right = edges_of(
        [(beside, blocks_from(1))], 2 * row_count, *edges, early_right
    )
    diagonal, edges, early_right, wide_bias = lax.optimization_barrier(
        (diagonal, edges, early_right, wide_bias)
    )
    early = (exchange(early_right, 1), own_blocks + blocks_from(1))
    *edges, late_right = edges_of(
        [(diagonal, blocks_from(3)), (near, blocks_from(2))], 0, *edges
    )
    late = (exchange(late_right, 1), blocks_from(3) + blocks_from(2))

    left, right, gate, pairs = edges
    triangle, across = call(
        functools.partial(near_triangle_kernel, row_count, chips, half // 2, [early[1]]),
        (tall, tall),
        (left, right, early[0]),
    )
    part = half // 2 * res
    in_part, own_shape = shaped(f32, part, channels), shaped(f32, row_count * res, channels)
    att_part = shaped(bf16, part, channels)
    shared = (norms, w_tri_out, left, gate, pairs)
    scratch = (pltpu.VMEM((part, channels), f32),)
    across, after_a, att_a = call(
        functools.partial(own_inputs_kernel, row_count, chips, late[1]),
        (tall, in_part, att_part),
        shared + (late[0], triangle, across),
        {7: 0},
        scratch=scratch,
    )
    far_att_a = exchange(att_a, 1)
    att_b = call(
        functools.partial(other_inputs_kernel, row_count, chips),
        att_part,
        shared + (triangle, across),
        scratch=scratch,
    )
    far_att_b = exchange(att_b, 1)

    def attention_scratch(keys, projected):
        return (
            pltpu.VMEM((-(-keys // 8) * 8 * res, channels), f32),
            pltpu.VMEM((projected * res, channels), f32),
            pltpu.VMEM((projected * res, channels), f32),
            pltpu.VMEM((row_count, 40, channels), f32),
        )

    sums, query, att_gate, after_own = call(
        functools.partial(most_attention_kernel, row_count, chips),
        (shaped(f32, row_count, 3, res, channels), own_shape, own_shape, own_shape),
        (valid_column, same_head, w_query, w_att_gate, w_key, w_value, wide_bias)
        + (att_a, att_b, far_att_a, after_a),
        scratch=attention_scratch(3 * half // 2, 3 * half // 2),
    )
    return call(
        functools.partial(attention_kernel, row_count, chips),
        shaped(bf16, *pair_rep.shape),
        (valid_column, same_head, w_key, w_value, w_att_out, wide_bias, far_att_b)
        + (query, att_gate, after_own, sums),
        scratch=attention_scratch(half // 2, half // 2),
    )


def per_device(pair_rep, residue_valid, *parameters):
    row_count, res, channels = pair_rep.shape
    devices = res // row_count
    if res % 48 == 0 and devices == 16 and 40 * res * res * channels <= 32 * 1024 * 1024:
        return on_whole_complex(pair_rep, residue_valid, *parameters)
    return split_over_devices(pair_rep, residue_valid, *parameters)


def solution(mesh):
    return jax.shard_map(
        per_device,
        mesh=mesh,
        in_specs=(
            P(("groups", "row"), None, None),
            P("groups"),
            P(),
            P(),
            P(),
            P(),
            P(),
            P(),
            P(),
            P(),
            P(),
            P(),
            P(),
            P(),
            P(),
            P(),
            P(),
        ),
        out_specs=P(("groups", "row"), None, None),
        check_vma=False,
    )
```

```python
import functools
import math

import jax
import jax.numpy as jnp
from jax import lax
from jax.experimental import pallas as pl
from jax.experimental.pallas import tpu as pltpu
from jax.sharding import PartitionSpec as P

HEADS = 4
HEAD_DIM = 32


def layer_norm(values, norm_gain, norm_bias, along_axis):
    centre = values - jnp.mean(values, axis=along_axis, keepdims=True)
    spread = jnp.mean(centre * centre, axis=along_axis, keepdims=True)
    return centre * lax.rsqrt(spread + 1e-05) * norm_gain + norm_bias


def attend(query_cols, key_cols, value_cols, whole_bias, key_mask):
    factor = 1.0 / math.sqrt(HEAD_DIM)
    scores = (
        jnp.einsum("kjhd,ijhd->jhki", key_cols, query_cols, preferred_element_type=jnp.float32)
        * factor
    )
    scores = scores + whole_bias.astype(jnp.float32)[None] + key_mask[None, None, :, None]
    scores = scores - jnp.max(scores, axis=2, keepdims=True)
    exponent = jnp.exp(scores)
    weights = (exponent / jnp.sum(exponent, axis=2, keepdims=True)).astype(jnp.bfloat16)
    return jnp.einsum("jhki,kjhd->ijhd", weights, value_cols, preferred_element_type=jnp.float32)


def split_over_devices(
    pair_rep,
    residue_valid,
    tri_norm_gain,
    tri_norm_bias,
    w_edges,
    w_tri_gate,
    out_norm_gain,
    out_norm_bias,
    w_tri_out,
    att_norm_gain,
    att_norm_bias,
    w_query,
    w_key,
    w_value,
    w_att_gate,
    w_pair_bias,
    w_att_out,
):
    row_count = pair_rep.shape[0]
    res_count = pair_rep.shape[1]
    channels = pair_rep.shape[2]
    hidden_width = HEADS * HEAD_DIM
    row_start = lax.axis_index("row") * row_count
    valid_flags = residue_valid.astype(jnp.float32)
    own_valid = lax.dynamic_slice_in_dim(valid_flags, row_start, row_count)
    normed = layer_norm(pair_rep.astype(jnp.float32), tri_norm_gain, tri_norm_bias, 2).astype(
        jnp.bfloat16
    )
    projected = jnp.einsum("ikd,de->eik", normed, w_edges, preferred_element_type=jnp.float32)
    projected = projected.reshape(4, channels, row_count, res_count)
    pair_mask = (own_valid[:, None] * valid_flags[None, :])[None, :, :]
    left_edges = (jax.nn.sigmoid(projected[1]) * projected[0] * pair_mask).astype(jnp.bfloat16)
    right_edges = (jax.nn.sigmoid(projected[3]) * projected[2] * pair_mask).astype(jnp.bfloat16)
    left_cols, right_cols = (
        lax.all_to_all(left_edges, "row", split_axis=0, concat_axis=1, tiled=True),
        lax.all_to_all(right_edges, "row", split_axis=0, concat_axis=1, tiled=True),
    )
    block_product = jnp.einsum(
        "cik,cjk->cij", left_cols, right_cols, preferred_element_type=jnp.float32
    ).astype(jnp.bfloat16)
    triangle = lax.all_to_all(block_product, "row", split_axis=1, concat_axis=0, tiled=True)
    tri_normed = layer_norm(
        triangle.astype(jnp.float32), out_norm_gain[:, None, None], out_norm_bias[:, None, None], 0
    ).astype(jnp.bfloat16)
    tri_gate = jax.nn.sigmoid(
        jnp.einsum("ijc,ce->ije", normed, w_tri_gate, preferred_element_type=jnp.float32)
    )
    tri_update = jnp.einsum(
        "cij,ce->ije", tri_normed, w_tri_out, preferred_element_type=jnp.float32
    )
    after_tri = pair_rep.astype(jnp.float32) + tri_gate * tri_update
    att_in = layer_norm(after_tri, att_norm_gain, att_norm_bias, 2).astype(jnp.bfloat16)
    pair_bias = jnp.einsum(
        "kic,ch->hki", att_in, w_pair_bias, preferred_element_type=jnp.float32
    ).astype(jnp.bfloat16)
    whole_bias = lax.all_gather(pair_bias, "row", axis=1, tiled=True)
    key_mask = 1000000000.0 * (valid_flags - 1.0)
    columns = lax.all_to_all(att_in, "row", split_axis=1, concat_axis=0, tiled=True)
    all_weights = jnp.concatenate([w_query, w_key, w_value, w_att_gate], axis=1)
    joined = jnp.dot(columns.reshape(-1, channels), all_weights, preferred_element_type=jnp.float32)
    query_cols = (
        joined[:, :hidden_width].astype(jnp.bfloat16).reshape(res_count, row_count, HEADS, HEAD_DIM)
    )
    key_cols = (
        joined[:, hidden_width : 2 * hidden_width]
        .astype(jnp.bfloat16)
        .reshape(res_count, row_count, HEADS, HEAD_DIM)
    )
    value_cols = (
        joined[:, 2 * hidden_width : 3 * hidden_width]
        .astype(jnp.bfloat16)
        .reshape(res_count, row_count, HEADS, HEAD_DIM)
    )
    gate_cols = jax.nn.sigmoid(joined[:, 3 * hidden_width :]).reshape(
        res_count, row_count, hidden_width
    )
    attended = attend(query_cols, key_cols, value_cols, whole_bias, key_mask)
    gated = (attended.reshape(res_count, row_count, hidden_width) * gate_cols).astype(jnp.bfloat16)
    gated_rows = lax.all_to_all(gated, "row", split_axis=0, concat_axis=1, tiled=True)
    final = after_tri + jnp.einsum(
        "ije,ec->ijc", gated_rows, w_att_out, preferred_element_type=jnp.float32
    )
    return final.astype(jnp.bfloat16)


def sigmoid(values):
    return 0.5 * jnp.tanh(0.5 * values) + 0.5


def row_norm(values, norm_gain, norm_bias):
    count = values.shape[1]
    centre = values - jnp.sum(values, axis=1, keepdims=True) * (1.0 / count)
    squares = jnp.sum(centre * centre, axis=1, keepdims=True)
    return centre * lax.rsqrt(squares + 1e-05 * count) * (norm_gain * count**0.5) + norm_bias


def dot(left, right):
    return jnp.dot(left, right, preferred_element_type=jnp.float32)


def rounded(values):
    return values.astype(jnp.bfloat16).astype(jnp.float32)


def chip_and_core():
    device = lax.axis_index("row")
    return lax.shift_right_logical(device, 1), jnp.bitwise_and(device, 1)


def rows_of_blocks(row_count, blocks):
    chip, _ = chip_and_core()
    return [(jnp.bitwise_xor(chip, bits), r) for bits in blocks for r in range(row_count)]


def edges_kernel(
    row_count, chips, pieces, send_row, makes_heads, valid_column, norms, weights, *refs
):
    pair_refs = refs[: len(pieces)]
    left_ref, right_ref, gate_ref, pairs_ref, send_ref = refs[-5:]
    if makes_heads:
        left_ref, right_ref, gate_ref, pairs_ref, send_ref, same_head_ref = refs[-6:]
        wide = same_head_ref.shape
        row = lax.broadcasted_iota(jnp.int32, wide, 0) // HEAD_DIM
        column = lax.broadcasted_iota(jnp.int32, wide, 1) // HEAD_DIM
        same_head_ref[...] = jnp.where(row == column, 1.0, 0.0).astype(jnp.bfloat16)
    f32, bf16 = jnp.float32, jnp.bfloat16
    res, channels = valid_column.shape
    _, core = chip_and_core()
    pairs = jnp.concatenate(
        [ref[...].astype(f32).reshape(-1, channels) for ref in pair_refs], axis=0
    )
    normed = row_norm(pairs, norms[0:1, :], norms[1:2, :]).astype(bf16)
    column = 0.5 * valid_column[...]
    rows_of = rows_of_blocks(row_count, [bits for piece in pieces for bits in piece])
    masks = jnp.concatenate(
        [
            column * valid_column[pl.ds((2 * chip + core) * row_count + r, 1), :]
            for chip, r in rows_of
        ],
        axis=0,
    )
    joined = dot(normed, weights[:, : 2 * channels])
    left = rounded((jnp.tanh(joined[:, channels:]) + 1.0) * joined[:, :channels] * masks)
    joined = dot(normed, weights[:, 2 * channels : 4 * channels])
    right = ((jnp.tanh(joined[:, channels:]) + 1.0) * joined[:, :channels] * masks).astype(bf16)
    gate = 0.5 * jnp.tanh(dot(normed, weights[:, 4 * channels :])) + 0.5
    for n, (chip, r) in enumerate(rows_of):
        rows = slice(n * res, (n + 1) * res)
        start = pl.multiple_of((chip * row_count + r) * res, res)
        send_ref[send_row + n] = right[rows]
        left_ref[pl.ds(start, res), :] = left[rows]
        place_right(right_ref, chips, chip, r, right[rows])
        gate_ref[pl.ds(start, res), :] = gate[rows]
        pairs_ref[pl.ds(start, res), :] = pairs[rows]


def place_right(right_ref, chips, chip, r, edges):
    res = edges.shape[0]
    start = pl.multiple_of((r * chips + chip) * res, res)
    right_ref[pl.ds(start, res), :] = edges.astype(jnp.float32)


def join(even, odd, shift):
    high = jnp.bitwise_and(lax.broadcasted_iota(jnp.int32, even.shape, 0), shift) > 0
    return jnp.where(high, odd, even) + pltpu.roll(jnp.where(high, even, odd), shift, 0)


def triangle_rows(
    row_count, chips, left_ref, right_ref, triangle_ref, first, count, core, triangle_first
):
    res = 2 * row_count * chips
    start = pl.multiple_of(first * res, res)
    block = 4
    for n in range(0, count, block):
        lefts = [left_ref[pl.ds(start + m * res, res), :] for m in range(n, n + block)]
        for r in range(row_count):
            sums = [[] for _ in range(block)]
            for chip in range(chips):
                at = (r * chips + chip) * res
                right = right_ref[at : at + res, :]
                for m in range(block):
                    product = lefts[m] * right
                    part = sum((product[k : k + 8] for k in range(8, res, 8)), product[:8])
                    shift = 1
                    while chip & shift:
                        part = join(sums[m].pop(), part, shift)
                        shift *= 2
                    sums[m].append(part)
            for m in range(block):
                place = (triangle_first + n + m) * res + core * row_count + r
                triangle_ref[pl.ds(place, chips, stride=2 * row_count), :] = rounded(sums[m][0])


def near_triangle_kernel(row_count, chips, chunk, left_ref, right_ref, triangle_ref):
    _, core = chip_and_core()

    def some_rows(step, carry):
        first = step * chunk
        triangle_rows(
            row_count, chips, left_ref, right_ref, triangle_ref, first, chunk, core, first
        )
        return carry

    lax.fori_loop(0, row_count * chips // chunk, some_rows, 0)


def attention_inputs(
    row_count, chips, first, norms, w_out, left_ref, gate_ref, pairs_ref, held_triangle, across_ref,
    triangle_ref,
):
    bf16 = jnp.bfloat16
    _, core = chip_and_core()
    half = row_count * chips
    tall = (half // 2) * 2 * half
    rows = pl.ds(pl.multiple_of(first * 2 * half, tall), tall)
    triangle_ref[...] = held_triangle[rows, :]
    triangle_rows(
        row_count, chips, left_ref, across_ref, triangle_ref, first, half // 2, 1 - core, 0
    )
    tri_normed = row_norm(triangle_ref[...], norms[2:3, :], norms[3:4, :]).astype(bf16)
    after_tri = pairs_ref[rows, :] + gate_ref[rows, :] * dot(tri_normed, w_out[...])
    att_in = row_norm(after_tri, norms[4:5, :], norms[5:6, :]).astype(bf16)
    return after_tri, att_in


def first_chip(chips, part):
    chip, _ = chip_and_core()
    return jnp.bitwise_xor(jnp.bitwise_and(chip, chips // 2), part * (chips // 2))


def own_inputs_kernel(
    row_count,
    chips,
    blocks,
    norms,
    w_out,
    left_ref,
    gate_ref,
    pairs_ref,
    early,
    late,
    triangle_ref,
    across_ref,
    after_ref,
    att_ref,
    scratch_ref,
):
    for received, senders in zip((early, late), blocks):
        for n, (chip, r) in enumerate(rows_of_blocks(row_count, senders)):
            place_right(across_ref, chips, chip, r, received[n])
    first = first_chip(chips, 0) * row_count
    refs = (left_ref, gate_ref, pairs_ref, triangle_ref, across_ref, scratch_ref)
    after_ref[...], att_ref[...] = attention_inputs(
        row_count, chips, first, norms, w_out, *refs
    )


def other_inputs_kernel(row_count, chips, norms, w_out, *refs):
    *refs, att_ref, scratch_ref = refs
    first = first_chip(chips, 1) * row_count
    _, att_ref[...] = attention_inputs(row_count, chips, first, norms, w_out, *refs, scratch_ref)


def keys_and_values(att, w_key, w_value, key_ref, value_ref):
    channels = key_ref.shape[1]
    key_value = jnp.concatenate([w_key[...], w_value[...]], axis=1)
    start = 0
    for values in att:
        rows = slice(start, start + values.shape[0])
        joined = dot(values, key_value)
        key_ref[rows, :] = rounded(joined[:, :channels])
        value_ref[rows, :] = rounded(joined[:, channels:])
        start = rows.stop


def column_bias(row_count, res, att, wide_bias, att_ref, bias_ref):
    start = 0
    for values in att:
        att_ref[start : start + values.shape[0], :] = values.astype(jnp.float32)
        start += values.shape[0]
    keys = start // res
    own = lax.axis_index("row") * row_count
    height = -(-keys // 8) * 8
    columns = [att_ref[pl.ds(own + r, height, stride=res), :] for r in range(row_count)]
    columns = jnp.concatenate(columns, axis=0).astype(jnp.bfloat16)
    bias = rounded(dot(columns, wide_bias[...]))
    for r in range(row_count):
        bias_ref[r, :height, :] = bias[r * height : (r + 1) * height]


def partial_attention(
    row_count, chips, query, parts, bias_ref, same_head, valid_column, sums, together
):
    bf16 = jnp.bfloat16
    res = 2 * row_count * chips
    channels = valid_column.shape[1]
    count = row_count * chips // 2
    for part, (core, first, key_of, value_of) in enumerate(parts):
        products = []
        for r in range(row_count):
            own_query = query[r * res : (r + 1) * res]
            row = [(key_of(n) * own_query).astype(bf16) for n in range(count)]
            pairs = [jnp.concatenate(row[n : n + 2], axis=1) for n in range(0, count, 2)]
            products.append(jnp.concatenate(pairs, axis=0))
        if together:
            scores = dot(jnp.concatenate(products, axis=0), same_head[...])
            tall = count // 2 * res
            scores = [scores[r * tall : (r + 1) * tall] for r in range(row_count)]
        else:
            scores = [dot(product, same_head[...]) for product in products]

        def score_of(n, r):
            lanes = slice(n % 2 * channels, (n % 2 + 1) * channels)
            k = (2 * (first + n // row_count) + core) * row_count + n % row_count
            key_mask = 1000000000.0 * (valid_column[pl.ds(k, 1), :] - 1.0)
            at = part * count + n
            shift = (bias_ref[r, at : at + 1, :] + key_mask) * math.log2(math.e)
            return scores[r][n // 2 * res : (n // 2 + 1) * res, lanes] + shift

        later = []
        for r, (maximum, total, mixed) in enumerate(sums):
            highest = score_of(0, r)
            for n in range(1, count):
                highest = jnp.maximum(highest, score_of(n, r))
            if maximum is None:
                maximum, total, mixed = highest, 0.0, 0.0
            else:
                highest = jnp.maximum(highest, maximum)
                scale = jnp.exp2(maximum - highest)
                maximum, total, mixed = highest, total * scale, mixed * scale
            for n in range(count):
                weight = jnp.exp2(score_of(n, r) - maximum)
                total = total + weight
                mixed = mixed + weight * value_of(n)
            later.append((maximum, total, mixed))
        sums = later
    return sums


def most_attention_kernel(
    row_count,
    chips,
    valid_column,
    same_head,
    w_query,
    w_gate,
    w_key,
    w_value,
    wide_bias,
    own_att_a,
    own_att_b,
    far_att_a,
    own_after,
    sums_ref,
    query_ref,
    gate_ref,
    after_ref,
    att_ref,
    key_ref,
    value_ref,
    bias_ref,
):
    chip, core = chip_and_core()
    res, channels = valid_column.shape
    own = row_count * res
    rows = pl.ds(pl.multiple_of(jnp.bitwise_and(chip, chips // 2 - 1) * own, own), own)
    own_in = own_att_a[rows, :]
    query = rounded(dot(own_in, w_query[...])) * (math.log2(math.e) / math.sqrt(HEAD_DIM))
    att = [ref[...] for ref in (own_att_a, own_att_b, far_att_a)]
    keys_and_values(att, w_key, w_value, key_ref, value_ref)
    column_bias(row_count, res, att, wide_bias, att_ref, bias_ref)
    count = row_count * chips // 2

    def rows_of(ref, first):
        return lambda n: ref[(first + n) * res : (first + n + 1) * res, :]

    a, b = first_chip(chips, 0), first_chip(chips, 1)
    parts = [
        (sender, first, rows_of(key_ref, n * count), rows_of(value_ref, n * count))
        for n, (sender, first) in enumerate(((core, a), (core, b), (1 - core, a)))
    ]
    none = [(None, None, None)] * row_count
    sums = partial_attention(
        row_count, chips, query, parts, bias_ref, same_head, valid_column, none, True
    )
    for r in range(row_count):
        for n, each in enumerate(sums[r]):
            sums_ref[r, n] = each
    query_ref[...] = query
    gate_ref[...] = sigmoid(dot(own_in, w_gate[...]))
    after_ref[...] = own_after[rows, :]


def attention_kernel(
    row_count,
    chips,
    valid_column,
    same_head,
    w_key,
    w_value,
    w_out,
    wide_bias,
    far_att_b,
    query_ref,
    gate_ref,
    after_ref,
    sums_ref,
    out_ref,
    att_ref,
    key_ref,
    value_ref,
    bias_ref,
):
    _, core = chip_and_core()
    res, channels = valid_column.shape
    far_att = far_att_b[...]
    keys_and_values([far_att], w_key, w_value, key_ref, value_ref)
    column_bias(row_count, res, [far_att], wide_bias, att_ref, bias_ref)

    def rows_of(ref):
        return lambda n: ref[n * res : (n + 1) * res, :]

    parts = ((1 - core, first_chip(chips, 1), rows_of(key_ref), rows_of(value_ref)),)
    sums = [tuple(sums_ref[r, n] for n in range(3)) for r in range(row_count)]
    sums = partial_attention(
        row_count, chips, query_ref[...], parts, bias_ref, same_head, valid_column, sums, False
    )
    attended = [mixed / total for _, total, mixed in sums]
    gated = (jnp.concatenate(attended, axis=0) * gate_ref[...]).astype(jnp.bfloat16)
    final = after_ref[...] + dot(gated, w_out[...])
    out_ref[...] = final.astype(jnp.bfloat16).reshape(row_count, res, channels)


def on_whole_complex(
    pair_rep,
    residue_valid,
    tri_norm_gain,
    tri_norm_bias,
    w_edges,
    w_tri_gate,
    out_norm_gain,
    out_norm_bias,
    w_tri_out,
    att_norm_gain,
    att_norm_bias,
    w_query,
    w_key,
    w_value,
    w_att_gate,
    w_pair_bias,
    w_att_out,
):
    row_count, res, channels = pair_rep.shape
    devices = res // row_count
    chips = devices // 2
    half = res // 2
    f32, bf16 = jnp.float32, jnp.bfloat16
    in_vmem = pl.BlockSpec(memory_space=pltpu.VMEM)

    def shaped(dtype, *shape):
        return jax.ShapeDtypeStruct(shape, dtype)

    def call(kernel, outs, operands, aliases=None, scratch=(), cost=2**25):
        return pl.pallas_call(
            kernel,
            out_shape=outs,
            in_specs=[in_vmem] * len(operands),
            out_specs=jax.tree.map(lambda _: in_vmem, outs),
            input_output_aliases=aliases or {},
            scratch_shapes=list(scratch),
            compiler_params=pltpu.CompilerParams(vmem_limit_bytes=24 * 1024 * 1024),
            cost_estimate=pl.CostEstimate(flops=2**20, bytes_accessed=cost, transcendentals=0),
        )(*operands)

    def exchange(values, bit):
        return lax.ppermute(values, "row", [(d, d ^ bit) for d in range(devices)])

    vectors = (
        tri_norm_gain,
        tri_norm_bias,
        out_norm_gain,
        out_norm_bias,
        att_norm_gain,
        att_norm_bias,
    )
    norms = jnp.stack(vectors)
    is_gate = lax.broadcasted_iota(jnp.int32, (1, 5 * channels), 1) // channels
    halves = jnp.where((is_gate == 0) | (is_gate == 2), 1.0, 0.5).astype(bf16)
    edge_weights = jnp.concatenate([w_edges, w_tri_gate], axis=1) * halves
    valid_column = jnp.broadcast_to(residue_valid.astype(f32)[:, None], (res, channels))

    head = lax.broadcasted_iota(jnp.int32, (HEADS, channels), 0)
    head_of_channel = lax.broadcasted_iota(jnp.int32, (HEADS, channels), 1) // HEAD_DIM
    repeat = jnp.where(head == head_of_channel, 1.0, 0.0).astype(bf16)
    wide_bias = dot(w_pair_bias, repeat).astype(bf16)

    kept = lax.dynamic_update_slice(
        jnp.zeros((2 * row_count, res, channels), bf16), pair_rep, (0, 0, 0)
    )
    far = exchange(pair_rep, devices // 2)
    far, kept, norms, edge_weights = lax.optimization_barrier((far, kept, norms, edge_weights))
    own = lax.dynamic_update_slice(kept, far, (row_count, 0, 0))
    own_blocks = (0, chips // 2)

    def blocks_from(bits):
        return tuple(s ^ bits for s in own_blocks)

    tall = shaped(f32, half * res, channels)

    def edges_of(pieces, send_row, *held):
        pairs = tuple(p for p, _ in pieces)
        blocks = tuple(b for _, b in pieces)
        operands = (valid_column, norms, edge_weights) + pairs + held
        first = len(operands) - len(held)
        return call(
            functools.partial(edges_kernel, row_count, chips, blocks, send_row, not held),
            (tall, tall, tall, tall, shaped(bf16, 4 * row_count, res, channels))
            + (() if held else (shaped(bf16, 2 * channels, 2 * channels),)),
            operands,
            {first + e: e for e in range(len(held))},
        )

    diagonal = exchange(own, 6)
    beside = exchange(own, 2)
    near = exchange(own, 4)
    *edges, early_right, same_head = edges_of([(own, own_blocks)], 0)
    diagonal, edges = lax.optimization_barrier((diagonal, edges))
    *edges, early_right = edges_of(
        [(diagonal, blocks_from(3))], 2 * row_count, *edges, early_right
    )
    early = (exchange(early_right, 1), own_blocks + blocks_from(3))
    beside, edges, wide_bias = lax.optimization_barrier((beside, edges, wide_bias))
    *edges, late_right = edges_of([(beside, blocks_from(1))], 0, *edges)
    near, edges, late_right = lax.optimization_barrier((near, edges, late_right))
    *edges, late_right = edges_of([(near, blocks_from(2))], 2 * row_count, *edges, late_right)
    late = (exchange(late_right, 1), blocks_from(1) + blocks_from(2))

    left, right, gate, pairs = edges
    triangle = call(
        functools.partial(near_triangle_kernel, row_count, chips, half // 2), tall, (left, right)
    )
    part = half // 2 * res
    in_part, own_shape = shaped(f32, part, channels), shaped(f32, row_count * res, channels)
    att_part = shaped(bf16, part, channels)
    shared = (norms, w_tri_out, left, gate, pairs)
    scratch = (pltpu.VMEM((part, channels), f32),)
    across, after_a, att_a = call(
        functools.partial(own_inputs_kernel, row_count, chips, (early[1], late[1])),
        (tall, in_part, att_part),
        shared + (early[0], late[0], triangle),
        scratch=scratch,
    )
    far_att_a = exchange(att_a, 1)
    att_b = call(
        functools.partial(other_inputs_kernel, row_count, chips),
        att_part,
        shared + (triangle, across),
        scratch=scratch,
    )
    far_att_b = exchange(att_b, 1)

    def attention_scratch(keys, projected):
        return (
            pltpu.VMEM((-(-keys // 8) * 8 * res, channels), f32),
            pltpu.VMEM((projected * res, channels), f32),
            pltpu.VMEM((projected * res, channels), f32),
            pltpu.VMEM((row_count, 40, channels), f32),
        )

    sums, query, att_gate, after_own = call(
        functools.partial(most_attention_kernel, row_count, chips),
        (shaped(f32, row_count, 3, res, channels), own_shape, own_shape, own_shape),
        (valid_column, same_head, w_query, w_att_gate, w_key, w_value, wide_bias)
        + (att_a, att_b, far_att_a, after_a),
        scratch=attention_scratch(3 * half // 2, 3 * half // 2),
    )
    return call(
        functools.partial(attention_kernel, row_count, chips),
        shaped(bf16, *pair_rep.shape),
        (valid_column, same_head, w_key, w_value, w_att_out, wide_bias, far_att_b)
        + (query, att_gate, after_own, sums),
        scratch=attention_scratch(half // 2, half // 2),
    )


def per_device(pair_rep, residue_valid, *parameters):
    row_count, res, channels = pair_rep.shape
    devices = res // row_count
    if res % 48 == 0 and devices == 16 and 40 * res * res * channels <= 32 * 1024 * 1024:
        return on_whole_complex(pair_rep, residue_valid, *parameters)
    return split_over_devices(pair_rep, residue_valid, *parameters)


def solution(mesh):
    return jax.shard_map(
        per_device,
        mesh=mesh,
        in_specs=(
            P(("groups", "row"), None, None),
            P("groups"),
            P(),
            P(),
            P(),
            P(),
            P(),
            P(),
            P(),
            P(),
            P(),
            P(),
            P(),
            P(),
            P(),
            P(),
            P(),
        ),
        out_specs=P(("groups", "row"), None, None),
        check_vma=False,
    )
```

```python
import functools
import math

import jax
import jax.numpy as jnp
from jax import lax
from jax.experimental import pallas as pl
from jax.experimental.pallas import tpu as pltpu
from jax.sharding import PartitionSpec as P

HEADS = 4
HEAD_DIM = 32


def layer_norm(values, norm_gain, norm_bias, along_axis):
    centre = values - jnp.mean(values, axis=along_axis, keepdims=True)
    spread = jnp.mean(centre * centre, axis=along_axis, keepdims=True)
    return centre * lax.rsqrt(spread + 1e-05) * norm_gain + norm_bias


def attend(query_cols, key_cols, value_cols, whole_bias, key_mask):
    factor = 1.0 / math.sqrt(HEAD_DIM)
    scores = (
        jnp.einsum("kjhd,ijhd->jhki", key_cols, query_cols, preferred_element_type=jnp.float32)
        * factor
    )
    scores = scores + whole_bias.astype(jnp.float32)[None] + key_mask[None, None, :, None]
    scores = scores - jnp.max(scores, axis=2, keepdims=True)
    exponent = jnp.exp(scores)
    weights = (exponent / jnp.sum(exponent, axis=2, keepdims=True)).astype(jnp.bfloat16)
    return jnp.einsum("jhki,kjhd->ijhd", weights, value_cols, preferred_element_type=jnp.float32)


def split_over_devices(
    pair_rep,
    residue_valid,
    tri_norm_gain,
    tri_norm_bias,
    w_edges,
    w_tri_gate,
    out_norm_gain,
    out_norm_bias,
    w_tri_out,
    att_norm_gain,
    att_norm_bias,
    w_query,
    w_key,
    w_value,
    w_att_gate,
    w_pair_bias,
    w_att_out,
):
    row_count = pair_rep.shape[0]
    res_count = pair_rep.shape[1]
    channels = pair_rep.shape[2]
    hidden_width = HEADS * HEAD_DIM
    row_start = lax.axis_index("row") * row_count
    valid_flags = residue_valid.astype(jnp.float32)
    own_valid = lax.dynamic_slice_in_dim(valid_flags, row_start, row_count)
    normed = layer_norm(pair_rep.astype(jnp.float32), tri_norm_gain, tri_norm_bias, 2).astype(
        jnp.bfloat16
    )
    projected = jnp.einsum("ikd,de->eik", normed, w_edges, preferred_element_type=jnp.float32)
    projected = projected.reshape(4, channels, row_count, res_count)
    pair_mask = (own_valid[:, None] * valid_flags[None, :])[None, :, :]
    left_edges = (jax.nn.sigmoid(projected[1]) * projected[0] * pair_mask).astype(jnp.bfloat16)
    right_edges = (jax.nn.sigmoid(projected[3]) * projected[2] * pair_mask).astype(jnp.bfloat16)
    left_cols, right_cols = (
        lax.all_to_all(left_edges, "row", split_axis=0, concat_axis=1, tiled=True),
        lax.all_to_all(right_edges, "row", split_axis=0, concat_axis=1, tiled=True),
    )
    block_product = jnp.einsum(
        "cik,cjk->cij", left_cols, right_cols, preferred_element_type=jnp.float32
    ).astype(jnp.bfloat16)
    triangle = lax.all_to_all(block_product, "row", split_axis=1, concat_axis=0, tiled=True)
    tri_normed = layer_norm(
        triangle.astype(jnp.float32), out_norm_gain[:, None, None], out_norm_bias[:, None, None], 0
    ).astype(jnp.bfloat16)
    tri_gate = jax.nn.sigmoid(
        jnp.einsum("ijc,ce->ije", normed, w_tri_gate, preferred_element_type=jnp.float32)
    )
    tri_update = jnp.einsum(
        "cij,ce->ije", tri_normed, w_tri_out, preferred_element_type=jnp.float32
    )
    after_tri = pair_rep.astype(jnp.float32) + tri_gate * tri_update
    att_in = layer_norm(after_tri, att_norm_gain, att_norm_bias, 2).astype(jnp.bfloat16)
    pair_bias = jnp.einsum(
        "kic,ch->hki", att_in, w_pair_bias, preferred_element_type=jnp.float32
    ).astype(jnp.bfloat16)
    whole_bias = lax.all_gather(pair_bias, "row", axis=1, tiled=True)
    key_mask = 1000000000.0 * (valid_flags - 1.0)
    columns = lax.all_to_all(att_in, "row", split_axis=1, concat_axis=0, tiled=True)
    all_weights = jnp.concatenate([w_query, w_key, w_value, w_att_gate], axis=1)
    joined = jnp.dot(columns.reshape(-1, channels), all_weights, preferred_element_type=jnp.float32)
    query_cols = (
        joined[:, :hidden_width].astype(jnp.bfloat16).reshape(res_count, row_count, HEADS, HEAD_DIM)
    )
    key_cols = (
        joined[:, hidden_width : 2 * hidden_width]
        .astype(jnp.bfloat16)
        .reshape(res_count, row_count, HEADS, HEAD_DIM)
    )
    value_cols = (
        joined[:, 2 * hidden_width : 3 * hidden_width]
        .astype(jnp.bfloat16)
        .reshape(res_count, row_count, HEADS, HEAD_DIM)
    )
    gate_cols = jax.nn.sigmoid(joined[:, 3 * hidden_width :]).reshape(
        res_count, row_count, hidden_width
    )
    attended = attend(query_cols, key_cols, value_cols, whole_bias, key_mask)
    gated = (attended.reshape(res_count, row_count, hidden_width) * gate_cols).astype(jnp.bfloat16)
    gated_rows = lax.all_to_all(gated, "row", split_axis=0, concat_axis=1, tiled=True)
    final = after_tri + jnp.einsum(
        "ije,ec->ijc", gated_rows, w_att_out, preferred_element_type=jnp.float32
    )
    return final.astype(jnp.bfloat16)


def sigmoid(values):
    return 0.5 * jnp.tanh(0.5 * values) + 0.5


def row_norm(values, norm_gain, norm_bias):
    count = values.shape[1]
    centre = values - jnp.sum(values, axis=1, keepdims=True) * (1.0 / count)
    squares = jnp.sum(centre * centre, axis=1, keepdims=True)
    return centre * lax.rsqrt(squares + 1e-05 * count) * (norm_gain * count**0.5) + norm_bias


def row_sums(values, same_half):
    half, channels = values.shape[0] // 2, values.shape[1]
    values = values.astype(jnp.bfloat16)
    sums = dot(jnp.concatenate([values[:half], values[half:]], axis=1), same_half[...])
    return jnp.concatenate([sums[:, :channels], sums[:, channels:]], axis=0)


def row_norm_by_products(values, total, norm_gain, norm_bias, same_half):
    count = values.shape[1]
    centre = values - total * (1.0 / count)
    squares = row_sums(centre * centre, same_half)
    return centre * lax.rsqrt(squares + 1e-05 * count) * (norm_gain * count**0.5) + norm_bias


def dot(left, right):
    return jnp.dot(left, right, preferred_element_type=jnp.float32)


def rounded(values):
    return values.astype(jnp.bfloat16).astype(jnp.float32)


def chip_and_core():
    device = lax.axis_index("row")
    return lax.shift_right_logical(device, 1), jnp.bitwise_and(device, 1)


def rows_of_blocks(row_count, blocks):
    chip, _ = chip_and_core()
    return [(jnp.bitwise_xor(chip, bits), r) for bits in blocks for r in range(row_count)]


def edges_kernel(
    row_count, chips, pieces, send_row, makes_heads, valid_column, norms, weights, *refs
):
    pair_refs = refs[: len(pieces)]
    left_ref, right_ref, gate_ref, pairs_ref, send_ref = refs[-5:]
    if makes_heads:
        left_ref, right_ref, gate_ref, pairs_ref, send_ref, *same_refs = refs[-7:]
        for same_ref, width in zip(same_refs, (HEAD_DIM, HEADS * HEAD_DIM)):
            row = lax.broadcasted_iota(jnp.int32, same_ref.shape, 0) // width
            column = lax.broadcasted_iota(jnp.int32, same_ref.shape, 1) // width
            same_ref[...] = jnp.where(row == column, 1.0, 0.0).astype(jnp.bfloat16)
    f32, bf16 = jnp.float32, jnp.bfloat16
    res, channels = valid_column.shape
    _, core = chip_and_core()
    pairs = jnp.concatenate(
        [ref[...].astype(f32).reshape(-1, channels) for ref in pair_refs], axis=0
    )
    normed = row_norm(pairs, norms[0:1, :], norms[1:2, :]).astype(bf16)
    column = 0.5 * valid_column[...]
    rows_of = rows_of_blocks(row_count, [bits for piece in pieces for bits in piece])
    masks = jnp.concatenate(
        [
            column * valid_column[pl.ds((2 * chip + core) * row_count + r, 1), :]
            for chip, r in rows_of
        ],
        axis=0,
    )
    joined = dot(normed, weights[:, : 2 * channels])
    left = rounded((jnp.tanh(joined[:, channels:]) + 1.0) * joined[:, :channels] * masks)
    joined = dot(normed, weights[:, 2 * channels : 4 * channels])
    right = ((jnp.tanh(joined[:, channels:]) + 1.0) * joined[:, :channels] * masks).astype(bf16)
    gate = 0.5 * jnp.tanh(dot(normed, weights[:, 4 * channels :])) + 0.5
    for n, (chip, r) in enumerate(rows_of):
        rows = slice(n * res, (n + 1) * res)
        start = pl.multiple_of((chip * row_count + r) * res, res)
        send_ref[send_row + n] = right[rows]
        left_ref[pl.ds(start, res), :] = left[rows]
        place_right(right_ref, chips, chip, r, right[rows])
        gate_ref[pl.ds(start, res), :] = gate[rows]
        pairs_ref[pl.ds(start, res), :] = pairs[rows]


def place_right(right_ref, chips, chip, r, edges):
    res = edges.shape[0]
    start = pl.multiple_of((r * chips + chip) * res, res)
    right_ref[pl.ds(start, res), :] = edges.astype(jnp.float32)


def join(even, odd, shift):
    high = jnp.bitwise_and(lax.broadcasted_iota(jnp.int32, even.shape, 0), shift) > 0
    return jnp.where(high, odd, even) + pltpu.roll(jnp.where(high, even, odd), shift, 0)


def triangle_rows(
    row_count, chips, left_ref, right_ref, triangle_ref, first, count, core, triangle_first
):
    res = 2 * row_count * chips
    start = pl.multiple_of(first * res, res)
    block = 4
    for n in range(0, count, block):
        lefts = [left_ref[pl.ds(start + m * res, res), :] for m in range(n, n + block)]
        for r in range(row_count):
            sums = [[] for _ in range(block)]
            for chip in range(chips):
                at = (r * chips + chip) * res
                right = right_ref[at : at + res, :]
                for m in range(block):
                    product = lefts[m] * right
                    part = sum((product[k : k + 8] for k in range(8, res, 8)), product[:8])
                    shift = 1
                    while chip & shift:
                        part = join(sums[m].pop(), part, shift)
                        shift *= 2
                    sums[m].append(part)
            for m in range(block):
                place = (triangle_first + n + m) * res + core * row_count + r
                triangle_ref[pl.ds(place, chips, stride=2 * row_count), :] = rounded(sums[m][0])


def near_triangle_kernel(row_count, chips, chunk, pieces, left_ref, right_ref, *refs):
    received, (triangle_ref, across_ref) = refs[:-2], refs[-2:]
    _, core = chip_and_core()

    def some_rows(step, carry):
        first = step * chunk
        triangle_rows(
            row_count, chips, left_ref, right_ref, triangle_ref, first, chunk, core, first
        )
        return carry

    for ref, blocks in zip(received, pieces):
        for n, (chip, r) in enumerate(rows_of_blocks(row_count, blocks)):
            place_right(across_ref, chips, chip, r, ref[n])
    lax.fori_loop(0, row_count * chips // chunk, some_rows, 0)


def attention_inputs(
    row_count,
    chips,
    first,
    norms,
    same_half,
    w_out,
    left_ref,
    gate_ref,
    pairs_ref,
    held_triangle,
    across_ref,
    triangle_ref,
):
    bf16 = jnp.bfloat16
    _, core = chip_and_core()
    half = row_count * chips
    tall = (half // 2) * 2 * half
    rows = pl.ds(pl.multiple_of(first * 2 * half, tall), tall)
    triangle_ref[...] = held_triangle[rows, :]
    triangle_rows(
        row_count, chips, left_ref, across_ref, triangle_ref, first, half // 2, 1 - core, 0
    )
    triangle = triangle_ref[...]
    total = row_sums(triangle, same_half)
    tri_normed = row_norm_by_products(
        triangle, total, norms[2:3, :], norms[3:4, :], same_half
    ).astype(bf16)
    after_tri = pairs_ref[rows, :] + gate_ref[rows, :] * dot(tri_normed, w_out[...])
    total = jnp.sum(after_tri, axis=1, keepdims=True)
    att_in = row_norm_by_products(
        after_tri, total, norms[4:5, :], norms[5:6, :], same_half
    ).astype(bf16)
    return after_tri, att_in


def first_chip(chips, part):
    chip, _ = chip_and_core()
    return jnp.bitwise_xor(jnp.bitwise_and(chip, chips // 2), part * (chips // 2))


def own_inputs_kernel(
    row_count,
    chips,
    blocks,
    norms,
    same_half,
    w_out,
    left_ref,
    gate_ref,
    pairs_ref,
    received,
    triangle_ref,
    held_across,
    across_ref,
    after_ref,
    att_ref,
    scratch_ref,
):
    for n, (chip, r) in enumerate(rows_of_blocks(row_count, blocks)):
        place_right(across_ref, chips, chip, r, received[n])
    first = first_chip(chips, 0) * row_count
    refs = (left_ref, gate_ref, pairs_ref, triangle_ref, across_ref, scratch_ref)
    after_ref[...], att_ref[...] = attention_inputs(
        row_count, chips, first, norms, same_half, w_out, *refs
    )


def other_inputs_kernel(row_count, chips, norms, same_half, w_out, *refs):
    *refs, att_ref, scratch_ref = refs
    first = first_chip(chips, 1) * row_count
    _, att_ref[...] = attention_inputs(
        row_count, chips, first, norms, same_half, w_out, *refs, scratch_ref
    )


def keys_and_values(att, w_key, w_value, key_ref, value_ref):
    channels = key_ref.shape[1]
    key_value = jnp.concatenate([w_key[...], w_value[...]], axis=1)
    start = 0
    for values in att:
        rows = slice(start, start + values.shape[0])
        joined = dot(values, key_value)
        key_ref[rows, :] = rounded(joined[:, :channels])
        value_ref[rows, :] = rounded(joined[:, channels:])
        start = rows.stop


def column_bias(row_count, res, att, wide_bias, att_ref, bias_ref):
    start = 0
    for values in att:
        att_ref[start : start + values.shape[0], :] = values.astype(jnp.float32)
        start += values.shape[0]
    keys = start // res
    own = lax.axis_index("row") * row_count
    height = -(-keys // 8) * 8
    columns = [att_ref[pl.ds(own + r, height, stride=res), :] for r in range(row_count)]
    columns = jnp.concatenate(columns, axis=0).astype(jnp.bfloat16)
    bias = rounded(dot(columns, wide_bias[...]))
    for r in range(row_count):
        bias_ref[r, :height, :] = bias[r * height : (r + 1) * height]


def partial_attention(
    row_count, chips, query, parts, bias_ref, same_head, valid_column, sums, together
):
    bf16 = jnp.bfloat16
    res = 2 * row_count * chips
    channels = valid_column.shape[1]
    count = row_count * chips // 2
    for part, (core, first, key_of, value_of) in enumerate(parts):
        products = []
        for r in range(row_count):
            own_query = query[r * res : (r + 1) * res]
            row = [(key_of(n) * own_query).astype(bf16) for n in range(count)]
            pairs = [jnp.concatenate(row[n : n + 2], axis=1) for n in range(0, count, 2)]
            products.append(jnp.concatenate(pairs, axis=0))
        if together:
            scores = dot(jnp.concatenate(products, axis=0), same_head[...])
            tall = count // 2 * res
            scores = [scores[r * tall : (r + 1) * tall] for r in range(row_count)]
        else:
            scores = [dot(product, same_head[...]) for product in products]

        def score_of(n, r):
            lanes = slice(n % 2 * channels, (n % 2 + 1) * channels)
            k = (2 * (first + n // row_count) + core) * row_count + n % row_count
            key_mask = 1000000000.0 * (valid_column[pl.ds(k, 1), :] - 1.0)
            at = part * count + n
            shift = (bias_ref[r, at : at + 1, :] + key_mask) * math.log2(math.e)
            return scores[r][n // 2 * res : (n // 2 + 1) * res, lanes] + shift

        later = []
        for r, (maximum, total, mixed) in enumerate(sums):
            highest = score_of(0, r)
            for n in range(1, count):
                highest = jnp.maximum(highest, score_of(n, r))
            if maximum is None:
                maximum, total, mixed = highest, 0.0, 0.0
            else:
                highest = jnp.maximum(highest, maximum)
                scale = jnp.exp2(maximum - highest)
                maximum, total, mixed = highest, total * scale, mixed * scale
            for n in range(count):
                weight = jnp.exp2(score_of(n, r) - maximum)
                total = total + weight
                mixed = mixed + weight * value_of(n)
            later.append((maximum, total, mixed))
        sums = later
    return sums


def most_attention_kernel(
    row_count,
    chips,
    valid_column,
    same_head,
    w_query,
    w_gate,
    w_key,
    w_value,
    wide_bias,
    own_att_a,
    own_att_b,
    far_att_a,
    own_after,
    sums_ref,
    query_ref,
    gate_ref,
    after_ref,
    att_ref,
    key_ref,
    value_ref,
    bias_ref,
):
    chip, core = chip_and_core()
    res, channels = valid_column.shape
    own = row_count * res
    rows = pl.ds(pl.multiple_of(jnp.bitwise_and(chip, chips // 2 - 1) * own, own), own)
    own_in = own_att_a[rows, :]
    query = rounded(dot(own_in, w_query[...])) * (math.log2(math.e) / math.sqrt(HEAD_DIM))
    att = [ref[...] for ref in (own_att_a, own_att_b, far_att_a)]
    keys_and_values(att, w_key, w_value, key_ref, value_ref)
    column_bias(row_count, res, att, wide_bias, att_ref, bias_ref)
    count = row_count * chips // 2

    def rows_of(ref, first):
        return lambda n: ref[(first + n) * res : (first + n + 1) * res, :]

    a, b = first_chip(chips, 0), first_chip(chips, 1)
    parts = [
        (sender, first, rows_of(key_ref, n * count), rows_of(value_ref, n * count))
        for n, (sender, first) in enumerate(((core, a), (core, b), (1 - core, a)))
    ]
    none = [(None, None, None)] * row_count
    sums = partial_attention(
        row_count, chips, query, parts, bias_ref, same_head, valid_column, none, True
    )
    for r in range(row_count):
        for n, each in enumerate(sums[r]):
            sums_ref[r, n] = each
    query_ref[...] = query
    gate_ref[...] = sigmoid(dot(own_in, w_gate[...]))
    after_ref[...] = own_after[rows, :]


def attention_kernel(
    row_count,
    chips,
    valid_column,
    same_head,
    w_key,
    w_value,
    w_out,
    wide_bias,
    far_att_b,
    query_ref,
    gate_ref,
    after_ref,
    sums_ref,
    out_ref,
    att_ref,
    key_ref,
    value_ref,
    bias_ref,
):
    _, core = chip_and_core()
    res, channels = valid_column.shape
    far_att = far_att_b[...]
    keys_and_values([far_att], w_key, w_value, key_ref, value_ref)
    column_bias(row_count, res, [far_att], wide_bias, att_ref, bias_ref)

    def rows_of(ref):
        return lambda n: ref[n * res : (n + 1) * res, :]

    parts = ((1 - core, first_chip(chips, 1), rows_of(key_ref), rows_of(value_ref)),)
    sums = [tuple(sums_ref[r, n] for n in range(3)) for r in range(row_count)]
    sums = partial_attention(
        row_count, chips, query_ref[...], parts, bias_ref, same_head, valid_column, sums, False
    )
    attended = [mixed / total for _, total, mixed in sums]
    gated = (jnp.concatenate(attended, axis=0) * gate_ref[...]).astype(jnp.bfloat16)
    final = after_ref[...] + dot(gated, w_out[...])
    out_ref[...] = final.astype(jnp.bfloat16).reshape(row_count, res, channels)


def on_whole_complex(
    pair_rep,
    residue_valid,
    tri_norm_gain,
    tri_norm_bias,
    w_edges,
    w_tri_gate,
    out_norm_gain,
    out_norm_bias,
    w_tri_out,
    att_norm_gain,
    att_norm_bias,
    w_query,
    w_key,
    w_value,
    w_att_gate,
    w_pair_bias,
    w_att_out,
):
    row_count, res, channels = pair_rep.shape
    devices = res // row_count
    chips = devices // 2
    half = res // 2
    f32, bf16 = jnp.float32, jnp.bfloat16
    in_vmem = pl.BlockSpec(memory_space=pltpu.VMEM)

    def shaped(dtype, *shape):
        return jax.ShapeDtypeStruct(shape, dtype)

    def call(kernel, outs, operands, aliases=None, scratch=(), cost=2**25):
        return pl.pallas_call(
            kernel,
            out_shape=outs,
            in_specs=[in_vmem] * len(operands),
            out_specs=jax.tree.map(lambda _: in_vmem, outs),
            input_output_aliases=aliases or {},
            scratch_shapes=list(scratch),
            compiler_params=pltpu.CompilerParams(vmem_limit_bytes=24 * 1024 * 1024),
            cost_estimate=pl.CostEstimate(flops=2**20, bytes_accessed=cost, transcendentals=0),
        )(*operands)

    def exchange(values, bit):
        return lax.ppermute(values, "row", [(d, d ^ bit) for d in range(devices)])

    vectors = (
        tri_norm_gain,
        tri_norm_bias,
        out_norm_gain,
        out_norm_bias,
        att_norm_gain,
        att_norm_bias,
    )
    norms = jnp.stack(vectors)
    is_gate = lax.broadcasted_iota(jnp.int32, (1, 5 * channels), 1) // channels
    halves = jnp.where((is_gate == 0) | (is_gate == 2), 1.0, 0.5).astype(bf16)
    edge_weights = jnp.concatenate([w_edges, w_tri_gate], axis=1) * halves
    valid_column = jnp.broadcast_to(residue_valid.astype(f32)[:, None], (res, channels))

    head = lax.broadcasted_iota(jnp.int32, (HEADS, channels), 0)
    head_of_channel = lax.broadcasted_iota(jnp.int32, (HEADS, channels), 1) // HEAD_DIM
    repeat = jnp.where(head == head_of_channel, 1.0, 0.0).astype(bf16)
    wide_bias = dot(w_pair_bias, repeat).astype(bf16)

    kept = lax.dynamic_update_slice(
        jnp.zeros((2 * row_count, res, channels), bf16), pair_rep, (0, 0, 0)
    )
    far = exchange(pair_rep, devices // 2)
    far, kept, norms, edge_weights = lax.optimization_barrier((far, kept, norms, edge_weights))
    own = lax.dynamic_update_slice(kept, far, (row_count, 0, 0))
    own_blocks = (0, chips // 2)

    def blocks_from(bits):
        return tuple(s ^ bits for s in own_blocks)

    tall = shaped(f32, half * res, channels)

    def edges_of(pieces, send_row, *held):
        pairs = tuple(p for p, _ in pieces)
        blocks = tuple(b for _, b in pieces)
        operands = (valid_column, norms, edge_weights) + pairs + held
        first = len(operands) - len(held)
        return call(
            functools.partial(edges_kernel, row_count, chips, blocks, send_row, not held),
            (tall, tall, tall, tall, shaped(bf16, 4 * row_count, res, channels))
            + (() if held else (shaped(bf16, 2 * channels, 2 * channels),) * 2),
            operands,
            {first + e: e for e in range(len(held))},
        )

    diagonal = exchange(own, 6)
    beside = exchange(own, 2)
    near = exchange(own, 4)
    *edges, early_right, same_head, same_half = edges_of([(own, own_blocks)], 0)
    diagonal, edges = lax.optimization_barrier((diagonal, edges))
    *edges, early_right = edges_of(
        [(diagonal, blocks_from(3))], 2 * row_count, *edges, early_right
    )
    beside, edges, early_right, wide_bias = lax.optimization_barrier(
        (beside, edges, early_right, wide_bias)
    )
    early = (exchange(early_right, 1), own_blocks + blocks_from(3))
    *edges, late_right = edges_of(
        [(beside, blocks_from(1)), (near, blocks_from(2))], 0, *edges
    )
    late = (exchange(late_right, 1), blocks_from(1) + blocks_from(2))

    left, right, gate, pairs = edges
    triangle, across = call(
        functools.partial(near_triangle_kernel, row_count, chips, half // 2, [early[1]]),
        (tall, tall),
        (left, right, early[0]),
    )
    part = half // 2 * res
    in_part, own_shape = shaped(f32, part, channels), shaped(f32, row_count * res, channels)
    att_part = shaped(bf16, part, channels)
    shared = (norms, same_half, w_tri_out, left, gate, pairs)
    scratch = (pltpu.VMEM((part, channels), f32),)
    across, after_a, att_a = call(
        functools.partial(own_inputs_kernel, row_count, chips, late[1]),
        (tall, in_part, att_part),
        shared + (late[0], triangle, across),
        {8: 0},
        scratch=scratch,
    )
    far_att_a = exchange(att_a, 1)
    att_b = call(
        functools.partial(other_inputs_kernel, row_count, chips),
        att_part,
        shared + (triangle, across),
        scratch=scratch,
    )
    far_att_b = exchange(att_b, 1)

    def attention_scratch(keys, projected):
        return (
            pltpu.VMEM((-(-keys // 8) * 8 * res, channels), f32),
            pltpu.VMEM((projected * res, channels), f32),
            pltpu.VMEM((projected * res, channels), f32),
            pltpu.VMEM((row_count, 40, channels), f32),
        )

    sums, query, att_gate, after_own = call(
        functools.partial(most_attention_kernel, row_count, chips),
        (shaped(f32, row_count, 3, res, channels), own_shape, own_shape, own_shape),
        (valid_column, same_head, w_query, w_att_gate, w_key, w_value, wide_bias)
        + (att_a, att_b, far_att_a, after_a),
        scratch=attention_scratch(3 * half // 2, 3 * half // 2),
    )
    return call(
        functools.partial(attention_kernel, row_count, chips),
        shaped(bf16, *pair_rep.shape),
        (valid_column, same_head, w_key, w_value, w_att_out, wide_bias, far_att_b)
        + (query, att_gate, after_own, sums),
        scratch=attention_scratch(half // 2, half // 2),
    )


def per_device(pair_rep, residue_valid, *parameters):
    row_count, res, channels = pair_rep.shape
    devices = res // row_count
    if res % 48 == 0 and devices == 16 and 40 * res * res * channels <= 32 * 1024 * 1024:
        return on_whole_complex(pair_rep, residue_valid, *parameters)
    return split_over_devices(pair_rep, residue_valid, *parameters)


def solution(mesh):
    return jax.shard_map(
        per_device,
        mesh=mesh,
        in_specs=(
            P(("groups", "row"), None, None),
            P("groups"),
            P(),
            P(),
            P(),
            P(),
            P(),
            P(),
            P(),
            P(),
            P(),
            P(),
            P(),
            P(),
            P(),
            P(),
            P(),
        ),
        out_specs=P(("groups", "row"), None, None),
        check_vma=False,
    )
```

```python
import functools
import math

import jax
import jax.numpy as jnp
from jax import lax
from jax.experimental import pallas as pl
from jax.experimental.pallas import tpu as pltpu
from jax.sharding import PartitionSpec as P

HEADS = 4
HEAD_DIM = 32


def layer_norm(values, norm_gain, norm_bias, along_axis):
    centre = values - jnp.mean(values, axis=along_axis, keepdims=True)
    spread = jnp.mean(centre * centre, axis=along_axis, keepdims=True)
    return centre * lax.rsqrt(spread + 1e-05) * norm_gain + norm_bias


def attend(query_cols, key_cols, value_cols, whole_bias, key_mask):
    factor = 1.0 / math.sqrt(HEAD_DIM)
    scores = (
        jnp.einsum("kjhd,ijhd->jhki", key_cols, query_cols, preferred_element_type=jnp.float32)
        * factor
    )
    scores = scores + whole_bias.astype(jnp.float32)[None] + key_mask[None, None, :, None]
    scores = scores - jnp.max(scores, axis=2, keepdims=True)
    exponent = jnp.exp(scores)
    weights = (exponent / jnp.sum(exponent, axis=2, keepdims=True)).astype(jnp.bfloat16)
    return jnp.einsum("jhki,kjhd->ijhd", weights, value_cols, preferred_element_type=jnp.float32)


def split_over_devices(
    pair_rep,
    residue_valid,
    tri_norm_gain,
    tri_norm_bias,
    w_edges,
    w_tri_gate,
    out_norm_gain,
    out_norm_bias,
    w_tri_out,
    att_norm_gain,
    att_norm_bias,
    w_query,
    w_key,
    w_value,
    w_att_gate,
    w_pair_bias,
    w_att_out,
):
    row_count = pair_rep.shape[0]
    res_count = pair_rep.shape[1]
    channels = pair_rep.shape[2]
    hidden_width = HEADS * HEAD_DIM
    row_start = lax.axis_index("row") * row_count
    valid_flags = residue_valid.astype(jnp.float32)
    own_valid = lax.dynamic_slice_in_dim(valid_flags, row_start, row_count)
    normed = layer_norm(pair_rep.astype(jnp.float32), tri_norm_gain, tri_norm_bias, 2).astype(
        jnp.bfloat16
    )
    projected = jnp.einsum("ikd,de->eik", normed, w_edges, preferred_element_type=jnp.float32)
    projected = projected.reshape(4, channels, row_count, res_count)
    pair_mask = (own_valid[:, None] * valid_flags[None, :])[None, :, :]
    left_edges = (jax.nn.sigmoid(projected[1]) * projected[0] * pair_mask).astype(jnp.bfloat16)
    right_edges = (jax.nn.sigmoid(projected[3]) * projected[2] * pair_mask).astype(jnp.bfloat16)
    left_cols, right_cols = (
        lax.all_to_all(left_edges, "row", split_axis=0, concat_axis=1, tiled=True),
        lax.all_to_all(right_edges, "row", split_axis=0, concat_axis=1, tiled=True),
    )
    block_product = jnp.einsum(
        "cik,cjk->cij", left_cols, right_cols, preferred_element_type=jnp.float32
    ).astype(jnp.bfloat16)
    triangle = lax.all_to_all(block_product, "row", split_axis=1, concat_axis=0, tiled=True)
    tri_normed = layer_norm(
        triangle.astype(jnp.float32), out_norm_gain[:, None, None], out_norm_bias[:, None, None], 0
    ).astype(jnp.bfloat16)
    tri_gate = jax.nn.sigmoid(
        jnp.einsum("ijc,ce->ije", normed, w_tri_gate, preferred_element_type=jnp.float32)
    )
    tri_update = jnp.einsum(
        "cij,ce->ije", tri_normed, w_tri_out, preferred_element_type=jnp.float32
    )
    after_tri = pair_rep.astype(jnp.float32) + tri_gate * tri_update
    att_in = layer_norm(after_tri, att_norm_gain, att_norm_bias, 2).astype(jnp.bfloat16)
    pair_bias = jnp.einsum(
        "kic,ch->hki", att_in, w_pair_bias, preferred_element_type=jnp.float32
    ).astype(jnp.bfloat16)
    whole_bias = lax.all_gather(pair_bias, "row", axis=1, tiled=True)
    key_mask = 1000000000.0 * (valid_flags - 1.0)
    columns = lax.all_to_all(att_in, "row", split_axis=1, concat_axis=0, tiled=True)
    all_weights = jnp.concatenate([w_query, w_key, w_value, w_att_gate], axis=1)
    joined = jnp.dot(columns.reshape(-1, channels), all_weights, preferred_element_type=jnp.float32)
    query_cols = (
        joined[:, :hidden_width].astype(jnp.bfloat16).reshape(res_count, row_count, HEADS, HEAD_DIM)
    )
    key_cols = (
        joined[:, hidden_width : 2 * hidden_width]
        .astype(jnp.bfloat16)
        .reshape(res_count, row_count, HEADS, HEAD_DIM)
    )
    value_cols = (
        joined[:, 2 * hidden_width : 3 * hidden_width]
        .astype(jnp.bfloat16)
        .reshape(res_count, row_count, HEADS, HEAD_DIM)
    )
    gate_cols = jax.nn.sigmoid(joined[:, 3 * hidden_width :]).reshape(
        res_count, row_count, hidden_width
    )
    attended = attend(query_cols, key_cols, value_cols, whole_bias, key_mask)
    gated = (attended.reshape(res_count, row_count, hidden_width) * gate_cols).astype(jnp.bfloat16)
    gated_rows = lax.all_to_all(gated, "row", split_axis=0, concat_axis=1, tiled=True)
    final = after_tri + jnp.einsum(
        "ije,ec->ijc", gated_rows, w_att_out, preferred_element_type=jnp.float32
    )
    return final.astype(jnp.bfloat16)


def sigmoid(values):
    return 0.5 * jnp.tanh(0.5 * values) + 0.5


def row_norm(values, norm_gain, norm_bias):
    count = values.shape[1]
    centre = values - jnp.sum(values, axis=1, keepdims=True) * (1.0 / count)
    squares = jnp.sum(centre * centre, axis=1, keepdims=True)
    return centre * lax.rsqrt(squares + 1e-05 * count) * (norm_gain * count**0.5) + norm_bias


def dot(left, right):
    return jnp.dot(left, right, preferred_element_type=jnp.float32)


def rounded(values):
    return values.astype(jnp.bfloat16).astype(jnp.float32)


def chip_and_core():
    device = lax.axis_index("row")
    return lax.shift_right_logical(device, 1), jnp.bitwise_and(device, 1)


def rows_of_blocks(row_count, blocks):
    chip, _ = chip_and_core()
    return [(jnp.bitwise_xor(chip, bits), r) for bits in blocks for r in range(row_count)]


def edges_kernel(
    row_count, chips, pieces, done, send_row, makes_heads, valid_column, norms, weights, *refs
):
    pair_refs = refs[: len(pieces)]
    left_ref, right_ref, gate_ref, pairs_ref, send_ref = refs[-5:]
    if makes_heads:
        left_ref, right_ref, gate_ref, pairs_ref, send_ref, same_head_ref = refs[-6:]
        wide = same_head_ref.shape
        row = lax.broadcasted_iota(jnp.int32, wide, 0) // HEAD_DIM
        column = lax.broadcasted_iota(jnp.int32, wide, 1) // HEAD_DIM
        same_head_ref[...] = jnp.where(row == column, 1.0, 0.0).astype(jnp.bfloat16)
    f32, bf16 = jnp.float32, jnp.bfloat16
    res, channels = valid_column.shape
    held_refs = refs[len(pieces) :]
    for chip, r in rows_of_blocks(row_count, done):
        held_rows = pl.ds(pl.multiple_of((chip * row_count + r) * res, res), res)
        held_columns = pl.ds(pl.multiple_of((r * chips + chip) * res, res), res)
        left_ref[held_rows, :] = held_refs[0][held_rows, :]
        right_ref[held_columns, :] = held_refs[1][held_columns, :]
        gate_ref[held_rows, :] = held_refs[2][held_rows, :]
        pairs_ref[held_rows, :] = held_refs[3][held_rows, :]
    if send_row:
        send_ref[:send_row] = held_refs[4][:send_row]
    _, core = chip_and_core()
    pairs = jnp.concatenate(
        [ref[...].astype(f32).reshape(-1, channels) for ref in pair_refs], axis=0
    )
    normed = row_norm(pairs, norms[0:1, :], norms[1:2, :]).astype(bf16)
    column = 0.5 * valid_column[...]
    rows_of = rows_of_blocks(row_count, [bits for piece in pieces for bits in piece])
    masks = jnp.concatenate(
        [
            column * valid_column[pl.ds((2 * chip + core) * row_count + r, 1), :]
            for chip, r in rows_of
        ],
        axis=0,
    )
    joined = dot(normed, weights[:, : 2 * channels])
    left = rounded((jnp.tanh(joined[:, channels:]) + 1.0) * joined[:, :channels] * masks)
    joined = dot(normed, weights[:, 2 * channels : 4 * channels])
    right = ((jnp.tanh(joined[:, channels:]) + 1.0) * joined[:, :channels] * masks).astype(bf16)
    gate = 0.5 * jnp.tanh(dot(normed, weights[:, 4 * channels :])) + 0.5
    for n, (chip, r) in enumerate(rows_of):
        rows = slice(n * res, (n + 1) * res)
        start = pl.multiple_of((chip * row_count + r) * res, res)
        send_ref[send_row + n] = right[rows]
        left_ref[pl.ds(start, res), :] = left[rows]
        place_right(right_ref, chips, chip, r, right[rows])
        gate_ref[pl.ds(start, res), :] = gate[rows]
        pairs_ref[pl.ds(start, res), :] = pairs[rows]


def place_right(right_ref, chips, chip, r, edges):
    res = edges.shape[0]
    start = pl.multiple_of((r * chips + chip) * res, res)
    right_ref[pl.ds(start, res), :] = edges.astype(jnp.float32)


def join(even, odd, shift):
    high = jnp.bitwise_and(lax.broadcasted_iota(jnp.int32, even.shape, 0), shift) > 0
    return jnp.where(high, odd, even) + pltpu.roll(jnp.where(high, even, odd), shift, 0)


def triangle_rows(
    row_count, chips, left_ref, right_ref, triangle_ref, first, count, core, triangle_first
):
    res = 2 * row_count * chips
    start = pl.multiple_of(first * res, res)
    block = 4
    for n in range(0, count, block):
        lefts = [left_ref[pl.ds(start + m * res, res), :] for m in range(n, n + block)]
        for r in range(row_count):
            sums = [[] for _ in range(block)]
            for chip in range(chips):
                at = (r * chips + chip) * res
                right = right_ref[at : at + res, :]
                for m in range(block):
                    product = lefts[m] * right
                    part = sum((product[k : k + 8] for k in range(8, res, 8)), product[:8])
                    shift = 1
                    while chip & shift:
                        part = join(sums[m].pop(), part, shift)
                        shift *= 2
                    sums[m].append(part)
            for m in range(block):
                place = (triangle_first + n + m) * res + core * row_count + r
                triangle_ref[pl.ds(place, chips, stride=2 * row_count), :] = rounded(sums[m][0])


def near_triangle_kernel(row_count, chips, chunk, left_ref, right_ref, triangle_ref):
    _, core = chip_and_core()

    def some_rows(step, carry):
        first = step * chunk
        triangle_rows(
            row_count, chips, left_ref, right_ref, triangle_ref, first, chunk, core, first
        )
        return carry

    lax.fori_loop(0, row_count * chips // chunk, some_rows, 0)


def attention_inputs(
    row_count, chips, first, norms, w_out, left_ref, gate_ref, pairs_ref, held_triangle, across_ref,
    triangle_ref,
):
    bf16 = jnp.bfloat16
    _, core = chip_and_core()
    half = row_count * chips
    tall = (half // 2) * 2 * half
    rows = pl.ds(pl.multiple_of(first * 2 * half, tall), tall)
    triangle_ref[...] = held_triangle[rows, :]
    triangle_rows(
        row_count, chips, left_ref, across_ref, triangle_ref, first, half // 2, 1 - core, 0
    )
    tri_normed = row_norm(triangle_ref[...], norms[2:3, :], norms[3:4, :]).astype(bf16)
    after_tri = pairs_ref[rows, :] + gate_ref[rows, :] * dot(tri_normed, w_out[...])
    att_in = row_norm(after_tri, norms[4:5, :], norms[5:6, :]).astype(bf16)
    return after_tri, att_in


def first_chip(chips, part):
    chip, _ = chip_and_core()
    return jnp.bitwise_xor(jnp.bitwise_and(chip, chips // 2), part * (chips // 2))


def own_inputs_kernel(
    row_count,
    chips,
    blocks,
    norms,
    w_out,
    left_ref,
    gate_ref,
    pairs_ref,
    early,
    late,
    triangle_ref,
    across_ref,
    after_ref,
    att_ref,
    scratch_ref,
):
    for received, senders in zip((early, late), blocks):
        for n, (chip, r) in enumerate(rows_of_blocks(row_count, senders)):
            place_right(across_ref, chips, chip, r, received[n])
    first = first_chip(chips, 0) * row_count
    refs = (left_ref, gate_ref, pairs_ref, triangle_ref, across_ref, scratch_ref)
    after_ref[...], att_ref[...] = attention_inputs(
        row_count, chips, first, norms, w_out, *refs
    )


def other_inputs_kernel(row_count, chips, norms, w_out, *refs):
    *refs, att_ref, scratch_ref = refs
    first = first_chip(chips, 1) * row_count
    _, att_ref[...] = attention_inputs(row_count, chips, first, norms, w_out, *refs, scratch_ref)


def keys_and_values(att, w_key, w_value, key_ref, value_ref):
    channels = key_ref.shape[1]
    key_value = jnp.concatenate([w_key[...], w_value[...]], axis=1)
    start = 0
    for values in att:
        rows = slice(start, start + values.shape[0])
        joined = dot(values, key_value)
        key_ref[rows, :] = rounded(joined[:, :channels])
        value_ref[rows, :] = rounded(joined[:, channels:])
        start = rows.stop


def column_bias(row_count, res, att, wide_bias, att_ref, bias_ref):
    start = 0
    for values in att:
        att_ref[start : start + values.shape[0], :] = values.astype(jnp.float32)
        start += values.shape[0]
    keys = start // res
    own = lax.axis_index("row") * row_count
    height = -(-keys // 8) * 8
    columns = [att_ref[pl.ds(own + r, height, stride=res), :] for r in range(row_count)]
    columns = jnp.concatenate(columns, axis=0).astype(jnp.bfloat16)
    bias = rounded(dot(columns, wide_bias[...]))
    for r in range(row_count):
        bias_ref[r, :height, :] = bias[r * height : (r + 1) * height]


def partial_attention(
    row_count, chips, query, parts, bias_ref, same_head, valid_column, sums, together
):
    bf16 = jnp.bfloat16
    res = 2 * row_count * chips
    channels = valid_column.shape[1]
    count = row_count * chips // 2
    for part, (core, first, key_of, value_of) in enumerate(parts):
        products = []
        for r in range(row_count):
            own_query = query[r * res : (r + 1) * res]
            row = [(key_of(n) * own_query).astype(bf16) for n in range(count)]
            pairs = [jnp.concatenate(row[n : n + 2], axis=1) for n in range(0, count, 2)]
            products.append(jnp.concatenate(pairs, axis=0))
        if together:
            scores = dot(jnp.concatenate(products, axis=0), same_head[...])
            tall = count // 2 * res
            scores = [scores[r * tall : (r + 1) * tall] for r in range(row_count)]
        else:
            scores = [dot(product, same_head[...]) for product in products]

        def score_of(n, r):
            lanes = slice(n % 2 * channels, (n % 2 + 1) * channels)
            k = (2 * (first + n // row_count) + core) * row_count + n % row_count
            key_mask = 1000000000.0 * (valid_column[pl.ds(k, 1), :] - 1.0)
            at = part * count + n
            shift = (bias_ref[r, at : at + 1, :] + key_mask) * math.log2(math.e)
            return scores[r][n // 2 * res : (n // 2 + 1) * res, lanes] + shift

        later = []
        for r, (maximum, total, mixed) in enumerate(sums):
            highest = score_of(0, r)
            for n in range(1, count):
                highest = jnp.maximum(highest, score_of(n, r))
            if maximum is None:
                maximum, total, mixed = highest, 0.0, 0.0
            else:
                highest = jnp.maximum(highest, maximum)
                scale = jnp.exp2(maximum - highest)
                maximum, total, mixed = highest, total * scale, mixed * scale
            for n in range(count):
                weight = jnp.exp2(score_of(n, r) - maximum)
                total = total + weight
                mixed = mixed + weight * value_of(n)
            later.append((maximum, total, mixed))
        sums = later
    return sums


def most_attention_kernel(
    row_count,
    chips,
    valid_column,
    same_head,
    w_query,
    w_gate,
    w_key,
    w_value,
    wide_bias,
    own_att_a,
    own_att_b,
    far_att_a,
    own_after,
    sums_ref,
    query_ref,
    gate_ref,
    after_ref,
    att_ref,
    key_ref,
    value_ref,
    bias_ref,
):
    chip, core = chip_and_core()
    res, channels = valid_column.shape
    own = row_count * res
    rows = pl.ds(pl.multiple_of(jnp.bitwise_and(chip, chips // 2 - 1) * own, own), own)
    own_in = own_att_a[rows, :]
    query = rounded(dot(own_in, w_query[...])) * (math.log2(math.e) / math.sqrt(HEAD_DIM))
    att = [ref[...] for ref in (own_att_a, own_att_b, far_att_a)]
    keys_and_values(att, w_key, w_value, key_ref, value_ref)
    column_bias(row_count, res, att, wide_bias, att_ref, bias_ref)
    count = row_count * chips // 2

    def rows_of(ref, first):
        return lambda n: ref[(first + n) * res : (first + n + 1) * res, :]

    a, b = first_chip(chips, 0), first_chip(chips, 1)
    parts = [
        (sender, first, rows_of(key_ref, n * count), rows_of(value_ref, n * count))
        for n, (sender, first) in enumerate(((core, a), (core, b), (1 - core, a)))
    ]
    none = [(None, None, None)] * row_count
    sums = partial_attention(
        row_count, chips, query, parts, bias_ref, same_head, valid_column, none, True
    )
    for r in range(row_count):
        for n, each in enumerate(sums[r]):
            sums_ref[r, n] = each
    query_ref[...] = query
    gate_ref[...] = sigmoid(dot(own_in, w_gate[...]))
    after_ref[...] = own_after[rows, :]


def attention_kernel(
    row_count,
    chips,
    valid_column,
    same_head,
    w_key,
    w_value,
    w_out,
    wide_bias,
    far_att_b,
    query_ref,
    gate_ref,
    after_ref,
    sums_ref,
    out_ref,
    att_ref,
    key_ref,
    value_ref,
    bias_ref,
):
    _, core = chip_and_core()
    res, channels = valid_column.shape
    far_att = far_att_b[...]
    keys_and_values([far_att], w_key, w_value, key_ref, value_ref)
    column_bias(row_count, res, [far_att], wide_bias, att_ref, bias_ref)

    def rows_of(ref):
        return lambda n: ref[n * res : (n + 1) * res, :]

    parts = ((1 - core, first_chip(chips, 1), rows_of(key_ref), rows_of(value_ref)),)
    sums = [tuple(sums_ref[r, n] for n in range(3)) for r in range(row_count)]
    sums = partial_attention(
        row_count, chips, query_ref[...], parts, bias_ref, same_head, valid_column, sums, False
    )
    attended = [mixed / total for _, total, mixed in sums]
    gated = (jnp.concatenate(attended, axis=0) * gate_ref[...]).astype(jnp.bfloat16)
    final = after_ref[...] + dot(gated, w_out[...])
    out_ref[...] = final.astype(jnp.bfloat16).reshape(row_count, res, channels)


def on_whole_complex(
    pair_rep,
    residue_valid,
    tri_norm_gain,
    tri_norm_bias,
    w_edges,
    w_tri_gate,
    out_norm_gain,
    out_norm_bias,
    w_tri_out,
    att_norm_gain,
    att_norm_bias,
    w_query,
    w_key,
    w_value,
    w_att_gate,
    w_pair_bias,
    w_att_out,
):
    row_count, res, channels = pair_rep.shape
    devices = res // row_count
    chips = devices // 2
    half = res // 2
    f32, bf16 = jnp.float32, jnp.bfloat16
    in_vmem = pl.BlockSpec(memory_space=pltpu.VMEM)

    def shaped(dtype, *shape):
        return jax.ShapeDtypeStruct(shape, dtype)

    def call(kernel, outs, operands, aliases=None, scratch=(), cost=2**25):
        return pl.pallas_call(
            kernel,
            out_shape=outs,
            in_specs=[in_vmem] * len(operands),
            out_specs=jax.tree.map(lambda _: in_vmem, outs),
            input_output_aliases=aliases or {},
            scratch_shapes=list(scratch),
            compiler_params=pltpu.CompilerParams(vmem_limit_bytes=24 * 1024 * 1024),
            cost_estimate=pl.CostEstimate(flops=2**20, bytes_accessed=cost, transcendentals=0),
        )(*operands)

    def exchange(values, bit):
        return lax.ppermute(values, "row", [(d, d ^ bit) for d in range(devices)])

    vectors = (
        tri_norm_gain,
        tri_norm_bias,
        out_norm_gain,
        out_norm_bias,
        att_norm_gain,
        att_norm_bias,
    )
    norms = jnp.stack(vectors)
    is_gate = lax.broadcasted_iota(jnp.int32, (1, 5 * channels), 1) // channels
    halves = jnp.where((is_gate == 0) | (is_gate == 2), 1.0, 0.5).astype(bf16)
    edge_weights = jnp.concatenate([w_edges, w_tri_gate], axis=1) * halves
    valid_column = jnp.broadcast_to(residue_valid.astype(f32)[:, None], (res, channels))

    head = lax.broadcasted_iota(jnp.int32, (HEADS, channels), 0)
    head_of_channel = lax.broadcasted_iota(jnp.int32, (HEADS, channels), 1) // HEAD_DIM
    repeat = jnp.where(head == head_of_channel, 1.0, 0.0).astype(bf16)
    wide_bias = dot(w_pair_bias, repeat).astype(bf16)

    kept = lax.dynamic_update_slice(
        jnp.zeros((2 * row_count, res, channels), bf16), pair_rep, (0, 0, 0)
    )
    far = exchange(pair_rep, devices // 2)
    far, kept, norms, edge_weights = lax.optimization_barrier((far, kept, norms, edge_weights))
    own = lax.dynamic_update_slice(kept, far, (row_count, 0, 0))
    own_blocks = (0, chips // 2)

    def blocks_from(bits):
        return tuple(s ^ bits for s in own_blocks)

    tall = shaped(f32, half * res, channels)

    def edges_of(pieces, done, send_row, *held):
        pairs = tuple(p for p, _ in pieces)
        blocks = tuple(b for _, b in pieces)
        operands = (valid_column, norms, edge_weights) + pairs + held
        return call(
            functools.partial(edges_kernel, row_count, chips, blocks, done, send_row, not held),
            (tall, tall, tall, tall, shaped(bf16, 4 * row_count, res, channels))
            + (() if held else (shaped(bf16, 2 * channels, 2 * channels),)),
            operands,
        )

    diagonal = exchange(own, 6)
    beside = exchange(own, 2)
    near = exchange(own, 4)
    *edges, early_right, same_head = edges_of([(own, own_blocks)], (), 0)
    diagonal, edges = lax.optimization_barrier((diagonal, edges))
    *edges, early_right = edges_of(
        [(diagonal, blocks_from(3))], own_blocks, 2 * row_count, *edges, early_right
    )
    beside, edges, early_right, wide_bias = lax.optimization_barrier(
        (beside, edges, early_right, wide_bias)
    )
    early = (exchange(early_right, 1), own_blocks + blocks_from(3))
    *edges, late_right = edges_of(
        [(beside, blocks_from(1)), (near, blocks_from(2))], early[1], 0, *edges
    )
    late = (exchange(late_right, 1), blocks_from(1) + blocks_from(2))

    left, right, gate, pairs = edges
    triangle = call(
        functools.partial(near_triangle_kernel, row_count, chips, half // 2), tall, (left, right)
    )
    part = half // 2 * res
    in_part, own_shape = shaped(f32, part, channels), shaped(f32, row_count * res, channels)
    att_part = shaped(bf16, part, channels)
    shared = (norms, w_tri_out, left, gate, pairs)
    scratch = (pltpu.VMEM((part, channels), f32),)
    across, after_a, att_a = call(
        functools.partial(own_inputs_kernel, row_count, chips, (early[1], late[1])),
        (tall, in_part, att_part),
        shared + (early[0], late[0], triangle),
        scratch=scratch,
    )
    far_att_a = exchange(att_a, 1)
    att_b = call(
        functools.partial(other_inputs_kernel, row_count, chips),
        att_part,
        shared + (triangle, across),
        scratch=scratch,
    )
    far_att_b = exchange(att_b, 1)

    def attention_scratch(keys, projected):
        return (
            pltpu.VMEM((-(-keys // 8) * 8 * res, channels), f32),
            pltpu.VMEM((projected * res, channels), f32),
            pltpu.VMEM((projected * res, channels), f32),
            pltpu.VMEM((row_count, 40, channels), f32),
        )

    sums, query, att_gate, after_own = call(
        functools.partial(most_attention_kernel, row_count, chips),
        (shaped(f32, row_count, 3, res, channels), own_shape, own_shape, own_shape),
        (valid_column, same_head, w_query, w_att_gate, w_key, w_value, wide_bias)
        + (att_a, att_b, far_att_a, after_a),
        scratch=attention_scratch(3 * half // 2, 3 * half // 2),
    )
    return call(
        functools.partial(attention_kernel, row_count, chips),
        shaped(bf16, *pair_rep.shape),
        (valid_column, same_head, w_key, w_value, w_att_out, wide_bias, far_att_b)
        + (query, att_gate, after_own, sums),
        scratch=attention_scratch(half // 2, half // 2),
    )


def per_device(pair_rep, residue_valid, *parameters):
    row_count, res, channels = pair_rep.shape
    devices = res // row_count
    if res % 48 == 0 and devices == 16 and 40 * res * res * channels <= 32 * 1024 * 1024:
        return on_whole_complex(pair_rep, residue_valid, *parameters)
    return split_over_devices(pair_rep, residue_valid, *parameters)


def solution(mesh):
    return jax.shard_map(
        per_device,
        mesh=mesh,
        in_specs=(
            P(("groups", "row"), None, None),
            P("groups"),
            P(),
            P(),
            P(),
            P(),
            P(),
            P(),
            P(),
            P(),
            P(),
            P(),
            P(),
            P(),
            P(),
            P(),
            P(),
        ),
        out_specs=P(("groups", "row"), None, None),
        check_vma=False,
    )
```

```python
import functools
import math

import jax
import jax.numpy as jnp
from jax import lax
from jax.experimental import pallas as pl
from jax.experimental.pallas import tpu as pltpu
from jax.sharding import PartitionSpec as P

HEADS = 4
HEAD_DIM = 32


def layer_norm(values, norm_gain, norm_bias, along_axis):
    centre = values - jnp.mean(values, axis=along_axis, keepdims=True)
    spread = jnp.mean(centre * centre, axis=along_axis, keepdims=True)
    return centre * lax.rsqrt(spread + 1e-05) * norm_gain + norm_bias


def attend(query_cols, key_cols, value_cols, whole_bias, key_mask):
    factor = 1.0 / math.sqrt(HEAD_DIM)
    scores = (
        jnp.einsum("kjhd,ijhd->jhki", key_cols, query_cols, preferred_element_type=jnp.float32)
        * factor
    )
    scores = scores + whole_bias.astype(jnp.float32)[None] + key_mask[None, None, :, None]
    scores = scores - jnp.max(scores, axis=2, keepdims=True)
    exponent = jnp.exp(scores)
    weights = (exponent / jnp.sum(exponent, axis=2, keepdims=True)).astype(jnp.bfloat16)
    return jnp.einsum("jhki,kjhd->ijhd", weights, value_cols, preferred_element_type=jnp.float32)


def split_over_devices(
    pair_rep,
    residue_valid,
    tri_norm_gain,
    tri_norm_bias,
    w_edges,
    w_tri_gate,
    out_norm_gain,
    out_norm_bias,
    w_tri_out,
    att_norm_gain,
    att_norm_bias,
    w_query,
    w_key,
    w_value,
    w_att_gate,
    w_pair_bias,
    w_att_out,
):
    row_count = pair_rep.shape[0]
    res_count = pair_rep.shape[1]
    channels = pair_rep.shape[2]
    hidden_width = HEADS * HEAD_DIM
    row_start = lax.axis_index("row") * row_count
    valid_flags = residue_valid.astype(jnp.float32)
    own_valid = lax.dynamic_slice_in_dim(valid_flags, row_start, row_count)
    normed = layer_norm(pair_rep.astype(jnp.float32), tri_norm_gain, tri_norm_bias, 2).astype(
        jnp.bfloat16
    )
    projected = jnp.einsum("ikd,de->eik", normed, w_edges, preferred_element_type=jnp.float32)
    projected = projected.reshape(4, channels, row_count, res_count)
    pair_mask = (own_valid[:, None] * valid_flags[None, :])[None, :, :]
    left_edges = (jax.nn.sigmoid(projected[1]) * projected[0] * pair_mask).astype(jnp.bfloat16)
    right_edges = (jax.nn.sigmoid(projected[3]) * projected[2] * pair_mask).astype(jnp.bfloat16)
    left_cols, right_cols = (
        lax.all_to_all(left_edges, "row", split_axis=0, concat_axis=1, tiled=True),
        lax.all_to_all(right_edges, "row", split_axis=0, concat_axis=1, tiled=True),
    )
    block_product = jnp.einsum(
        "cik,cjk->cij", left_cols, right_cols, preferred_element_type=jnp.float32
    ).astype(jnp.bfloat16)
    triangle = lax.all_to_all(block_product, "row", split_axis=1, concat_axis=0, tiled=True)
    tri_normed = layer_norm(
        triangle.astype(jnp.float32), out_norm_gain[:, None, None], out_norm_bias[:, None, None], 0
    ).astype(jnp.bfloat16)
    tri_gate = jax.nn.sigmoid(
        jnp.einsum("ijc,ce->ije", normed, w_tri_gate, preferred_element_type=jnp.float32)
    )
    tri_update = jnp.einsum(
        "cij,ce->ije", tri_normed, w_tri_out, preferred_element_type=jnp.float32
    )
    after_tri = pair_rep.astype(jnp.float32) + tri_gate * tri_update
    att_in = layer_norm(after_tri, att_norm_gain, att_norm_bias, 2).astype(jnp.bfloat16)
    pair_bias = jnp.einsum(
        "kic,ch->hki", att_in, w_pair_bias, preferred_element_type=jnp.float32
    ).astype(jnp.bfloat16)
    whole_bias = lax.all_gather(pair_bias, "row", axis=1, tiled=True)
    key_mask = 1000000000.0 * (valid_flags - 1.0)
    columns = lax.all_to_all(att_in, "row", split_axis=1, concat_axis=0, tiled=True)
    all_weights = jnp.concatenate([w_query, w_key, w_value, w_att_gate], axis=1)
    joined = jnp.dot(columns.reshape(-1, channels), all_weights, preferred_element_type=jnp.float32)
    query_cols = (
        joined[:, :hidden_width].astype(jnp.bfloat16).reshape(res_count, row_count, HEADS, HEAD_DIM)
    )
    key_cols = (
        joined[:, hidden_width : 2 * hidden_width]
        .astype(jnp.bfloat16)
        .reshape(res_count, row_count, HEADS, HEAD_DIM)
    )
    value_cols = (
        joined[:, 2 * hidden_width : 3 * hidden_width]
        .astype(jnp.bfloat16)
        .reshape(res_count, row_count, HEADS, HEAD_DIM)
    )
    gate_cols = jax.nn.sigmoid(joined[:, 3 * hidden_width :]).reshape(
        res_count, row_count, hidden_width
    )
    attended = attend(query_cols, key_cols, value_cols, whole_bias, key_mask)
    gated = (attended.reshape(res_count, row_count, hidden_width) * gate_cols).astype(jnp.bfloat16)
    gated_rows = lax.all_to_all(gated, "row", split_axis=0, concat_axis=1, tiled=True)
    final = after_tri + jnp.einsum(
        "ije,ec->ijc", gated_rows, w_att_out, preferred_element_type=jnp.float32
    )
    return final.astype(jnp.bfloat16)


def sigmoid(values):
    return 0.5 * jnp.tanh(0.5 * values) + 0.5


def row_norm(values, norm_gain, norm_bias):
    count = values.shape[1]
    centre = values - jnp.sum(values, axis=1, keepdims=True) * (1.0 / count)
    squares = jnp.sum(centre * centre, axis=1, keepdims=True)
    return centre * lax.rsqrt(squares + 1e-05 * count) * (norm_gain * count**0.5) + norm_bias


def dot(left, right):
    return jnp.dot(left, right, preferred_element_type=jnp.float32)


def rounded(values):
    return values.astype(jnp.bfloat16).astype(jnp.float32)


def chip_and_core():
    device = lax.axis_index("row")
    return lax.shift_right_logical(device, 1), jnp.bitwise_and(device, 1)


def rows_of_blocks(row_count, blocks):
    chip, _ = chip_and_core()
    return [(jnp.bitwise_xor(chip, bits), r) for bits in blocks for r in range(row_count)]


def edges_kernel(
    row_count, chips, pieces, done, send_row, makes_heads, valid_column, norms, weights, *refs
):
    pair_refs = refs[: len(pieces)]
    left_ref, right_ref, gate_ref, pairs_ref, send_ref = refs[-5:]
    if makes_heads:
        left_ref, right_ref, gate_ref, pairs_ref, send_ref, same_head_ref = refs[-6:]
        wide = same_head_ref.shape
        row = lax.broadcasted_iota(jnp.int32, wide, 0) // HEAD_DIM
        column = lax.broadcasted_iota(jnp.int32, wide, 1) // HEAD_DIM
        same_head_ref[...] = jnp.where(row == column, 1.0, 0.0).astype(jnp.bfloat16)
    f32, bf16 = jnp.float32, jnp.bfloat16
    res, channels = valid_column.shape
    held_refs = refs[len(pieces) :]
    for chip, r in rows_of_blocks(row_count, done):
        held_rows = pl.ds(pl.multiple_of((chip * row_count + r) * res, res), res)
        held_columns = pl.ds(pl.multiple_of((r * chips + chip) * res, res), res)
        left_ref[held_rows, :] = held_refs[0][held_rows, :]
        right_ref[held_columns, :] = held_refs[1][held_columns, :]
        gate_ref[held_rows, :] = held_refs[2][held_rows, :]
        pairs_ref[held_rows, :] = held_refs[3][held_rows, :]
    if send_row:
        send_ref[:send_row] = held_refs[4][:send_row]
    _, core = chip_and_core()
    pairs = jnp.concatenate(
        [ref[...].astype(f32).reshape(-1, channels) for ref in pair_refs], axis=0
    )
    normed = row_norm(pairs, norms[0:1, :], norms[1:2, :]).astype(bf16)
    column = 0.5 * valid_column[...]
    rows_of = rows_of_blocks(row_count, [bits for piece in pieces for bits in piece])
    masks = jnp.concatenate(
        [
            column * valid_column[pl.ds((2 * chip + core) * row_count + r, 1), :]
            for chip, r in rows_of
        ],
        axis=0,
    )
    joined = dot(normed, weights[:, : 2 * channels])
    left = rounded((jnp.tanh(joined[:, channels:]) + 1.0) * joined[:, :channels] * masks)
    joined = dot(normed, weights[:, 2 * channels : 4 * channels])
    right = ((jnp.tanh(joined[:, channels:]) + 1.0) * joined[:, :channels] * masks).astype(bf16)
    gate = 0.5 * jnp.tanh(dot(normed, weights[:, 4 * channels :])) + 0.5
    for n, (chip, r) in enumerate(rows_of):
        rows = slice(n * res, (n + 1) * res)
        start = pl.multiple_of((chip * row_count + r) * res, res)
        send_ref[send_row + n] = right[rows]
        left_ref[pl.ds(start, res), :] = left[rows]
        place_right(right_ref, chips, chip, r, right[rows])
        gate_ref[pl.ds(start, res), :] = gate[rows]
        pairs_ref[pl.ds(start, res), :] = pairs[rows]


def place_right(right_ref, chips, chip, r, edges):
    res = edges.shape[0]
    start = pl.multiple_of((r * chips + chip) * res, res)
    right_ref[pl.ds(start, res), :] = edges.astype(jnp.float32)


def join(even, odd, shift):
    high = jnp.bitwise_and(lax.broadcasted_iota(jnp.int32, even.shape, 0), shift) > 0
    return jnp.where(high, odd, even) + pltpu.roll(jnp.where(high, even, odd), shift, 0)


def triangle_rows(
    row_count, chips, left_ref, right_ref, triangle_ref, first, count, core, triangle_first
):
    res = 2 * row_count * chips
    start = pl.multiple_of(first * res, res)
    block = 4
    for n in range(0, count, block):
        lefts = [left_ref[pl.ds(start + m * res, res), :] for m in range(n, n + block)]
        for r in range(row_count):
            sums = [[] for _ in range(block)]
            for chip in range(chips):
                at = (r * chips + chip) * res
                right = right_ref[at : at + res, :]
                for m in range(block):
                    product = lefts[m] * right
                    part = sum((product[k : k + 8] for k in range(8, res, 8)), product[:8])
                    shift = 1
                    while chip & shift:
                        part = join(sums[m].pop(), part, shift)
                        shift *= 2
                    sums[m].append(part)
            for m in range(block):
                place = (triangle_first + n + m) * res + core * row_count + r
                triangle_ref[pl.ds(place, chips, stride=2 * row_count), :] = rounded(sums[m][0])


def near_triangle_kernel(row_count, chips, chunk, pieces, left_ref, right_ref, *refs):
    received, (triangle_ref, across_ref) = refs[:-2], refs[-2:]
    _, core = chip_and_core()

    def some_rows(step, carry):
        first = step * chunk
        triangle_rows(
            row_count, chips, left_ref, right_ref, triangle_ref, first, chunk, core, first
        )
        return carry

    for ref, blocks in zip(received, pieces):
        for n, (chip, r) in enumerate(rows_of_blocks(row_count, blocks)):
            place_right(across_ref, chips, chip, r, ref[n])
    lax.fori_loop(0, row_count * chips // chunk, some_rows, 0)


def attention_inputs(
    row_count, chips, first, norms, w_out, left_ref, gate_ref, pairs_ref, held_triangle, across_ref,
    triangle_ref,
):
    bf16 = jnp.bfloat16
    _, core = chip_and_core()
    half = row_count * chips
    tall = (half // 2) * 2 * half
    rows = pl.ds(pl.multiple_of(first * 2 * half, tall), tall)
    triangle_ref[...] = held_triangle[rows, :]
    triangle_rows(
        row_count, chips, left_ref, across_ref, triangle_ref, first, half // 2, 1 - core, 0
    )
    tri_normed = row_norm(triangle_ref[...], norms[2:3, :], norms[3:4, :]).astype(bf16)
    after_tri = pairs_ref[rows, :] + gate_ref[rows, :] * dot(tri_normed, w_out[...])
    att_in = row_norm(after_tri, norms[4:5, :], norms[5:6, :]).astype(bf16)
    return after_tri, att_in


def first_chip(chips, part):
    chip, _ = chip_and_core()
    return jnp.bitwise_xor(jnp.bitwise_and(chip, chips // 2), part * (chips // 2))


def own_inputs_kernel(
    row_count,
    chips,
    blocks,
    norms,
    w_out,
    left_ref,
    gate_ref,
    pairs_ref,
    received,
    triangle_ref,
    held_across,
    across_ref,
    after_ref,
    att_ref,
    scratch_ref,
):
    early, late = blocks
    res = held_across.shape[0] // (row_count * chips)
    for chip, r in rows_of_blocks(row_count, early):
        held = pl.ds(pl.multiple_of((r * chips + chip) * res, res), res)
        across_ref[held, :] = held_across[held, :]
    for n, (chip, r) in enumerate(rows_of_blocks(row_count, late)):
        place_right(across_ref, chips, chip, r, received[n])
    first = first_chip(chips, 0) * row_count
    refs = (left_ref, gate_ref, pairs_ref, triangle_ref, across_ref, scratch_ref)
    after_ref[...], att_ref[...] = attention_inputs(
        row_count, chips, first, norms, w_out, *refs
    )


def other_inputs_kernel(row_count, chips, norms, w_out, *refs):
    *refs, att_ref, scratch_ref = refs
    first = first_chip(chips, 1) * row_count
    _, att_ref[...] = attention_inputs(row_count, chips, first, norms, w_out, *refs, scratch_ref)


def keys_and_values(att, w_key, w_value, key_ref, value_ref):
    channels = key_ref.shape[1]
    key_value = jnp.concatenate([w_key[...], w_value[...]], axis=1)
    start = 0
    for values in att:
        rows = slice(start, start + values.shape[0])
        joined = dot(values, key_value)
        key_ref[rows, :] = rounded(joined[:, :channels])
        value_ref[rows, :] = rounded(joined[:, channels:])
        start = rows.stop


def column_bias(row_count, res, att, wide_bias, att_ref, bias_ref):
    start = 0
    for values in att:
        att_ref[start : start + values.shape[0], :] = values.astype(jnp.float32)
        start += values.shape[0]
    keys = start // res
    own = lax.axis_index("row") * row_count
    height = -(-keys // 8) * 8
    columns = [att_ref[pl.ds(own + r, height, stride=res), :] for r in range(row_count)]
    columns = jnp.concatenate(columns, axis=0).astype(jnp.bfloat16)
    bias = rounded(dot(columns, wide_bias[...]))
    for r in range(row_count):
        bias_ref[r, :height, :] = bias[r * height : (r + 1) * height]


def partial_attention(
    row_count, chips, query, parts, bias_ref, same_head, valid_column, sums, together
):
    bf16 = jnp.bfloat16
    res = 2 * row_count * chips
    channels = valid_column.shape[1]
    count = row_count * chips // 2
    for part, (core, first, key_of, value_of) in enumerate(parts):
        products = []
        for r in range(row_count):
            own_query = query[r * res : (r + 1) * res]
            row = [(key_of(n) * own_query).astype(bf16) for n in range(count)]
            pairs = [jnp.concatenate(row[n : n + 2], axis=1) for n in range(0, count, 2)]
            products.append(jnp.concatenate(pairs, axis=0))
        if together:
            scores = dot(jnp.concatenate(products, axis=0), same_head[...])
            tall = count // 2 * res
            scores = [scores[r * tall : (r + 1) * tall] for r in range(row_count)]
        else:
            scores = [dot(product, same_head[...]) for product in products]

        def score_of(n, r):
            lanes = slice(n % 2 * channels, (n % 2 + 1) * channels)
            k = (2 * (first + n // row_count) + core) * row_count + n % row_count
            key_mask = 1000000000.0 * (valid_column[pl.ds(k, 1), :] - 1.0)
            at = part * count + n
            shift = (bias_ref[r, at : at + 1, :] + key_mask) * math.log2(math.e)
            return scores[r][n // 2 * res : (n // 2 + 1) * res, lanes] + shift

        later = []
        for r, (maximum, total, mixed) in enumerate(sums):
            highest = score_of(0, r)
            for n in range(1, count):
                highest = jnp.maximum(highest, score_of(n, r))
            if maximum is None:
                maximum, total, mixed = highest, 0.0, 0.0
            else:
                highest = jnp.maximum(highest, maximum)
                scale = jnp.exp2(maximum - highest)
                maximum, total, mixed = highest, total * scale, mixed * scale
            for n in range(count):
                weight = jnp.exp2(score_of(n, r) - maximum)
                total = total + weight
                mixed = mixed + weight * value_of(n)
            later.append((maximum, total, mixed))
        sums = later
    return sums


def most_attention_kernel(
    row_count,
    chips,
    valid_column,
    same_head,
    w_query,
    w_gate,
    w_key,
    w_value,
    wide_bias,
    own_att_a,
    own_att_b,
    far_att_a,
    own_after,
    sums_ref,
    query_ref,
    gate_ref,
    after_ref,
    att_ref,
    key_ref,
    value_ref,
    bias_ref,
):
    chip, core = chip_and_core()
    res, channels = valid_column.shape
    own = row_count * res
    rows = pl.ds(pl.multiple_of(jnp.bitwise_and(chip, chips // 2 - 1) * own, own), own)
    own_in = own_att_a[rows, :]
    query = rounded(dot(own_in, w_query[...])) * (math.log2(math.e) / math.sqrt(HEAD_DIM))
    att = [ref[...] for ref in (own_att_a, own_att_b, far_att_a)]
    keys_and_values(att, w_key, w_value, key_ref, value_ref)
    column_bias(row_count, res, att, wide_bias, att_ref, bias_ref)
    count = row_count * chips // 2

    def rows_of(ref, first):
        return lambda n: ref[(first + n) * res : (first + n + 1) * res, :]

    a, b = first_chip(chips, 0), first_chip(chips, 1)
    parts = [
        (sender, first, rows_of(key_ref, n * count), rows_of(value_ref, n * count))
        for n, (sender, first) in enumerate(((core, a), (core, b), (1 - core, a)))
    ]
    none = [(None, None, None)] * row_count
    sums = partial_attention(
        row_count, chips, query, parts, bias_ref, same_head, valid_column, none, True
    )
    for r in range(row_count):
        for n, each in enumerate(sums[r]):
            sums_ref[r, n] = each
    query_ref[...] = query
    gate_ref[...] = sigmoid(dot(own_in, w_gate[...]))
    after_ref[...] = own_after[rows, :]


def attention_kernel(
    row_count,
    chips,
    valid_column,
    same_head,
    w_key,
    w_value,
    w_out,
    wide_bias,
    far_att_b,
    query_ref,
    gate_ref,
    after_ref,
    sums_ref,
    out_ref,
    att_ref,
    key_ref,
    value_ref,
    bias_ref,
):
    _, core = chip_and_core()
    res, channels = valid_column.shape
    far_att = far_att_b[...]
    keys_and_values([far_att], w_key, w_value, key_ref, value_ref)
    column_bias(row_count, res, [far_att], wide_bias, att_ref, bias_ref)

    def rows_of(ref):
        return lambda n: ref[n * res : (n + 1) * res, :]

    parts = ((1 - core, first_chip(chips, 1), rows_of(key_ref), rows_of(value_ref)),)
    sums = [tuple(sums_ref[r, n] for n in range(3)) for r in range(row_count)]
    sums = partial_attention(
        row_count, chips, query_ref[...], parts, bias_ref, same_head, valid_column, sums, False
    )
    attended = [mixed / total for _, total, mixed in sums]
    gated = (jnp.concatenate(attended, axis=0) * gate_ref[...]).astype(jnp.bfloat16)
    final = after_ref[...] + dot(gated, w_out[...])
    out_ref[...] = final.astype(jnp.bfloat16).reshape(row_count, res, channels)


def on_whole_complex(
    pair_rep,
    residue_valid,
    tri_norm_gain,
    tri_norm_bias,
    w_edges,
    w_tri_gate,
    out_norm_gain,
    out_norm_bias,
    w_tri_out,
    att_norm_gain,
    att_norm_bias,
    w_query,
    w_key,
    w_value,
    w_att_gate,
    w_pair_bias,
    w_att_out,
):
    row_count, res, channels = pair_rep.shape
    devices = res // row_count
    chips = devices // 2
    half = res // 2
    f32, bf16 = jnp.float32, jnp.bfloat16
    in_vmem = pl.BlockSpec(memory_space=pltpu.VMEM)

    def shaped(dtype, *shape):
        return jax.ShapeDtypeStruct(shape, dtype)

    def call(kernel, outs, operands, scratch=(), cost=2**25):
        return pl.pallas_call(
            kernel,
            out_shape=outs,
            in_specs=[in_vmem] * len(operands),
            out_specs=jax.tree.map(lambda _: in_vmem, outs),
            scratch_shapes=list(scratch),
            compiler_params=pltpu.CompilerParams(vmem_limit_bytes=24 * 1024 * 1024),
            cost_estimate=pl.CostEstimate(flops=2**20, bytes_accessed=cost, transcendentals=0),
        )(*operands)

    def exchange(values, bit):
        return lax.ppermute(values, "row", [(d, d ^ bit) for d in range(devices)])

    vectors = (
        tri_norm_gain,
        tri_norm_bias,
        out_norm_gain,
        out_norm_bias,
        att_norm_gain,
        att_norm_bias,
    )
    norms = jnp.stack(vectors)
    is_gate = lax.broadcasted_iota(jnp.int32, (1, 5 * channels), 1) // channels
    halves = jnp.where((is_gate == 0) | (is_gate == 2), 1.0, 0.5).astype(bf16)
    edge_weights = jnp.concatenate([w_edges, w_tri_gate], axis=1) * halves
    valid_column = jnp.broadcast_to(residue_valid.astype(f32)[:, None], (res, channels))

    head = lax.broadcasted_iota(jnp.int32, (HEADS, channels), 0)
    head_of_channel = lax.broadcasted_iota(jnp.int32, (HEADS, channels), 1) // HEAD_DIM
    repeat = jnp.where(head == head_of_channel, 1.0, 0.0).astype(bf16)
    wide_bias = dot(w_pair_bias, repeat).astype(bf16)

    kept = lax.dynamic_update_slice(
        jnp.zeros((2 * row_count, res, channels), bf16), pair_rep, (0, 0, 0)
    )
    far = exchange(pair_rep, devices // 2)
    far, kept, norms, edge_weights = lax.optimization_barrier((far, kept, norms, edge_weights))
    own = lax.dynamic_update_slice(kept, far, (row_count, 0, 0))
    own_blocks = (0, chips // 2)

    def blocks_from(bits):
        return tuple(s ^ bits for s in own_blocks)

    tall = shaped(f32, half * res, channels)

    def edges_of(pieces, done, send_row, *held):
        pairs = tuple(p for p, _ in pieces)
        blocks = tuple(b for _, b in pieces)
        operands = (valid_column, norms, edge_weights) + pairs + held
        return call(
            functools.partial(edges_kernel, row_count, chips, blocks, done, send_row, not held),
            (tall, tall, tall, tall, shaped(bf16, 4 * row_count, res, channels))
            + (() if held else (shaped(bf16, 2 * channels, 2 * channels),)),
            operands,
        )

    diagonal = exchange(own, 6)
    beside = exchange(own, 2)
    near = exchange(own, 4)
    *edges, early_right, same_head = edges_of([(own, own_blocks)], (), 0)
    diagonal, edges = lax.optimization_barrier((diagonal, edges))
    *edges, early_right = edges_of(
        [(diagonal, blocks_from(3))], own_blocks, 2 * row_count, *edges, early_right
    )
    beside, edges, early_right, wide_bias = lax.optimization_barrier(
        (beside, edges, early_right, wide_bias)
    )
    early = (exchange(early_right, 1), own_blocks + blocks_from(3))
    *edges, late_right = edges_of(
        [(beside, blocks_from(1)), (near, blocks_from(2))], early[1], 0, *edges
    )
    late = (exchange(late_right, 1), blocks_from(1) + blocks_from(2))

    left, right, gate, pairs = edges
    triangle, across = call(
        functools.partial(near_triangle_kernel, row_count, chips, half // 2, [early[1]]),
        (tall, tall),
        (left, right, early[0]),
    )
    part = half // 2 * res
    in_part, own_shape = shaped(f32, part, channels), shaped(f32, row_count * res, channels)
    att_part = shaped(bf16, part, channels)
    shared = (norms, w_tri_out, left, gate, pairs)
    scratch = (pltpu.VMEM((part, channels), f32),)
    across, after_a, att_a = call(
        functools.partial(own_inputs_kernel, row_count, chips, (early[1], late[1])),
        (tall, in_part, att_part),
        shared + (late[0], triangle, across),
        scratch=scratch,
    )
    far_att_a = exchange(att_a, 1)
    att_b = call(
        functools.partial(other_inputs_kernel, row_count, chips),
        att_part,
        shared + (triangle, across),
        scratch=scratch,
    )
    far_att_b = exchange(att_b, 1)

    def attention_scratch(keys, projected):
        return (
            pltpu.VMEM((-(-keys // 8) * 8 * res, channels), f32),
            pltpu.VMEM((projected * res, channels), f32),
            pltpu.VMEM((projected * res, channels), f32),
            pltpu.VMEM((row_count, 40, channels), f32),
        )

    sums, query, att_gate, after_own = call(
        functools.partial(most_attention_kernel, row_count, chips),
        (shaped(f32, row_count, 3, res, channels), own_shape, own_shape, own_shape),
        (valid_column, same_head, w_query, w_att_gate, w_key, w_value, wide_bias)
        + (att_a, att_b, far_att_a, after_a),
        scratch=attention_scratch(3 * half // 2, 3 * half // 2),
    )
    return call(
        functools.partial(attention_kernel, row_count, chips),
        shaped(bf16, *pair_rep.shape),
        (valid_column, same_head, w_key, w_value, w_att_out, wide_bias, far_att_b)
        + (query, att_gate, after_own, sums),
        scratch=attention_scratch(half // 2, half // 2),
    )


def per_device(pair_rep, residue_valid, *parameters):
    row_count, res, channels = pair_rep.shape
    devices = res // row_count
    if res % 48 == 0 and devices == 16 and 40 * res * res * channels <= 32 * 1024 * 1024:
        return on_whole_complex(pair_rep, residue_valid, *parameters)
    return split_over_devices(pair_rep, residue_valid, *parameters)


def solution(mesh):
    return jax.shard_map(
        per_device,
        mesh=mesh,
        in_specs=(
            P(("groups", "row"), None, None),
            P("groups"),
            P(),
            P(),
            P(),
            P(),
            P(),
            P(),
            P(),
            P(),
            P(),
            P(),
            P(),
            P(),
            P(),
            P(),
            P(),
        ),
        out_specs=P(("groups", "row"), None, None),
        check_vma=False,
    )
```

```python
import functools
import math

import jax
import jax.numpy as jnp
from jax import lax
from jax.experimental import pallas as pl
from jax.experimental.pallas import tpu as pltpu
from jax.sharding import PartitionSpec as P

HEADS = 4
HEAD_DIM = 32


def layer_norm(values, norm_gain, norm_bias, along_axis):
    centre = values - jnp.mean(values, axis=along_axis, keepdims=True)
    spread = jnp.mean(centre * centre, axis=along_axis, keepdims=True)
    return centre * lax.rsqrt(spread + 1e-05) * norm_gain + norm_bias


def attend(query_cols, key_cols, value_cols, whole_bias, key_mask):
    factor = 1.0 / math.sqrt(HEAD_DIM)
    scores = (
        jnp.einsum("kjhd,ijhd->jhki", key_cols, query_cols, preferred_element_type=jnp.float32)
        * factor
    )
    scores = scores + whole_bias.astype(jnp.float32)[None] + key_mask[None, None, :, None]
    scores = scores - jnp.max(scores, axis=2, keepdims=True)
    exponent = jnp.exp(scores)
    weights = (exponent / jnp.sum(exponent, axis=2, keepdims=True)).astype(jnp.bfloat16)
    return jnp.einsum("jhki,kjhd->ijhd", weights, value_cols, preferred_element_type=jnp.float32)


def split_over_devices(
    pair_rep,
    residue_valid,
    tri_norm_gain,
    tri_norm_bias,
    w_edges,
    w_tri_gate,
    out_norm_gain,
    out_norm_bias,
    w_tri_out,
    att_norm_gain,
    att_norm_bias,
    w_query,
    w_key,
    w_value,
    w_att_gate,
    w_pair_bias,
    w_att_out,
):
    row_count = pair_rep.shape[0]
    res_count = pair_rep.shape[1]
    channels = pair_rep.shape[2]
    hidden_width = HEADS * HEAD_DIM
    row_start = lax.axis_index("row") * row_count
    valid_flags = residue_valid.astype(jnp.float32)
    own_valid = lax.dynamic_slice_in_dim(valid_flags, row_start, row_count)
    normed = layer_norm(pair_rep.astype(jnp.float32), tri_norm_gain, tri_norm_bias, 2).astype(
        jnp.bfloat16
    )
    projected = jnp.einsum("ikd,de->eik", normed, w_edges, preferred_element_type=jnp.float32)
    projected = projected.reshape(4, channels, row_count, res_count)
    pair_mask = (own_valid[:, None] * valid_flags[None, :])[None, :, :]
    left_edges = (jax.nn.sigmoid(projected[1]) * projected[0] * pair_mask).astype(jnp.bfloat16)
    right_edges = (jax.nn.sigmoid(projected[3]) * projected[2] * pair_mask).astype(jnp.bfloat16)
    left_cols, right_cols = (
        lax.all_to_all(left_edges, "row", split_axis=0, concat_axis=1, tiled=True),
        lax.all_to_all(right_edges, "row", split_axis=0, concat_axis=1, tiled=True),
    )
    block_product = jnp.einsum(
        "cik,cjk->cij", left_cols, right_cols, preferred_element_type=jnp.float32
    ).astype(jnp.bfloat16)
    triangle = lax.all_to_all(block_product, "row", split_axis=1, concat_axis=0, tiled=True)
    tri_normed = layer_norm(
        triangle.astype(jnp.float32), out_norm_gain[:, None, None], out_norm_bias[:, None, None], 0
    ).astype(jnp.bfloat16)
    tri_gate = jax.nn.sigmoid(
        jnp.einsum("ijc,ce->ije", normed, w_tri_gate, preferred_element_type=jnp.float32)
    )
    tri_update = jnp.einsum(
        "cij,ce->ije", tri_normed, w_tri_out, preferred_element_type=jnp.float32
    )
    after_tri = pair_rep.astype(jnp.float32) + tri_gate * tri_update
    att_in = layer_norm(after_tri, att_norm_gain, att_norm_bias, 2).astype(jnp.bfloat16)
    pair_bias = jnp.einsum(
        "kic,ch->hki", att_in, w_pair_bias, preferred_element_type=jnp.float32
    ).astype(jnp.bfloat16)
    whole_bias = lax.all_gather(pair_bias, "row", axis=1, tiled=True)
    key_mask = 1000000000.0 * (valid_flags - 1.0)
    columns = lax.all_to_all(att_in, "row", split_axis=1, concat_axis=0, tiled=True)
    all_weights = jnp.concatenate([w_query, w_key, w_value, w_att_gate], axis=1)
    joined = jnp.dot(columns.reshape(-1, channels), all_weights, preferred_element_type=jnp.float32)
    query_cols = (
        joined[:, :hidden_width].astype(jnp.bfloat16).reshape(res_count, row_count, HEADS, HEAD_DIM)
    )
    key_cols = (
        joined[:, hidden_width : 2 * hidden_width]
        .astype(jnp.bfloat16)
        .reshape(res_count, row_count, HEADS, HEAD_DIM)
    )
    value_cols = (
        joined[:, 2 * hidden_width : 3 * hidden_width]
        .astype(jnp.bfloat16)
        .reshape(res_count, row_count, HEADS, HEAD_DIM)
    )
    gate_cols = jax.nn.sigmoid(joined[:, 3 * hidden_width :]).reshape(
        res_count, row_count, hidden_width
    )
    attended = attend(query_cols, key_cols, value_cols, whole_bias, key_mask)
    gated = (attended.reshape(res_count, row_count, hidden_width) * gate_cols).astype(jnp.bfloat16)
    gated_rows = lax.all_to_all(gated, "row", split_axis=0, concat_axis=1, tiled=True)
    final = after_tri + jnp.einsum(
        "ije,ec->ijc", gated_rows, w_att_out, preferred_element_type=jnp.float32
    )
    return final.astype(jnp.bfloat16)


def sigmoid(values):
    return 0.5 * jnp.tanh(0.5 * values) + 0.5


def row_norm(values, norm_gain, norm_bias):
    count = values.shape[1]
    centre = values - jnp.sum(values, axis=1, keepdims=True) * (1.0 / count)
    squares = jnp.sum(centre * centre, axis=1, keepdims=True)
    return centre * lax.rsqrt(squares + 1e-05 * count) * (norm_gain * count**0.5) + norm_bias


def dot(left, right):
    return jnp.dot(left, right, preferred_element_type=jnp.float32)


def rounded(values):
    return values.astype(jnp.bfloat16).astype(jnp.float32)


def chip_and_core():
    device = lax.axis_index("row")
    return lax.shift_right_logical(device, 1), jnp.bitwise_and(device, 1)


def rows_of_blocks(row_count, blocks):
    chip, _ = chip_and_core()
    return [(jnp.bitwise_xor(chip, bits), r) for bits in blocks for r in range(row_count)]


def edges_kernel(
    row_count, chips, pieces, done, send_row, makes_heads, valid_column, norms, weights, *refs
):
    pair_refs = refs[: len(pieces)]
    left_ref, right_ref, gate_ref, pairs_ref, send_ref = refs[-5:]
    if makes_heads:
        left_ref, right_ref, gate_ref, pairs_ref, send_ref, same_head_ref = refs[-6:]
        wide = same_head_ref.shape
        row = lax.broadcasted_iota(jnp.int32, wide, 0) // HEAD_DIM
        column = lax.broadcasted_iota(jnp.int32, wide, 1) // HEAD_DIM
        same_head_ref[...] = jnp.where(row == column, 1.0, 0.0).astype(jnp.bfloat16)
    f32, bf16 = jnp.float32, jnp.bfloat16
    res, channels = valid_column.shape
    held_refs = refs[len(pieces) :]
    for chip, r in rows_of_blocks(row_count, done):
        held_rows = pl.ds(pl.multiple_of((chip * row_count + r) * res, res), res)
        held_columns = pl.ds(pl.multiple_of((r * chips + chip) * res, res), res)
        left_ref[held_rows, :] = held_refs[0][held_rows, :]
        right_ref[held_columns, :] = held_refs[1][held_columns, :]
        gate_ref[held_rows, :] = held_refs[2][held_rows, :]
        pairs_ref[held_rows, :] = held_refs[3][held_rows, :]
    if send_row:
        send_ref[:send_row] = held_refs[4][:send_row]
    _, core = chip_and_core()
    pairs = jnp.concatenate(
        [ref[...].astype(f32).reshape(-1, channels) for ref in pair_refs], axis=0
    )
    normed = row_norm(pairs, norms[0:1, :], norms[1:2, :]).astype(bf16)
    column = 0.5 * valid_column[...]
    rows_of = rows_of_blocks(row_count, [bits for piece in pieces for bits in piece])
    masks = jnp.concatenate(
        [
            column * valid_column[pl.ds((2 * chip + core) * row_count + r, 1), :]
            for chip, r in rows_of
        ],
        axis=0,
    )
    joined = dot(normed, weights[:, : 2 * channels])
    left = rounded((jnp.tanh(joined[:, channels:]) + 1.0) * joined[:, :channels] * masks)
    joined = dot(normed, weights[:, 2 * channels : 4 * channels])
    right = ((jnp.tanh(joined[:, channels:]) + 1.0) * joined[:, :channels] * masks).astype(bf16)
    gate_weights = weights[:, 4 * channels :]
    nothing = jnp.zeros_like(gate_weights)
    gate_weights = jnp.concatenate(
        [
            jnp.concatenate([gate_weights, nothing], axis=1),
            jnp.concatenate([nothing, gate_weights], axis=1),
        ],
        axis=0,
    )
    middle = normed.shape[0] // 2
    joined = dot(jnp.concatenate([normed[:middle], normed[middle:]], axis=1), gate_weights)
    joined = jnp.concatenate([joined[:, :channels], joined[:, channels:]], axis=0)
    gate = 0.5 * jnp.tanh(joined) + 0.5
    for n, (chip, r) in enumerate(rows_of):
        rows = slice(n * res, (n + 1) * res)
        start = pl.multiple_of((chip * row_count + r) * res, res)
        send_ref[send_row + n] = right[rows]
        left_ref[pl.ds(start, res), :] = left[rows]
        place_right(right_ref, chips, chip, r, right[rows])
        gate_ref[pl.ds(start, res), :] = gate[rows]
        pairs_ref[pl.ds(start, res), :] = pairs[rows]


def place_right(right_ref, chips, chip, r, edges):
    res = edges.shape[0]
    start = pl.multiple_of((r * chips + chip) * res, res)
    right_ref[pl.ds(start, res), :] = edges.astype(jnp.float32)


def join(even, odd, shift):
    high = jnp.bitwise_and(lax.broadcasted_iota(jnp.int32, even.shape, 0), shift) > 0
    return jnp.where(high, odd, even) + pltpu.roll(jnp.where(high, even, odd), shift, 0)


def triangle_rows(
    row_count, chips, left_ref, right_ref, triangle_ref, first, count, core, triangle_first
):
    res = 2 * row_count * chips
    start = pl.multiple_of(first * res, res)
    block = 4
    for n in range(0, count, block):
        lefts = [left_ref[pl.ds(start + m * res, res), :] for m in range(n, n + block)]
        for r in range(row_count):
            sums = [[] for _ in range(block)]
            for chip in range(chips):
                at = (r * chips + chip) * res
                right = right_ref[at : at + res, :]
                for m in range(block):
                    product = lefts[m] * right
                    part = sum((product[k : k + 8] for k in range(8, res, 8)), product[:8])
                    shift = 1
                    while chip & shift:
                        part = join(sums[m].pop(), part, shift)
                        shift *= 2
                    sums[m].append(part)
            for m in range(block):
                place = (triangle_first + n + m) * res + core * row_count + r
                triangle_ref[pl.ds(place, chips, stride=2 * row_count), :] = rounded(sums[m][0])


def near_triangle_kernel(row_count, chips, chunk, pieces, left_ref, right_ref, *refs):
    received, (triangle_ref, across_ref) = refs[:-2], refs[-2:]
    _, core = chip_and_core()

    def some_rows(step, carry):
        first = step * chunk
        triangle_rows(
            row_count, chips, left_ref, right_ref, triangle_ref, first, chunk, core, first
        )
        return carry

    for ref, blocks in zip(received, pieces):
        for n, (chip, r) in enumerate(rows_of_blocks(row_count, blocks)):
            place_right(across_ref, chips, chip, r, ref[n])
    lax.fori_loop(0, row_count * chips // chunk, some_rows, 0)


def attention_inputs(
    row_count, chips, first, norms, w_out, left_ref, gate_ref, pairs_ref, held_triangle, across_ref,
    triangle_ref,
):
    bf16 = jnp.bfloat16
    _, core = chip_and_core()
    half = row_count * chips
    tall = (half // 2) * 2 * half
    rows = pl.ds(pl.multiple_of(first * 2 * half, tall), tall)
    triangle_ref[...] = held_triangle[rows, :]
    triangle_rows(
        row_count, chips, left_ref, across_ref, triangle_ref, first, half // 2, 1 - core, 0
    )
    tri_normed = row_norm(triangle_ref[...], norms[2:3, :], norms[3:4, :]).astype(bf16)
    after_tri = pairs_ref[rows, :] + gate_ref[rows, :] * dot(tri_normed, w_out[...])
    att_in = row_norm(after_tri, norms[4:5, :], norms[5:6, :]).astype(bf16)
    return after_tri, att_in


def first_chip(chips, part):
    chip, _ = chip_and_core()
    return jnp.bitwise_xor(jnp.bitwise_and(chip, chips // 2), part * (chips // 2))


def own_inputs_kernel(
    row_count,
    chips,
    blocks,
    norms,
    w_out,
    left_ref,
    gate_ref,
    pairs_ref,
    received,
    triangle_ref,
    held_across,
    across_ref,
    after_ref,
    att_ref,
    scratch_ref,
):
    early, late = blocks
    res = held_across.shape[0] // (row_count * chips)
    for chip, r in rows_of_blocks(row_count, early):
        held = pl.ds(pl.multiple_of((r * chips + chip) * res, res), res)
        across_ref[held, :] = held_across[held, :]
    for n, (chip, r) in enumerate(rows_of_blocks(row_count, late)):
        place_right(across_ref, chips, chip, r, received[n])
    first = first_chip(chips, 0) * row_count
    refs = (left_ref, gate_ref, pairs_ref, triangle_ref, across_ref, scratch_ref)
    after_ref[...], att_ref[...] = attention_inputs(
        row_count, chips, first, norms, w_out, *refs
    )


def other_inputs_kernel(row_count, chips, norms, w_out, *refs):
    *refs, att_ref, scratch_ref = refs
    first = first_chip(chips, 1) * row_count
    _, att_ref[...] = attention_inputs(row_count, chips, first, norms, w_out, *refs, scratch_ref)


def keys_and_values(att, w_key, w_value, key_ref, value_ref):
    channels = key_ref.shape[1]
    key_value = jnp.concatenate([w_key[...], w_value[...]], axis=1)
    start = 0
    for values in att:
        rows = slice(start, start + values.shape[0])
        joined = dot(values, key_value)
        key_ref[rows, :] = rounded(joined[:, :channels])
        value_ref[rows, :] = rounded(joined[:, channels:])
        start = rows.stop


def column_bias(row_count, res, att, wide_bias, att_ref, bias_ref):
    start = 0
    for values in att:
        att_ref[start : start + values.shape[0], :] = values.astype(jnp.float32)
        start += values.shape[0]
    keys = start // res
    own = lax.axis_index("row") * row_count
    height = -(-keys // 8) * 8
    columns = [att_ref[pl.ds(own + r, height, stride=res), :] for r in range(row_count)]
    columns = jnp.concatenate(columns, axis=0).astype(jnp.bfloat16)
    bias = rounded(dot(columns, wide_bias[...]))
    for r in range(row_count):
        bias_ref[r, :height, :] = bias[r * height : (r + 1) * height]


def partial_attention(
    row_count, chips, query, parts, bias_ref, same_head, valid_column, sums, together
):
    bf16 = jnp.bfloat16
    res = 2 * row_count * chips
    channels = valid_column.shape[1]
    count = row_count * chips // 2
    for part, (core, first, key_of, value_of) in enumerate(parts):
        products = []
        for r in range(row_count):
            own_query = query[r * res : (r + 1) * res]
            row = [(key_of(n) * own_query).astype(bf16) for n in range(count)]
            pairs = [jnp.concatenate(row[n : n + 2], axis=1) for n in range(0, count, 2)]
            products.append(jnp.concatenate(pairs, axis=0))
        if together:
            scores = dot(jnp.concatenate(products, axis=0), same_head[...])
            tall = count // 2 * res
            scores = [scores[r * tall : (r + 1) * tall] for r in range(row_count)]
        else:
            scores = [dot(product, same_head[...]) for product in products]

        def score_of(n, r):
            lanes = slice(n % 2 * channels, (n % 2 + 1) * channels)
            k = (2 * (first + n // row_count) + core) * row_count + n % row_count
            key_mask = 1000000000.0 * (valid_column[pl.ds(k, 1), :] - 1.0)
            at = part * count + n
            shift = (bias_ref[r, at : at + 1, :] + key_mask) * math.log2(math.e)
            return scores[r][n // 2 * res : (n // 2 + 1) * res, lanes] + shift

        later = []
        for r, (maximum, total, mixed) in enumerate(sums):
            highest = score_of(0, r)
            for n in range(1, count):
                highest = jnp.maximum(highest, score_of(n, r))
            if maximum is None:
                maximum, total, mixed = highest, 0.0, 0.0
            else:
                highest = jnp.maximum(highest, maximum)
                scale = jnp.exp2(maximum - highest)
                maximum, total, mixed = highest, total * scale, mixed * scale
            for n in range(count):
                weight = jnp.exp2(score_of(n, r) - maximum)
                total = total + weight
                mixed = mixed + weight * value_of(n)
            later.append((maximum, total, mixed))
        sums = later
    return sums


def most_attention_kernel(
    row_count,
    chips,
    valid_column,
    same_head,
    w_query,
    w_gate,
    w_key,
    w_value,
    wide_bias,
    own_att_a,
    own_att_b,
    far_att_a,
    own_after,
    sums_ref,
    query_ref,
    gate_ref,
    after_ref,
    att_ref,
    key_ref,
    value_ref,
    bias_ref,
):
    chip, core = chip_and_core()
    res, channels = valid_column.shape
    own = row_count * res
    rows = pl.ds(pl.multiple_of(jnp.bitwise_and(chip, chips // 2 - 1) * own, own), own)
    own_in = own_att_a[rows, :]
    query = rounded(dot(own_in, w_query[...])) * (math.log2(math.e) / math.sqrt(HEAD_DIM))
    att = [ref[...] for ref in (own_att_a, own_att_b, far_att_a)]
    keys_and_values(att, w_key, w_value, key_ref, value_ref)
    column_bias(row_count, res, att, wide_bias, att_ref, bias_ref)
    count = row_count * chips // 2

    def rows_of(ref, first):
        return lambda n: ref[(first + n) * res : (first + n + 1) * res, :]

    a, b = first_chip(chips, 0), first_chip(chips, 1)
    parts = [
        (sender, first, rows_of(key_ref, n * count), rows_of(value_ref, n * count))
        for n, (sender, first) in enumerate(((core, a), (core, b), (1 - core, a)))
    ]
    none = [(None, None, None)] * row_count
    sums = partial_attention(
        row_count, chips, query, parts, bias_ref, same_head, valid_column, none, True
    )
    for r in range(row_count):
        for n, each in enumerate(sums[r]):
            sums_ref[r, n] = each
    query_ref[...] = query
    gate_ref[...] = sigmoid(dot(own_in, w_gate[...]))
    after_ref[...] = own_after[rows, :]


def attention_kernel(
    row_count,
    chips,
    valid_column,
    same_head,
    w_key,
    w_value,
    w_out,
    wide_bias,
    far_att_b,
    query_ref,
    gate_ref,
    after_ref,
    sums_ref,
    out_ref,
    att_ref,
    key_ref,
    value_ref,
    bias_ref,
):
    _, core = chip_and_core()
    res, channels = valid_column.shape
    far_att = far_att_b[...]
    keys_and_values([far_att], w_key, w_value, key_ref, value_ref)
    column_bias(row_count, res, [far_att], wide_bias, att_ref, bias_ref)

    def rows_of(ref):
        return lambda n: ref[n * res : (n + 1) * res, :]

    parts = ((1 - core, first_chip(chips, 1), rows_of(key_ref), rows_of(value_ref)),)
    sums = [tuple(sums_ref[r, n] for n in range(3)) for r in range(row_count)]
    sums = partial_attention(
        row_count, chips, query_ref[...], parts, bias_ref, same_head, valid_column, sums, False
    )
    attended = [mixed / total for _, total, mixed in sums]
    gated = (jnp.concatenate(attended, axis=0) * gate_ref[...]).astype(jnp.bfloat16)
    final = after_ref[...] + dot(gated, w_out[...])
    out_ref[...] = final.astype(jnp.bfloat16).reshape(row_count, res, channels)


def on_whole_complex(
    pair_rep,
    residue_valid,
    tri_norm_gain,
    tri_norm_bias,
    w_edges,
    w_tri_gate,
    out_norm_gain,
    out_norm_bias,
    w_tri_out,
    att_norm_gain,
    att_norm_bias,
    w_query,
    w_key,
    w_value,
    w_att_gate,
    w_pair_bias,
    w_att_out,
):
    row_count, res, channels = pair_rep.shape
    devices = res // row_count
    chips = devices // 2
    half = res // 2
    f32, bf16 = jnp.float32, jnp.bfloat16
    in_vmem = pl.BlockSpec(memory_space=pltpu.VMEM)

    def shaped(dtype, *shape):
        return jax.ShapeDtypeStruct(shape, dtype)

    def call(kernel, outs, operands, scratch=(), cost=2**25):
        return pl.pallas_call(
            kernel,
            out_shape=outs,
            in_specs=[in_vmem] * len(operands),
            out_specs=jax.tree.map(lambda _: in_vmem, outs),
            scratch_shapes=list(scratch),
            compiler_params=pltpu.CompilerParams(vmem_limit_bytes=24 * 1024 * 1024),
            cost_estimate=pl.CostEstimate(flops=2**20, bytes_accessed=cost, transcendentals=0),
        )(*operands)

    def exchange(values, bit):
        return lax.ppermute(values, "row", [(d, d ^ bit) for d in range(devices)])

    vectors = (
        tri_norm_gain,
        tri_norm_bias,
        out_norm_gain,
        out_norm_bias,
        att_norm_gain,
        att_norm_bias,
    )
    norms = jnp.stack(vectors)
    is_gate = lax.broadcasted_iota(jnp.int32, (1, 5 * channels), 1) // channels
    halves = jnp.where((is_gate == 0) | (is_gate == 2), 1.0, 0.5).astype(bf16)
    edge_weights = jnp.concatenate([w_edges, w_tri_gate], axis=1) * halves
    valid_column = jnp.broadcast_to(residue_valid.astype(f32)[:, None], (res, channels))

    head = lax.broadcasted_iota(jnp.int32, (HEADS, channels), 0)
    head_of_channel = lax.broadcasted_iota(jnp.int32, (HEADS, channels), 1) // HEAD_DIM
    repeat = jnp.where(head == head_of_channel, 1.0, 0.0).astype(bf16)
    wide_bias = dot(w_pair_bias, repeat).astype(bf16)

    kept = lax.dynamic_update_slice(
        jnp.zeros((2 * row_count, res, channels), bf16), pair_rep, (0, 0, 0)
    )
    far = exchange(pair_rep, devices // 2)
    far, kept, norms, edge_weights = lax.optimization_barrier((far, kept, norms, edge_weights))
    own = lax.dynamic_update_slice(kept, far, (row_count, 0, 0))
    own_blocks = (0, chips // 2)

    def blocks_from(bits):
        return tuple(s ^ bits for s in own_blocks)

    tall = shaped(f32, half * res, channels)

    def edges_of(pieces, done, send_row, *held):
        pairs = tuple(p for p, _ in pieces)
        blocks = tuple(b for _, b in pieces)
        operands = (valid_column, norms, edge_weights) + pairs + held
        return call(
            functools.partial(edges_kernel, row_count, chips, blocks, done, send_row, not held),
            (tall, tall, tall, tall, shaped(bf16, 4 * row_count, res, channels))
            + (() if held else (shaped(bf16, 2 * channels, 2 * channels),)),
            operands,
        )

    diagonal = exchange(own, 6)
    beside = exchange(own, 2)
    near = exchange(own, 4)
    *edges, early_right, same_head = edges_of([(own, own_blocks)], (), 0)
    diagonal, edges = lax.optimization_barrier((diagonal, edges))
    *edges, early_right = edges_of(
        [(diagonal, blocks_from(3))], own_blocks, 2 * row_count, *edges, early_right
    )
    beside, edges, early_right, wide_bias = lax.optimization_barrier(
        (beside, edges, early_right, wide_bias)
    )
    early = (exchange(early_right, 1), own_blocks + blocks_from(3))
    *edges, late_right = edges_of(
        [(beside, blocks_from(1)), (near, blocks_from(2))], early[1], 0, *edges
    )
    late = (exchange(late_right, 1), blocks_from(1) + blocks_from(2))

    left, right, gate, pairs = edges
    triangle, across = call(
        functools.partial(near_triangle_kernel, row_count, chips, half // 2, [early[1]]),
        (tall, tall),
        (left, right, early[0]),
    )
    part = half // 2 * res
    in_part, own_shape = shaped(f32, part, channels), shaped(f32, row_count * res, channels)
    att_part = shaped(bf16, part, channels)
    shared = (norms, w_tri_out, left, gate, pairs)
    scratch = (pltpu.VMEM((part, channels), f32),)
    across, after_a, att_a = call(
        functools.partial(own_inputs_kernel, row_count, chips, (early[1], late[1])),
        (tall, in_part, att_part),
        shared + (late[0], triangle, across),
        scratch=scratch,
    )
    far_att_a = exchange(att_a, 1)
    att_b = call(
        functools.partial(other_inputs_kernel, row_count, chips),
        att_part,
        shared + (triangle, across),
        scratch=scratch,
    )
    far_att_b = exchange(att_b, 1)

    def attention_scratch(keys, projected):
        return (
            pltpu.VMEM((-(-keys // 8) * 8 * res, channels), f32),
            pltpu.VMEM((projected * res, channels), f32),
            pltpu.VMEM((projected * res, channels), f32),
            pltpu.VMEM((row_count, 40, channels), f32),
        )

    sums, query, att_gate, after_own = call(
        functools.partial(most_attention_kernel, row_count, chips),
        (shaped(f32, row_count, 3, res, channels), own_shape, own_shape, own_shape),
        (valid_column, same_head, w_query, w_att_gate, w_key, w_value, wide_bias)
        + (att_a, att_b, far_att_a, after_a),
        scratch=attention_scratch(3 * half // 2, 3 * half // 2),
    )
    return call(
        functools.partial(attention_kernel, row_count, chips),
        shaped(bf16, *pair_rep.shape),
        (valid_column, same_head, w_key, w_value, w_att_out, wide_bias, far_att_b)
        + (query, att_gate, after_own, sums),
        scratch=attention_scratch(half // 2, half // 2),
    )


def per_device(pair_rep, residue_valid, *parameters):
    row_count, res, channels = pair_rep.shape
    devices = res // row_count
    if res % 48 == 0 and devices == 16 and 40 * res * res * channels <= 32 * 1024 * 1024:
        return on_whole_complex(pair_rep, residue_valid, *parameters)
    return split_over_devices(pair_rep, residue_valid, *parameters)


def solution(mesh):
    return jax.shard_map(
        per_device,
        mesh=mesh,
        in_specs=(
            P(("groups", "row"), None, None),
            P("groups"),
            P(),
            P(),
            P(),
            P(),
            P(),
            P(),
            P(),
            P(),
            P(),
            P(),
            P(),
            P(),
            P(),
            P(),
            P(),
        ),
        out_specs=P(("groups", "row"), None, None),
        check_vma=False,
    )
```

```python
import functools
import math

import jax
import jax.numpy as jnp
from jax import lax
from jax.experimental import pallas as pl
from jax.experimental.pallas import tpu as pltpu
from jax.sharding import PartitionSpec as P

HEADS = 4
HEAD_DIM = 32


def layer_norm(values, norm_gain, norm_bias, along_axis):
    centre = values - jnp.mean(values, axis=along_axis, keepdims=True)
    spread = jnp.mean(centre * centre, axis=along_axis, keepdims=True)
    return centre * lax.rsqrt(spread + 1e-05) * norm_gain + norm_bias


def attend(query_cols, key_cols, value_cols, whole_bias, key_mask):
    factor = 1.0 / math.sqrt(HEAD_DIM)
    scores = (
        jnp.einsum("kjhd,ijhd->jhki", key_cols, query_cols, preferred_element_type=jnp.float32)
        * factor
    )
    scores = scores + whole_bias.astype(jnp.float32)[None] + key_mask[None, None, :, None]
    scores = scores - jnp.max(scores, axis=2, keepdims=True)
    exponent = jnp.exp(scores)
    weights = (exponent / jnp.sum(exponent, axis=2, keepdims=True)).astype(jnp.bfloat16)
    return jnp.einsum("jhki,kjhd->ijhd", weights, value_cols, preferred_element_type=jnp.float32)


def split_over_devices(
    pair_rep,
    residue_valid,
    tri_norm_gain,
    tri_norm_bias,
    w_edges,
    w_tri_gate,
    out_norm_gain,
    out_norm_bias,
    w_tri_out,
    att_norm_gain,
    att_norm_bias,
    w_query,
    w_key,
    w_value,
    w_att_gate,
    w_pair_bias,
    w_att_out,
):
    row_count = pair_rep.shape[0]
    res_count = pair_rep.shape[1]
    channels = pair_rep.shape[2]
    hidden_width = HEADS * HEAD_DIM
    row_start = lax.axis_index("row") * row_count
    valid_flags = residue_valid.astype(jnp.float32)
    own_valid = lax.dynamic_slice_in_dim(valid_flags, row_start, row_count)
    normed = layer_norm(pair_rep.astype(jnp.float32), tri_norm_gain, tri_norm_bias, 2).astype(
        jnp.bfloat16
    )
    projected = jnp.einsum("ikd,de->eik", normed, w_edges, preferred_element_type=jnp.float32)
    projected = projected.reshape(4, channels, row_count, res_count)
    pair_mask = (own_valid[:, None] * valid_flags[None, :])[None, :, :]
    left_edges = (jax.nn.sigmoid(projected[1]) * projected[0] * pair_mask).astype(jnp.bfloat16)
    right_edges = (jax.nn.sigmoid(projected[3]) * projected[2] * pair_mask).astype(jnp.bfloat16)
    left_cols, right_cols = (
        lax.all_to_all(left_edges, "row", split_axis=0, concat_axis=1, tiled=True),
        lax.all_to_all(right_edges, "row", split_axis=0, concat_axis=1, tiled=True),
    )
    block_product = jnp.einsum(
        "cik,cjk->cij", left_cols, right_cols, preferred_element_type=jnp.float32
    ).astype(jnp.bfloat16)
    triangle = lax.all_to_all(block_product, "row", split_axis=1, concat_axis=0, tiled=True)
    tri_normed = layer_norm(
        triangle.astype(jnp.float32), out_norm_gain[:, None, None], out_norm_bias[:, None, None], 0
    ).astype(jnp.bfloat16)
    tri_gate = jax.nn.sigmoid(
        jnp.einsum("ijc,ce->ije", normed, w_tri_gate, preferred_element_type=jnp.float32)
    )
    tri_update = jnp.einsum(
        "cij,ce->ije", tri_normed, w_tri_out, preferred_element_type=jnp.float32
    )
    after_tri = pair_rep.astype(jnp.float32) + tri_gate * tri_update
    att_in = layer_norm(after_tri, att_norm_gain, att_norm_bias, 2).astype(jnp.bfloat16)
    pair_bias = jnp.einsum(
        "kic,ch->hki", att_in, w_pair_bias, preferred_element_type=jnp.float32
    ).astype(jnp.bfloat16)
    whole_bias = lax.all_gather(pair_bias, "row", axis=1, tiled=True)
    key_mask = 1000000000.0 * (valid_flags - 1.0)
    columns = lax.all_to_all(att_in, "row", split_axis=1, concat_axis=0, tiled=True)
    all_weights = jnp.concatenate([w_query, w_key, w_value, w_att_gate], axis=1)
    joined = jnp.dot(columns.reshape(-1, channels), all_weights, preferred_element_type=jnp.float32)
    query_cols = (
        joined[:, :hidden_width].astype(jnp.bfloat16).reshape(res_count, row_count, HEADS, HEAD_DIM)
    )
    key_cols = (
        joined[:, hidden_width : 2 * hidden_width]
        .astype(jnp.bfloat16)
        .reshape(res_count, row_count, HEADS, HEAD_DIM)
    )
    value_cols = (
        joined[:, 2 * hidden_width : 3 * hidden_width]
        .astype(jnp.bfloat16)
        .reshape(res_count, row_count, HEADS, HEAD_DIM)
    )
    gate_cols = jax.nn.sigmoid(joined[:, 3 * hidden_width :]).reshape(
        res_count, row_count, hidden_width
    )
    attended = attend(query_cols, key_cols, value_cols, whole_bias, key_mask)
    gated = (attended.reshape(res_count, row_count, hidden_width) * gate_cols).astype(jnp.bfloat16)
    gated_rows = lax.all_to_all(gated, "row", split_axis=0, concat_axis=1, tiled=True)
    final = after_tri + jnp.einsum(
        "ije,ec->ijc", gated_rows, w_att_out, preferred_element_type=jnp.float32
    )
    return final.astype(jnp.bfloat16)


def sigmoid(values):
    return 0.5 * jnp.tanh(0.5 * values) + 0.5


def row_norm(values, norm_gain, norm_bias):
    count = values.shape[1]
    centre = values - jnp.sum(values, axis=1, keepdims=True) * (1.0 / count)
    squares = jnp.sum(centre * centre, axis=1, keepdims=True)
    return centre * lax.rsqrt(squares + 1e-05 * count) * (norm_gain * count**0.5) + norm_bias


def dot(left, right):
    return jnp.dot(left, right, preferred_element_type=jnp.float32)


def rounded(values):
    return values.astype(jnp.bfloat16).astype(jnp.float32)


def chip_and_core():
    device = lax.axis_index("row")
    return lax.shift_right_logical(device, 1), jnp.bitwise_and(device, 1)


def rows_of_blocks(row_count, blocks):
    chip, _ = chip_and_core()
    return [(jnp.bitwise_xor(chip, bits), r) for bits in blocks for r in range(row_count)]


def edges_kernel(
    row_count, chips, pieces, done, send_row, makes_heads, valid_column, norms, weights, *refs
):
    pair_refs = refs[: len(pieces)]
    left_ref, right_ref, gate_ref, pairs_ref, send_ref = refs[-5:]
    if makes_heads:
        left_ref, right_ref, gate_ref, pairs_ref, send_ref, same_head_ref = refs[-6:]
        wide = same_head_ref.shape
        row = lax.broadcasted_iota(jnp.int32, wide, 0) // HEAD_DIM
        column = lax.broadcasted_iota(jnp.int32, wide, 1) // HEAD_DIM
        same_head_ref[...] = jnp.where(row == column, 1.0, 0.0).astype(jnp.bfloat16)
    f32, bf16 = jnp.float32, jnp.bfloat16
    res, channels = valid_column.shape
    held_refs = refs[len(pieces) :]
    for chip, r in rows_of_blocks(row_count, done):
        held_rows = pl.ds(pl.multiple_of((chip * row_count + r) * res, res), res)
        held_columns = pl.ds(pl.multiple_of((r * chips + chip) * res, res), res)
        left_ref[held_rows, :] = held_refs[0][held_rows, :]
        right_ref[held_columns, :] = held_refs[1][held_columns, :]
        gate_ref[held_rows, :] = held_refs[2][held_rows, :]
        pairs_ref[held_rows, :] = held_refs[3][held_rows, :]
    if send_row:
        send_ref[:send_row] = held_refs[4][:send_row]
    _, core = chip_and_core()
    pairs = jnp.concatenate(
        [ref[...].astype(f32).reshape(-1, channels) for ref in pair_refs], axis=0
    )
    normed = row_norm(pairs, norms[0:1, :], norms[1:2, :]).astype(bf16)
    column = 0.5 * valid_column[...]
    rows_of = rows_of_blocks(row_count, [bits for piece in pieces for bits in piece])
    masks = jnp.concatenate(
        [
            column * valid_column[pl.ds((2 * chip + core) * row_count + r, 1), :]
            for chip, r in rows_of
        ],
        axis=0,
    )
    joined = dot(normed, weights[:, : 2 * channels])
    left = rounded((jnp.tanh(joined[:, channels:]) + 1.0) * joined[:, :channels] * masks)
    joined = dot(normed, weights[:, 2 * channels : 4 * channels])
    right = ((jnp.tanh(joined[:, channels:]) + 1.0) * joined[:, :channels] * masks).astype(bf16)
    gate = 0.5 * jnp.tanh(dot(normed, weights[:, 4 * channels :])) + 0.5
    for n, (chip, r) in enumerate(rows_of):
        rows = slice(n * res, (n + 1) * res)
        start = pl.multiple_of((chip * row_count + r) * res, res)
        send_ref[send_row + n] = right[rows]
        left_ref[pl.ds(start, res), :] = left[rows]
        place_right(right_ref, chips, chip, r, right[rows])
        gate_ref[pl.ds(start, res), :] = gate[rows]
        pairs_ref[pl.ds(start, res), :] = pairs[rows]


def place_right(right_ref, chips, chip, r, edges):
    res = edges.shape[0]
    start = pl.multiple_of((r * chips + chip) * res, res)
    right_ref[pl.ds(start, res), :] = edges.astype(jnp.float32)


def join(even, odd, shift):
    high = jnp.bitwise_and(lax.broadcasted_iota(jnp.int32, even.shape, 0), shift) > 0
    return jnp.where(high, odd, even) + pltpu.roll(jnp.where(high, even, odd), shift, 0)


def triangle_rows(
    row_count, chips, left_ref, right_ref, triangle_ref, first, count, core, triangle_first
):
    res = 2 * row_count * chips
    start = pl.multiple_of(first * res, res)
    block = 4
    for n in range(0, count, block):
        lefts = [left_ref[pl.ds(start + m * res, res), :] for m in range(n, n + block)]
        for r in range(row_count):
            sums = [[] for _ in range(block)]
            for chip in range(chips):
                at = (r * chips + chip) * res
                right = right_ref[at : at + res, :]
                for m in range(block):
                    product = lefts[m] * right
                    part = sum((product[k : k + 8] for k in range(8, res, 8)), product[:8])
                    shift = 1
                    while chip & shift:
                        part = join(sums[m].pop(), part, shift)
                        shift *= 2
                    sums[m].append(part)
            for m in range(block):
                place = (triangle_first + n + m) * res + core * row_count + r
                triangle_ref[pl.ds(place, chips, stride=2 * row_count), :] = rounded(sums[m][0])


def near_triangle_kernel(row_count, chips, chunk, pieces, left_ref, right_ref, *refs):
    received, (triangle_ref, across_ref) = refs[:-2], refs[-2:]
    _, core = chip_and_core()

    def some_rows(step, carry):
        first = step * chunk
        triangle_rows(
            row_count, chips, left_ref, right_ref, triangle_ref, first, chunk, core, first
        )
        return carry

    for ref, blocks in zip(received, pieces):
        for n, (chip, r) in enumerate(rows_of_blocks(row_count, blocks)):
            place_right(across_ref, chips, chip, r, ref[n])
    lax.fori_loop(0, row_count * chips // chunk, some_rows, 0)


def attention_inputs(
    row_count, chips, first, norms, w_out, left_ref, gate_ref, pairs_ref, held_triangle, across_ref,
    triangle_ref,
):
    bf16 = jnp.bfloat16
    _, core = chip_and_core()
    half = row_count * chips
    tall = (half // 2) * 2 * half
    rows = pl.ds(pl.multiple_of(first * 2 * half, tall), tall)
    triangle_ref[...] = held_triangle[rows, :]
    triangle_rows(
        row_count, chips, left_ref, across_ref, triangle_ref, first, half // 2, 1 - core, 0
    )
    tri_normed = row_norm(triangle_ref[...], norms[2:3, :], norms[3:4, :]).astype(bf16)
    after_tri = pairs_ref[rows, :] + gate_ref[rows, :] * dot(tri_normed, w_out[...])
    att_in = row_norm(after_tri, norms[4:5, :], norms[5:6, :]).astype(bf16)
    return after_tri, att_in


def first_chip(chips, part):
    chip, _ = chip_and_core()
    return jnp.bitwise_xor(jnp.bitwise_and(chip, chips // 2), part * (chips // 2))


def own_inputs_kernel(
    row_count,
    chips,
    blocks,
    norms,
    w_out,
    left_ref,
    gate_ref,
    pairs_ref,
    received,
    triangle_ref,
    held_across,
    across_ref,
    after_ref,
    att_ref,
    scratch_ref,
):
    early, late = blocks
    res = held_across.shape[0] // (row_count * chips)
    for chip, r in rows_of_blocks(row_count, early):
        held = pl.ds(pl.multiple_of((r * chips + chip) * res, res), res)
        across_ref[held, :] = held_across[held, :]
    for n, (chip, r) in enumerate(rows_of_blocks(row_count, late)):
        place_right(across_ref, chips, chip, r, received[n])
    first = first_chip(chips, 0) * row_count
    refs = (left_ref, gate_ref, pairs_ref, triangle_ref, across_ref, scratch_ref)
    after_ref[...], att_ref[...] = attention_inputs(
        row_count, chips, first, norms, w_out, *refs
    )


def other_inputs_kernel(row_count, chips, norms, w_out, *refs):
    *refs, att_ref, scratch_ref = refs
    first = first_chip(chips, 1) * row_count
    _, att_ref[...] = attention_inputs(row_count, chips, first, norms, w_out, *refs, scratch_ref)


def keys_and_values(att, w_key, w_value, key_ref, value_ref):
    channels = key_ref.shape[1]
    key_value = jnp.concatenate([w_key[...], w_value[...]], axis=1)
    start = 0
    for values in att:
        rows = slice(start, start + values.shape[0])
        joined = dot(values, key_value)
        key_ref[rows, :] = rounded(joined[:, :channels])
        value_ref[rows, :] = rounded(joined[:, channels:])
        start = rows.stop


def column_bias(row_count, res, att, wide_bias, att_ref, bias_ref):
    start = 0
    for values in att:
        att_ref[start : start + values.shape[0], :] = values.astype(jnp.float32)
        start += values.shape[0]
    keys = start // res
    own = lax.axis_index("row") * row_count
    height = -(-keys // 8) * 8
    columns = [att_ref[pl.ds(own + r, height, stride=res), :] for r in range(row_count)]
    columns = jnp.concatenate(columns, axis=0).astype(jnp.bfloat16)
    bias = rounded(dot(columns, wide_bias[...]))
    for r in range(row_count):
        bias_ref[r, :height, :] = bias[r * height : (r + 1) * height]


def partial_attention(
    row_count, chips, query, parts, bias_ref, same_head, valid_column, sums, together
):
    bf16 = jnp.bfloat16
    res = 2 * row_count * chips
    channels = valid_column.shape[1]
    count = row_count * chips // 2
    for part, (core, first, key_of, value_of) in enumerate(parts):
        products = []
        for r in range(row_count):
            own_query = query[r * res : (r + 1) * res]
            row = [(key_of(n) * own_query).astype(bf16) for n in range(count)]
            pairs = [jnp.concatenate(row[n : n + 2], axis=1) for n in range(0, count, 2)]
            products.append(jnp.concatenate(pairs, axis=0))
        if together:
            scores = dot(jnp.concatenate(products, axis=0), same_head[...])
            tall = count // 2 * res
            scores = [scores[r * tall : (r + 1) * tall] for r in range(row_count)]
        else:
            scores = [dot(product, same_head[...]) for product in products]

        shifts = []
        for n in range(count):
            k = (2 * (first + n // row_count) + core) * row_count + n % row_count
            key_mask = 1000000000.0 * (valid_column[pl.ds(k, 1), :] - 1.0)
            at = part * count + n
            shifts.append(
                [
                    (bias_ref[r, at : at + 1, :] + key_mask) * math.log2(math.e)
                    for r in range(row_count)
                ]
            )

        def score_of(n, r):
            lanes = slice(n % 2 * channels, (n % 2 + 1) * channels)
            return scores[r][n // 2 * res : (n // 2 + 1) * res, lanes] + shifts[n][r]

        later = []
        for r, (maximum, total, mixed) in enumerate(sums):
            highest = score_of(0, r)
            for n in range(1, count):
                highest = jnp.maximum(highest, score_of(n, r))
            if maximum is None:
                maximum, total, mixed = highest, 0.0, 0.0
            else:
                highest = jnp.maximum(highest, maximum)
                scale = jnp.exp2(maximum - highest)
                maximum, total, mixed = highest, total * scale, mixed * scale
            for n in range(count):
                weight = jnp.exp2(score_of(n, r) - maximum)
                total = total + weight
                mixed = mixed + weight * value_of(n)
            later.append((maximum, total, mixed))
        sums = later
    return sums


def most_attention_kernel(
    row_count,
    chips,
    valid_column,
    same_head,
    w_query,
    w_gate,
    w_key,
    w_value,
    wide_bias,
    own_att_a,
    own_att_b,
    far_att_a,
    own_after,
    sums_ref,
    query_ref,
    gate_ref,
    after_ref,
    att_ref,
    key_ref,
    value_ref,
    bias_ref,
):
    chip, core = chip_and_core()
    res, channels = valid_column.shape
    own = row_count * res
    rows = pl.ds(pl.multiple_of(jnp.bitwise_and(chip, chips // 2 - 1) * own, own), own)
    own_in = own_att_a[rows, :]
    query = rounded(dot(own_in, w_query[...])) * (math.log2(math.e) / math.sqrt(HEAD_DIM))
    att = [ref[...] for ref in (own_att_a, own_att_b, far_att_a)]
    keys_and_values(att, w_key, w_value, key_ref, value_ref)
    column_bias(row_count, res, att, wide_bias, att_ref, bias_ref)
    count = row_count * chips // 2

    def rows_of(ref, first):
        return lambda n: ref[(first + n) * res : (first + n + 1) * res, :]

    a, b = first_chip(chips, 0), first_chip(chips, 1)
    parts = [
        (sender, first, rows_of(key_ref, n * count), rows_of(value_ref, n * count))
        for n, (sender, first) in enumerate(((core, a), (core, b), (1 - core, a)))
    ]
    none = [(None, None, None)] * row_count
    sums = partial_attention(
        row_count, chips, query, parts, bias_ref, same_head, valid_column, none, True
    )
    for r in range(row_count):
        for n, each in enumerate(sums[r]):
            sums_ref[r, n] = each
    query_ref[...] = query
    gate_ref[...] = sigmoid(dot(own_in, w_gate[...]))
    after_ref[...] = own_after[rows, :]


def attention_kernel(
    row_count,
    chips,
    valid_column,
    same_head,
    w_key,
    w_value,
    w_out,
    wide_bias,
    far_att_b,
    query_ref,
    gate_ref,
    after_ref,
    sums_ref,
    out_ref,
    att_ref,
    key_ref,
    value_ref,
    bias_ref,
):
    _, core = chip_and_core()
    res, channels = valid_column.shape
    far_att = far_att_b[...]
    keys_and_values([far_att], w_key, w_value, key_ref, value_ref)
    column_bias(row_count, res, [far_att], wide_bias, att_ref, bias_ref)

    def rows_of(ref):
        return lambda n: ref[n * res : (n + 1) * res, :]

    parts = ((1 - core, first_chip(chips, 1), rows_of(key_ref), rows_of(value_ref)),)
    sums = [tuple(sums_ref[r, n] for n in range(3)) for r in range(row_count)]
    sums = partial_attention(
        row_count, chips, query_ref[...], parts, bias_ref, same_head, valid_column, sums, False
    )
    attended = [mixed / total for _, total, mixed in sums]
    gated = (jnp.concatenate(attended, axis=0) * gate_ref[...]).astype(jnp.bfloat16)
    final = after_ref[...] + dot(gated, w_out[...])
    out_ref[...] = final.astype(jnp.bfloat16).reshape(row_count, res, channels)


def on_whole_complex(
    pair_rep,
    residue_valid,
    tri_norm_gain,
    tri_norm_bias,
    w_edges,
    w_tri_gate,
    out_norm_gain,
    out_norm_bias,
    w_tri_out,
    att_norm_gain,
    att_norm_bias,
    w_query,
    w_key,
    w_value,
    w_att_gate,
    w_pair_bias,
    w_att_out,
):
    row_count, res, channels = pair_rep.shape
    devices = res // row_count
    chips = devices // 2
    half = res // 2
    f32, bf16 = jnp.float32, jnp.bfloat16
    in_vmem = pl.BlockSpec(memory_space=pltpu.VMEM)

    def shaped(dtype, *shape):
        return jax.ShapeDtypeStruct(shape, dtype)

    def call(kernel, outs, operands, scratch=(), cost=2**25):
        return pl.pallas_call(
            kernel,
            out_shape=outs,
            in_specs=[in_vmem] * len(operands),
            out_specs=jax.tree.map(lambda _: in_vmem, outs),
            scratch_shapes=list(scratch),
            compiler_params=pltpu.CompilerParams(vmem_limit_bytes=24 * 1024 * 1024),
            cost_estimate=pl.CostEstimate(flops=2**20, bytes_accessed=cost, transcendentals=0),
        )(*operands)

    def exchange(values, bit):
        return lax.ppermute(values, "row", [(d, d ^ bit) for d in range(devices)])

    vectors = (
        tri_norm_gain,
        tri_norm_bias,
        out_norm_gain,
        out_norm_bias,
        att_norm_gain,
        att_norm_bias,
    )
    norms = jnp.stack(vectors)
    is_gate = lax.broadcasted_iota(jnp.int32, (1, 5 * channels), 1) // channels
    halves = jnp.where((is_gate == 0) | (is_gate == 2), 1.0, 0.5).astype(bf16)
    edge_weights = jnp.concatenate([w_edges, w_tri_gate], axis=1) * halves
    valid_column = jnp.broadcast_to(residue_valid.astype(f32)[:, None], (res, channels))

    head = lax.broadcasted_iota(jnp.int32, (HEADS, channels), 0)
    head_of_channel = lax.broadcasted_iota(jnp.int32, (HEADS, channels), 1) // HEAD_DIM
    repeat = jnp.where(head == head_of_channel, 1.0, 0.0).astype(bf16)
    wide_bias = dot(w_pair_bias, repeat).astype(bf16)

    kept = lax.dynamic_update_slice(
        jnp.zeros((2 * row_count, res, channels), bf16), pair_rep, (0, 0, 0)
    )
    far = exchange(pair_rep, devices // 2)
    far, kept, norms, edge_weights = lax.optimization_barrier((far, kept, norms, edge_weights))
    own = lax.dynamic_update_slice(kept, far, (row_count, 0, 0))
    own_blocks = (0, chips // 2)

    def blocks_from(bits):
        return tuple(s ^ bits for s in own_blocks)

    tall = shaped(f32, half * res, channels)

    def edges_of(pieces, done, send_row, *held):
        pairs = tuple(p for p, _ in pieces)
        blocks = tuple(b for _, b in pieces)
        operands = (valid_column, norms, edge_weights) + pairs + held
        return call(
            functools.partial(edges_kernel, row_count, chips, blocks, done, send_row, not held),
            (tall, tall, tall, tall, shaped(bf16, 4 * row_count, res, channels))
            + (() if held else (shaped(bf16, 2 * channels, 2 * channels),)),
            operands,
        )

    diagonal = exchange(own, 6)
    beside = exchange(own, 2)
    near = exchange(own, 4)
    *edges, early_right, same_head = edges_of([(own, own_blocks)], (), 0)
    diagonal, edges = lax.optimization_barrier((diagonal, edges))
    *edges, early_right = edges_of(
        [(diagonal, blocks_from(3))], own_blocks, 2 * row_count, *edges, early_right
    )
    beside, edges, early_right, wide_bias = lax.optimization_barrier(
        (beside, edges, early_right, wide_bias)
    )
    early = (exchange(early_right, 1), own_blocks + blocks_from(3))
    *edges, late_right = edges_of(
        [(beside, blocks_from(1)), (near, blocks_from(2))], early[1], 0, *edges
    )
    late = (exchange(late_right, 1), blocks_from(1) + blocks_from(2))

    left, right, gate, pairs = edges
    triangle, across = call(
        functools.partial(near_triangle_kernel, row_count, chips, half // 2, [early[1]]),
        (tall, tall),
        (left, right, early[0]),
    )
    part = half // 2 * res
    in_part, own_shape = shaped(f32, part, channels), shaped(f32, row_count * res, channels)
    att_part = shaped(bf16, part, channels)
    shared = (norms, w_tri_out, left, gate, pairs)
    scratch = (pltpu.VMEM((part, channels), f32),)
    across, after_a, att_a = call(
        functools.partial(own_inputs_kernel, row_count, chips, (early[1], late[1])),
        (tall, in_part, att_part),
        shared + (late[0], triangle, across),
        scratch=scratch,
    )
    far_att_a = exchange(att_a, 1)
    att_b = call(
        functools.partial(other_inputs_kernel, row_count, chips),
        att_part,
        shared + (triangle, across),
        scratch=scratch,
    )
    far_att_b = exchange(att_b, 1)

    def attention_scratch(keys, projected):
        return (
            pltpu.VMEM((-(-keys // 8) * 8 * res, channels), f32),
            pltpu.VMEM((projected * res, channels), f32),
            pltpu.VMEM((projected * res, channels), f32),
            pltpu.VMEM((row_count, 40, channels), f32),
        )

    sums, query, att_gate, after_own = call(
        functools.partial(most_attention_kernel, row_count, chips),
        (shaped(f32, row_count, 3, res, channels), own_shape, own_shape, own_shape),
        (valid_column, same_head, w_query, w_att_gate, w_key, w_value, wide_bias)
        + (att_a, att_b, far_att_a, after_a),
        scratch=attention_scratch(3 * half // 2, 3 * half // 2),
    )
    return call(
        functools.partial(attention_kernel, row_count, chips),
        shaped(bf16, *pair_rep.shape),
        (valid_column, same_head, w_key, w_value, w_att_out, wide_bias, far_att_b)
        + (query, att_gate, after_own, sums),
        scratch=attention_scratch(half // 2, half // 2),
    )


def per_device(pair_rep, residue_valid, *parameters):
    row_count, res, channels = pair_rep.shape
    devices = res // row_count
    if res % 48 == 0 and devices == 16 and 40 * res * res * channels <= 32 * 1024 * 1024:
        return on_whole_complex(pair_rep, residue_valid, *parameters)
    return split_over_devices(pair_rep, residue_valid, *parameters)


def solution(mesh):
    return jax.shard_map(
        per_device,
        mesh=mesh,
        in_specs=(
            P(("groups", "row"), None, None),
            P("groups"),
            P(),
            P(),
            P(),
            P(),
            P(),
            P(),
            P(),
            P(),
            P(),
            P(),
            P(),
            P(),
            P(),
            P(),
            P(),
        ),
        out_specs=P(("groups", "row"), None, None),
        check_vma=False,
    )
```
